32 devices in a mesh: ens: 2 (over x), tile: 16 (over z, y, core).
Axes of the slice: x: 2, y: 2, z: 4, core: 2. Of those that a mesh axis runs over, the one named last changes fastest.
Arguments:
- rain: bfloat16 [8192, 256], P(('ens', 'tile')), parts along dimension 0, may hold values from 0.049804688 to 8
- soil: float32 [8192], P(('ens', 'tile')), parts along dimension 0, may hold values from 0.5 to 4
- tile_area: float32 [8192], P(('ens', 'tile')), parts along dimension 0, may hold values from 0.25 to 2
- tile_dest: int32 [8192, 1], P(('ens', 'tile')), parts along dimension 0, may hold values from 0 to 15; in each aligned block of 256 rows (0 to 255, 256 to 511, ...) at most 32 rows name the same one
- tile_reach: int32 [8192], P(('ens', 'tile')), parts along dimension 0, may hold values from 0 to 255
- reach_basin: int32 [8192], P(('ens', 'tile')), parts along dimension 0, may hold values from 0 to 31
- reach_kind: int32 [8192], P(('ens', 'tile')), parts along dimension 0, may hold values from 0 to 7
- reach_lag: int32 [8192], P(('ens', 'tile')), parts along dimension 0, may hold values from 0 to 72
- irf: float32 [8, 48], replicated, may hold values from 0.004166667 to 0.041666668
- outlet_level: int32 [1024], P(('ens', 'tile')), parts along dimension 0, may hold values from 0 to 2, as said below
- outlet_parent: int32 [1024], P(('ens', 'tile')), parts along dimension 0, may hold values from -1 to 511, as said below
Outputs:
- section: float32 [1024, 256], P(('ens', 'tile')), parts along dimension 0
The draws below stay inside these ranges and needn't reach their ends.
There are 2 independent parts, one for each index of `ens`. The reference program is written for one: setup_inputs(seed, part) draws one part's arguments, and reference() takes and returns one part's arrays. A program takes and returns all parts, laid end to end along the dimension named above; an argument that names none is the same for every part. Nothing has to cross between parts.
Inputs may be any that keep to these rules, and one draw needn't show every extreme that they name: `tile_dest`: among the rows of one device, at most 32 name the same owner. `outlet_level`: on every device, half of the 32 outlets have level 0, a quarter level 1 and a quarter level 2. `outlet_parent`: an outlet of level 0 drains to an outlet of level 1, one of level 1 to one of level 2, and one of level 2 has -1. Of the outlets of one level on one device, at most 2 drain to outlets of one device; for each of the levels 0 and 1 some device receives exactly 2 from every device.
All inputs are finite; a program needn't handle non-finite values.
Results may differ from the reference program's by a relative error of at most 0.0003.
Values may be sent and summed in bfloat16 or wider, within the bound.
No kernel may reach another device: no remote copies, remote signals or barrier semaphores. Data moves between devices by JAX's collectives and lax.ppermute only.
A program may use at most 64 MiB of HBM per device.

```python
import math
import jax
import jax.numpy as jnp
import numpy as np
from jax import lax

TILE_DEV = 256
HOURS = 256
R_DEV = 256
B_DEV = 32
KINDS = 8
KLEN = 48
MAXLAG = 72
LINK = 6
CAP = 32
CAPT = 2
TILES = 4096
REACHES = 4096
OUTLETS = 512
N_TILE = 16


def tree_layout(key):
    owners = OUTLETS // B_DEV
    first_count = B_DEV // 2
    second_count = B_DEV // 4
    subkeys = jax.random.split(key, 7)
    orders = jax.vmap(lambda subkey: jax.random.permutation(subkey, B_DEV))(jax.random.split(subkeys[0], owners)).astype(jnp.int32)
    rank_index = jnp.arange(B_DEV, dtype=jnp.int32)
    rank_level = jnp.where(rank_index < first_count, 0, jnp.where(rank_index < first_count + second_count, 1, 2)).astype(jnp.int32)
    row_index = jnp.broadcast_to(jnp.arange(owners, dtype=jnp.int32)[:, None], (owners, B_DEV))
    levels = jnp.zeros((owners, B_DEV), jnp.int32).at[row_index, orders].set(jnp.broadcast_to(rank_level, (owners, B_DEV)))

    def parents_of(level_count, base, pool_count, hub_key, spread_key, pick_key):
        hub_owner = jax.random.randint(hub_key, (), 0, owners)
        spread = jax.random.permutation(spread_key, owners - 1).astype(jnp.int32)
        group_index = jnp.arange(level_count, dtype=jnp.int32) // CAPT
        sources = jnp.arange(owners, dtype=jnp.int32)[:, None]
        elsewhere = (hub_owner + 1 + (sources + spread[group_index][None, :]) % (owners - 1)) % owners
        targets = jnp.where(group_index[None, :] == 0, hub_owner, elsewhere)
        picked = jax.random.randint(pick_key, (owners, level_count), 0, pool_count)
        parent_pos = orders[targets, base + picked]
        return targets * B_DEV + parent_pos
    first_parent = parents_of(first_count, first_count, second_count, subkeys[1], subkeys[2], subkeys[3])
    second_parent = parents_of(second_count, first_count + second_count, second_count, subkeys[4], subkeys[5], subkeys[6])
    rank_parent = jnp.concatenate([first_parent, second_parent, jnp.full((owners, second_count), -1, jnp.int32)], axis=1)
    parents = jnp.zeros((owners, B_DEV), jnp.int32).at[row_index, orders].set(rank_parent)
    return (levels.reshape(-1), parents.reshape(-1))


def draw_outlet_level(key, part):
    return tree_layout(key)[0]


def draw_outlet_parent(key, part):
    return tree_layout(key)[1]


def plant(drawn, stream_key, least, largest):
    index_at = [jax.random.randint(jax.random.fold_in(stream_key, axis), (), 0, length) for axis, length in enumerate(drawn.shape)]
    widest = drawn.shape.index(max(drawn.shape))
    next_to = index_at[:widest] + [(index_at[widest] + 1) % drawn.shape[widest]] + index_at[widest + 1:]
    return drawn.at[tuple(index_at)].set(least).at[tuple(next_to)].set(largest)


def steps_of(own_key, dims, shards, low, top_value):
    factor_of, own = 1.0, jax.random.fold_in(own_key, 6)
    for axis_at, parts in shards:
        steps = jnp.exp(jax.random.uniform(jax.random.fold_in(own, axis_at), (parts,), jnp.float32, low / len(shards), top_value / len(shards)))
        factor_of = factor_of * jnp.repeat(steps, dims[axis_at] // parts).reshape([-1 if axis == axis_at else 1 for axis in range(len(dims))])
    return factor_of


def shared_out(rng, own, number, rows, amount, top, reach, lean):
    order = jax.random.permutation(rng, amount)
    heavy_load, common = shares(amount, rows * top, reach, lean, True), shares(amount, rows * top, reach, lean, False)
    places = jnp.arange(amount)

    def named(lengths, offset_by):
        used = int((lengths > 0).sum())
        fixed = max(1, used // 4)
        passed = fixed + (places - fixed + offset_by * (used - fixed)) % max(1, amount - fixed)
        return jnp.zeros((amount,), jnp.int32).at[order[jnp.where(places < fixed, places, passed)]].set(jnp.asarray(lengths, jnp.int32))

    lengths = jnp.where(number % 4 == 0, named(heavy_load, number // 4), named(common, number - number // 4 - 1))
    mixed = jax.random.permutation(jax.random.fold_in(own, 3), amount)
    source_of, receiver = mixed[0:amount // 2 * 2:2], mixed[1:amount // 2 * 2:2]
    slack = jnp.minimum(lengths[source_of] - 1, reach - lengths[receiver]) // 2
    slack = jnp.where((source_of == order[0]) | (receiver == order[0]) | (lengths[receiver] == 0), 0, jnp.maximum(slack, 0))
    passed = jax.random.randint(jax.random.fold_in(own, 4), (amount // 2,), 0, 1 << 20) % (slack + 1)
    lengths = lengths.at[source_of].add(-passed).at[receiver].add(passed)
    labels = jnp.searchsorted(jnp.cumsum(lengths), jnp.arange(rows * top), side="right").astype(jnp.int32)
    grid = labels.reshape(top, rows).T
    grid = grid[jax.random.permutation(jax.random.fold_in(own, 1), rows)]
    offset_by = jax.random.randint(jax.random.fold_in(own, 2), (rows, 1), 0, top)
    return jnp.take_along_axis(grid, (jnp.arange(top)[None, :] + offset_by) % top, axis=1)


def shares(count, total, reach, skew, full):
    weights = [(1 << 20) // math.isqrt(standing ** skew) + 1 for standing in range(1, count + 1)]
    largest = reach if full else min(reach, max(-(-total // count), total * weights[0] // sum(weights)))
    least = 1 if total - largest >= count - 1 else 0
    counts, surplus = [largest] + [least] * (count - 1), total - largest - least * (count - 1)
    while surplus > 0:
        free = [i for i in range(1, count) if counts[i] < largest] or [i for i in range(1, count) if counts[i] < reach]
        mass, remaining = sum([weights[i] for i in free]), surplus
        for i in free:
            extra = min(reach - counts[i], max(1, remaining * weights[i] // mass), surplus)
            counts[i] = counts[i] + extra
            surplus = surplus - extra
    return np.array(counts)


def setup_inputs(seed: int = 0, part: int = 0) -> dict:
    streams_of = jax.random.split(jax.random.key(seed), 12)
    part_splits = jax.random.split(jax.random.fold_in(streams_of[11], part), 12)
    rain = jnp.clip(jnp.exp(math.log(8.0) - 5.0790877 * jax.random.uniform(part_splits[0], (TILES, HOURS), jnp.float32) ** steps_of(part_splits[0], (TILES, HOURS), ((0, 16),), -0.2, 0.2)), 0.049804688, 8.0).astype(jnp.bfloat16)
    soil = jnp.clip(jnp.exp(math.log(4.0) - 2.0794415 * jax.random.uniform(part_splits[1], (TILES,), jnp.float32) ** steps_of(part_splits[1], (TILES,), ((0, 16),), -0.2, 0.2)), 0.5, 4.0)
    tile_area = jnp.clip(jnp.exp(math.log(2.0) - 2.0794415 * jax.random.uniform(part_splits[2], (TILES,), jnp.float32) ** steps_of(part_splits[2], (TILES,), ((0, 16),), -0.2, 0.2)), 0.25, 2.0)
    tile_dest_keys = jax.random.split(jax.random.fold_in(part_splits[3], 1), TILES // TILE_DEV)
    tile_dest_turns = jax.random.permutation(jax.random.fold_in(part_splits[3], 3), TILES // TILE_DEV)
    tile_dest = jax.vmap(lambda own, number: shared_out(jax.random.fold_in(part_splits[3], 2), own, number, TILE_DEV, N_TILE, 1, CAP, 2))(tile_dest_keys, tile_dest_turns).reshape((TILES, 1))
    tile_reach = plant(jax.random.randint(part_splits[4], (TILES,), 0, R_DEV), jax.random.fold_in(part_splits[4], 1), 0, R_DEV - 1).astype(jnp.int32)
    reach_basin = plant(jax.random.randint(part_splits[5], (REACHES,), 0, B_DEV), jax.random.fold_in(part_splits[5], 1), 0, B_DEV - 1).astype(jnp.int32)
    reach_kind = plant(jax.random.randint(part_splits[6], (REACHES,), 0, KINDS), jax.random.fold_in(part_splits[6], 1), 0, KINDS - 1).astype(jnp.int32)
    reach_lag = plant(jax.random.randint(part_splits[7], (REACHES,), 0, MAXLAG + 1), jax.random.fold_in(part_splits[7], 1), 0, MAXLAG).astype(jnp.int32)
    irf = jnp.clip(jnp.exp(jax.random.uniform(streams_of[8], (KINDS, KLEN), jnp.float32, math.log(0.004166667), math.log(0.041666668))), 0.004166667, 0.041666668)
    outlet_level = draw_outlet_level(jax.random.fold_in(jax.random.fold_in(streams_of[11], part), 71), part)
    outlet_parent = draw_outlet_parent(jax.random.fold_in(jax.random.fold_in(streams_of[11], part), 71), part)
    return {"rain": rain, "soil": soil, "tile_area": tile_area, "tile_dest": tile_dest, "tile_reach": tile_reach, "reach_basin": reach_basin, "reach_kind": reach_kind, "reach_lag": reach_lag, "irf": irf, "outlet_level": outlet_level, "outlet_parent": outlet_parent}


def delayed(values, delay):
    padding = jnp.zeros(values.shape[:-1] + (delay,), values.dtype)
    return jnp.concatenate([padding, values[..., :values.shape[-1] - delay]], axis=-1)


def reference(rain, soil, tile_area, tile_dest, tile_reach, reach_basin, reach_kind, reach_lag, irf, outlet_level, outlet_parent):
    rainfall = rain.astype(jnp.float32)
    storage = soil[:, None]
    excess = jnp.maximum(rainfall - 0.2 * storage, 0.0)
    runoff_rows = (tile_area[:, None] * excess * excess / (rainfall + 0.8 * storage)).astype(jnp.bfloat16)
    reach_id = (tile_dest[:, 0] * R_DEV + tile_reach).astype(jnp.int32)
    inflow = jax.ops.segment_sum(runoff_rows.astype(jnp.float32), reach_id, num_segments=REACHES)
    hour_index = jnp.arange(HOURS, dtype=jnp.int32)
    source_hour = hour_index[None, :] - reach_lag[:, None]
    lagged = jnp.where(source_hour >= 0, jnp.take_along_axis(inflow, jnp.maximum(source_hour, 0).astype(jnp.int32), axis=1), 0.0)
    owner_index = jnp.arange(REACHES, dtype=jnp.int32) // R_DEV
    group_index = ((owner_index * B_DEV + reach_basin) * KINDS + reach_kind).astype(jnp.int32)
    pooled = jax.ops.segment_sum(lagged, group_index, num_segments=OUTLETS * KINDS).reshape(OUTLETS, KINDS, HOURS)
    padded = jnp.pad(pooled, ((0, 0), (0, 0), (KLEN - 1, 0)))
    outflow = jnp.zeros((OUTLETS, HOURS), jnp.float32)
    for tap_index in range(KLEN):
        window = padded[:, :, KLEN - 1 - tap_index:KLEN - 1 - tap_index + HOURS]
        outflow = outflow + jnp.einsum("okt,k->ot", window, irf[:, tap_index], precision=lax.Precision.HIGHEST)
    for tree_level in range(2):
        chosen = outlet_level == tree_level
        moving = jnp.where(chosen[:, None], delayed(outflow, LINK), 0.0)
        target = jnp.where(chosen, outlet_parent, OUTLETS).astype(jnp.int32)
        outflow = outflow + jax.ops.segment_sum(moving, target, num_segments=OUTLETS + 1)[:OUTLETS]
    return jnp.log(1.0 + outflow)
```

```python
import jax
import jax.numpy as jnp
from jax import lax
from jax.experimental import pallas as pl
from jax.experimental.pallas import tpu as pltpu
from jax.sharding import PartitionSpec as P

LINK = 6
LANES = 128
VMEM_BYTES = 40 * 1024 * 1024

NT = (((1,), (1,)), ((), ()))
NN = (((1,), (0,)), ((), ()))


def iota(shape, axis):
    return lax.broadcasted_iota(jnp.int32, shape, axis)


def split(values):
    high = values.astype(jnp.bfloat16)
    return high, (values - high.astype(jnp.float32)).astype(jnp.bfloat16)


def later(values, hours):
    rows = values.shape[0]
    if hours % 8 == 0:
        padding = jnp.zeros((hours, values.shape[1]), values.dtype)
        return jnp.concatenate([padding, values[: rows - hours]], axis=0)
    return jnp.where(iota(values.shape, 0) < hours, 0.0, pltpu.roll(values, hours, 0))


def prepare_kernel(rain_ref, soil_ref, area_ref, irf_ref, runoff_ref, response_ref):
    hours = rain_ref.shape[1]
    kinds, taps = irf_ref.shape
    rainfall = rain_ref[...].astype(jnp.float32).T
    storage = soil_ref[...]
    excess = jnp.maximum(rainfall - 0.2 * storage, 0.0)
    runoff = area_ref[...] * excess * excess / (rainfall + 0.8 * storage)
    runoff_ref[...] = runoff.astype(jnp.bfloat16).astype(jnp.float32)
    backward = (
        iota((taps, hours), 1) == lax.rem(hours - iota((taps, hours), 0), hours)
    ).astype(jnp.float32)
    reversed_taps = lax.dot_general(
        irf_ref[...], backward, NN, precision=lax.Precision.HIGHEST, preferred_element_type=jnp.float32
    )
    causal = iota((hours, hours), 1) <= iota((hours, hours), 0)
    for kind in range(kinds):
        row = jnp.broadcast_to(reversed_taps[kind : kind + 1], (hours, hours))
        matrix = jnp.where(causal, pltpu.roll(row, 0, 1, stride=1, stride_axis=0), 0.0)
        high, low = split(matrix)
        response_ref[:hours, kind * hours : (kind + 1) * hours] = high
        response_ref[hours:, kind * hours : (kind + 1) * hours] = low


def route_kernel(
    runoff_ref, response_ref, meta_ref, dest_ref, reach_ref, flow_ref, *, kinds, reach_rows, basin_rows
):
    hours, tiles = runoff_ref.shape
    owners = meta_ref.shape[0]
    outlets = owners * basin_rows
    shift = basin_rows.bit_length() - 1
    dest = dest_ref[...]
    reach = reach_ref[...]

    def table(first, count):
        return jnp.concatenate([meta_ref[:, first + j, :] for j in range(count)], axis=1)

    spans = reach_rows // LANES
    basin_table = table(0, spans)
    kind_table = table(spans, spans)
    lag_table = table(2 * spans, spans)
    parent_table = meta_ref[:, 3 * spans, :]
    group_table = basin_table * kinds + kind_table
    reach_table = (
        jnp.concatenate([group_table, lag_table], axis=1).astype(jnp.float32).T.astype(jnp.bfloat16)
    )
    tree_table = jnp.concatenate(
        [lax.shift_right_arithmetic(parent_table, shift) + 1, parent_table & (basin_rows - 1)], axis=1
    )
    tree_table = tree_table.astype(jnp.float32).T.astype(jnp.bfloat16)

    def marks(row, count, offset=0):
        return (iota((count, tiles), 0) + offset == row).astype(jnp.float32).astype(jnp.bfloat16)

    def picked(values, chosen):
        return jnp.sum(jnp.where(chosen, values, 0.0), axis=0, keepdims=True).astype(jnp.int32)

    def lookup(table_rows, mark):
        return lax.dot_general(table_rows, mark, NN, preferred_element_type=jnp.float32)

    owner_marks = marks(dest, owners)
    by_reach = lookup(reach_table, owner_marks)
    at_reach = iota((reach_rows, tiles), 0) == reach
    group = picked(by_reach[:reach_rows], at_reach)
    lag = picked(by_reach[reach_rows:], at_reach)
    basin = group // kinds
    kind = group - basin * kinds

    def parent_of(owner_mark, local):
        by_basin = lookup(tree_table, owner_mark)
        at_basin = iota((basin_rows, tiles), 0) == local
        return (
            picked(by_basin[:basin_rows], at_basin),
            picked(by_basin[LANES : LANES + basin_rows], at_basin),
        )

    parent_owner, parent_local = parent_of(owner_marks, basin)
    second_owner, second_local = parent_of(marks(parent_owner, owners, 1), parent_local)
    targets = [
        dest * basin_rows + basin,
        (parent_owner - 1) * basin_rows + parent_local,
        (second_owner - 1) * basin_rows + second_local,
    ]

    lagged = runoff_ref[...]
    step = 64
    while step:
        lagged = jnp.where((lag & step) != 0, later(lagged, step), lagged)
        step //= 2
    lagged = lagged.astype(jnp.bfloat16)
    by_kind = jnp.concatenate(
        [
            lagged * (kind == k).astype(jnp.float32).astype(jnp.bfloat16)
            for k in range(kinds)
        ],
        axis=0,
    )
    routed = lax.dot_general(response_ref[...], by_kind, NN, preferred_element_type=jnp.float32)
    routed = routed[:hours] + routed[hours:]
    pieces, placements = [], []
    for target in targets:
        pieces.extend(split(routed))
        mark = marks(target, outlets)
        placements.extend([mark, mark])
        routed = later(routed, LINK)
    flow_ref[...] = lax.dot_general(
        jnp.concatenate(placements, axis=1),
        jnp.concatenate(pieces, axis=1),
        NT,
        preferred_element_type=jnp.float32,
    )


def finish_kernel(parts_ref, section_ref):
    section_ref[...] = jnp.log(1.0 + jnp.sum(parts_ref[...], axis=0))


def per_device(
    rain,
    soil,
    tile_area,
    tile_dest,
    tile_reach,
    reach_basin,
    reach_kind,
    reach_lag,
    irf,
    outlet_level,
    outlet_parent,
):
    owners = lax.axis_size("tile")
    tile_rows, hours = rain.shape
    basin_rows = outlet_parent.shape[0]
    kinds = irf.shape[0]
    params = pltpu.CompilerParams(vmem_limit_bytes=VMEM_BYTES)

    meta = jnp.concatenate(
        [
            reach_basin,
            reach_kind,
            reach_lag,
            outlet_parent,
            jnp.zeros((2 * LANES - basin_rows,), jnp.int32),
        ]
    ).reshape(-1, LANES)
    meta = lax.all_to_all(
        jnp.broadcast_to(meta[None], (owners,) + meta.shape), "tile", split_axis=0, concat_axis=0, tiled=True
    )

    runoff, response = pl.pallas_call(
        prepare_kernel,
        out_shape=(
            jax.ShapeDtypeStruct((hours, tile_rows), jnp.float32),
            jax.ShapeDtypeStruct((2 * hours, kinds * hours), jnp.bfloat16),
        ),
        compiler_params=params,
        name="prepare",
    )(rain, soil.reshape(1, -1), tile_area.reshape(1, -1), irf)

    flow = pl.pallas_call(
        lambda *refs: route_kernel(
            *refs, kinds=kinds, reach_rows=reach_basin.shape[0], basin_rows=basin_rows
        ),
        out_shape=jax.ShapeDtypeStruct((owners * basin_rows, hours), jnp.float32),
        compiler_params=params,
        name="route",
    )(runoff, response, meta, tile_dest.reshape(1, -1), tile_reach.reshape(1, -1))

    parts = lax.all_to_all(
        flow.reshape(owners, basin_rows, hours), "tile", split_axis=0, concat_axis=0, tiled=True
    )
    return pl.pallas_call(
        finish_kernel,
        out_shape=jax.ShapeDtypeStruct((basin_rows, hours), jnp.float32),
        compiler_params=params,
        name="finish",
    )(parts)


def solution(mesh):
    rows = P(("ens", "tile"))
    table = P(("ens", "tile"), None)
    in_specs = (table, rows, rows, table, rows, rows, rows, rows, P(), rows, rows)
    return jax.shard_map(
        per_device, mesh=mesh, in_specs=in_specs, out_specs=table, check_vma=False
    )
```

```python
import math

import jax
import jax.numpy as jnp
from jax import lax
from jax.experimental import pallas as pl
from jax.experimental.pallas import tpu as pltpu
from jax.sharding import PartitionSpec as P

LINK = 6
LANES = 128
VMEM_BYTES = 40 * 1024 * 1024
CODE_TOP = 32767
CODE_OCTAVES = 44
CODE_LOWEST = -26
CODE_SCALE = 2 * CODE_TOP / (CODE_OCTAVES * math.log(2.0))
CODE_LEAST = 2.0**CODE_LOWEST
CODE_ZERO = -CODE_TOP + 1 - CODE_LOWEST * math.log(2.0) * CODE_SCALE

NT = (((1,), (1,)), ((), ()))
NN = (((1,), (0,)), ((), ()))


def iota(shape, axis):
    return lax.broadcasted_iota(jnp.int32, shape, axis)


def split(values):
    high = values.astype(jnp.bfloat16)
    return high, (values - high.astype(jnp.float32)).astype(jnp.bfloat16)


def later(values, hours):
    rows = values.shape[0]
    if hours % 8 == 0:
        padding = jnp.zeros((hours, values.shape[1]), values.dtype)
        return jnp.concatenate([padding, values[: rows - hours]], axis=0)
    return jnp.where(iota(values.shape, 0) < hours, 0.0, pltpu.roll(values, hours, 0))


def prepare_kernel(
    rain_hbm, soil_hbm, area_hbm, dest_hbm, reach_hbm, irf_hbm,
    runoff_ref, response_ref, dest_ref, reach_ref,
    rain_ref, soil_ref, area_ref, irf_ref, arrived,
):
    copies = [
        pltpu.make_async_copy(source, target, arrived.at[j])
        for j, (source, target) in enumerate(
            [
                (rain_hbm, rain_ref),
                (soil_hbm, soil_ref),
                (area_hbm, area_ref),
                (irf_hbm, irf_ref),
                (dest_hbm, dest_ref),
                (reach_hbm, reach_ref),
            ]
        )
    ]
    for copy in copies:
        copy.start()
    for copy in copies:
        copy.wait()
    hours = rain_ref.shape[1]
    kinds, taps = irf_ref.shape
    rainfall = rain_ref[...].astype(jnp.float32).T
    storage = soil_ref[...]
    excess = jnp.maximum(rainfall - 0.2 * storage, 0.0)
    runoff = area_ref[...] * excess * excess / (rainfall + 0.8 * storage)
    runoff_ref[...] = runoff.astype(jnp.bfloat16).astype(jnp.float32)
    backward = (
        iota((taps, hours), 1) == lax.rem(hours - iota((taps, hours), 0), hours)
    ).astype(jnp.float32)
    reversed_taps = lax.dot_general(
        irf_ref[...], backward, NN, precision=lax.Precision.HIGHEST, preferred_element_type=jnp.float32
    )
    causal = iota((hours, hours), 1) <= iota((hours, hours), 0)
    for kind in range(kinds):
        row = jnp.broadcast_to(reversed_taps[kind : kind + 1], (hours, hours))
        matrix = jnp.where(causal, pltpu.roll(row, 0, 1, stride=1, stride_axis=0), 0.0)
        high, low = split(matrix)
        response_ref[:hours, kind * hours : (kind + 1) * hours] = high
        response_ref[hours:, kind * hours : (kind + 1) * hours] = low


def route_kernel(*refs, kinds, reach_rows, basin_rows):
    *piece_refs, runoff_ref, response_ref, dest_ref, reach_ref, flow_ref = refs
    hours, tiles = runoff_ref.shape
    owners = len(piece_refs)
    outlets = owners * basin_rows
    shift = basin_rows.bit_length() - 1
    me = lax.axis_index("tile")
    dest = dest_ref[...]
    reach = reach_ref[...]

    stack = jnp.concatenate([piece[...] for piece in piece_refs], axis=0)
    spans = reach_rows // LANES
    fields = piece_refs[0].shape[0]
    field = iota(stack.shape, 0) % fields
    stack = jnp.where(field == 3 * spans, lax.shift_right_arithmetic(stack, shift) + 1, stack)
    stack = jnp.where(field == 3 * spans + 1, stack & (basin_rows - 1), stack)
    stack = stack.astype(jnp.float32).T.astype(jnp.bfloat16)

    def marks(row, count):
        return (iota((count, tiles), 0) == row).astype(jnp.float32).astype(jnp.bfloat16)

    def picked(values, chosen):
        return jnp.sum(jnp.where(chosen, values, 0.0), axis=0, keepdims=True).astype(jnp.int32)

    def lookup(owner, first, count):
        place = lax.rem(me - owner + owners, owners) * fields
        place = jnp.where(owner < 0, -fields, place)
        mark = jnp.concatenate([marks(place + first + j, owners * fields) for j in range(count)], axis=1)
        found = lax.dot_general(stack, mark, NN, preferred_element_type=jnp.float32)
        return [found[:, j * tiles : (j + 1) * tiles] for j in range(count)]

    by_reach = lookup(dest, 0, 3 * spans)
    at_reach = [iota((LANES, tiles), 0) + j * LANES == reach for j in range(spans)]
    basin, kind, lag = [
        sum(picked(by_reach[c * spans + j], at_reach[j]) for j in range(spans)) for c in range(3)
    ]

    def parent_of(owner, local):
        by_basin = lookup(owner, 3 * spans, 2)
        at_basin = iota((LANES, tiles), 0) == local
        return picked(by_basin[0], at_basin) - 1, picked(by_basin[1], at_basin)

    parent_owner, parent_local = parent_of(dest, basin)
    second_owner, second_local = parent_of(parent_owner, parent_local)
    targets = [
        dest * basin_rows + basin,
        parent_owner * basin_rows + parent_local,
        second_owner * basin_rows + second_local,
    ]

    lagged = runoff_ref[...]
    step = 64
    while step:
        lagged = jnp.where((lag & step) != 0, later(lagged, step), lagged)
        step //= 2
    lagged = lagged.astype(jnp.bfloat16)
    by_kind = jnp.concatenate(
        [
            lagged * (kind == k).astype(jnp.float32).astype(jnp.bfloat16)
            for k in range(kinds)
        ],
        axis=0,
    )
    routed = lax.dot_general(response_ref[...], by_kind, NN, preferred_element_type=jnp.float32)
    routed = routed[:hours] + routed[hours:]
    pieces, placements = [], []
    for target in targets:
        pieces.extend(split(routed))
        mark = marks(target, outlets)
        placements.extend([mark, mark])
        routed = later(routed, LINK)
    flow = lax.dot_general(
        jnp.concatenate(placements, axis=1),
        jnp.concatenate(pieces, axis=1),
        NT,
        preferred_element_type=jnp.float32,
    )
    level = jnp.log(jnp.maximum(flow, CODE_LEAST)) * CODE_SCALE + CODE_ZERO
    level = jnp.minimum(jnp.round(level), CODE_TOP).astype(jnp.int32)
    flow_ref[...] = jnp.where(flow < CODE_LEAST, -CODE_TOP, level).astype(jnp.int16)


def finish_kernel(parts_ref, section_ref):
    level = parts_ref[...].astype(jnp.int32)
    flow = jnp.exp((level.astype(jnp.float32) - CODE_ZERO) * (1.0 / CODE_SCALE))
    flow = jnp.sum(jnp.where(level == -CODE_TOP, 0.0, flow), axis=0)
    section_ref[...] = jnp.log(1.0 + flow)


def per_device(
    rain,
    soil,
    tile_area,
    tile_dest,
    tile_reach,
    reach_basin,
    reach_kind,
    reach_lag,
    irf,
    outlet_level,
    outlet_parent,
):
    owners = lax.axis_size("tile")
    tile_rows, hours = rain.shape
    basin_rows = outlet_parent.shape[0]
    kinds = irf.shape[0]
    params = pltpu.CompilerParams(vmem_limit_bytes=VMEM_BYTES)

    parent_rows = jnp.pad(outlet_parent, (0, LANES - basin_rows))
    meta = jnp.concatenate([reach_basin, reach_kind, reach_lag, parent_rows, parent_rows])
    meta = meta.reshape(-1, LANES)
    metas = [meta] + [
        lax.ppermute(meta, "tile", [(i, (i + step) % owners) for i in range(owners)])
        for step in range(1, owners)
    ]

    held = pl.BlockSpec(memory_space=pltpu.HBM)
    row = (1, tile_rows)
    runoff, response, dest, reach = pl.pallas_call(
        prepare_kernel,
        out_shape=(
            jax.ShapeDtypeStruct((hours, tile_rows), jnp.float32),
            jax.ShapeDtypeStruct((2 * hours, kinds * hours), jnp.bfloat16),
            jax.ShapeDtypeStruct(row, jnp.int32),
            jax.ShapeDtypeStruct(row, jnp.int32),
        ),
        in_specs=[held] * 6,
        scratch_shapes=[
            pltpu.VMEM(rain.shape, rain.dtype),
            pltpu.VMEM(row, jnp.float32),
            pltpu.VMEM(row, jnp.float32),
            pltpu.VMEM(irf.shape, jnp.float32),
            pltpu.SemaphoreType.DMA((6,)),
        ],
        compiler_params=params,
        name="prepare",
    )(
        rain,
        soil.reshape(row),
        tile_area.reshape(row),
        tile_dest.reshape(row),
        tile_reach.reshape(row),
        irf,
    )

    flow = pl.pallas_call(
        lambda *refs: route_kernel(
            *refs, kinds=kinds, reach_rows=reach_basin.shape[0], basin_rows=basin_rows
        ),
        out_shape=jax.ShapeDtypeStruct((owners * basin_rows, hours), jnp.int16),
        compiler_params=params,
        name="route",
    )(*metas, runoff, response, dest, reach)

    parts = lax.all_to_all(
        flow.reshape(owners, basin_rows, hours), "tile", split_axis=0, concat_axis=0, tiled=True
    )
    return pl.pallas_call(
        finish_kernel,
        out_shape=jax.ShapeDtypeStruct((basin_rows, hours), jnp.float32),
        compiler_params=params,
        name="finish",
    )(parts)


def solution(mesh):
    rows = P(("ens", "tile"))
    table = P(("ens", "tile"), None)
    in_specs = (table, rows, rows, table, rows, rows, rows, rows, P(), rows, rows)
    return jax.shard_map(
        per_device, mesh=mesh, in_specs=in_specs, out_specs=table, check_vma=False
    )
```

```python
import math

import jax
import jax.numpy as jnp
from jax import lax
from jax.experimental import pallas as pl
from jax.experimental.pallas import tpu as pltpu
from jax.sharding import PartitionSpec as P

LINK = 6
LANES = 128
VMEM_BYTES = 40 * 1024 * 1024
CODE_TOP = 32767
CODE_OCTAVES = 44
CODE_LOWEST = -26
CODE_SCALE = 2 * CODE_TOP / (CODE_OCTAVES * math.log(2.0))
CODE_LEAST = 2.0**CODE_LOWEST
CODE_ZERO = -CODE_TOP + 1 - CODE_LOWEST * math.log(2.0) * CODE_SCALE

NT = (((1,), (1,)), ((), ()))
NN = (((1,), (0,)), ((), ()))


def iota(shape, axis):
    return lax.broadcasted_iota(jnp.int32, shape, axis)


def split(values):
    high = values.astype(jnp.bfloat16)
    return high, (values - high.astype(jnp.float32)).astype(jnp.bfloat16)


def later(values, hours):
    rows = values.shape[0]
    if hours % 8 == 0:
        padding = jnp.zeros((hours, values.shape[1]), values.dtype)
        return jnp.concatenate([padding, values[: rows - hours]], axis=0)
    return jnp.where(iota(values.shape, 0) < hours, 0.0, pltpu.roll(values, hours, 0))


def prepare_kernel(
    rain_hbm, soil_hbm, area_hbm, dest_hbm, reach_hbm, irf_hbm,
    runoff_ref, response_ref, dest_ref, reach_ref,
    rain_ref, soil_ref, area_ref, irf_ref, arrived,
):
    copies = [
        pltpu.make_async_copy(source, target, arrived.at[j])
        for j, (source, target) in enumerate(
            [
                (rain_hbm, rain_ref),
                (soil_hbm, soil_ref),
                (area_hbm, area_ref),
                (irf_hbm, irf_ref),
                (dest_hbm, dest_ref),
                (reach_hbm, reach_ref),
            ]
        )
    ]
    for copy in copies:
        copy.start()
    for copy in copies:
        copy.wait()
    hours = rain_ref.shape[1]
    kinds, taps = irf_ref.shape
    rainfall = rain_ref[...].astype(jnp.float32).T
    storage = soil_ref[...]
    excess = jnp.maximum(rainfall - 0.2 * storage, 0.0)
    runoff = area_ref[...] * excess * excess / (rainfall + 0.8 * storage)
    runoff_ref[...] = runoff.astype(jnp.bfloat16).astype(jnp.float32)
    backward = (
        iota((taps, hours), 1) == lax.rem(hours - iota((taps, hours), 0), hours)
    ).astype(jnp.float32)
    reversed_taps = lax.dot_general(
        irf_ref[...], backward, NN, precision=lax.Precision.HIGHEST, preferred_element_type=jnp.float32
    )
    causal = iota((hours, hours), 1) <= iota((hours, hours), 0)
    for kind in range(kinds):
        row = jnp.broadcast_to(reversed_taps[kind : kind + 1], (hours, hours))
        matrix = jnp.where(causal, pltpu.roll(row, 0, 1, stride=1, stride_axis=0), 0.0)
        high, low = split(matrix)
        response_ref[:hours, kind * hours : (kind + 1) * hours] = high
        response_ref[hours:, kind * hours : (kind + 1) * hours] = low


def route_kernel(
    meta_ref, runoff_ref, response_ref, dest_ref, reach_ref, flow_ref, *, owners, kinds, reach_rows, basin_rows
):
    hours, tiles = runoff_ref.shape
    outlets = owners * basin_rows
    shift = basin_rows.bit_length() - 1
    dest = dest_ref[...]
    reach = reach_ref[...]

    stack = meta_ref[...]
    spans = reach_rows // LANES
    fields = stack.shape[0] // owners
    field = iota(stack.shape, 0) % fields
    parents = jnp.where(field == 3 * spans, stack, pltpu.roll(stack, 1, 0))
    stack = jnp.where(field == 3 * spans, lax.shift_right_arithmetic(parents, shift) + 1, stack)
    stack = jnp.where(field == 3 * spans + 1, parents & (basin_rows - 1), stack)
    stack = stack.astype(jnp.float32).T.astype(jnp.bfloat16)

    def marks(row, count):
        return (iota((count, tiles), 0) == row).astype(jnp.float32).astype(jnp.bfloat16)

    def picked(values, chosen):
        return jnp.sum(jnp.where(chosen, values, 0.0), axis=0, keepdims=True).astype(jnp.int32)

    def lookup(owner, first, count):
        place = owner * fields
        mark = jnp.concatenate([marks(place + first + j, owners * fields) for j in range(count)], axis=1)
        found = lax.dot_general(stack, mark, NN, preferred_element_type=jnp.float32)
        return [found[:, j * tiles : (j + 1) * tiles] for j in range(count)]

    by_reach = lookup(dest, 0, 3 * spans)
    at_reach = [iota((LANES, tiles), 0) + j * LANES == reach for j in range(spans)]
    basin, kind, lag = [
        sum(picked(by_reach[c * spans + j], at_reach[j]) for j in range(spans)) for c in range(3)
    ]

    def parent_of(owner, local):
        by_basin = lookup(owner, 3 * spans, 2)
        at_basin = iota((LANES, tiles), 0) == local
        return picked(by_basin[0], at_basin) - 1, picked(by_basin[1], at_basin)

    parent_owner, parent_local = parent_of(dest, basin)
    second_owner, second_local = parent_of(parent_owner, parent_local)
    targets = [
        dest * basin_rows + basin,
        parent_owner * basin_rows + parent_local,
        second_owner * basin_rows + second_local,
    ]

    lagged = runoff_ref[...]
    step = 64
    while step:
        lagged = jnp.where((lag & step) != 0, later(lagged, step), lagged)
        step //= 2
    lagged = lagged.astype(jnp.bfloat16)
    by_kind = jnp.concatenate(
        [
            lagged * (kind == k).astype(jnp.float32).astype(jnp.bfloat16)
            for k in range(kinds)
        ],
        axis=0,
    )
    routed = lax.dot_general(response_ref[...], by_kind, NN, preferred_element_type=jnp.float32)
    routed = routed[:hours] + routed[hours:]
    pieces, placements = [], []
    for target in targets:
        pieces.extend(split(routed))
        mark = marks(target, outlets)
        placements.extend([mark, mark])
        routed = later(routed, LINK)
    flow = lax.dot_general(
        jnp.concatenate(placements, axis=1),
        jnp.concatenate(pieces, axis=1),
        NT,
        preferred_element_type=jnp.float32,
    )
    level = jnp.log(jnp.maximum(flow, CODE_LEAST)) * CODE_SCALE + CODE_ZERO
    level = jnp.minimum(jnp.round(level), CODE_TOP).astype(jnp.int32)
    flow_ref[...] = jnp.where(flow < CODE_LEAST, -CODE_TOP, level).astype(jnp.int16)


def finish_kernel(parts_ref, section_ref):
    level = parts_ref[...].astype(jnp.int32)
    flow = jnp.exp((level.astype(jnp.float32) - CODE_ZERO) * (1.0 / CODE_SCALE))
    flow = jnp.sum(jnp.where(level == -CODE_TOP, 0.0, flow), axis=0)
    section_ref[...] = jnp.log(1.0 + flow)


def per_device(
    rain,
    soil,
    tile_area,
    tile_dest,
    tile_reach,
    reach_basin,
    reach_kind,
    reach_lag,
    irf,
    outlet_level,
    outlet_parent,
):
    owners = lax.axis_size("tile")
    tile_rows, hours = rain.shape
    basin_rows = outlet_parent.shape[0]
    kinds = irf.shape[0]
    params = pltpu.CompilerParams(vmem_limit_bytes=VMEM_BYTES)

    meta = jnp.concatenate(
        [
            reach_basin,
            reach_kind,
            reach_lag,
            outlet_parent,
            jnp.zeros((2 * LANES - basin_rows,), jnp.int32),
        ]
    ).reshape(-1, LANES)
    near = 1 << ((owners.bit_length() - 1) // 2)
    far = owners // near
    near_groups = [[f * near + j for j in range(near)] for f in range(far)]
    far_groups = [[f * near + j for f in range(far)] for j in range(near)]
    for groups in (near_groups, far_groups):
        meta = lax.all_to_all(
            jnp.broadcast_to(meta[None], (len(groups[0]),) + meta.shape),
            "tile",
            split_axis=0,
            concat_axis=0,
            axis_index_groups=groups,
            tiled=True,
        ).reshape(-1, LANES)

    held = pl.BlockSpec(memory_space=pltpu.HBM)
    row = (1, tile_rows)
    runoff, response, dest, reach = pl.pallas_call(
        prepare_kernel,
        out_shape=(
            jax.ShapeDtypeStruct((hours, tile_rows), jnp.float32),
            jax.ShapeDtypeStruct((2 * hours, kinds * hours), jnp.bfloat16),
            jax.ShapeDtypeStruct(row, jnp.int32),
            jax.ShapeDtypeStruct(row, jnp.int32),
        ),
        in_specs=[held] * 6,
        scratch_shapes=[
            pltpu.VMEM(rain.shape, rain.dtype),
            pltpu.VMEM(row, jnp.float32),
            pltpu.VMEM(row, jnp.float32),
            pltpu.VMEM(irf.shape, jnp.float32),
            pltpu.SemaphoreType.DMA((6,)),
        ],
        compiler_params=params,
        name="prepare",
    )(
        rain,
        soil.reshape(row),
        tile_area.reshape(row),
        tile_dest.reshape(row),
        tile_reach.reshape(row),
        irf,
    )

    flow = pl.pallas_call(
        lambda *refs: route_kernel(
            *refs, owners=owners, kinds=kinds, reach_rows=reach_basin.shape[0], basin_rows=basin_rows
        ),
        out_shape=jax.ShapeDtypeStruct((owners * basin_rows, hours), jnp.int16),
        compiler_params=params,
        name="route",
    )(meta, runoff, response, dest, reach)

    parts = lax.all_to_all(
        flow.reshape(owners, basin_rows, hours), "tile", split_axis=0, concat_axis=0, tiled=True
    )
    return pl.pallas_call(
        finish_kernel,
        out_shape=jax.ShapeDtypeStruct((basin_rows, hours), jnp.float32),
        compiler_params=params,
        name="finish",
    )(parts)


def solution(mesh):
    rows = P(("ens", "tile"))
    table = P(("ens", "tile"), None)
    in_specs = (table, rows, rows, table, rows, rows, rows, rows, P(), rows, rows)
    return jax.shard_map(
        per_device, mesh=mesh, in_specs=in_specs, out_specs=table, check_vma=False
    )
```

```python
import math

import jax
import jax.numpy as jnp
from jax import lax
from jax.experimental import pallas as pl
from jax.experimental.pallas import tpu as pltpu
from jax.sharding import PartitionSpec as P

LINK = 6
LANES = 128
VMEM_BYTES = 40 * 1024 * 1024
CODE_TOP = 32767
CODE_OCTAVES = 44
CODE_LOWEST = -26
CODE_SCALE = 2 * CODE_TOP / (CODE_OCTAVES * math.log(2.0))
CODE_LEAST = 2.0**CODE_LOWEST
CODE_ZERO = -CODE_TOP + 1 - CODE_LOWEST * math.log(2.0) * CODE_SCALE

NT = (((1,), (1,)), ((), ()))
NN = (((1,), (0,)), ((), ()))


def iota(shape, axis):
    return lax.broadcasted_iota(jnp.int32, shape, axis)


def split(values):
    high = values.astype(jnp.bfloat16)
    return high, (values - high.astype(jnp.float32)).astype(jnp.bfloat16)


def later(values, hours):
    rows = values.shape[0]
    if hours % 8 == 0:
        padding = jnp.zeros((hours, values.shape[1]), values.dtype)
        return jnp.concatenate([padding, values[: rows - hours]], axis=0)
    return jnp.where(iota(values.shape, 0) < hours, 0.0, pltpu.roll(values, hours, 0))


def prepare_kernel(rain_ref, tile_ref, irf_ref, runoff_ref, response_ref):
    hours = rain_ref.shape[1]
    kinds, taps = irf_ref.shape
    rainfall = rain_ref[...].astype(jnp.float32).T
    storage = tile_ref[0:1]
    excess = jnp.maximum(rainfall - 0.2 * storage, 0.0)
    runoff = tile_ref[1:2] * excess * excess / (rainfall + 0.8 * storage)
    runoff_ref[...] = runoff.astype(jnp.bfloat16).astype(jnp.float32)
    backward = (
        iota((taps, hours), 1) == lax.rem(hours - iota((taps, hours), 0), hours)
    ).astype(jnp.float32)
    reversed_taps = lax.dot_general(
        irf_ref[...], backward, NN, precision=lax.Precision.HIGHEST, preferred_element_type=jnp.float32
    )
    causal = iota((hours, hours), 1) <= iota((hours, hours), 0)
    for kind in range(kinds):
        row = jnp.broadcast_to(reversed_taps[kind : kind + 1], (hours, hours))
        matrix = jnp.where(causal, pltpu.roll(row, 0, 1, stride=1, stride_axis=0), 0.0)
        high, low = split(matrix)
        response_ref[:hours, kind * hours : (kind + 1) * hours] = high
        response_ref[hours:, kind * hours : (kind + 1) * hours] = low


def route_kernel(
    meta_ref, runoff_ref, response_ref, tile_ref, flow_ref, *, owners, kinds, reach_rows, basin_rows
):
    hours, tiles = runoff_ref.shape
    outlets = owners * basin_rows
    shift = basin_rows.bit_length() - 1
    dest = tile_ref[0:1]
    reach = tile_ref[1:2]

    stack = meta_ref[...]
    spans = reach_rows // LANES
    fields = stack.shape[0] // owners
    field = iota(stack.shape, 0) % fields
    parents = jnp.where(field == 3 * spans, stack, pltpu.roll(stack, 1, 0))
    stack = jnp.where(field == 3 * spans, lax.shift_right_arithmetic(parents, shift) + 1, stack)
    stack = jnp.where(field == 3 * spans + 1, parents & (basin_rows - 1), stack)
    stack = stack.astype(jnp.float32).T.astype(jnp.bfloat16)

    def marks(row, count):
        return (iota((count, tiles), 0) == row).astype(jnp.float32).astype(jnp.bfloat16)

    def picked(values, chosen):
        return jnp.sum(jnp.where(chosen, values, 0.0), axis=0, keepdims=True).astype(jnp.int32)

    def lookup(owner, first, count):
        place = owner * fields
        mark = jnp.concatenate([marks(place + first + j, owners * fields) for j in range(count)], axis=1)
        found = lax.dot_general(stack, mark, NN, preferred_element_type=jnp.float32)
        return [found[:, j * tiles : (j + 1) * tiles] for j in range(count)]

    by_reach = lookup(dest, 0, 3 * spans)
    at_reach = [iota((LANES, tiles), 0) + j * LANES == reach for j in range(spans)]
    basin, kind, lag = [
        sum(picked(by_reach[c * spans + j], at_reach[j]) for j in range(spans)) for c in range(3)
    ]

    def parent_of(owner, local):
        by_basin = lookup(owner, 3 * spans, 2)
        at_basin = iota((LANES, tiles), 0) == local
        return picked(by_basin[0], at_basin) - 1, picked(by_basin[1], at_basin)

    parent_owner, parent_local = parent_of(dest, basin)
    second_owner, second_local = parent_of(parent_owner, parent_local)
    targets = [
        dest * basin_rows + basin,
        parent_owner * basin_rows + parent_local,
        second_owner * basin_rows + second_local,
    ]

    lagged = runoff_ref[...]
    step = 64
    while step:
        lagged = jnp.where((lag & step) != 0, later(lagged, step), lagged)
        step //= 2
    lagged = lagged.astype(jnp.bfloat16)
    by_kind = jnp.concatenate(
        [
            lagged * (kind == k).astype(jnp.float32).astype(jnp.bfloat16)
            for k in range(kinds)
        ],
        axis=0,
    )
    routed = lax.dot_general(response_ref[...], by_kind, NN, preferred_element_type=jnp.float32)
    routed = routed[:hours] + routed[hours:]
    pieces, placements = [], []
    for target in targets:
        pieces.extend(split(routed))
        mark = marks(target, outlets)
        placements.extend([mark, mark])
        routed = later(routed, LINK)
    flow = lax.dot_general(
        jnp.concatenate(placements, axis=1),
        jnp.concatenate(pieces, axis=1),
        NT,
        preferred_element_type=jnp.float32,
    )
    level = jnp.log(jnp.maximum(flow, CODE_LEAST)) * CODE_SCALE + CODE_ZERO
    level = jnp.minimum(jnp.round(level), CODE_TOP).astype(jnp.int32)
    flow_ref[...] = jnp.where(flow < CODE_LEAST, -CODE_TOP, level).astype(jnp.int16)


def finish_kernel(parts_ref, section_ref):
    level = parts_ref[...].astype(jnp.int32)
    flow = jnp.exp((level.astype(jnp.float32) - CODE_ZERO) * (1.0 / CODE_SCALE))
    flow = jnp.sum(jnp.where(level == -CODE_TOP, 0.0, flow), axis=0)
    section_ref[...] = jnp.log(1.0 + flow)


def per_device(
    rain,
    soil,
    tile_area,
    tile_dest,
    tile_reach,
    reach_basin,
    reach_kind,
    reach_lag,
    irf,
    outlet_level,
    outlet_parent,
):
    owners = lax.axis_size("tile")
    tile_rows, hours = rain.shape
    basin_rows = outlet_parent.shape[0]
    kinds = irf.shape[0]
    params = pltpu.CompilerParams(vmem_limit_bytes=VMEM_BYTES)

    meta = jnp.concatenate(
        [
            reach_basin,
            reach_kind,
            reach_lag,
            outlet_parent,
            jnp.zeros((2 * LANES - basin_rows,), jnp.int32),
        ]
    ).reshape(-1, LANES)
    meta = lax.all_to_all(
        jnp.broadcast_to(meta[None], (owners,) + meta.shape), "tile", split_axis=0, concat_axis=0, tiled=True
    ).reshape(-1, LANES)

    runoff, response = pl.pallas_call(
        prepare_kernel,
        out_shape=(
            jax.ShapeDtypeStruct((hours, tile_rows), jnp.float32),
            jax.ShapeDtypeStruct((2 * hours, kinds * hours), jnp.bfloat16),
        ),
        compiler_params=params,
        name="prepare",
    )(rain, jnp.stack([soil, tile_area]), irf)

    flow = pl.pallas_call(
        lambda *refs: route_kernel(
            *refs, owners=owners, kinds=kinds, reach_rows=reach_basin.shape[0], basin_rows=basin_rows
        ),
        out_shape=jax.ShapeDtypeStruct((owners * basin_rows, hours), jnp.int16),
        compiler_params=params,
        name="route",
    )(meta, runoff, response, jnp.stack([tile_dest[:, 0], tile_reach]))

    parts = lax.all_to_all(
        flow.reshape(owners, basin_rows, hours), "tile", split_axis=0, concat_axis=0, tiled=True
    )
    return pl.pallas_call(
        finish_kernel,
        out_shape=jax.ShapeDtypeStruct((basin_rows, hours), jnp.float32),
        compiler_params=params,
        name="finish",
    )(parts)


def solution(mesh):
    rows = P(("ens", "tile"))
    table = P(("ens", "tile"), None)
    in_specs = (table, rows, rows, table, rows, rows, rows, rows, P(), rows, rows)
    return jax.shard_map(
        per_device, mesh=mesh, in_specs=in_specs, out_specs=table, check_vma=False
    )
```

```python
import math

import jax
import jax.numpy as jnp
from jax import lax
from jax.experimental import pallas as pl
from jax.experimental.pallas import tpu as pltpu
from jax.sharding import PartitionSpec as P

LINK = 6
LANES = 128
VMEM_BYTES = 40 * 1024 * 1024
CODE_TOP = 32767
CODE_OCTAVES = 44
CODE_LOWEST = -26
CODE_SCALE = 2 * CODE_TOP / (CODE_OCTAVES * math.log(2.0))
CODE_LEAST = 2.0**CODE_LOWEST
CODE_ZERO = -CODE_TOP + 1 - CODE_LOWEST * math.log(2.0) * CODE_SCALE

NT = (((1,), (1,)), ((), ()))
NN = (((1,), (0,)), ((), ()))


def iota(shape, axis):
    return lax.broadcasted_iota(jnp.int32, shape, axis)


def split(values):
    high = values.astype(jnp.bfloat16)
    return high, (values - high.astype(jnp.float32)).astype(jnp.bfloat16)


def later(values, hours):
    rows = values.shape[0]
    if hours % 8 == 0:
        padding = jnp.zeros((hours, values.shape[1]), values.dtype)
        return jnp.concatenate([padding, values[: rows - hours]], axis=0)
    return jnp.where(iota(values.shape, 0) < hours, 0.0, pltpu.roll(values, hours, 0))


def load(sources, targets, arrived):
    copies = [
        pltpu.make_async_copy(source, target, arrived.at[j])
        for j, (source, target) in enumerate(zip(sources, targets))
    ]
    for copy in copies:
        copy.start()
    for copy in copies:
        copy.wait()


def pack_kernel(basin_hbm, kind_hbm, lag_hbm, parent_hbm, meta_ref, basin_ref, kind_ref, lag_ref, parent_ref, arrived):
    load(
        (basin_hbm, kind_hbm, lag_hbm, parent_hbm),
        (basin_ref, kind_ref, lag_ref, parent_ref),
        arrived,
    )
    owners, fields, _ = meta_ref.shape
    rows = [
        values[:, first : first + LANES]
        for values in (basin_ref[...], kind_ref[...], lag_ref[...])
        for first in range(0, values.shape[1], LANES)
    ]
    parents = parent_ref[...]
    empty = jnp.zeros((1, LANES - parents.shape[1]), jnp.int32)
    rows.append(jnp.concatenate([parents, empty], axis=1))
    rows.extend([jnp.zeros((1, LANES), jnp.int32)] * (fields - len(rows)))
    block = jnp.concatenate(rows, axis=0)
    for owner in range(owners):
        meta_ref[owner] = block


def prepare_kernel(
    rain_hbm, soil_hbm, area_hbm, irf_hbm, dest_hbm, reach_hbm,
    runoff_ref, response_ref, dest_ref, reach_ref,
    rain_ref, soil_ref, area_ref, irf_ref, arrived,
):
    load(
        (rain_hbm, soil_hbm, area_hbm, irf_hbm, dest_hbm, reach_hbm),
        (rain_ref, soil_ref, area_ref, irf_ref, dest_ref, reach_ref),
        arrived,
    )
    hours = rain_ref.shape[1]
    kinds, taps = irf_ref.shape
    rainfall = rain_ref[...].astype(jnp.float32).T
    storage = soil_ref[...]
    excess = jnp.maximum(rainfall - 0.2 * storage, 0.0)
    runoff = area_ref[...] * excess * excess / (rainfall + 0.8 * storage)
    runoff_ref[...] = runoff.astype(jnp.bfloat16).astype(jnp.float32)
    backward = (
        iota((taps, hours), 1) == lax.rem(hours - iota((taps, hours), 0), hours)
    ).astype(jnp.float32)
    reversed_taps = lax.dot_general(
        irf_ref[...], backward, NN, precision=lax.Precision.HIGHEST, preferred_element_type=jnp.float32
    )
    causal = iota((hours, hours), 1) <= iota((hours, hours), 0)
    for kind in range(kinds):
        row = jnp.broadcast_to(reversed_taps[kind : kind + 1], (hours, hours))
        matrix = jnp.where(causal, pltpu.roll(row, 0, 1, stride=1, stride_axis=0), 0.0)
        high, low = split(matrix)
        response_ref[:hours, kind * hours : (kind + 1) * hours] = high
        response_ref[hours:, kind * hours : (kind + 1) * hours] = low


def route_kernel(
    meta_ref, runoff_ref, response_ref, dest_ref, reach_ref, flow_ref, *, owners, kinds, reach_rows, basin_rows
):
    hours, tiles = runoff_ref.shape
    outlets = owners * basin_rows
    shift = basin_rows.bit_length() - 1
    dest = dest_ref[...]
    reach = reach_ref[...]

    stack = meta_ref[...]
    spans = reach_rows // LANES
    fields = stack.shape[0] // owners
    field = iota(stack.shape, 0) % fields
    parents = jnp.where(field == 3 * spans, stack, pltpu.roll(stack, 1, 0))
    stack = jnp.where(field == 3 * spans, lax.shift_right_arithmetic(parents, shift) + 1, stack)
    stack = jnp.where(field == 3 * spans + 1, parents & (basin_rows - 1), stack)
    stack = stack.astype(jnp.float32).T.astype(jnp.bfloat16)

    def marks(row, count):
        return (iota((count, tiles), 0) == row).astype(jnp.float32).astype(jnp.bfloat16)

    def picked(values, chosen):
        return jnp.sum(jnp.where(chosen, values, 0.0), axis=0, keepdims=True).astype(jnp.int32)

    def lookup(owner, first, count):
        place = owner * fields
        mark = jnp.concatenate([marks(place + first + j, owners * fields) for j in range(count)], axis=1)
        found = lax.dot_general(stack, mark, NN, preferred_element_type=jnp.float32)
        return [found[:, j * tiles : (j + 1) * tiles] for j in range(count)]

    by_reach = lookup(dest, 0, 3 * spans)
    at_reach = [iota((LANES, tiles), 0) + j * LANES == reach for j in range(spans)]
    basin, kind, lag = [
        sum(picked(by_reach[c * spans + j], at_reach[j]) for j in range(spans)) for c in range(3)
    ]

    def parent_of(owner, local):
        by_basin = lookup(owner, 3 * spans, 2)
        at_basin = iota((LANES, tiles), 0) == local
        return picked(by_basin[0], at_basin) - 1, picked(by_basin[1], at_basin)

    parent_owner, parent_local = parent_of(dest, basin)
    second_owner, second_local = parent_of(parent_owner, parent_local)
    targets = [
        dest * basin_rows + basin,
        parent_owner * basin_rows + parent_local,
        second_owner * basin_rows + second_local,
    ]

    lagged = runoff_ref[...]
    step = 64
    while step:
        lagged = jnp.where((lag & step) != 0, later(lagged, step), lagged)
        step //= 2
    lagged = lagged.astype(jnp.bfloat16)
    by_kind = jnp.concatenate(
        [
            lagged * (kind == k).astype(jnp.float32).astype(jnp.bfloat16)
            for k in range(kinds)
        ],
        axis=0,
    )
    routed = lax.dot_general(response_ref[...], by_kind, NN, preferred_element_type=jnp.float32)
    routed = routed[:hours] + routed[hours:]
    pieces, placements = [], []
    for target in targets:
        pieces.extend(split(routed))
        mark = marks(target, outlets)
        placements.extend([mark, mark])
        routed = later(routed, LINK)
    flow = lax.dot_general(
        jnp.concatenate(placements, axis=1),
        jnp.concatenate(pieces, axis=1),
        NT,
        preferred_element_type=jnp.float32,
    )
    level = jnp.log(jnp.maximum(flow, CODE_LEAST)) * CODE_SCALE + CODE_ZERO
    level = jnp.minimum(jnp.round(level), CODE_TOP).astype(jnp.int32)
    flow_ref[...] = jnp.where(flow < CODE_LEAST, -CODE_TOP, level).astype(jnp.int16)


def finish_kernel(parts_ref, section_ref):
    level = parts_ref[...].astype(jnp.int32)
    flow = jnp.exp((level.astype(jnp.float32) - CODE_ZERO) * (1.0 / CODE_SCALE))
    flow = jnp.sum(jnp.where(level == -CODE_TOP, 0.0, flow), axis=0)
    section_ref[...] = jnp.log(1.0 + flow)


def per_device(
    rain,
    soil,
    tile_area,
    tile_dest,
    tile_reach,
    reach_basin,
    reach_kind,
    reach_lag,
    irf,
    outlet_level,
    outlet_parent,
):
    owners = lax.axis_size("tile")
    tile_rows, hours = rain.shape
    basin_rows = outlet_parent.shape[0]
    kinds = irf.shape[0]
    params = pltpu.CompilerParams(vmem_limit_bytes=VMEM_BYTES)

    row = (1, tile_rows)
    fields = 8 * pl.cdiv(3 * reach_basin.size // LANES + 2, 8)

    def in_hbm(values, shape):
        return pltpu.with_memory_space_constraint(values.reshape(shape), pltpu.HBM)

    held = pl.BlockSpec(memory_space=pltpu.HBM)
    meta = pl.pallas_call(
        pack_kernel,
        out_shape=jax.ShapeDtypeStruct((owners, fields, LANES), jnp.int32),
        in_specs=[held] * 4,
        scratch_shapes=[
            pltpu.VMEM((1, reach_basin.size), jnp.int32),
            pltpu.VMEM((1, reach_basin.size), jnp.int32),
            pltpu.VMEM((1, reach_basin.size), jnp.int32),
            pltpu.VMEM((1, basin_rows), jnp.int32),
            pltpu.SemaphoreType.DMA((4,)),
        ],
        compiler_params=params,
        name="pack",
    )(
        in_hbm(reach_basin, (1, -1)),
        in_hbm(reach_kind, (1, -1)),
        in_hbm(reach_lag, (1, -1)),
        in_hbm(outlet_parent, (1, -1)),
    )
    meta = lax.all_to_all(meta, "tile", split_axis=0, concat_axis=0, tiled=True).reshape(-1, LANES)

    runoff, response, dest, reach = pl.pallas_call(
        prepare_kernel,
        out_shape=(
            jax.ShapeDtypeStruct((hours, tile_rows), jnp.float32),
            jax.ShapeDtypeStruct((2 * hours, kinds * hours), jnp.bfloat16),
            jax.ShapeDtypeStruct(row, jnp.int32),
            jax.ShapeDtypeStruct(row, jnp.int32),
        ),
        in_specs=[held] * 6,
        scratch_shapes=[
            pltpu.VMEM(rain.shape, rain.dtype),
            pltpu.VMEM(row, jnp.float32),
            pltpu.VMEM(row, jnp.float32),
            pltpu.VMEM(irf.shape, jnp.float32),
            pltpu.SemaphoreType.DMA((6,)),
        ],
        compiler_params=params,
        name="prepare",
    )(
        in_hbm(rain, rain.shape),
        in_hbm(soil, row),
        in_hbm(tile_area, row),
        in_hbm(irf, irf.shape),
        in_hbm(tile_dest, row),
        in_hbm(tile_reach, row),
    )

    flow = pl.pallas_call(
        lambda *refs: route_kernel(
            *refs, owners=owners, kinds=kinds, reach_rows=reach_basin.shape[0], basin_rows=basin_rows
        ),
        out_shape=jax.ShapeDtypeStruct((owners * basin_rows, hours), jnp.int16),
        compiler_params=params,
        name="route",
    )(meta, runoff, response, dest, reach)

    parts = lax.all_to_all(
        flow.reshape(owners, basin_rows, hours), "tile", split_axis=0, concat_axis=0, tiled=True
    )
    return pl.pallas_call(
        finish_kernel,
        out_shape=jax.ShapeDtypeStruct((basin_rows, hours), jnp.float32),
        compiler_params=params,
        name="finish",
    )(parts)


def solution(mesh):
    rows = P(("ens", "tile"))
    table = P(("ens", "tile"), None)
    in_specs = (table, rows, rows, table, rows, rows, rows, rows, P(), rows, rows)
    return jax.shard_map(
        per_device, mesh=mesh, in_specs=in_specs, out_specs=table, check_vma=False
    )
```

```python
import math

import jax
import jax.numpy as jnp
from jax import lax
from jax.experimental import pallas as pl
from jax.experimental.pallas import tpu as pltpu
from jax.sharding import PartitionSpec as P

LINK = 6
LANES = 128
VMEM_BYTES = 40 * 1024 * 1024
CODE_TOP = 32767
CODE_OCTAVES = 44
CODE_LOWEST = -26
CODE_SCALE = 2 * CODE_TOP / (CODE_OCTAVES * math.log(2.0))
CODE_LEAST = 2.0**CODE_LOWEST
CODE_ZERO = -CODE_TOP + 1 - CODE_LOWEST * math.log(2.0) * CODE_SCALE

NT = (((1,), (1,)), ((), ()))
NN = (((1,), (0,)), ((), ()))


def iota(shape, axis):
    return lax.broadcasted_iota(jnp.int32, shape, axis)


def split(values):
    high = values.astype(jnp.bfloat16)
    return high, (values - high.astype(jnp.float32)).astype(jnp.bfloat16)


def later(values, hours):
    rows = values.shape[0]
    if hours % 8 == 0:
        padding = jnp.zeros((hours, values.shape[1]), values.dtype)
        return jnp.concatenate([padding, values[: rows - hours]], axis=0)
    return jnp.where(iota(values.shape, 0) < hours, 0.0, pltpu.roll(values, hours, 0))


def load(sources, targets, arrived):
    copies = [
        pltpu.make_async_copy(source, target, arrived.at[j])
        for j, (source, target) in enumerate(zip(sources, targets))
    ]
    for copy in copies:
        copy.start()
    for copy in copies:
        copy.wait()


def prepare_kernel(*refs):
    sources, refs = refs[:10], refs[10:]
    meta_ref, runoff_ref, response_ref, dest_ref, reach_ref, *scratch, arrived = refs
    basin_ref, kind_ref, lag_ref, parent_ref, rain_ref, soil_ref, area_ref, irf_ref = scratch
    load(sources, (*scratch, dest_ref, reach_ref), arrived)
    owners, fields, _ = meta_ref.shape
    rows = [
        values[:, first : first + LANES]
        for values in (basin_ref[...], kind_ref[...], lag_ref[...])
        for first in range(0, values.shape[1], LANES)
    ]
    parents = parent_ref[...]
    empty = jnp.zeros((1, LANES - parents.shape[1]), jnp.int32)
    rows.append(jnp.concatenate([parents, empty], axis=1))
    rows.extend([jnp.zeros((1, LANES), jnp.int32)] * (fields - len(rows)))
    block = jnp.concatenate(rows, axis=0)
    for owner in range(owners):
        meta_ref[owner] = block

    hours = rain_ref.shape[1]
    kinds, taps = irf_ref.shape
    rainfall = rain_ref[...].astype(jnp.float32).T
    storage = soil_ref[...]
    excess = jnp.maximum(rainfall - 0.2 * storage, 0.0)
    runoff = area_ref[...] * excess * excess / (rainfall + 0.8 * storage)
    runoff_ref[...] = runoff.astype(jnp.bfloat16).astype(jnp.float32)
    backward = (
        iota((taps, hours), 1) == lax.rem(hours - iota((taps, hours), 0), hours)
    ).astype(jnp.float32)
    reversed_taps = lax.dot_general(
        irf_ref[...], backward, NN, precision=lax.Precision.HIGHEST, preferred_element_type=jnp.float32
    )
    causal = iota((hours, hours), 1) <= iota((hours, hours), 0)
    for kind in range(kinds):
        row = jnp.broadcast_to(reversed_taps[kind : kind + 1], (hours, hours))
        matrix = jnp.where(causal, pltpu.roll(row, 0, 1, stride=1, stride_axis=0), 0.0)
        high, low = split(matrix)
        response_ref[:hours, kind * hours : (kind + 1) * hours] = high
        response_ref[hours:, kind * hours : (kind + 1) * hours] = low


def route_kernel(
    meta_ref, runoff_ref, response_ref, dest_ref, reach_ref, flow_ref, *, owners, kinds, reach_rows, basin_rows
):
    hours, tiles = runoff_ref.shape
    outlets = owners * basin_rows
    shift = basin_rows.bit_length() - 1
    dest = dest_ref[...]
    reach = reach_ref[...]

    stack = meta_ref[...]
    spans = reach_rows // LANES
    fields = stack.shape[0] // owners
    field = iota(stack.shape, 0) % fields
    parents = jnp.where(field == 3 * spans, stack, pltpu.roll(stack, 1, 0))
    stack = jnp.where(field == 3 * spans, lax.shift_right_arithmetic(parents, shift) + 1, stack)
    stack = jnp.where(field == 3 * spans + 1, parents & (basin_rows - 1), stack)
    stack = stack.astype(jnp.float32).T.astype(jnp.bfloat16)

    def marks(row, count):
        return (iota((count, tiles), 0) == row).astype(jnp.float32).astype(jnp.bfloat16)

    def picked(values, chosen):
        return jnp.sum(jnp.where(chosen, values, 0.0), axis=0, keepdims=True).astype(jnp.int32)

    def lookup(owner, first, count):
        place = owner * fields
        mark = jnp.concatenate([marks(place + first + j, owners * fields) for j in range(count)], axis=1)
        found = lax.dot_general(stack, mark, NN, preferred_element_type=jnp.float32)
        return [found[:, j * tiles : (j + 1) * tiles] for j in range(count)]

    by_reach = lookup(dest, 0, 3 * spans)
    at_reach = [iota((LANES, tiles), 0) + j * LANES == reach for j in range(spans)]
    basin, kind, lag = [
        sum(picked(by_reach[c * spans + j], at_reach[j]) for j in range(spans)) for c in range(3)
    ]

    def parent_of(owner, local):
        by_basin = lookup(owner, 3 * spans, 2)
        at_basin = iota((LANES, tiles), 0) == local
        return picked(by_basin[0], at_basin) - 1, picked(by_basin[1], at_basin)

    parent_owner, parent_local = parent_of(dest, basin)
    second_owner, second_local = parent_of(parent_owner, parent_local)
    targets = [
        dest * basin_rows + basin,
        parent_owner * basin_rows + parent_local,
        second_owner * basin_rows + second_local,
    ]

    lagged = runoff_ref[...]
    step = 64
    while step:
        lagged = jnp.where((lag & step) != 0, later(lagged, step), lagged)
        step //= 2
    lagged = lagged.astype(jnp.bfloat16)
    by_kind = jnp.concatenate(
        [
            lagged * (kind == k).astype(jnp.float32).astype(jnp.bfloat16)
            for k in range(kinds)
        ],
        axis=0,
    )
    routed = lax.dot_general(response_ref[...], by_kind, NN, preferred_element_type=jnp.float32)
    routed = routed[:hours] + routed[hours:]
    pieces, placements = [], []
    for target in targets:
        pieces.extend(split(routed))
        mark = marks(target, outlets)
        placements.extend([mark, mark])
        routed = later(routed, LINK)
    flow = lax.dot_general(
        jnp.concatenate(placements, axis=1),
        jnp.concatenate(pieces, axis=1),
        NT,
        preferred_element_type=jnp.float32,
    )
    level = jnp.log(jnp.maximum(flow, CODE_LEAST)) * CODE_SCALE + CODE_ZERO
    level = jnp.minimum(jnp.round(level), CODE_TOP).astype(jnp.int32)
    flow_ref[...] = jnp.where(flow < CODE_LEAST, -CODE_TOP, level).astype(jnp.int16)


def finish_kernel(parts_ref, section_ref):
    level = parts_ref[...].astype(jnp.int32)
    flow = jnp.exp((level.astype(jnp.float32) - CODE_ZERO) * (1.0 / CODE_SCALE))
    flow = jnp.sum(jnp.where(level == -CODE_TOP, 0.0, flow), axis=0)
    section_ref[...] = jnp.log(1.0 + flow)


def per_device(
    rain,
    soil,
    tile_area,
    tile_dest,
    tile_reach,
    reach_basin,
    reach_kind,
    reach_lag,
    irf,
    outlet_level,
    outlet_parent,
):
    owners = lax.axis_size("tile")
    tile_rows, hours = rain.shape
    basin_rows = outlet_parent.shape[0]
    kinds = irf.shape[0]
    params = pltpu.CompilerParams(vmem_limit_bytes=VMEM_BYTES)

    row = (1, tile_rows)
    fields = 8 * pl.cdiv(3 * reach_basin.size // LANES + 2, 8)
    arguments = [
        pltpu.with_memory_space_constraint(values.reshape(shape), pltpu.HBM)
        for values, shape in (
            (reach_basin, (1, -1)),
            (reach_kind, (1, -1)),
            (reach_lag, (1, -1)),
            (outlet_parent, (1, -1)),
            (rain, rain.shape),
            (soil, row),
            (tile_area, row),
            (irf, irf.shape),
            (tile_dest, row),
            (tile_reach, row),
        )
    ]
    meta, runoff, response, dest, reach = pl.pallas_call(
        prepare_kernel,
        out_shape=(
            jax.ShapeDtypeStruct((owners, fields, LANES), jnp.int32),
            jax.ShapeDtypeStruct((hours, tile_rows), jnp.float32),
            jax.ShapeDtypeStruct((2 * hours, kinds * hours), jnp.bfloat16),
            jax.ShapeDtypeStruct(row, jnp.int32),
            jax.ShapeDtypeStruct(row, jnp.int32),
        ),
        in_specs=[pl.BlockSpec(memory_space=pltpu.HBM)] * len(arguments),
        scratch_shapes=[pltpu.VMEM(values.shape, values.dtype) for values in arguments[:-2]]
        + [pltpu.SemaphoreType.DMA((len(arguments),))],
        compiler_params=params,
        name="prepare",
    )(*arguments)
    meta = lax.all_to_all(meta, "tile", split_axis=0, concat_axis=0, tiled=True).reshape(-1, LANES)

    flow = pl.pallas_call(
        lambda *refs: route_kernel(
            *refs, owners=owners, kinds=kinds, reach_rows=reach_basin.shape[0], basin_rows=basin_rows
        ),
        out_shape=jax.ShapeDtypeStruct((owners * basin_rows, hours), jnp.int16),
        compiler_params=params,
        name="route",
    )(meta, runoff, response, dest, reach)

    parts = lax.all_to_all(
        flow.reshape(owners, basin_rows, hours), "tile", split_axis=0, concat_axis=0, tiled=True
    )
    return pl.pallas_call(
        finish_kernel,
        out_shape=jax.ShapeDtypeStruct((basin_rows, hours), jnp.float32),
        compiler_params=params,
        name="finish",
    )(parts)


def solution(mesh):
    rows = P(("ens", "tile"))
    table = P(("ens", "tile"), None)
    in_specs = (table, rows, rows, table, rows, rows, rows, rows, P(), rows, rows)
    return jax.shard_map(
        per_device, mesh=mesh, in_specs=in_specs, out_specs=table, check_vma=False
    )
```

```python
import math

import jax
import jax.numpy as jnp
from jax import lax
from jax.experimental import pallas as pl
from jax.experimental.pallas import tpu as pltpu
from jax.sharding import PartitionSpec as P

LINK = 6
LANES = 128
VMEM_BYTES = 40 * 1024 * 1024
CODE_TOP = 32767
CODE_OCTAVES = 44
CODE_LOWEST = -26
CODE_SCALE = 2 * CODE_TOP / (CODE_OCTAVES * math.log(2.0))
CODE_LEAST = 2.0**CODE_LOWEST
CODE_ZERO = -CODE_TOP + 1 - CODE_LOWEST * math.log(2.0) * CODE_SCALE

NT = (((1,), (1,)), ((), ()))
NN = (((1,), (0,)), ((), ()))


def iota(shape, axis):
    return lax.broadcasted_iota(jnp.int32, shape, axis)


def split(values):
    high = values.astype(jnp.bfloat16)
    return high, (values - high.astype(jnp.float32)).astype(jnp.bfloat16)


def later(values, hours):
    rows = values.shape[0]
    if hours % 8 == 0:
        padding = jnp.zeros((hours, values.shape[1]), values.dtype)
        return jnp.concatenate([padding, values[: rows - hours]], axis=0)
    return jnp.where(iota(values.shape, 0) < hours, 0.0, pltpu.roll(values, hours, 0))


def load(sources, targets, arrived):
    copies = [
        pltpu.make_async_copy(source, target, arrived.at[j])
        for j, (source, target) in enumerate(zip(sources, targets))
    ]
    for copy in copies:
        copy.start()
    for copy in copies:
        copy.wait()


def prepare_kernel(*refs):
    sources, (runoff_ref, response_ref, dest_ref, reach_ref, *scratch, arrived) = refs[:6], refs[6:]
    rain_ref, soil_ref, area_ref, irf_ref = scratch
    load(sources, (*scratch, dest_ref, reach_ref), arrived)
    hours = rain_ref.shape[1]
    kinds, taps = irf_ref.shape
    rainfall = rain_ref[...].astype(jnp.float32).T
    storage = soil_ref[...]
    excess = jnp.maximum(rainfall - 0.2 * storage, 0.0)
    runoff = area_ref[...] * excess * excess / (rainfall + 0.8 * storage)
    runoff_ref[...] = runoff.astype(jnp.bfloat16).astype(jnp.float32)
    backward = (
        iota((taps, hours), 1) == lax.rem(hours - iota((taps, hours), 0), hours)
    ).astype(jnp.float32)
    reversed_taps = lax.dot_general(
        irf_ref[...], backward, NN, precision=lax.Precision.HIGHEST, preferred_element_type=jnp.float32
    )
    causal = iota((hours, hours), 1) <= iota((hours, hours), 0)
    for kind in range(kinds):
        row = jnp.broadcast_to(reversed_taps[kind : kind + 1], (hours, hours))
        matrix = jnp.where(causal, pltpu.roll(row, 0, 1, stride=1, stride_axis=0), 0.0)
        high, low = split(matrix)
        response_ref[:hours, kind * hours : (kind + 1) * hours] = high
        response_ref[hours:, kind * hours : (kind + 1) * hours] = low


def route_kernel(*refs, owners, kinds, reach_rows, basin_rows):
    *meta_refs, runoff_ref, response_ref, dest_ref, reach_ref, flow_ref = refs
    me = lax.axis_index("tile")
    hours, tiles = runoff_ref.shape
    outlets = owners * basin_rows
    shift = basin_rows.bit_length() - 1
    dest = dest_ref[...]
    reach = reach_ref[...]

    stack = jnp.concatenate([meta_ref[...] for meta_ref in meta_refs], axis=0)
    spans = reach_rows // LANES
    fields = stack.shape[0] // owners
    field = iota(stack.shape, 0) % fields
    parents = jnp.where(field == 3 * spans, stack, pltpu.roll(stack, 1, 0))
    stack = jnp.where(field == 3 * spans, lax.shift_right_arithmetic(parents, shift) + 1, stack)
    stack = jnp.where(field == 3 * spans + 1, parents & (basin_rows - 1), stack)
    stack = stack.astype(jnp.float32).T.astype(jnp.bfloat16)

    def marks(row, count):
        return (iota((count, tiles), 0) == row).astype(jnp.float32).astype(jnp.bfloat16)

    def picked(values, chosen):
        return jnp.sum(jnp.where(chosen, values, 0.0), axis=0, keepdims=True).astype(jnp.int32)

    def lookup(owner, first, count):
        place = jnp.where(owner < 0, -1, owner ^ me) * fields
        mark = jnp.concatenate([marks(place + first + j, owners * fields) for j in range(count)], axis=1)
        found = lax.dot_general(stack, mark, NN, preferred_element_type=jnp.float32)
        return [found[:, j * tiles : (j + 1) * tiles] for j in range(count)]

    by_reach = lookup(dest, 0, 3 * spans)
    at_reach = [iota((LANES, tiles), 0) + j * LANES == reach for j in range(spans)]
    basin, kind, lag = [
        sum(picked(by_reach[c * spans + j], at_reach[j]) for j in range(spans)) for c in range(3)
    ]

    def parent_of(owner, local):
        by_basin = lookup(owner, 3 * spans, 2)
        at_basin = iota((LANES, tiles), 0) == local
        return picked(by_basin[0], at_basin) - 1, picked(by_basin[1], at_basin)

    parent_owner, parent_local = parent_of(dest, basin)
    second_owner, second_local = parent_of(parent_owner, parent_local)
    targets = [
        dest * basin_rows + basin,
        parent_owner * basin_rows + parent_local,
        second_owner * basin_rows + second_local,
    ]

    lagged = runoff_ref[...]
    step = 64
    while step:
        lagged = jnp.where((lag & step) != 0, later(lagged, step), lagged)
        step //= 2
    lagged = lagged.astype(jnp.bfloat16)
    by_kind = jnp.concatenate(
        [
            lagged * (kind == k).astype(jnp.float32).astype(jnp.bfloat16)
            for k in range(kinds)
        ],
        axis=0,
    )
    routed = lax.dot_general(response_ref[...], by_kind, NN, preferred_element_type=jnp.float32)
    routed = routed[:hours] + routed[hours:]
    pieces, placements = [], []
    for target in targets:
        pieces.extend(split(routed))
        mark = marks(target, outlets)
        placements.extend([mark, mark])
        routed = later(routed, LINK)
    flow = lax.dot_general(
        jnp.concatenate(placements, axis=1),
        jnp.concatenate(pieces, axis=1),
        NT,
        preferred_element_type=jnp.float32,
    )
    level = jnp.log(jnp.maximum(flow, CODE_LEAST)) * CODE_SCALE + CODE_ZERO
    level = jnp.minimum(jnp.round(level), CODE_TOP).astype(jnp.int32)
    flow_ref[...] = jnp.where(flow < CODE_LEAST, -CODE_TOP, level).astype(jnp.int16)


def finish_kernel(parts_ref, section_ref):
    level = parts_ref[...].astype(jnp.int32)
    flow = jnp.exp((level.astype(jnp.float32) - CODE_ZERO) * (1.0 / CODE_SCALE))
    flow = jnp.sum(jnp.where(level == -CODE_TOP, 0.0, flow), axis=0)
    section_ref[...] = jnp.log(1.0 + flow)


def per_device(
    rain,
    soil,
    tile_area,
    tile_dest,
    tile_reach,
    reach_basin,
    reach_kind,
    reach_lag,
    irf,
    outlet_level,
    outlet_parent,
):
    owners = lax.axis_size("tile")
    tile_rows, hours = rain.shape
    basin_rows = outlet_parent.shape[0]
    kinds = irf.shape[0]
    params = pltpu.CompilerParams(vmem_limit_bytes=VMEM_BYTES)

    metas = [
        jnp.concatenate(
            [
                reach_basin,
                reach_kind,
                reach_lag,
                outlet_parent,
                jnp.zeros((2 * LANES - basin_rows,), jnp.int32),
            ]
        ).reshape(-1, LANES)
    ]
    held = 1
    while held < owners:
        radix = min(4, owners // held)
        block = jnp.concatenate(metas, axis=0) if len(metas) > 1 else metas[0]
        metas = [block] + [
            lax.ppermute(block, "tile", [(i, i ^ (held * step)) for i in range(owners)])
            for step in range(1, radix)
        ]
        held *= radix

    row = (1, tile_rows)
    arguments = [
        pltpu.with_memory_space_constraint(values.reshape(shape), pltpu.HBM)
        for values, shape in (
            (rain, rain.shape),
            (soil, row),
            (tile_area, row),
            (irf, irf.shape),
            (tile_dest, row),
            (tile_reach, row),
        )
    ]
    runoff, response, dest, reach = pl.pallas_call(
        prepare_kernel,
        out_shape=(
            jax.ShapeDtypeStruct((hours, tile_rows), jnp.float32),
            jax.ShapeDtypeStruct((2 * hours, kinds * hours), jnp.bfloat16),
            jax.ShapeDtypeStruct(row, jnp.int32),
            jax.ShapeDtypeStruct(row, jnp.int32),
        ),
        in_specs=[pl.BlockSpec(memory_space=pltpu.HBM)] * len(arguments),
        scratch_shapes=[pltpu.VMEM(values.shape, values.dtype) for values in arguments[:-2]]
        + [pltpu.SemaphoreType.DMA((len(arguments),))],
        compiler_params=params,
        name="prepare",
    )(*arguments)

    flow = pl.pallas_call(
        lambda *refs: route_kernel(
            *refs, owners=owners, kinds=kinds, reach_rows=reach_basin.shape[0], basin_rows=basin_rows
        ),
        out_shape=jax.ShapeDtypeStruct((owners * basin_rows, hours), jnp.int16),
        compiler_params=params,
        name="route",
    )(*metas, runoff, response, dest, reach)

    parts = lax.all_to_all(
        flow.reshape(owners, basin_rows, hours), "tile", split_axis=0, concat_axis=0, tiled=True
    )
    return pl.pallas_call(
        finish_kernel,
        out_shape=jax.ShapeDtypeStruct((basin_rows, hours), jnp.float32),
        compiler_params=params,
        name="finish",
    )(parts)


def solution(mesh):
    rows = P(("ens", "tile"))
    table = P(("ens", "tile"), None)
    in_specs = (table, rows, rows, table, rows, rows, rows, rows, P(), rows, rows)
    return jax.shard_map(
        per_device, mesh=mesh, in_specs=in_specs, out_specs=table, check_vma=False
    )
```

```python
import math

import jax
import jax.numpy as jnp
from jax import lax
from jax.experimental import pallas as pl
from jax.experimental.pallas import tpu as pltpu
from jax.sharding import PartitionSpec as P

LINK = 6
LANES = 128
CORES = 2
ID_ROWS = 16
VMEM_BYTES = 40 * 1024 * 1024
CODE_TOP = 32767
CODE_OCTAVES = 44
CODE_LOWEST = -26
CODE_SCALE = 2 * CODE_TOP / (CODE_OCTAVES * math.log(2.0))
CODE_FLOOR = 2.0 ** (2 * CODE_LOWEST)
CODE_ZERO = -CODE_TOP + 1 - CODE_LOWEST * math.log(2.0) * CODE_SCALE

NT = (((1,), (1,)), ((), ()))
NN = (((1,), (0,)), ((), ()))


def iota(shape, axis):
    return lax.broadcasted_iota(jnp.int32, shape, axis)


def split(values):
    high = values.astype(jnp.bfloat16)
    return high, (values - high.astype(jnp.float32)).astype(jnp.bfloat16)


def later(values, hours):
    rows = values.shape[0]
    if hours % 8 == 0:
        padding = jnp.zeros((hours, values.shape[1]), values.dtype)
        return jnp.concatenate([padding, values[: rows - hours]], axis=0)
    return jnp.where(iota(values.shape, 0) < hours, 0.0, pltpu.roll(values, hours, 0))


def load(sources, targets, arrived):
    copies = [
        pltpu.make_async_copy(source, target, arrived.at[j])
        for j, (source, target) in enumerate(zip(sources, targets))
    ]
    for copy in copies:
        copy.start()
    for copy in copies:
        copy.wait()


def pack_kernel(basin_hbm, kind_hbm, lag_hbm, parent_hbm, meta_ref, basin_ref, kind_ref, lag_ref, parent_ref, arrived):
    load(
        (basin_hbm, kind_hbm, lag_hbm, parent_hbm),
        (basin_ref, kind_ref, lag_ref, parent_ref),
        arrived,
    )
    owners, fields, _ = meta_ref.shape
    rows = [
        values[:, first : first + LANES]
        for values in (basin_ref[...], kind_ref[...], lag_ref[...])
        for first in range(0, values.shape[1], LANES)
    ]
    parents = parent_ref[...]
    empty = jnp.zeros((1, LANES - parents.shape[1]), jnp.int32)
    rows.append(jnp.concatenate([parents, empty], axis=1))
    rows.extend([jnp.zeros((1, LANES), jnp.int32)] * (fields - len(rows)))
    block = jnp.concatenate(rows, axis=0)
    for owner in range(owners):
        meta_ref[owner] = block


def prepare_kernel(
    rain_hbm, soil_hbm, area_hbm, irf_hbm, dest_hbm, reach_hbm,
    tiles_ref, response_ref,
    rain_ref, soil_ref, area_ref, irf_ref, dest_ref, reach_ref, arrived,
):
    load(
        (rain_hbm, soil_hbm, area_hbm, irf_hbm, dest_hbm, reach_hbm),
        (rain_ref, soil_ref, area_ref, irf_ref, dest_ref, reach_ref),
        arrived,
    )
    hours = rain_ref.shape[1]
    kinds, taps = irf_ref.shape
    rainfall = rain_ref[...].astype(jnp.float32).T
    storage = soil_ref[...]
    excess = jnp.maximum(rainfall - 0.2 * storage, 0.0)
    runoff = area_ref[...] * excess * excess / (rainfall + 0.8 * storage)
    tiles_ref[:hours] = runoff.astype(jnp.bfloat16)
    place = iota((ID_ROWS, rain_ref.shape[0]), 0)
    ids = jnp.where(place == 0, dest_ref[...], jnp.where(place == 1, reach_ref[...], 0))
    tiles_ref[hours:] = ids.astype(jnp.float32).astype(jnp.bfloat16)
    backward = (
        iota((taps, hours), 1) == lax.rem(hours - iota((taps, hours), 0), hours)
    ).astype(jnp.float32)
    reversed_taps = lax.dot_general(
        irf_ref[...], backward, NN, precision=lax.Precision.HIGHEST, preferred_element_type=jnp.float32
    )
    causal = iota((hours, hours), 1) <= iota((hours, hours), 0)
    for kind in range(kinds):
        row = jnp.broadcast_to(reversed_taps[kind : kind + 1], (hours, hours))
        matrix = jnp.where(causal, pltpu.roll(row, 0, 1, stride=1, stride_axis=0), 0.0)
        high, low = split(matrix)
        response_ref[:hours, kind * hours : (kind + 1) * hours] = high
        response_ref[hours:, kind * hours : (kind + 1) * hours] = low


def respond_kernel(own_ref, other_ref, response_ref, responses_ref):
    kinds, hours, _ = responses_ref.shape
    runoff = jnp.concatenate([own_ref[:hours], other_ref[:hours]], axis=1)
    for kind in range(kinds):
        both = lax.dot_general(
            response_ref[:, kind * hours : (kind + 1) * hours], runoff, NN, preferred_element_type=jnp.float32
        )
        responses_ref[kind] = both[:hours] + both[hours:]


def route_kernel(meta_ref, own_ref, other_ref, responses_ref, flow_ref, *, owners, reach_rows, basin_rows):
    kinds, hours, tiles = responses_ref.shape
    outlets = flow_ref.shape[0]
    core = lax.rem(lax.axis_index("tile"), CORES)
    shift = basin_rows.bit_length() - 1
    ids = jnp.concatenate([own_ref[hours:], other_ref[hours:]], axis=1).astype(jnp.float32)
    dest = ids[0:1].astype(jnp.int32)
    reach = ids[1:2].astype(jnp.int32)

    stack = meta_ref[...]
    spans = reach_rows // LANES
    fields = stack.shape[0] // owners
    field = iota(stack.shape, 0) % fields
    parents = jnp.where(field == 3 * spans, stack, pltpu.roll(stack, 1, 0))
    stack = jnp.where(field == 3 * spans, lax.shift_right_arithmetic(parents, shift) + 1, stack)
    stack = jnp.where(field == 3 * spans + 1, parents & (basin_rows - 1), stack)
    stack = stack.astype(jnp.float32).T.astype(jnp.bfloat16)

    def marks(row, count):
        return (iota((count, tiles), 0) == row).astype(jnp.float32).astype(jnp.bfloat16)

    def picked(values, chosen):
        return jnp.sum(jnp.where(chosen, values, 0.0), axis=0, keepdims=True).astype(jnp.int32)

    def lookup(owner, first, count):
        place = owner * fields
        mark = jnp.concatenate([marks(place + first + j, owners * fields) for j in range(count)], axis=1)
        found = lax.dot_general(stack, mark, NN, preferred_element_type=jnp.float32)
        return [found[:, j * tiles : (j + 1) * tiles] for j in range(count)]

    by_reach = lookup(dest, 0, 3 * spans)
    at_reach = [iota((LANES, tiles), 0) + j * LANES == reach for j in range(spans)]
    basin, kind, lag = [
        sum(picked(by_reach[c * spans + j], at_reach[j]) for j in range(spans)) for c in range(3)
    ]

    def parent_of(owner, local):
        by_basin = lookup(owner, 3 * spans, 2)
        at_basin = iota((LANES, tiles), 0) == local
        return picked(by_basin[0], at_basin) - 1, picked(by_basin[1], at_basin)

    parent_owner, parent_local = parent_of(dest, basin)
    second_owner, second_local = parent_of(parent_owner, parent_local)
    def row_of(owner, local):
        return jnp.where((owner & (CORES - 1)) == core, (owner // CORES) * basin_rows + local, -1)

    targets = [
        row_of(dest, basin),
        jnp.where(parent_owner < 0, -1, row_of(parent_owner, parent_local)),
        jnp.where(second_owner < 0, -1, row_of(second_owner, second_local)),
    ]

    routed = responses_ref[0]
    for k in range(1, kinds):
        routed = jnp.where(kind == k, responses_ref[k], routed)
    step = 64
    while step:
        routed = jnp.where((lag & step) != 0, later(routed, step), routed)
        step //= 2
    pieces, placements = [], []
    for target in targets:
        pieces.extend(split(routed))
        mark = marks(target, outlets)
        placements.extend([mark, mark])
        routed = later(routed, LINK)
    flow = lax.dot_general(
        jnp.concatenate(placements, axis=1),
        jnp.concatenate(pieces, axis=1),
        NT,
        preferred_element_type=jnp.float32,
    )
    level = jnp.log(jnp.maximum(flow, CODE_FLOOR)) * CODE_SCALE + (CODE_ZERO + CODE_TOP + 0.5)
    level = jnp.clip(level, 0.0, 2.0 * CODE_TOP).astype(jnp.int32) - CODE_TOP
    flow_ref[...] = level.astype(jnp.int16)


def finish_kernel(parts_ref, section_ref):
    level = parts_ref[...].astype(jnp.int32)
    flow = jnp.exp((level.astype(jnp.float32) - CODE_ZERO) * (1.0 / CODE_SCALE))
    flow = jnp.sum(jnp.where(level == -CODE_TOP, 0.0, flow), axis=0)
    section_ref[...] = jnp.log(1.0 + flow)


def per_device(
    rain,
    soil,
    tile_area,
    tile_dest,
    tile_reach,
    reach_basin,
    reach_kind,
    reach_lag,
    irf,
    outlet_level,
    outlet_parent,
):
    owners = lax.axis_size("tile")
    tile_rows, hours = rain.shape
    basin_rows = outlet_parent.shape[0]
    kinds = irf.shape[0]
    params = pltpu.CompilerParams(vmem_limit_bytes=VMEM_BYTES)

    row = (1, tile_rows)
    fields = 8 * pl.cdiv(3 * reach_basin.size // LANES + 2, 8)

    def in_hbm(values, shape):
        return pltpu.with_memory_space_constraint(values.reshape(shape), pltpu.HBM)

    held = pl.BlockSpec(memory_space=pltpu.HBM)
    meta = pl.pallas_call(
        pack_kernel,
        out_shape=jax.ShapeDtypeStruct((owners, fields, LANES), jnp.int32),
        in_specs=[held] * 4,
        scratch_shapes=[
            pltpu.VMEM((1, reach_basin.size), jnp.int32),
            pltpu.VMEM((1, reach_basin.size), jnp.int32),
            pltpu.VMEM((1, reach_basin.size), jnp.int32),
            pltpu.VMEM((1, basin_rows), jnp.int32),
            pltpu.SemaphoreType.DMA((4,)),
        ],
        compiler_params=params,
        name="pack",
    )(
        in_hbm(reach_basin, (1, -1)),
        in_hbm(reach_kind, (1, -1)),
        in_hbm(reach_lag, (1, -1)),
        in_hbm(outlet_parent, (1, -1)),
    )
    meta = lax.all_to_all(meta, "tile", split_axis=0, concat_axis=0, tiled=True).reshape(-1, LANES)

    tiles, response = pl.pallas_call(
        prepare_kernel,
        out_shape=(
            jax.ShapeDtypeStruct((hours + ID_ROWS, tile_rows), jnp.bfloat16),
            jax.ShapeDtypeStruct((2 * hours, kinds * hours), jnp.bfloat16),
        ),
        in_specs=[held] * 6,
        scratch_shapes=[
            pltpu.VMEM(rain.shape, rain.dtype),
            pltpu.VMEM(row, jnp.float32),
            pltpu.VMEM(row, jnp.float32),
            pltpu.VMEM(irf.shape, jnp.float32),
            pltpu.VMEM(row, jnp.int32),
            pltpu.VMEM(row, jnp.int32),
            pltpu.SemaphoreType.DMA((6,)),
        ],
        compiler_params=params,
        name="prepare",
    )(
        in_hbm(rain, rain.shape),
        in_hbm(soil, row),
        in_hbm(tile_area, row),
        in_hbm(irf, irf.shape),
        in_hbm(tile_dest, row),
        in_hbm(tile_reach, row),
    )
    others = lax.ppermute(tiles, "tile", [(i, i ^ 1) for i in range(owners)])

    responses = pl.pallas_call(
        respond_kernel,
        out_shape=jax.ShapeDtypeStruct((kinds, hours, CORES * tile_rows), jnp.float32),
        compiler_params=params,
        name="respond",
    )(tiles, others, response)

    flow = pl.pallas_call(
        lambda *refs: route_kernel(
            *refs, owners=owners, reach_rows=reach_basin.shape[0], basin_rows=basin_rows
        ),
        out_shape=jax.ShapeDtypeStruct((owners // CORES * basin_rows, hours), jnp.int16),
        compiler_params=params,
        name="route",
    )(meta, tiles, others, responses)

    parts = lax.all_to_all(
        flow.reshape(owners // CORES, basin_rows, hours),
        "tile",
        split_axis=0,
        concat_axis=0,
        axis_index_groups=[list(range(core, owners, CORES)) for core in range(CORES)],
        tiled=True,
    )
    return pl.pallas_call(
        finish_kernel,
        out_shape=jax.ShapeDtypeStruct((basin_rows, hours), jnp.float32),
        compiler_params=params,
        name="finish",
    )(parts)


def solution(mesh):
    rows = P(("ens", "tile"))
    table = P(("ens", "tile"), None)
    in_specs = (table, rows, rows, table, rows, rows, rows, rows, P(), rows, rows)
    return jax.shard_map(
        per_device, mesh=mesh, in_specs=in_specs, out_specs=table, check_vma=False
    )
```

```python
import math

import jax
import jax.numpy as jnp
from jax import lax
from jax.experimental import pallas as pl
from jax.experimental.pallas import tpu as pltpu
from jax.sharding import PartitionSpec as P

LINK = 6
LANES = 128
CORES = 2
ID_ROWS = 16
VMEM_BYTES = 40 * 1024 * 1024
CODE_TOP = 32767
CODE_OCTAVES = 44
CODE_LOWEST = -26
CODE_SCALE = 2 * CODE_TOP / (CODE_OCTAVES * math.log(2.0))
CODE_FLOOR = 2.0 ** (2 * CODE_LOWEST)
CODE_ZERO = -CODE_TOP + 1 - CODE_LOWEST * math.log(2.0) * CODE_SCALE

NT = (((1,), (1,)), ((), ()))
NN = (((1,), (0,)), ((), ()))


def iota(shape, axis):
    return lax.broadcasted_iota(jnp.int32, shape, axis)


def split(values):
    high = values.astype(jnp.bfloat16)
    return high, (values - high.astype(jnp.float32)).astype(jnp.bfloat16)


def later(values, hours):
    rows = values.shape[0]
    if hours % 8 == 0:
        padding = jnp.zeros((hours, values.shape[1]), values.dtype)
        return jnp.concatenate([padding, values[: rows - hours]], axis=0)
    return jnp.where(iota(values.shape, 0) < hours, 0.0, pltpu.roll(values, hours, 0))


def load(sources, targets, arrived):
    copies = [
        pltpu.make_async_copy(source, target, arrived.at[j])
        for j, (source, target) in enumerate(zip(sources, targets))
    ]
    for copy in copies:
        copy.start()
    for copy in copies:
        copy.wait()


def prepare_kernel(*refs, early):
    sources, refs = refs[:10], refs[10:]
    meta_ref, tiles_ref, response_ref, late_response_ref, *scratch, arrived = refs
    load(sources, scratch, arrived)
    (
        basin_ref, kind_ref, lag_ref, parent_ref, rain_ref, soil_ref, area_ref, irf_ref, dest_ref, reach_ref,
    ) = scratch
    owners, fields, _ = meta_ref.shape
    rows = [
        values[:, first : first + LANES]
        for values in (basin_ref[...], kind_ref[...], lag_ref[...])
        for first in range(0, values.shape[1], LANES)
    ]
    parents = parent_ref[...]
    empty = jnp.zeros((1, LANES - parents.shape[1]), jnp.int32)
    rows.append(jnp.concatenate([parents, empty], axis=1))
    rows.extend([jnp.zeros((1, LANES), jnp.int32)] * (fields - len(rows)))
    block = jnp.concatenate(rows, axis=0)
    for owner in range(owners):
        meta_ref[owner] = block
    hours = rain_ref.shape[1]
    kinds, taps = irf_ref.shape
    rainfall = rain_ref[...].astype(jnp.float32).T
    storage = soil_ref[...]
    excess = jnp.maximum(rainfall - 0.2 * storage, 0.0)
    runoff = area_ref[...] * excess * excess / (rainfall + 0.8 * storage)
    tiles_ref[:hours] = runoff.astype(jnp.bfloat16)
    place = iota((ID_ROWS, rain_ref.shape[0]), 0)
    ids = jnp.where(place == 0, dest_ref[...], jnp.where(place == 1, reach_ref[...], 0))
    tiles_ref[hours:] = ids.astype(jnp.float32).astype(jnp.bfloat16)
    backward = (
        iota((taps, hours), 1) == lax.rem(hours - iota((taps, hours), 0), hours)
    ).astype(jnp.float32)
    reversed_taps = lax.dot_general(
        irf_ref[...], backward, NN, precision=lax.Precision.HIGHEST, preferred_element_type=jnp.float32
    )
    causal = iota((hours, hours), 1) <= iota((hours, hours), 0)
    for kind in range(kinds):
        row = jnp.broadcast_to(reversed_taps[kind : kind + 1], (hours, hours))
        matrix = jnp.where(causal, pltpu.roll(row, 0, 1, stride=1, stride_axis=0), 0.0)
        high, low = split(matrix)
        target = response_ref if kind < early else late_response_ref
        first = hours * (kind if kind < early else kind - early)
        target[:hours, first : first + hours] = high
        target[hours:, first : first + hours] = low


def respond_kernel(own_ref, other_ref, response_ref, responses_ref):
    kinds, hours, _ = responses_ref.shape
    runoff = jnp.concatenate([own_ref[:hours], other_ref[:hours]], axis=1)
    for kind in range(kinds):
        both = lax.dot_general(
            response_ref[:, kind * hours : (kind + 1) * hours], runoff, NN, preferred_element_type=jnp.float32
        )
        responses_ref[kind] = both[:hours] + both[hours:]


def route_kernel(
    meta_ref, own_ref, other_ref, responses_ref, late_response_ref, flow_ref, *, owners, reach_rows, basin_rows
):
    early, hours, tiles = responses_ref.shape
    late = late_response_ref.shape[1] // hours
    outlets = flow_ref.shape[0]
    core = lax.rem(lax.axis_index("tile"), CORES)
    shift = basin_rows.bit_length() - 1
    ids = jnp.concatenate([own_ref[hours:], other_ref[hours:]], axis=1).astype(jnp.float32)
    dest = ids[0:1].astype(jnp.int32)
    reach = ids[1:2].astype(jnp.int32)

    stack = meta_ref[...]
    spans = reach_rows // LANES
    fields = stack.shape[0] // owners
    field = iota(stack.shape, 0) % fields
    parents = jnp.where(field == 3 * spans, stack, pltpu.roll(stack, 1, 0))
    stack = jnp.where(field == 3 * spans, lax.shift_right_arithmetic(parents, shift) + 1, stack)
    stack = jnp.where(field == 3 * spans + 1, parents & (basin_rows - 1), stack)
    stack = stack.astype(jnp.float32).T.astype(jnp.bfloat16)

    def marks(row, count):
        return (iota((count, tiles), 0) == row).astype(jnp.float32).astype(jnp.bfloat16)

    def picked(values, chosen):
        return jnp.sum(jnp.where(chosen, values, 0.0), axis=0, keepdims=True).astype(jnp.int32)

    def lookup(owner, first, count):
        place = owner * fields
        mark = jnp.concatenate([marks(place + first + j, owners * fields) for j in range(count)], axis=1)
        found = lax.dot_general(stack, mark, NN, preferred_element_type=jnp.float32)
        return [found[:, j * tiles : (j + 1) * tiles] for j in range(count)]

    by_reach = lookup(dest, 0, 3 * spans)
    at_reach = [iota((LANES, tiles), 0) + j * LANES == reach for j in range(spans)]
    basin, kind, lag = [
        sum(picked(by_reach[c * spans + j], at_reach[j]) for j in range(spans)) for c in range(3)
    ]

    def parent_of(owner, local):
        by_basin = lookup(owner, 3 * spans, 2)
        at_basin = iota((LANES, tiles), 0) == local
        return picked(by_basin[0], at_basin) - 1, picked(by_basin[1], at_basin)

    parent_owner, parent_local = parent_of(dest, basin)
    second_owner, second_local = parent_of(parent_owner, parent_local)
    def row_of(owner, local):
        return jnp.where((owner & (CORES - 1)) == core, (owner // CORES) * basin_rows + local, -1)

    targets = [
        row_of(dest, basin),
        jnp.where(parent_owner < 0, -1, row_of(parent_owner, parent_local)),
        jnp.where(second_owner < 0, -1, row_of(second_owner, second_local)),
    ]

    runoff = jnp.concatenate([own_ref[:hours], other_ref[:hours]], axis=1)
    by_kind = jnp.concatenate(
        [
            runoff * (kind == early + k).astype(jnp.float32).astype(jnp.bfloat16)
            for k in range(late)
        ],
        axis=0,
    )
    both = lax.dot_general(late_response_ref[...], by_kind, NN, preferred_element_type=jnp.float32)
    routed = both[:hours] + both[hours:]
    for k in range(early):
        routed = jnp.where(kind == k, responses_ref[k], routed)
    step = 64
    while step:
        routed = jnp.where((lag & step) != 0, later(routed, step), routed)
        step //= 2
    pieces, placements = [], []
    for target in targets:
        pieces.extend(split(routed))
        mark = marks(target, outlets)
        placements.extend([mark, mark])
        routed = later(routed, LINK)
    flow = lax.dot_general(
        jnp.concatenate(placements, axis=1),
        jnp.concatenate(pieces, axis=1),
        NT,
        preferred_element_type=jnp.float32,
    )
    level = jnp.log(jnp.maximum(flow, CODE_FLOOR)) * CODE_SCALE + (CODE_ZERO + CODE_TOP + 0.5)
    level = jnp.clip(level, 0.0, 2.0 * CODE_TOP).astype(jnp.int32) - CODE_TOP
    flow_ref[...] = level.astype(jnp.int16)


def finish_kernel(parts_ref, section_ref):
    level = parts_ref[...].astype(jnp.int32)
    flow = jnp.exp((level.astype(jnp.float32) - CODE_ZERO) * (1.0 / CODE_SCALE))
    flow = jnp.sum(jnp.where(level == -CODE_TOP, 0.0, flow), axis=0)
    section_ref[...] = jnp.log(1.0 + flow)


def per_device(
    rain,
    soil,
    tile_area,
    tile_dest,
    tile_reach,
    reach_basin,
    reach_kind,
    reach_lag,
    irf,
    outlet_level,
    outlet_parent,
):
    owners = lax.axis_size("tile")
    tile_rows, hours = rain.shape
    basin_rows = outlet_parent.shape[0]
    kinds = irf.shape[0]
    params = pltpu.CompilerParams(vmem_limit_bytes=VMEM_BYTES)

    row = (1, tile_rows)
    fields = 8 * pl.cdiv(3 * reach_basin.size // LANES + 2, 8)

    arguments = [
        pltpu.with_memory_space_constraint(values.reshape(shape), pltpu.HBM)
        for values, shape in (
            (reach_basin, (1, -1)),
            (reach_kind, (1, -1)),
            (reach_lag, (1, -1)),
            (outlet_parent, (1, -1)),
            (rain, rain.shape),
            (soil, row),
            (tile_area, row),
            (irf, irf.shape),
            (tile_dest, row),
            (tile_reach, row),
        )
    ]
    early = kinds // 2
    meta, tiles, response, late_response = pl.pallas_call(
        lambda *refs: prepare_kernel(*refs, early=early),
        out_shape=(
            jax.ShapeDtypeStruct((owners, fields, LANES), jnp.int32),
            jax.ShapeDtypeStruct((hours + ID_ROWS, tile_rows), jnp.bfloat16),
            jax.ShapeDtypeStruct((2 * hours, early * hours), jnp.bfloat16),
            jax.ShapeDtypeStruct((2 * hours, (kinds - early) * hours), jnp.bfloat16),
        ),
        in_specs=[pl.BlockSpec(memory_space=pltpu.HBM)] * len(arguments),
        scratch_shapes=[pltpu.VMEM(values.shape, values.dtype) for values in arguments]
        + [pltpu.SemaphoreType.DMA((len(arguments),))],
        compiler_params=params,
        name="prepare",
    )(*arguments)
    meta = lax.all_to_all(meta, "tile", split_axis=0, concat_axis=0, tiled=True).reshape(-1, LANES)
    others = lax.ppermute(tiles, "tile", [(i, i ^ 1) for i in range(owners)])

    responses = pl.pallas_call(
        respond_kernel,
        out_shape=jax.ShapeDtypeStruct((early, hours, CORES * tile_rows), jnp.float32),
        compiler_params=params,
        name="respond",
    )(tiles, others, response)

    flow = pl.pallas_call(
        lambda *refs: route_kernel(
            *refs, owners=owners, reach_rows=reach_basin.shape[0], basin_rows=basin_rows
        ),
        out_shape=jax.ShapeDtypeStruct((owners // CORES * basin_rows, hours), jnp.int16),
        compiler_params=params,
        name="route",
    )(meta, tiles, others, responses, late_response)

    parts = lax.all_to_all(
        flow.reshape(owners // CORES, basin_rows, hours),
        "tile",
        split_axis=0,
        concat_axis=0,
        axis_index_groups=[list(range(core, owners, CORES)) for core in range(CORES)],
        tiled=True,
    )
    return pl.pallas_call(
        finish_kernel,
        out_shape=jax.ShapeDtypeStruct((basin_rows, hours), jnp.float32),
        compiler_params=params,
        name="finish",
    )(parts)


def solution(mesh):
    rows = P(("ens", "tile"))
    table = P(("ens", "tile"), None)
    in_specs = (table, rows, rows, table, rows, rows, rows, rows, P(), rows, rows)
    return jax.shard_map(
        per_device, mesh=mesh, in_specs=in_specs, out_specs=table, check_vma=False
    )
```

```python
import math

import jax
import jax.numpy as jnp
from jax import lax
from jax.experimental import pallas as pl
from jax.experimental.pallas import tpu as pltpu
from jax.sharding import PartitionSpec as P

LINK = 6
LANES = 128
CORES = 2
ID_ROWS = 16
VMEM_BYTES = 40 * 1024 * 1024
CODE_TOP = 32767
CODE_OCTAVES = 44
CODE_LOWEST = -26
CODE_SCALE = 2 * CODE_TOP / (CODE_OCTAVES * math.log(2.0))
CODE_FLOOR = 2.0 ** (2 * CODE_LOWEST)
CODE_ZERO = -CODE_TOP + 1 - CODE_LOWEST * math.log(2.0) * CODE_SCALE

SMALL = pl.CostEstimate(flops=1, bytes_accessed=1, transcendentals=0)
NT = (((1,), (1,)), ((), ()))
NN = (((1,), (0,)), ((), ()))


def iota(shape, axis):
    return lax.broadcasted_iota(jnp.int32, shape, axis)


def split(values):
    high = values.astype(jnp.bfloat16)
    return high, (values - high.astype(jnp.float32)).astype(jnp.bfloat16)


def later(values, hours):
    rows = values.shape[0]
    if hours % 8 == 0:
        padding = jnp.zeros((hours, values.shape[1]), values.dtype)
        return jnp.concatenate([padding, values[: rows - hours]], axis=0)
    return jnp.where(iota(values.shape, 0) < hours, 0.0, pltpu.roll(values, hours, 0))


def load(sources, targets, arrived):
    copies = [
        pltpu.make_async_copy(source, target, arrived.at[j])
        for j, (source, target) in enumerate(zip(sources, targets))
    ]
    for copy in copies:
        copy.start()
    for copy in copies:
        copy.wait()


def pack_kernel(basin_hbm, kind_hbm, lag_hbm, parent_hbm, meta_ref, basin_ref, kind_ref, lag_ref, parent_ref, arrived):
    load(
        (basin_hbm, kind_hbm, lag_hbm, parent_hbm),
        (basin_ref, kind_ref, lag_ref, parent_ref),
        arrived,
    )
    owners, fields, _ = meta_ref.shape
    rows = [
        values[:, first : first + LANES]
        for values in (basin_ref[...], kind_ref[...], lag_ref[...])
        for first in range(0, values.shape[1], LANES)
    ]
    parents = parent_ref[...]
    empty = jnp.zeros((1, LANES - parents.shape[1]), jnp.int32)
    rows.append(jnp.concatenate([parents, empty], axis=1))
    rows.extend([jnp.zeros((1, LANES), jnp.int32)] * (fields - len(rows)))
    block = jnp.concatenate(rows, axis=0)
    for owner in range(owners):
        meta_ref[owner] = block


def prepare_kernel(after_hbm, *refs, early):
    del after_hbm
    sources, (tiles_ref, response_ref, late_response_ref, *scratch, arrived) = refs[:6], refs[6:]
    rain_ref, soil_ref, area_ref, irf_ref, dest_ref, reach_ref = scratch
    load(sources, scratch, arrived)
    hours = rain_ref.shape[1]
    kinds, taps = irf_ref.shape
    rainfall = rain_ref[...].astype(jnp.float32).T
    storage = soil_ref[...]
    excess = jnp.maximum(rainfall - 0.2 * storage, 0.0)
    runoff = area_ref[...] * excess * excess / (rainfall + 0.8 * storage)
    tiles_ref[:hours] = runoff.astype(jnp.bfloat16)
    place = iota((ID_ROWS, rain_ref.shape[0]), 0)
    ids = jnp.where(place == 0, dest_ref[...], jnp.where(place == 1, reach_ref[...], 0))
    tiles_ref[hours:] = ids.astype(jnp.float32).astype(jnp.bfloat16)
    backward = (
        iota((taps, hours), 1) == lax.rem(hours - iota((taps, hours), 0), hours)
    ).astype(jnp.float32)
    reversed_taps = lax.dot_general(
        irf_ref[...], backward, NN, precision=lax.Precision.HIGHEST, preferred_element_type=jnp.float32
    )
    causal = iota((hours, hours), 1) <= iota((hours, hours), 0)
    for kind in range(kinds):
        row = jnp.broadcast_to(reversed_taps[kind : kind + 1], (hours, hours))
        matrix = jnp.where(causal, pltpu.roll(row, 0, 1, stride=1, stride_axis=0), 0.0)
        high, low = split(matrix)
        target = response_ref if kind < early else late_response_ref
        first = hours * (kind if kind < early else kind - early)
        target[:hours, first : first + hours] = high
        target[hours:, first : first + hours] = low


def respond_kernel(own_ref, other_ref, response_ref, responses_ref):
    kinds, hours, _ = responses_ref.shape
    runoff = jnp.concatenate([own_ref[:hours], other_ref[:hours]], axis=1)
    for kind in range(kinds):
        both = lax.dot_general(
            response_ref[:, kind * hours : (kind + 1) * hours], runoff, NN, preferred_element_type=jnp.float32
        )
        responses_ref[kind] = both[:hours] + both[hours:]


def route_kernel(
    meta_ref, own_ref, other_ref, responses_ref, late_response_ref, flow_ref, *, owners, reach_rows, basin_rows
):
    early, hours, tiles = responses_ref.shape
    late = late_response_ref.shape[1] // hours
    outlets = flow_ref.shape[0]
    core = lax.rem(lax.axis_index("tile"), CORES)
    shift = basin_rows.bit_length() - 1
    ids = jnp.concatenate([own_ref[hours:], other_ref[hours:]], axis=1).astype(jnp.float32)
    dest = ids[0:1].astype(jnp.int32)
    reach = ids[1:2].astype(jnp.int32)

    stack = meta_ref[...]
    spans = reach_rows // LANES
    fields = stack.shape[0] // owners
    field = iota(stack.shape, 0) % fields
    parents = jnp.where(field == 3 * spans, stack, pltpu.roll(stack, 1, 0))
    stack = jnp.where(field == 3 * spans, lax.shift_right_arithmetic(parents, shift) + 1, stack)
    stack = jnp.where(field == 3 * spans + 1, parents & (basin_rows - 1), stack)
    stack = stack.astype(jnp.float32).T.astype(jnp.bfloat16)

    def marks(row, count):
        return (iota((count, tiles), 0) == row).astype(jnp.float32).astype(jnp.bfloat16)

    def picked(values, chosen):
        return jnp.sum(jnp.where(chosen, values, 0.0), axis=0, keepdims=True).astype(jnp.int32)

    def lookup(owner, first, count):
        place = owner * fields
        mark = jnp.concatenate([marks(place + first + j, owners * fields) for j in range(count)], axis=1)
        found = lax.dot_general(stack, mark, NN, preferred_element_type=jnp.float32)
        return [found[:, j * tiles : (j + 1) * tiles] for j in range(count)]

    by_reach = lookup(dest, 0, 3 * spans)
    at_reach = [iota((LANES, tiles), 0) + j * LANES == reach for j in range(spans)]
    basin, kind, lag = [
        sum(picked(by_reach[c * spans + j], at_reach[j]) for j in range(spans)) for c in range(3)
    ]

    def parent_of(owner, local):
        by_basin = lookup(owner, 3 * spans, 2)
        at_basin = iota((LANES, tiles), 0) == local
        return picked(by_basin[0], at_basin) - 1, picked(by_basin[1], at_basin)

    parent_owner, parent_local = parent_of(dest, basin)
    second_owner, second_local = parent_of(parent_owner, parent_local)
    def row_of(owner, local):
        return jnp.where((owner & (CORES - 1)) == core, (owner // CORES) * basin_rows + local, -1)

    targets = [
        row_of(dest, basin),
        jnp.where(parent_owner < 0, -1, row_of(parent_owner, parent_local)),
        jnp.where(second_owner < 0, -1, row_of(second_owner, second_local)),
    ]

    runoff = jnp.concatenate([own_ref[:hours], other_ref[:hours]], axis=1)
    by_kind = jnp.concatenate(
        [
            runoff * (kind == early + k).astype(jnp.float32).astype(jnp.bfloat16)
            for k in range(late)
        ],
        axis=0,
    )
    both = lax.dot_general(late_response_ref[...], by_kind, NN, preferred_element_type=jnp.float32)
    routed = both[:hours] + both[hours:]
    for k in range(early):
        routed = jnp.where(kind == k, responses_ref[k], routed)
    step = 64
    while step:
        routed = jnp.where((lag & step) != 0, later(routed, step), routed)
        step //= 2
    pieces, placements = [], []
    for target in targets:
        pieces.extend(split(routed))
        mark = marks(target, outlets)
        placements.extend([mark, mark])
        routed = later(routed, LINK)
    flow = lax.dot_general(
        jnp.concatenate(placements, axis=1),
        jnp.concatenate(pieces, axis=1),
        NT,
        preferred_element_type=jnp.float32,
    )
    level = jnp.log(jnp.maximum(flow, CODE_FLOOR)) * CODE_SCALE + (CODE_ZERO + CODE_TOP + 0.5)
    level = jnp.clip(level, 0.0, 2.0 * CODE_TOP).astype(jnp.int32) - CODE_TOP
    flow_ref[...] = level.astype(jnp.int16)


def finish_kernel(parts_ref, section_ref):
    level = parts_ref[...].astype(jnp.int32)
    flow = jnp.exp((level.astype(jnp.float32) - CODE_ZERO) * (1.0 / CODE_SCALE))
    flow = jnp.sum(jnp.where(level == -CODE_TOP, 0.0, flow), axis=0)
    section_ref[...] = jnp.log(1.0 + flow)


def per_device(
    rain,
    soil,
    tile_area,
    tile_dest,
    tile_reach,
    reach_basin,
    reach_kind,
    reach_lag,
    irf,
    outlet_level,
    outlet_parent,
):
    owners = lax.axis_size("tile")
    tile_rows, hours = rain.shape
    basin_rows = outlet_parent.shape[0]
    kinds = irf.shape[0]
    params = pltpu.CompilerParams(vmem_limit_bytes=VMEM_BYTES)

    row = (1, tile_rows)
    fields = 8 * pl.cdiv(3 * reach_basin.size // LANES + 2, 8)

    held = pl.BlockSpec(memory_space=pltpu.HBM)

    def in_hbm(values, shape):
        return pltpu.with_memory_space_constraint(values.reshape(shape), pltpu.HBM)

    def loaded(arguments):
        shapes = [pltpu.VMEM(values.shape, values.dtype) for values in arguments]
        return shapes + [pltpu.SemaphoreType.DMA((len(arguments),))]

    numbers = [in_hbm(values, (1, -1)) for values in (reach_basin, reach_kind, reach_lag, outlet_parent)]
    packed = pl.pallas_call(
        pack_kernel,
        out_shape=jax.ShapeDtypeStruct((owners, fields, LANES), jnp.int32),
        in_specs=[held] * len(numbers),
        scratch_shapes=loaded(numbers),
        compiler_params=params,
        cost_estimate=SMALL,
        name="pack",
    )(*numbers)
    meta = lax.all_to_all(packed, "tile", split_axis=0, concat_axis=0, tiled=True).reshape(-1, LANES)

    arguments = [
        in_hbm(rain, rain.shape),
        in_hbm(soil, row),
        in_hbm(tile_area, row),
        in_hbm(irf, irf.shape),
        in_hbm(tile_dest, row),
        in_hbm(tile_reach, row),
    ]
    early = kinds // 2
    tiles, response, late_response = pl.pallas_call(
        lambda *refs: prepare_kernel(*refs, early=early),
        out_shape=(
            jax.ShapeDtypeStruct((hours + ID_ROWS, tile_rows), jnp.bfloat16),
            jax.ShapeDtypeStruct((2 * hours, early * hours), jnp.bfloat16),
            jax.ShapeDtypeStruct((2 * hours, (kinds - early) * hours), jnp.bfloat16),
        ),
        in_specs=[held] * (len(arguments) + 1),
        scratch_shapes=loaded(arguments),
        compiler_params=params,
        cost_estimate=SMALL,
        name="prepare",
    )(in_hbm(packed, packed.shape), *arguments)
    others = lax.ppermute(tiles, "tile", [(i, i ^ 1) for i in range(owners)])

    responses = pl.pallas_call(
        respond_kernel,
        out_shape=jax.ShapeDtypeStruct((early, hours, CORES * tile_rows), jnp.float32),
        compiler_params=params,
        cost_estimate=SMALL,
        name="respond",
    )(tiles, others, response)

    flow = pl.pallas_call(
        lambda *refs: route_kernel(
            *refs, owners=owners, reach_rows=reach_basin.shape[0], basin_rows=basin_rows
        ),
        out_shape=jax.ShapeDtypeStruct((owners // CORES * basin_rows, hours), jnp.int16),
        compiler_params=params,
        name="route",
    )(meta, tiles, others, responses, late_response)

    parts = lax.all_to_all(
        flow.reshape(owners // CORES, basin_rows, hours),
        "tile",
        split_axis=0,
        concat_axis=0,
        axis_index_groups=[list(range(core, owners, CORES)) for core in range(CORES)],
        tiled=True,
    )
    return pl.pallas_call(
        finish_kernel,
        out_shape=jax.ShapeDtypeStruct((basin_rows, hours), jnp.float32),
        compiler_params=params,
        name="finish",
    )(parts)


def solution(mesh):
    rows = P(("ens", "tile"))
    table = P(("ens", "tile"), None)
    in_specs = (table, rows, rows, table, rows, rows, rows, rows, P(), rows, rows)
    return jax.shard_map(
        per_device, mesh=mesh, in_specs=in_specs, out_specs=table, check_vma=False
    )
```

```python
import math

import jax
import jax.numpy as jnp
from jax import lax
from jax.experimental import pallas as pl
from jax.experimental.pallas import tpu as pltpu
from jax.sharding import PartitionSpec as P

LINK = 6
LANES = 128
CORES = 2
FIELDS = 8
VMEM_BYTES = 40 * 1024 * 1024
CODE_TOP = 32767
CODE_OCTAVES = 44
CODE_LOWEST = -26
CODE_SCALE = 2 * CODE_TOP / (CODE_OCTAVES * math.log(2.0))
CODE_FLOOR = 2.0 ** (2 * CODE_LOWEST)
CODE_ZERO = -CODE_TOP + 1 - CODE_LOWEST * math.log(2.0) * CODE_SCALE

SMALL = pl.CostEstimate(flops=1, bytes_accessed=1, transcendentals=0)
NT = (((1,), (1,)), ((), ()))
NN = (((1,), (0,)), ((), ()))


def iota(shape, axis):
    return lax.broadcasted_iota(jnp.int32, shape, axis)


def split(values):
    high = values.astype(jnp.bfloat16)
    return high, (values - high.astype(jnp.float32)).astype(jnp.bfloat16)


def one_hot(row, count):
    return (iota((count, row.shape[1]), 0) == row).astype(jnp.float32).astype(jnp.bfloat16)


def later_rows(values, hours):
    rows = values.shape[0]
    if hours % 8 == 0:
        padding = jnp.zeros((hours, values.shape[1]), values.dtype)
        return jnp.concatenate([padding, values[: rows - hours]], axis=0)
    return jnp.where(iota(values.shape, 0) < hours, 0.0, pltpu.roll(values, hours, 0))


def later_lanes(values, hours):
    return jnp.where(iota(values.shape, 1) < hours, 0.0, pltpu.roll(values, hours, 1))


def load(sources, targets, arrived):
    copies = [
        pltpu.make_async_copy(source, target, arrived.at[j])
        for j, (source, target) in enumerate(zip(sources, targets))
    ]
    for copy in copies:
        copy.start()
    for copy in copies:
        copy.wait()


def lane_rows(values):
    return [values[:, first : first + LANES] for first in range(0, values.shape[1], LANES)]


def pack_kernel(*refs, basin_rows):
    sources, (meta_ref, side_ref, *scratch, arrived) = refs[:8], refs[8:]
    load(sources, scratch, arrived)
    basin, kind, lag, parent, soil, area, dest, reach = [ref[...] for ref in scratch]
    shift = basin_rows.bit_length() - 1
    empty = jnp.zeros((1, LANES - basin_rows), jnp.int32)
    rows = lane_rows(basin) + lane_rows(kind) + lane_rows(lag)
    rows.append(jnp.concatenate([lax.shift_right_arithmetic(parent, shift) + 1, empty], axis=1))
    rows.append(jnp.concatenate([parent & (basin_rows - 1), empty], axis=1))
    block = jnp.concatenate(rows, axis=0).astype(jnp.float32)
    meta_ref[...] = jnp.concatenate([block] * (meta_ref.shape[0] // FIELDS), axis=0).astype(jnp.bfloat16)
    side_ref[...] = jnp.concatenate(
        lane_rows(soil)
        + lane_rows(area)
        + lane_rows(dest.astype(jnp.float32))
        + lane_rows(reach.astype(jnp.float32)),
        axis=0,
    )


def prepare_kernel(
    rain_hbm, irf_hbm, other_rain_ref, side_ref, other_side_ref,
    runoff_ref, ids_ref, responses_ref, late_response_ref,
    rain_ref, irf_ref, arrived,
):
    load((rain_hbm, irf_hbm), (rain_ref, irf_ref), arrived)
    tile_rows, hours = rain_ref.shape
    kinds, taps = irf_ref.shape
    early = responses_ref.shape[0]
    spans = tile_rows // LANES
    sides = (side_ref[...], other_side_ref[...])

    def side_row(item):
        return jnp.concatenate(
            [side[j : j + 1] for side in sides for j in range(item * spans, (item + 1) * spans)], axis=1
        )

    rainfall = jnp.concatenate(
        [rain_ref[...].astype(jnp.float32).T, other_rain_ref[...].astype(jnp.float32).T], axis=1
    )
    storage = side_row(0)
    excess = jnp.maximum(rainfall - 0.2 * storage, 0.0)
    runoff = (side_row(1) * excess * excess / (rainfall + 0.8 * storage)).astype(jnp.bfloat16)
    runoff_ref[...] = runoff
    ids_ref[...] = jnp.concatenate([side_row(2), side_row(3)] * 4, axis=0).astype(jnp.int32)
    backward = (
        iota((taps, hours), 1) == lax.rem(hours - iota((taps, hours), 0), hours)
    ).astype(jnp.float32)
    reversed_taps = lax.dot_general(
        irf_ref[...], backward, NN, precision=lax.Precision.HIGHEST, preferred_element_type=jnp.float32
    )
    causal = iota((hours, hours), 1) <= iota((hours, hours), 0)
    for kind in range(kinds):
        row = jnp.broadcast_to(reversed_taps[kind : kind + 1], (hours, hours))
        matrix = jnp.where(causal, pltpu.roll(row, 0, 1, stride=1, stride_axis=0), 0.0)
        matrix = jnp.concatenate(split(matrix), axis=0)
        if kind < early:
            both = lax.dot_general(matrix, runoff, NN, preferred_element_type=jnp.float32)
            responses_ref[kind] = both[:hours] + both[hours:]
        else:
            late_response_ref[:, (kind - early) * hours : (kind - early + 1) * hours] = matrix


def route_kernel(meta_ref, runoff_ref, ids_ref, responses_ref, late_response_ref, flow_ref, stack_ref, *, basin_rows):
    early, hours, tiles = responses_ref.shape
    late = late_response_ref.shape[1] // hours
    outlets = flow_ref.shape[0]
    owners = meta_ref.shape[0] // FIELDS
    core = lax.rem(lax.axis_index("tile"), CORES)
    dest = ids_ref[0:1]
    reach = ids_ref[1:2]

    stack_ref[...] = meta_ref[...].astype(jnp.float32)

    def table(field):
        return stack_ref[pl.ds(field, owners, stride=FIELDS), :].astype(jnp.bfloat16)

    def picked(values, owner):
        chosen = iota((owners, tiles), 0) == owner
        return jnp.sum(jnp.where(chosen, values, 0.0), axis=0, keepdims=True).astype(jnp.int32)

    spans = (FIELDS - 2) // 3
    reach_table = jnp.concatenate(
        [
            jnp.concatenate([table(item * spans + j) for j in range(spans)], axis=1)
            for item in range(3)
        ],
        axis=0,
    )
    by_reach = lax.dot_general(
        reach_table, one_hot(reach, spans * LANES), NN, preferred_element_type=jnp.float32
    )
    basin, kind, lag = [picked(by_reach[j * owners : (j + 1) * owners], dest) for j in range(3)]
    tree_table = jnp.concatenate([table(3 * spans), table(3 * spans + 1)], axis=0)

    def parent_of(owner, local):
        by_basin = lax.dot_general(
            tree_table, one_hot(local, LANES), NN, preferred_element_type=jnp.float32
        )
        return picked(by_basin[:owners], owner) - 1, picked(by_basin[owners:], owner)

    parent_owner, parent_local = parent_of(dest, basin)
    second_owner, second_local = parent_of(parent_owner, parent_local)

    def row_of(owner, local):
        mine = jnp.logical_and(owner >= 0, (owner & (CORES - 1)) == core)
        return jnp.where(mine, (owner // CORES) * basin_rows + local, -1)

    placements = jnp.concatenate(
        [
            one_hot(row_of(owner, local), outlets)
            for owner, local in (
                (dest, basin),
                (parent_owner, parent_local),
                (second_owner, second_local),
            )
        ],
        axis=0,
    )

    runoff = runoff_ref[...]
    by_kind = jnp.concatenate(
        [
            runoff * (kind == early + k).astype(jnp.float32).astype(jnp.bfloat16)
            for k in range(late)
        ],
        axis=0,
    )
    both = lax.dot_general(late_response_ref[...], by_kind, NN, preferred_element_type=jnp.float32)
    routed = both[:hours] + both[hours:]
    for k in range(early):
        routed = jnp.where(kind == k, responses_ref[k], routed)
    step = 64
    while step:
        routed = jnp.where((lag & step) != 0, later_rows(routed, step), routed)
        step //= 2
    flows = lax.dot_general(
        jnp.concatenate([placements, placements], axis=1),
        jnp.concatenate(split(routed), axis=1),
        NT,
        preferred_element_type=jnp.float32,
    )
    flow = later_lanes(flows[2 * outlets :], LINK)
    flow = later_lanes(flows[outlets : 2 * outlets] + flow, LINK)
    flow = flows[:outlets] + flow
    level = jnp.log(jnp.maximum(flow, CODE_FLOOR)) * CODE_SCALE + (CODE_ZERO + CODE_TOP + 0.5)
    level = jnp.clip(level, 0.0, 2.0 * CODE_TOP).astype(jnp.int32) - CODE_TOP
    flow_ref[...] = level.astype(jnp.int16)


def finish_kernel(parts_ref, section_ref):
    level = parts_ref[...].astype(jnp.int32)
    flow = jnp.exp((level.astype(jnp.float32) - CODE_ZERO) * (1.0 / CODE_SCALE))
    flow = jnp.sum(jnp.where(level == -CODE_TOP, 0.0, flow), axis=0)
    section_ref[...] = jnp.log(1.0 + flow)


def per_device(
    rain,
    soil,
    tile_area,
    tile_dest,
    tile_reach,
    reach_basin,
    reach_kind,
    reach_lag,
    irf,
    outlet_level,
    outlet_parent,
):
    owners = lax.axis_size("tile")
    tile_rows, hours = rain.shape
    basin_rows = outlet_parent.shape[0]
    kinds = irf.shape[0]
    params = pltpu.CompilerParams(vmem_limit_bytes=VMEM_BYTES)
    held = pl.BlockSpec(memory_space=pltpu.HBM)
    whole = pl.BlockSpec(memory_space=pltpu.VMEM)

    def in_hbm(values, shape):
        return pltpu.with_memory_space_constraint(values.reshape(shape), pltpu.HBM)

    def loaded(arguments):
        shapes = [pltpu.VMEM(values.shape, values.dtype) for values in arguments]
        return shapes + [pltpu.SemaphoreType.DMA((len(arguments),))]

    swap = [(i, i ^ 1) for i in range(owners)]
    other_rain = lax.ppermute(rain, "tile", swap)

    numbers = [
        in_hbm(values, (1, -1))
        for values in (
            reach_basin, reach_kind, reach_lag, outlet_parent, soil, tile_area, tile_dest, tile_reach,
        )
    ]
    meta, side = pl.pallas_call(
        lambda *refs: pack_kernel(*refs, basin_rows=basin_rows),
        out_shape=(
            jax.ShapeDtypeStruct((owners * FIELDS, LANES), jnp.bfloat16),
            jax.ShapeDtypeStruct((4 * tile_rows // LANES, LANES), jnp.float32),
        ),
        in_specs=[held] * len(numbers),
        scratch_shapes=loaded(numbers),
        compiler_params=params,
        cost_estimate=SMALL,
        name="pack",
    )(*numbers)
    meta = lax.all_to_all(
        meta.reshape(owners, FIELDS, LANES), "tile", split_axis=0, concat_axis=0, tiled=True
    ).reshape(-1, LANES)
    other_side = lax.ppermute(side, "tile", swap)

    early = kinds // 2
    chip_tiles = CORES * tile_rows
    runoff, ids, responses, late_response = pl.pallas_call(
        prepare_kernel,
        out_shape=(
            jax.ShapeDtypeStruct((hours, chip_tiles), jnp.bfloat16),
            jax.ShapeDtypeStruct((8, chip_tiles), jnp.int32),
            jax.ShapeDtypeStruct((early, hours, chip_tiles), jnp.float32),
            jax.ShapeDtypeStruct((2 * hours, (kinds - early) * hours), jnp.bfloat16),
        ),
        in_specs=[held, held, whole, whole, whole],
        scratch_shapes=loaded((rain, irf)),
        compiler_params=params,
        cost_estimate=SMALL,
        name="prepare",
    )(in_hbm(rain, rain.shape), in_hbm(irf, irf.shape), other_rain, side, other_side)

    flow = pl.pallas_call(
        lambda *refs: route_kernel(*refs, basin_rows=basin_rows),
        out_shape=jax.ShapeDtypeStruct((owners // CORES * basin_rows, hours), jnp.int16),
        scratch_shapes=[pltpu.VMEM(meta.shape, jnp.float32)],
        compiler_params=params,
        name="route",
    )(meta, runoff, ids, responses, late_response)

    parts = lax.all_to_all(
        flow.reshape(owners // CORES, basin_rows, hours),
        "tile",
        split_axis=0,
        concat_axis=0,
        axis_index_groups=[list(range(core, owners, CORES)) for core in range(CORES)],
        tiled=True,
    )
    return pl.pallas_call(
        finish_kernel,
        out_shape=jax.ShapeDtypeStruct((basin_rows, hours), jnp.float32),
        compiler_params=params,
        name="finish",
    )(parts)


def solution(mesh):
    rows = P(("ens", "tile"))
    table = P(("ens", "tile"), None)
    in_specs = (table, rows, rows, table, rows, rows, rows, rows, P(), rows, rows)
    return jax.shard_map(
        per_device, mesh=mesh, in_specs=in_specs, out_specs=table, check_vma=False
    )
```

```python
import math

import jax
import jax.numpy as jnp
from jax import lax
from jax.experimental import pallas as pl
from jax.experimental.pallas import tpu as pltpu
from jax.sharding import PartitionSpec as P

LINK = 6
LANES = 128
CORES = 2
FIELDS = 8
SIDE_ROWS = 16
VMEM_BYTES = 40 * 1024 * 1024
CODE_TOP = 32767
CODE_OCTAVES = 44
CODE_LOWEST = -26
CODE_SCALE = 2 * CODE_TOP / (CODE_OCTAVES * math.log(2.0))
CODE_FLOOR = 2.0 ** (2 * CODE_LOWEST)
CODE_ZERO = -CODE_TOP + 1 - CODE_LOWEST * math.log(2.0) * CODE_SCALE

SMALL = pl.CostEstimate(flops=1, bytes_accessed=1, transcendentals=0)
NT = (((1,), (1,)), ((), ()))
NN = (((1,), (0,)), ((), ()))


def iota(shape, axis):
    return lax.broadcasted_iota(jnp.int32, shape, axis)


def split(values):
    high = values.astype(jnp.bfloat16)
    return high, (values - high.astype(jnp.float32)).astype(jnp.bfloat16)


def one_hot(row, count):
    return (iota((count, row.shape[1]), 0) == row).astype(jnp.float32).astype(jnp.bfloat16)


def later_rows(values, hours):
    rows = values.shape[0]
    if hours % 8 == 0:
        padding = jnp.zeros((hours, values.shape[1]), values.dtype)
        return jnp.concatenate([padding, values[: rows - hours]], axis=0)
    return jnp.where(iota(values.shape, 0) < hours, 0.0, pltpu.roll(values, hours, 0))


def later_lanes(values, hours):
    return jnp.where(iota(values.shape, 1) < hours, 0.0, pltpu.roll(values, hours, 1))


def load(sources, targets, arrived):
    copies = [
        pltpu.make_async_copy(source, target, arrived.at[j])
        for j, (source, target) in enumerate(zip(sources, targets))
    ]
    for copy in copies:
        copy.start()
    for copy in copies:
        copy.wait()


def lane_rows(values):
    return [values[:, first : first + LANES] for first in range(0, values.shape[1], LANES)]


def parts_of(values):
    high = values.astype(jnp.bfloat16).astype(jnp.float32)
    middle = (values - high).astype(jnp.bfloat16).astype(jnp.float32)
    return [high, middle, values - high - middle]


def pack_kernel(*refs, basin_rows):
    sources, (meta_ref, block_ref, *scratch, arrived) = refs[:9], refs[9:]
    hours = block_ref.shape[1]
    tile_rows = block_ref.shape[0] - SIDE_ROWS
    load(sources, (*scratch, block_ref.at[pl.ds(0, tile_rows)]), arrived)
    basin, kind, lag, parent, soil, area, dest, reach = [ref[...] for ref in scratch]
    shift = basin_rows.bit_length() - 1
    empty = jnp.zeros((1, LANES - basin_rows), jnp.int32)
    rows = lane_rows(basin) + lane_rows(kind) + lane_rows(lag)
    rows.append(jnp.concatenate([lax.shift_right_arithmetic(parent, shift) + 1, empty], axis=1))
    rows.append(jnp.concatenate([parent & (basin_rows - 1), empty], axis=1))
    numbers = jnp.concatenate(rows, axis=0).astype(jnp.float32)
    meta_ref[...] = jnp.concatenate([numbers] * (meta_ref.shape[0] // FIELDS), axis=0).astype(jnp.bfloat16)
    sides = parts_of(soil) + parts_of(area) + [dest.astype(jnp.float32), reach.astype(jnp.float32)]
    sides = jnp.concatenate(sides + [jnp.zeros((SIDE_ROWS - len(sides), tile_rows), jnp.float32)], axis=0)
    block_ref[tile_rows:] = sides.astype(jnp.bfloat16)


def response_matrix(reversed_taps):
    hours = reversed_taps.shape[1]
    causal = iota((hours, hours), 1) <= iota((hours, hours), 0)
    row = jnp.broadcast_to(reversed_taps, (hours, hours))
    matrix = jnp.where(causal, pltpu.roll(row, 0, 1, stride=1, stride_axis=0), 0.0)
    return jnp.concatenate(split(matrix), axis=0)


def prepare_kernel(irf_hbm, own_ref, other_ref, runoff_ref, ids_ref, taps_ref, responses_ref, irf_ref, arrived):
    copy = pltpu.make_async_copy(irf_hbm, irf_ref, arrived.at[0])
    copy.start()
    hours = own_ref.shape[1]
    tile_rows = own_ref.shape[0] - SIDE_ROWS
    kinds, taps = irf_ref.shape
    sides = jnp.concatenate([own_ref[tile_rows:], other_ref[tile_rows:]], axis=1).astype(jnp.float32)
    rainfall = jnp.concatenate(
        [ref[:tile_rows].astype(jnp.float32).T for ref in (own_ref, other_ref)], axis=1
    )
    storage = sides[0:1] + sides[1:2] + sides[2:3]
    area = sides[3:4] + sides[4:5] + sides[5:6]
    excess = jnp.maximum(rainfall - 0.2 * storage, 0.0)
    runoff = (area * excess * excess / (rainfall + 0.8 * storage)).astype(jnp.bfloat16)
    runoff_ref[...] = runoff
    ids_ref[...] = sides[:8].astype(jnp.int32)
    backward = (
        iota((taps, hours), 1) == lax.rem(hours - iota((taps, hours), 0), hours)
    ).astype(jnp.float32)
    copy.wait()
    reversed_taps = lax.dot_general(
        irf_ref[...], backward, NN, precision=lax.Precision.HIGHEST, preferred_element_type=jnp.float32
    )
    taps_ref[...] = reversed_taps
    for kind in range(responses_ref.shape[0]):
        both = lax.dot_general(
            response_matrix(reversed_taps[kind : kind + 1]), runoff, NN, preferred_element_type=jnp.float32
        )
        responses_ref[kind] = both[:hours] + both[hours:]


def route_kernel(meta_ref, runoff_ref, ids_ref, taps_ref, responses_ref, flow_ref, stack_ref, *, basin_rows):
    early, hours, tiles = responses_ref.shape
    kinds = taps_ref.shape[0]
    outlets = flow_ref.shape[0]
    owners = meta_ref.shape[0] // FIELDS
    core = lax.rem(lax.axis_index("tile"), CORES)
    dest = ids_ref[6:7]
    reach = ids_ref[7:8]

    stack_ref[...] = meta_ref[...].astype(jnp.float32)

    def table(field):
        return stack_ref[pl.ds(field, owners, stride=FIELDS), :].astype(jnp.bfloat16)

    def picked(values, owner):
        chosen = iota((owners, tiles), 0) == owner
        return jnp.sum(jnp.where(chosen, values, 0.0), axis=0, keepdims=True).astype(jnp.int32)

    spans = (FIELDS - 2) // 3
    reach_table = jnp.concatenate(
        [
            jnp.concatenate([table(item * spans + j) for j in range(spans)], axis=1)
            for item in range(3)
        ],
        axis=0,
    )
    by_reach = lax.dot_general(
        reach_table, one_hot(reach, spans * LANES), NN, preferred_element_type=jnp.float32
    )
    basin, kind, lag = [picked(by_reach[j * owners : (j + 1) * owners], dest) for j in range(3)]
    tree_table = jnp.concatenate([table(3 * spans), table(3 * spans + 1)], axis=0)

    def parent_of(owner, local):
        by_basin = lax.dot_general(
            tree_table, one_hot(local, LANES), NN, preferred_element_type=jnp.float32
        )
        return picked(by_basin[:owners], owner) - 1, picked(by_basin[owners:], owner)

    parent_owner, parent_local = parent_of(dest, basin)
    second_owner, second_local = parent_of(parent_owner, parent_local)

    def row_of(owner, local):
        mine = jnp.logical_and(owner >= 0, (owner & (CORES - 1)) == core)
        return jnp.where(mine, (owner // CORES) * basin_rows + local, -1)

    placements = jnp.concatenate(
        [
            one_hot(row_of(owner, local), outlets)
            for owner, local in (
                (dest, basin),
                (parent_owner, parent_local),
                (second_owner, second_local),
            )
        ],
        axis=0,
    )

    runoff = runoff_ref[...]
    by_kind = jnp.concatenate(
        [
            runoff * (kind == k).astype(jnp.float32).astype(jnp.bfloat16)
            for k in range(early, kinds)
        ],
        axis=0,
    )
    matrices = jnp.concatenate(
        [response_matrix(taps_ref[k : k + 1]) for k in range(early, kinds)], axis=1
    )
    both = lax.dot_general(matrices, by_kind, NN, preferred_element_type=jnp.float32)
    routed = both[:hours] + both[hours:]
    for k in range(early):
        routed = jnp.where(kind == k, responses_ref[k], routed)
    step = 64
    while step:
        routed = jnp.where((lag & step) != 0, later_rows(routed, step), routed)
        step //= 2
    flows = lax.dot_general(
        jnp.concatenate([placements, placements], axis=1),
        jnp.concatenate(split(routed), axis=1),
        NT,
        preferred_element_type=jnp.float32,
    )
    flow = later_lanes(flows[2 * outlets :], LINK)
    flow = later_lanes(flows[outlets : 2 * outlets] + flow, LINK)
    flow = flows[:outlets] + flow
    level = jnp.log(jnp.maximum(flow, CODE_FLOOR)) * CODE_SCALE + (CODE_ZERO + CODE_TOP + 0.5)
    level = jnp.clip(level, 0.0, 2.0 * CODE_TOP).astype(jnp.int32) - CODE_TOP
    flow_ref[...] = level.astype(jnp.int16)


def finish_kernel(parts_ref, section_ref):
    level = parts_ref[...].astype(jnp.int32)
    flow = jnp.exp((level.astype(jnp.float32) - CODE_ZERO) * (1.0 / CODE_SCALE))
    flow = jnp.sum(jnp.where(level == -CODE_TOP, 0.0, flow), axis=0)
    section_ref[...] = jnp.log(1.0 + flow)


def per_device(
    rain,
    soil,
    tile_area,
    tile_dest,
    tile_reach,
    reach_basin,
    reach_kind,
    reach_lag,
    irf,
    outlet_level,
    outlet_parent,
):
    owners = lax.axis_size("tile")
    tile_rows, hours = rain.shape
    basin_rows = outlet_parent.shape[0]
    kinds = irf.shape[0]
    params = pltpu.CompilerParams(vmem_limit_bytes=VMEM_BYTES)
    held = pl.BlockSpec(memory_space=pltpu.HBM)
    whole = pl.BlockSpec(memory_space=pltpu.VMEM)
    block = (tile_rows + SIDE_ROWS, hours)

    def in_hbm(values, shape):
        return pltpu.with_memory_space_constraint(values.reshape(shape), pltpu.HBM)

    numbers = [
        in_hbm(values, (1, -1))
        for values in (
            reach_basin, reach_kind, reach_lag, outlet_parent, soil, tile_area, tile_dest, tile_reach,
        )
    ]
    meta, own = pl.pallas_call(
        lambda *refs: pack_kernel(*refs, basin_rows=basin_rows),
        out_shape=(
            jax.ShapeDtypeStruct((owners * FIELDS, LANES), jnp.bfloat16),
            jax.ShapeDtypeStruct(block, jnp.bfloat16),
        ),
        in_specs=[held] * (len(numbers) + 1),
        scratch_shapes=[pltpu.VMEM(values.shape, values.dtype) for values in numbers]
        + [pltpu.SemaphoreType.DMA((len(numbers) + 1,))],
        compiler_params=params,
        cost_estimate=SMALL,
        name="pack",
    )(*numbers, in_hbm(rain, rain.shape))
    other = lax.ppermute(own, "tile", [(i, i ^ 1) for i in range(owners)])
    meta = lax.all_to_all(
        meta.reshape(owners, FIELDS, LANES), "tile", split_axis=0, concat_axis=0, tiled=True
    ).reshape(-1, LANES)

    chip_tiles = CORES * tile_rows
    early = kinds * 3 // 4
    runoff, ids, taps, responses = pl.pallas_call(
        prepare_kernel,
        out_shape=(
            jax.ShapeDtypeStruct((hours, chip_tiles), jnp.bfloat16),
            jax.ShapeDtypeStruct((8, chip_tiles), jnp.int32),
            jax.ShapeDtypeStruct((kinds, hours), jnp.float32),
            jax.ShapeDtypeStruct((early, hours, chip_tiles), jnp.float32),
        ),
        in_specs=[held, whole, whole],
        scratch_shapes=[pltpu.VMEM(irf.shape, irf.dtype), pltpu.SemaphoreType.DMA((1,))],
        compiler_params=params,
        cost_estimate=SMALL,
        name="prepare",
    )(in_hbm(irf, irf.shape), own, other)

    flow = pl.pallas_call(
        lambda *refs: route_kernel(*refs, basin_rows=basin_rows),
        out_shape=jax.ShapeDtypeStruct((owners // CORES * basin_rows, hours), jnp.int16),
        scratch_shapes=[pltpu.VMEM(meta.shape, jnp.float32)],
        compiler_params=params,
        name="route",
    )(meta, runoff, ids, taps, responses)

    parts = lax.all_to_all(
        flow.reshape(owners // CORES, basin_rows, hours),
        "tile",
        split_axis=0,
        concat_axis=0,
        axis_index_groups=[list(range(core, owners, CORES)) for core in range(CORES)],
        tiled=True,
    )
    return pl.pallas_call(
        finish_kernel,
        out_shape=jax.ShapeDtypeStruct((basin_rows, hours), jnp.float32),
        compiler_params=params,
        name="finish",
    )(parts)


def solution(mesh):
    rows = P(("ens", "tile"))
    table = P(("ens", "tile"), None)
    in_specs = (table, rows, rows, table, rows, rows, rows, rows, P(), rows, rows)
    return jax.shard_map(
        per_device, mesh=mesh, in_specs=in_specs, out_specs=table, check_vma=False
    )
```

```python
import math

import jax
import jax.numpy as jnp
from jax import lax
from jax.experimental import pallas as pl
from jax.experimental.pallas import tpu as pltpu
from jax.sharding import PartitionSpec as P

LINK = 6
LANES = 128
CORES = 2
FIELDS = 8
SIDE_ROWS = 16
VMEM_BYTES = 40 * 1024 * 1024
CODE_TOP = 32767
CODE_OCTAVES = 44
CODE_LOWEST = -26
CODE_SCALE = 2 * CODE_TOP / (CODE_OCTAVES * math.log(2.0))
CODE_FLOOR = 2.0 ** (2 * CODE_LOWEST)
CODE_ZERO = -CODE_TOP + 1 - CODE_LOWEST * math.log(2.0) * CODE_SCALE

SMALL = pl.CostEstimate(flops=1, bytes_accessed=1, transcendentals=0)
NT = (((1,), (1,)), ((), ()))
NN = (((1,), (0,)), ((), ()))


def iota(shape, axis):
    return lax.broadcasted_iota(jnp.int32, shape, axis)


def split(values):
    high = values.astype(jnp.bfloat16)
    return high, (values - high.astype(jnp.float32)).astype(jnp.bfloat16)


def one_hot(row, count):
    return (iota((count, row.shape[1]), 0) == row).astype(jnp.float32).astype(jnp.bfloat16)


def later_rows(values, hours):
    rows = values.shape[0]
    if hours % 8 == 0:
        padding = jnp.zeros((hours, values.shape[1]), values.dtype)
        return jnp.concatenate([padding, values[: rows - hours]], axis=0)
    return jnp.where(iota(values.shape, 0) < hours, 0.0, pltpu.roll(values, hours, 0))


def later_lanes(values, hours):
    return jnp.where(iota(values.shape, 1) < hours, 0.0, pltpu.roll(values, hours, 1))


def lane_rows(values):
    return [values[:, first : first + LANES] for first in range(0, values.shape[1], LANES)]


def parts_of(values):
    high = values.astype(jnp.bfloat16).astype(jnp.float32)
    middle = (values - high).astype(jnp.bfloat16).astype(jnp.float32)
    return [high, middle, values - high - middle]


def pack_kernel(*refs, basin_rows):
    sources, (meta_hbm, block_ref, *scratch, meta_ref, arrived) = refs[:9], refs[9:]
    tile_rows = block_ref.shape[0] - SIDE_ROWS
    targets = (*scratch, block_ref.at[pl.ds(0, tile_rows)])
    copies = [
        pltpu.make_async_copy(source, target, arrived.at[j])
        for j, (source, target) in enumerate(zip(sources, targets))
    ]
    for copy in copies:
        copy.start()
    for copy in copies[:4]:
        copy.wait()
    basin, kind, lag, parent = [ref[...] for ref in scratch[:4]]
    shift = basin_rows.bit_length() - 1
    empty = jnp.zeros((1, LANES - basin_rows), jnp.int32)
    rows = lane_rows(basin) + lane_rows(kind) + lane_rows(lag)
    rows.append(jnp.concatenate([lax.shift_right_arithmetic(parent, shift) + 1, empty], axis=1))
    rows.append(jnp.concatenate([parent & (basin_rows - 1), empty], axis=1))
    numbers = jnp.concatenate(rows, axis=0).astype(jnp.float32)
    meta_ref[...] = jnp.concatenate([numbers] * (meta_ref.shape[0] // FIELDS), axis=0).astype(jnp.bfloat16)
    leaving = pltpu.make_async_copy(meta_ref, meta_hbm, arrived.at[len(copies)])
    leaving.start()
    for copy in copies[4:8]:
        copy.wait()
    soil, area, dest, reach = [ref[...] for ref in scratch[4:]]
    sides = parts_of(soil) + parts_of(area) + [dest.astype(jnp.float32), reach.astype(jnp.float32)]
    sides = jnp.concatenate(sides + [jnp.zeros((SIDE_ROWS - len(sides), tile_rows), jnp.float32)], axis=0)
    block_ref[tile_rows:] = sides.astype(jnp.bfloat16)
    copies[8].wait()
    leaving.wait()


def prepare_kernel(
    irf_hbm, own_ref, other_ref, runoff_ref, dest_ref, reach_marks_ref, late_ref, responses_ref, irf_ref, arrived
):
    copy = pltpu.make_async_copy(irf_hbm, irf_ref, arrived.at[0])
    copy.start()
    hours = own_ref.shape[1]
    half = hours // 2
    tile_rows = own_ref.shape[0] - SIDE_ROWS
    kinds, taps = irf_ref.shape
    early = responses_ref.shape[0]
    sides = jnp.concatenate([own_ref[tile_rows:], other_ref[tile_rows:]], axis=1).astype(jnp.float32)
    rainfall = jnp.concatenate(
        [ref[:tile_rows].astype(jnp.float32).T for ref in (own_ref, other_ref)], axis=1
    )
    storage = sides[0:1] + sides[1:2] + sides[2:3]
    area = sides[3:4] + sides[4:5] + sides[5:6]
    excess = jnp.maximum(rainfall - 0.2 * storage, 0.0)
    runoff = (area * excess * excess / (rainfall + 0.8 * storage)).astype(jnp.bfloat16)
    runoff_ref[...] = runoff
    dest_ref[...] = jnp.broadcast_to(sides[6:7], dest_ref.shape).astype(jnp.int32)
    reach_marks_ref[...] = one_hot(sides[7:8].astype(jnp.int32), reach_marks_ref.shape[0])
    backward = (
        iota((taps, hours), 1) == lax.rem(hours - iota((taps, hours), 0), hours)
    ).astype(jnp.float32)
    copy.wait()
    reversed_taps = lax.dot_general(
        irf_ref[...], backward, NN, precision=lax.Precision.HIGHEST, preferred_element_type=jnp.float32
    )
    causal = iota((half, hours), 1) <= iota((half, hours), 0) + half
    for kind in range(kinds):
        row = jnp.broadcast_to(reversed_taps[kind : kind + 1], (half, hours))
        matrix = jnp.where(causal, pltpu.roll(row, half, 1, stride=1, stride_axis=0), 0.0)
        matrix = jnp.concatenate(split(matrix), axis=0)
        if kind < early:
            responses_ref[kind] = respond(matrix, runoff)
        else:
            late_ref[:, (kind - early) * hours : (kind - early + 1) * hours] = matrix


def respond(matrices, runoffs):
    hours = matrices.shape[0]
    half = hours // 2
    count = matrices.shape[1] // hours

    def halves(values, axis, first):
        pieces = [
            lax.slice_in_dim(values, j * hours + first, j * hours + first + half, axis=axis)
            for j in range(count)
        ]
        return jnp.concatenate(pieces, axis=axis)

    earlier = lax.dot_general(
        halves(matrices, 1, half), halves(runoffs, 0, 0), NN, preferred_element_type=jnp.float32
    )
    later = lax.dot_general(matrices, runoffs, NN, preferred_element_type=jnp.float32)
    return jnp.concatenate([earlier[:half] + earlier[half:], later[:half] + later[half:]], axis=0)


def route_kernel(
    meta_ref, runoff_ref, dest_ref, reach_marks_ref, late_ref, responses_ref, flow_ref, stack_ref, *, basin_rows
):
    early, hours, tiles = responses_ref.shape
    late = late_ref.shape[1] // hours
    outlets = flow_ref.shape[0]
    owners = meta_ref.shape[0] // FIELDS
    core = lax.rem(lax.axis_index("tile"), CORES)
    dest = dest_ref[0:1]

    stack_ref[...] = meta_ref[...].astype(jnp.float32)

    def table(field):
        return stack_ref[pl.ds(field, owners, stride=FIELDS), :].astype(jnp.bfloat16)

    def picked(values, owner):
        chosen = iota((owners, tiles), 0) == owner
        return jnp.sum(jnp.where(chosen, values, 0.0), axis=0, keepdims=True).astype(jnp.int32)

    spans = (FIELDS - 2) // 3
    reach_table = jnp.concatenate(
        [
            jnp.concatenate([table(item * spans + j) for j in range(spans)], axis=1)
            for item in range(3)
        ],
        axis=0,
    )
    by_reach = lax.dot_general(
        reach_table, reach_marks_ref[...], NN, preferred_element_type=jnp.float32
    )
    basin, kind, lag = [picked(by_reach[j * owners : (j + 1) * owners], dest) for j in range(3)]
    tree_table = jnp.concatenate([table(3 * spans), table(3 * spans + 1)], axis=0)

    def parent_of(owner, local):
        by_basin = lax.dot_general(
            tree_table, one_hot(local, LANES), NN, preferred_element_type=jnp.float32
        )
        return picked(by_basin[:owners], owner) - 1, picked(by_basin[owners:], owner)

    parent_owner, parent_local = parent_of(dest, basin)
    second_owner, second_local = parent_of(parent_owner, parent_local)

    def row_of(owner, local):
        mine = jnp.logical_and(owner >= 0, (owner & (CORES - 1)) == core)
        return jnp.where(mine, (owner // CORES) * basin_rows + local, -1)

    placements = jnp.concatenate(
        [
            one_hot(row_of(owner, local), outlets)
            for owner, local in (
                (dest, basin),
                (parent_owner, parent_local),
                (second_owner, second_local),
            )
        ],
        axis=0,
    )

    runoff = runoff_ref[...]
    by_kind = jnp.concatenate(
        [
            runoff * (kind == early + k).astype(jnp.float32).astype(jnp.bfloat16)
            for k in range(late)
        ],
        axis=0,
    )
    routed = respond(late_ref[...], by_kind)
    for k in range(early):
        routed = jnp.where(kind == k, responses_ref[k], routed)
    step = 64
    while step:
        routed = jnp.where((lag & step) != 0, later_rows(routed, step), routed)
        step //= 2
    flows = lax.dot_general(
        jnp.concatenate([placements, placements], axis=1),
        jnp.concatenate(split(routed), axis=1),
        NT,
        preferred_element_type=jnp.float32,
    )
    flow = later_lanes(flows[2 * outlets :], LINK)
    flow = later_lanes(flows[outlets : 2 * outlets] + flow, LINK)
    flow = flows[:outlets] + flow
    level = jnp.log(jnp.maximum(flow, CODE_FLOOR)) * CODE_SCALE + (CODE_ZERO + CODE_TOP + 0.5)
    level = jnp.clip(level, 0.0, 2.0 * CODE_TOP).astype(jnp.int32) - CODE_TOP
    flow_ref[...] = level.astype(jnp.int16)


def finish_kernel(parts_ref, section_ref):
    level = parts_ref[...].astype(jnp.int32)
    flow = jnp.exp((level.astype(jnp.float32) - CODE_ZERO) * (1.0 / CODE_SCALE))
    flow = jnp.sum(jnp.where(level == -CODE_TOP, 0.0, flow), axis=0)
    section_ref[...] = jnp.log(1.0 + flow)


def per_device(
    rain,
    soil,
    tile_area,
    tile_dest,
    tile_reach,
    reach_basin,
    reach_kind,
    reach_lag,
    irf,
    outlet_level,
    outlet_parent,
):
    owners = lax.axis_size("tile")
    tile_rows, hours = rain.shape
    basin_rows = outlet_parent.shape[0]
    kinds = irf.shape[0]
    params = pltpu.CompilerParams(vmem_limit_bytes=VMEM_BYTES)
    held = pl.BlockSpec(memory_space=pltpu.HBM)
    whole = pl.BlockSpec(memory_space=pltpu.VMEM)
    block = (tile_rows + SIDE_ROWS, hours)

    def in_hbm(values, shape):
        return pltpu.with_memory_space_constraint(values.reshape(shape), pltpu.HBM)

    numbers = [
        in_hbm(values, (1, -1))
        for values in (
            reach_basin, reach_kind, reach_lag, outlet_parent, soil, tile_area, tile_dest, tile_reach,
        )
    ]
    meta, own = pl.pallas_call(
        lambda *refs: pack_kernel(*refs, basin_rows=basin_rows),
        out_shape=(
            jax.ShapeDtypeStruct((owners * FIELDS, LANES), jnp.bfloat16),
            jax.ShapeDtypeStruct(block, jnp.bfloat16),
        ),
        in_specs=[held] * (len(numbers) + 1),
        out_specs=(held, whole),
        scratch_shapes=[pltpu.VMEM(values.shape, values.dtype) for values in numbers]
        + [
            pltpu.VMEM((owners * FIELDS, LANES), jnp.bfloat16),
            pltpu.SemaphoreType.DMA((len(numbers) + 2,)),
        ],
        compiler_params=params,
        cost_estimate=SMALL,
        name="pack",
    )(*numbers, in_hbm(rain, rain.shape))
    other = lax.ppermute(own, "tile", [(i, i ^ 1) for i in range(owners)])
    meta = lax.all_to_all(
        meta.reshape(owners, FIELDS, LANES), "tile", split_axis=0, concat_axis=0, tiled=True
    ).reshape(-1, LANES)

    chip_tiles = CORES * tile_rows
    early = kinds // 2
    prepared = pl.pallas_call(
        prepare_kernel,
        out_shape=(
            jax.ShapeDtypeStruct((hours, chip_tiles), jnp.bfloat16),
            jax.ShapeDtypeStruct((8, chip_tiles), jnp.int32),
            jax.ShapeDtypeStruct((reach_basin.size, chip_tiles), jnp.bfloat16),
            jax.ShapeDtypeStruct((hours, (kinds - early) * hours), jnp.bfloat16),
            jax.ShapeDtypeStruct((early, hours, chip_tiles), jnp.float32),
        ),
        in_specs=[held, whole, whole],
        scratch_shapes=[pltpu.VMEM(irf.shape, irf.dtype), pltpu.SemaphoreType.DMA((1,))],
        compiler_params=params,
        cost_estimate=SMALL,
        name="prepare",
    )(in_hbm(irf, irf.shape), own, other)

    flow = pl.pallas_call(
        lambda *refs: route_kernel(*refs, basin_rows=basin_rows),
        out_shape=jax.ShapeDtypeStruct((owners // CORES * basin_rows, hours), jnp.int16),
        scratch_shapes=[pltpu.VMEM(meta.shape, jnp.float32)],
        compiler_params=params,
        name="route",
    )(meta, *prepared)

    parts = lax.all_to_all(
        flow.reshape(owners // CORES, basin_rows, hours),
        "tile",
        split_axis=0,
        concat_axis=0,
        axis_index_groups=[list(range(core, owners, CORES)) for core in range(CORES)],
        tiled=True,
    )
    return pl.pallas_call(
        finish_kernel,
        out_shape=jax.ShapeDtypeStruct((basin_rows, hours), jnp.float32),
        compiler_params=params,
        name="finish",
    )(parts)


def solution(mesh):
    rows = P(("ens", "tile"))
    table = P(("ens", "tile"), None)
    in_specs = (table, rows, rows, table, rows, rows, rows, rows, P(), rows, rows)
    return jax.shard_map(
        per_device, mesh=mesh, in_specs=in_specs, out_specs=table, check_vma=False
    )
```

```python
import math

import jax
import jax.numpy as jnp
from jax import lax
from jax.experimental import pallas as pl
from jax.experimental.pallas import tpu as pltpu
from jax.sharding import PartitionSpec as P

LINK = 6
LANES = 128
CORES = 2
FIELDS = 8
SIDE_ROWS = 16
VMEM_BYTES = 40 * 1024 * 1024
CODE_TOP = 32767
CODE_OCTAVES = 44
CODE_LOWEST = -26
CODE_SCALE = 2 * CODE_TOP / (CODE_OCTAVES * math.log(2.0))
CODE_FLOOR = 2.0 ** (2 * CODE_LOWEST)
CODE_ZERO = -CODE_TOP + 1 - CODE_LOWEST * math.log(2.0) * CODE_SCALE

SMALL = pl.CostEstimate(flops=1, bytes_accessed=1, transcendentals=0)
NT = (((1,), (1,)), ((), ()))
NN = (((1,), (0,)), ((), ()))


def iota(shape, axis):
    return lax.broadcasted_iota(jnp.int32, shape, axis)


def split(values):
    high = values.astype(jnp.bfloat16)
    return high, (values - high.astype(jnp.float32)).astype(jnp.bfloat16)


def one_hot(row, count):
    return (iota((count, row.shape[1]), 0) == row).astype(jnp.float32).astype(jnp.bfloat16)


def later_rows(values, hours):
    rows = values.shape[0]
    if hours % 8 == 0:
        padding = jnp.zeros((hours, values.shape[1]), values.dtype)
        return jnp.concatenate([padding, values[: rows - hours]], axis=0)
    rolled = pltpu.roll(values, hours, 0)
    first = jnp.where(iota((8, values.shape[1]), 0) < hours, 0.0, rolled[:8])
    return jnp.concatenate([first, rolled[8:]], axis=0)


def later_lanes(values, hours):
    rolled = pltpu.roll(values, hours, 1)
    first = jnp.where(iota((values.shape[0], LANES), 1) < hours, 0.0, rolled[:, :LANES])
    return jnp.concatenate([first, rolled[:, LANES:]], axis=1)


def lane_rows(values):
    return [values[:, first : first + LANES] for first in range(0, values.shape[1], LANES)]


def parts_of(values):
    high = values.astype(jnp.bfloat16).astype(jnp.float32)
    middle = (values - high).astype(jnp.bfloat16).astype(jnp.float32)
    return [high, middle, values - high - middle]


def pack_kernel(*refs, basin_rows):
    sources, (meta_ref, block_ref, *scratch, arrived) = refs[:9], refs[9:]
    tile_rows = block_ref.shape[0] - SIDE_ROWS
    targets = (*scratch, block_ref.at[pl.ds(0, tile_rows)])
    copies = [
        pltpu.make_async_copy(source, target, arrived.at[j])
        for j, (source, target) in enumerate(zip(sources, targets))
    ]
    for copy in copies:
        copy.start()
    for copy in copies[:4]:
        copy.wait()
    basin, kind, lag, parent = [ref[...] for ref in scratch[:4]]
    shift = basin_rows.bit_length() - 1
    empty = jnp.zeros((1, LANES - basin_rows), jnp.int32)
    rows = lane_rows(basin) + lane_rows(kind) + lane_rows(lag)
    rows.append(jnp.concatenate([lax.shift_right_arithmetic(parent, shift) + 1, empty], axis=1))
    rows.append(jnp.concatenate([parent & (basin_rows - 1), empty], axis=1))
    numbers = jnp.concatenate(rows, axis=0).astype(jnp.float32)
    meta_ref[...] = jnp.concatenate([numbers] * (meta_ref.shape[0] // FIELDS), axis=0).astype(jnp.bfloat16)
    for copy in copies[4:8]:
        copy.wait()
    soil, area, dest, reach = [ref[...] for ref in scratch[4:]]
    sides = parts_of(soil) + parts_of(area) + [dest.astype(jnp.float32), reach.astype(jnp.float32)]
    sides = jnp.concatenate(sides + [jnp.zeros((SIDE_ROWS - len(sides), tile_rows), jnp.float32)], axis=0)
    block_ref[tile_rows:] = sides.astype(jnp.bfloat16)
    copies[8].wait()


def prepare_kernel(
    irf_hbm, own_ref, other_ref, runoff_ref, dest_ref, reach_marks_ref, late_ref, responses_ref, irf_ref, arrived
):
    copy = pltpu.make_async_copy(irf_hbm, irf_ref, arrived.at[0])
    copy.start()
    hours = own_ref.shape[1]
    half = hours // 2
    tile_rows = own_ref.shape[0] - SIDE_ROWS
    kinds, taps = irf_ref.shape
    early = responses_ref.shape[0]
    sides = jnp.concatenate([own_ref[tile_rows:], other_ref[tile_rows:]], axis=1).astype(jnp.float32)
    rainfall = jnp.concatenate(
        [ref[:tile_rows].astype(jnp.float32).T for ref in (own_ref, other_ref)], axis=1
    )
    storage = sides[0:1] + sides[1:2] + sides[2:3]
    area = sides[3:4] + sides[4:5] + sides[5:6]
    excess = jnp.maximum(rainfall - 0.2 * storage, 0.0)
    runoff = (area * excess * excess / (rainfall + 0.8 * storage)).astype(jnp.bfloat16)
    runoff_ref[...] = runoff
    dest_ref[...] = jnp.broadcast_to(sides[6:7], dest_ref.shape).astype(jnp.int32)
    reach_marks_ref[...] = one_hot(sides[7:8].astype(jnp.int32), reach_marks_ref.shape[0])
    backward = (
        iota((taps, hours), 1) == lax.rem(hours - iota((taps, hours), 0), hours)
    ).astype(jnp.float32)
    copy.wait()
    reversed_taps = lax.dot_general(
        irf_ref[...], backward, NN, precision=lax.Precision.HIGHEST, preferred_element_type=jnp.float32
    )
    causal = iota((half, hours), 1) <= iota((half, hours), 0) + half
    for kind in range(kinds):
        row = jnp.broadcast_to(reversed_taps[kind : kind + 1], (half, hours))
        matrix = jnp.where(causal, pltpu.roll(row, half, 1, stride=1, stride_axis=0), 0.0)
        matrix = jnp.concatenate(split(matrix), axis=0)
        if kind < early:
            responses_ref[kind] = respond(matrix, runoff)
        else:
            late_ref[:, (kind - early) * hours : (kind - early + 1) * hours] = matrix


def respond(matrices, runoffs):
    hours = matrices.shape[0]
    half = hours // 2
    count = matrices.shape[1] // hours

    def halves(values, axis, first):
        pieces = [
            lax.slice_in_dim(values, j * hours + first, j * hours + first + half, axis=axis)
            for j in range(count)
        ]
        return jnp.concatenate(pieces, axis=axis)

    earlier = lax.dot_general(
        halves(matrices, 1, half), halves(runoffs, 0, 0), NN, preferred_element_type=jnp.float32
    )
    later = lax.dot_general(matrices, runoffs, NN, preferred_element_type=jnp.float32)
    return jnp.concatenate([earlier[:half] + earlier[half:], later[:half] + later[half:]], axis=0)


def route_kernel(
    meta_ref, runoff_ref, dest_ref, reach_marks_ref, late_ref, responses_ref, flow_ref, stack_ref, *, basin_rows
):
    early, hours, tiles = responses_ref.shape
    late = late_ref.shape[1] // hours
    outlets = flow_ref.shape[0]
    owners = meta_ref.shape[0] // FIELDS
    core = lax.rem(lax.axis_index("tile"), CORES)
    dest = dest_ref[0:1]

    stack_ref[...] = meta_ref[...].astype(jnp.float32)

    def table(field):
        return stack_ref[pl.ds(field, owners, stride=FIELDS), :].astype(jnp.bfloat16)

    def picked(values, owner):
        chosen = iota((owners, tiles), 0) == owner
        return jnp.sum(jnp.where(chosen, values, 0.0), axis=0, keepdims=True).astype(jnp.int32)

    spans = (FIELDS - 2) // 3
    reach_table = jnp.concatenate(
        [
            jnp.concatenate([table(item * spans + j) for j in range(spans)], axis=1)
            for item in range(3)
        ],
        axis=0,
    )
    by_reach = lax.dot_general(
        reach_table, reach_marks_ref[...], NN, preferred_element_type=jnp.float32
    )
    basin, kind, lag = [picked(by_reach[j * owners : (j + 1) * owners], dest) for j in range(3)]
    tree_table = jnp.concatenate([table(3 * spans), table(3 * spans + 1)], axis=0)

    def parent_of(owner, local):
        by_basin = lax.dot_general(
            tree_table, one_hot(local, LANES), NN, preferred_element_type=jnp.float32
        )
        return picked(by_basin[:owners], owner) - 1, picked(by_basin[owners:], owner)

    parent_owner, parent_local = parent_of(dest, basin)
    second_owner, second_local = parent_of(parent_owner, parent_local)

    def row_of(owner, local):
        mine = jnp.logical_and(owner >= 0, (owner & (CORES - 1)) == core)
        return jnp.where(mine, (owner // CORES) * basin_rows + local, -1)

    placements = jnp.concatenate(
        [
            one_hot(row_of(owner, local), outlets)
            for owner, local in (
                (dest, basin),
                (parent_owner, parent_local),
                (second_owner, second_local),
            )
        ],
        axis=0,
    )

    runoff = runoff_ref[...]
    by_kind = jnp.concatenate(
        [
            runoff * (kind == early + k).astype(jnp.float32).astype(jnp.bfloat16)
            for k in range(late)
        ],
        axis=0,
    )
    routed = respond(late_ref[...], by_kind)
    for k in range(early):
        routed = jnp.where(kind == k, responses_ref[k], routed)
    step = 64
    while step:
        routed = jnp.where((lag & step) != 0, later_rows(routed, step), routed)
        step //= 2
    flows = lax.dot_general(
        jnp.concatenate([placements, placements], axis=1),
        jnp.concatenate(split(routed), axis=1),
        NT,
        preferred_element_type=jnp.float32,
    )
    flow = later_lanes(flows[2 * outlets :], LINK)
    flow = later_lanes(flows[outlets : 2 * outlets] + flow, LINK)
    flow = flows[:outlets] + flow
    level = jnp.log(jnp.maximum(flow, CODE_FLOOR)) * CODE_SCALE + (CODE_ZERO + CODE_TOP + 0.5)
    level = jnp.clip(level, 0.0, 2.0 * CODE_TOP).astype(jnp.int32) - CODE_TOP
    flow_ref[...] = level.astype(jnp.int16)


def finish_kernel(parts_ref, section_ref):
    level = parts_ref[...].astype(jnp.int32)
    flow = jnp.exp((level.astype(jnp.float32) - CODE_ZERO) * (1.0 / CODE_SCALE))
    flow = jnp.sum(jnp.where(level == -CODE_TOP, 0.0, flow), axis=0)
    section_ref[...] = jnp.log(1.0 + flow)


def per_device(
    rain,
    soil,
    tile_area,
    tile_dest,
    tile_reach,
    reach_basin,
    reach_kind,
    reach_lag,
    irf,
    outlet_level,
    outlet_parent,
):
    owners = lax.axis_size("tile")
    tile_rows, hours = rain.shape
    basin_rows = outlet_parent.shape[0]
    kinds = irf.shape[0]
    params = pltpu.CompilerParams(vmem_limit_bytes=VMEM_BYTES)
    held = pl.BlockSpec(memory_space=pltpu.HBM)
    whole = pl.BlockSpec(memory_space=pltpu.VMEM)
    block = (tile_rows + SIDE_ROWS, hours)

    def in_hbm(values, shape):
        return pltpu.with_memory_space_constraint(values.reshape(shape), pltpu.HBM)

    numbers = [
        in_hbm(values, (1, -1))
        for values in (
            reach_basin, reach_kind, reach_lag, outlet_parent, soil, tile_area, tile_dest, tile_reach,
        )
    ]
    meta, own = pl.pallas_call(
        lambda *refs: pack_kernel(*refs, basin_rows=basin_rows),
        out_shape=(
            pltpu.VMEM((owners * FIELDS, LANES), jnp.bfloat16),
            jax.ShapeDtypeStruct(block, jnp.bfloat16),
        ),
        in_specs=[held] * (len(numbers) + 1),
        out_specs=(whole, whole),
        scratch_shapes=[pltpu.VMEM(values.shape, values.dtype) for values in numbers]
        + [pltpu.SemaphoreType.DMA((len(numbers) + 1,))],
        compiler_params=params,
        cost_estimate=SMALL,
        name="pack",
    )(*numbers, in_hbm(rain, rain.shape))
    other = lax.ppermute(own, "tile", [(i, i ^ 1) for i in range(owners)])
    meta = lax.all_to_all(
        meta.reshape(owners, FIELDS, LANES), "tile", split_axis=0, concat_axis=0, tiled=True
    ).reshape(-1, LANES)

    chip_tiles = CORES * tile_rows
    early = kinds // 2
    prepared = pl.pallas_call(
        prepare_kernel,
        out_shape=(
            jax.ShapeDtypeStruct((hours, chip_tiles), jnp.bfloat16),
            jax.ShapeDtypeStruct((8, chip_tiles), jnp.int32),
            jax.ShapeDtypeStruct((reach_basin.size, chip_tiles), jnp.bfloat16),
            jax.ShapeDtypeStruct((hours, (kinds - early) * hours), jnp.bfloat16),
            jax.ShapeDtypeStruct((early, hours, chip_tiles), jnp.float32),
        ),
        in_specs=[held, whole, whole],
        scratch_shapes=[pltpu.VMEM(irf.shape, irf.dtype), pltpu.SemaphoreType.DMA((1,))],
        compiler_params=params,
        cost_estimate=SMALL,
        name="prepare",
    )(in_hbm(irf, irf.shape), own, other)

    flow = pl.pallas_call(
        lambda *refs: route_kernel(*refs, basin_rows=basin_rows),
        out_shape=jax.ShapeDtypeStruct((owners // CORES * basin_rows, hours), jnp.int16),
        scratch_shapes=[pltpu.VMEM(meta.shape, jnp.float32)],
        compiler_params=params,
        name="route",
    )(meta, *prepared)

    parts = lax.all_to_all(
        flow.reshape(owners // CORES, basin_rows, hours),
        "tile",
        split_axis=0,
        concat_axis=0,
        axis_index_groups=[list(range(core, owners, CORES)) for core in range(CORES)],
        tiled=True,
    )
    return pl.pallas_call(
        finish_kernel,
        out_shape=jax.ShapeDtypeStruct((basin_rows, hours), jnp.float32),
        compiler_params=params,
        name="finish",
    )(parts)


def solution(mesh):
    rows = P(("ens", "tile"))
    table = P(("ens", "tile"), None)
    in_specs = (table, rows, rows, table, rows, rows, rows, rows, P(), rows, rows)
    return jax.shard_map(
        per_device, mesh=mesh, in_specs=in_specs, out_specs=table, check_vma=False
    )
```

```python
import math

import jax
import jax.numpy as jnp
from jax import lax
from jax.experimental import pallas as pl
from jax.experimental.pallas import tpu as pltpu
from jax.sharding import PartitionSpec as P

LINK = 6
LANES = 128
CORES = 2
FIELDS = 8
SIDE_ROWS = 16
VMEM_BYTES = 40 * 1024 * 1024
CHUNK = 64
CODE_TOP = 32767
CODE_OCTAVES = 44
CODE_LOWEST = -26
CODE_SCALE = 2 * CODE_TOP / (CODE_OCTAVES * math.log(2.0))
CODE_FLOOR = 2.0 ** (2 * CODE_LOWEST)
CODE_ZERO = -CODE_TOP + 1 - CODE_LOWEST * math.log(2.0) * CODE_SCALE

SMALL = pl.CostEstimate(flops=1, bytes_accessed=1, transcendentals=0)
NT = (((1,), (1,)), ((), ()))
NN = (((1,), (0,)), ((), ()))


def iota(shape, axis):
    return lax.broadcasted_iota(jnp.int32, shape, axis)


def split(values):
    high = values.astype(jnp.bfloat16)
    return high, (values - high.astype(jnp.float32)).astype(jnp.bfloat16)


def one_hot(row, count):
    return (iota((count, row.shape[1]), 0) == row).astype(jnp.float32).astype(jnp.bfloat16)


def later_rows(values, hours):
    rows = values.shape[0]
    if hours % 8 == 0:
        padding = jnp.zeros((hours, values.shape[1]), values.dtype)
        return jnp.concatenate([padding, values[: rows - hours]], axis=0)
    rolled = pltpu.roll(values, hours, 0)
    first = jnp.where(iota((8, values.shape[1]), 0) < hours, 0.0, rolled[:8])
    return jnp.concatenate([first, rolled[8:]], axis=0)


def later_lanes(values, hours):
    rolled = pltpu.roll(values, hours, 1)
    first = jnp.where(iota((values.shape[0], LANES), 1) < hours, 0.0, rolled[:, :LANES])
    return jnp.concatenate([first, rolled[:, LANES:]], axis=1)


def lane_rows(values):
    return [values[:, first : first + LANES] for first in range(0, values.shape[1], LANES)]


def parts_of(values):
    high = values.astype(jnp.bfloat16).astype(jnp.float32)
    middle = (values - high).astype(jnp.bfloat16).astype(jnp.float32)
    return [high, middle, values - high - middle]


def pack_kernel(*refs, basin_rows):
    sources, (meta_hbm, block_ref, *scratch, meta_ref, arrived) = refs[:9], refs[9:]
    tile_rows = block_ref.shape[0] - SIDE_ROWS
    targets = (*scratch, block_ref.at[pl.ds(0, tile_rows)])
    copies = [
        pltpu.make_async_copy(source, target, arrived.at[j])
        for j, (source, target) in enumerate(zip(sources, targets))
    ]
    for copy in copies:
        copy.start()
    for copy in copies[:4]:
        copy.wait()
    basin, kind, lag, parent = [ref[...] for ref in scratch[:4]]
    shift = basin_rows.bit_length() - 1
    empty = jnp.zeros((1, LANES - basin_rows), jnp.int32)
    rows = lane_rows(basin) + lane_rows(kind) + lane_rows(lag)
    rows.append(jnp.concatenate([lax.shift_right_arithmetic(parent, shift) + 1, empty], axis=1))
    rows.append(jnp.concatenate([parent & (basin_rows - 1), empty], axis=1))
    numbers = jnp.concatenate(rows, axis=0).astype(jnp.float32)
    meta_ref[...] = jnp.concatenate([numbers] * (meta_ref.shape[0] // FIELDS), axis=0).astype(jnp.bfloat16)
    leaving = pltpu.make_async_copy(meta_ref, meta_hbm, arrived.at[len(copies)])
    leaving.start()
    for copy in copies[4:8]:
        copy.wait()
    soil, area, dest, reach = [ref[...] for ref in scratch[4:]]
    sides = parts_of(soil) + parts_of(area) + [dest.astype(jnp.float32), reach.astype(jnp.float32)]
    sides = jnp.concatenate(sides + [jnp.zeros((SIDE_ROWS - len(sides), tile_rows), jnp.float32)], axis=0)
    block_ref[tile_rows:] = sides.astype(jnp.bfloat16)
    copies[8].wait()
    leaving.wait()


def prepare_kernel(
    irf_hbm, own_ref, other_ref, runoff_ref, dest_ref, reach_marks_ref, late_ref, responses_ref, irf_ref, arrived
):
    copy = pltpu.make_async_copy(irf_hbm, irf_ref, arrived.at[0])
    copy.start()
    hours = own_ref.shape[1]
    half = hours // 2
    tile_rows = own_ref.shape[0] - SIDE_ROWS
    kinds, taps = irf_ref.shape
    early = responses_ref.shape[0]
    sides = jnp.concatenate([own_ref[tile_rows:], other_ref[tile_rows:]], axis=1).astype(jnp.float32)
    rainfall = jnp.concatenate(
        [ref[:tile_rows].astype(jnp.float32).T for ref in (own_ref, other_ref)], axis=1
    )
    storage = sides[0:1] + sides[1:2] + sides[2:3]
    area = sides[3:4] + sides[4:5] + sides[5:6]
    excess = jnp.maximum(rainfall - 0.2 * storage, 0.0)
    runoff = (area * excess * excess / (rainfall + 0.8 * storage)).astype(jnp.bfloat16)
    runoff_ref[...] = runoff
    dest_ref[...] = jnp.broadcast_to(sides[6:7], dest_ref.shape).astype(jnp.int32)
    reach_marks_ref[...] = one_hot(sides[7:8].astype(jnp.int32), reach_marks_ref.shape[0])
    backward = (
        iota((taps, hours), 1) == lax.rem(hours - iota((taps, hours), 0), hours)
    ).astype(jnp.float32)
    copy.wait()
    reversed_taps = lax.dot_general(
        irf_ref[...], backward, NN, precision=lax.Precision.HIGHEST, preferred_element_type=jnp.float32
    )
    causal = iota((half, hours), 1) <= iota((half, hours), 0) + half
    for kind in range(kinds):
        row = jnp.broadcast_to(reversed_taps[kind : kind + 1], (half, hours))
        matrix = jnp.where(causal, pltpu.roll(row, half, 1, stride=1, stride_axis=0), 0.0)
        matrix = jnp.concatenate(split(matrix), axis=0)
        if kind < early:
            responses_ref[kind] = respond(matrix, runoff)
        else:
            late_ref[:, (kind - early) * hours : (kind - early + 1) * hours] = matrix


def respond(matrices, runoffs):
    hours = matrices.shape[0]
    half = hours // 2
    count = matrices.shape[1] // hours

    def halves(values, axis, first):
        pieces = [
            lax.slice_in_dim(values, j * hours + first, j * hours + first + half, axis=axis)
            for j in range(count)
        ]
        return jnp.concatenate(pieces, axis=axis)

    earlier = lax.dot_general(
        halves(matrices, 1, half), halves(runoffs, 0, 0), NN, preferred_element_type=jnp.float32
    )
    later = lax.dot_general(matrices, runoffs, NN, preferred_element_type=jnp.float32)
    return jnp.concatenate([earlier[:half] + earlier[half:], later[:half] + later[half:]], axis=0)


def route_kernel(
    meta_ref, runoff_ref, dest_ref, reach_marks_ref, late_ref, responses_ref, flow_ref, stack_ref, *, basin_rows
):
    early, hours, tiles = responses_ref.shape
    late = late_ref.shape[1] // hours
    outlets = flow_ref.shape[0]
    owners = meta_ref.shape[0] // FIELDS
    core = lax.rem(lax.axis_index("tile"), CORES)
    dest = dest_ref[0:1]

    stack_ref[...] = meta_ref[...].astype(jnp.float32)

    def table(field):
        return stack_ref[pl.ds(field, owners, stride=FIELDS), :].astype(jnp.bfloat16)

    def picked(values, owner):
        chosen = iota((owners, tiles), 0) == owner
        return jnp.sum(jnp.where(chosen, values, 0.0), axis=0, keepdims=True).astype(jnp.int32)

    spans = (FIELDS - 2) // 3
    reach_table = jnp.concatenate(
        [
            jnp.concatenate([table(item * spans + j) for j in range(spans)], axis=1)
            for item in range(3)
        ],
        axis=0,
    )
    by_reach = lax.dot_general(
        reach_table, reach_marks_ref[...], NN, preferred_element_type=jnp.float32
    )
    basin, kind, lag = [picked(by_reach[j * owners : (j + 1) * owners], dest) for j in range(3)]
    tree_table = jnp.concatenate([table(3 * spans), table(3 * spans + 1)], axis=0)

    def parent_of(owner, local):
        by_basin = lax.dot_general(
            tree_table, one_hot(local, LANES), NN, preferred_element_type=jnp.float32
        )
        return picked(by_basin[:owners], owner) - 1, picked(by_basin[owners:], owner)

    parent_owner, parent_local = parent_of(dest, basin)
    second_owner, second_local = parent_of(parent_owner, parent_local)

    def row_of(owner, local):
        mine = jnp.logical_and(owner >= 0, (owner & (CORES - 1)) == core)
        return jnp.where(mine, (owner // CORES) * basin_rows + local, -1)

    placements = jnp.concatenate(
        [
            one_hot(row_of(owner, local), outlets)
            for owner, local in (
                (dest, basin),
                (parent_owner, parent_local),
                (second_owner, second_local),
            )
        ],
        axis=0,
    )

    highs, lows = [], []
    for first in range(0, tiles, 2 * LANES):
        wide = slice(first, first + 2 * LANES)
        runoff = runoff_ref[:, wide]
        by_kind = jnp.concatenate(
            [
                runoff * (kind[:, wide] == early + k).astype(jnp.float32).astype(jnp.bfloat16)
                for k in range(late)
            ],
            axis=0,
        )
        both = respond(late_ref[...], by_kind)
        for start in (0, LANES):
            lanes = slice(first + start, first + start + LANES)
            routed = both[:, start : start + LANES]
            for k in range(early):
                routed = jnp.where(kind[:, lanes] == k, responses_ref[k, :, lanes], routed)
            step = 64
            while step:
                routed = jnp.where((lag[:, lanes] & step) != 0, later_rows(routed, step), routed)
                step //= 2
            high, low = split(routed)
            highs.append(high)
            lows.append(low)
    flows = lax.dot_general(
        jnp.concatenate([placements, placements], axis=1),
        jnp.concatenate(highs + lows, axis=1),
        NT,
        preferred_element_type=jnp.float32,
    )
    for first in range(0, outlets, CHUNK):
        direct, second, third = [
            flows[j * outlets + first : j * outlets + first + CHUNK] for j in range(3)
        ]
        flow = direct + later_lanes(second + later_lanes(third, LINK), LINK)
        level = jnp.log(jnp.maximum(flow, CODE_FLOOR)) * CODE_SCALE + (CODE_ZERO + CODE_TOP + 0.5)
        level = jnp.clip(level, 0.0, 2.0 * CODE_TOP).astype(jnp.int32) - CODE_TOP
        flow_ref[first : first + CHUNK] = level.astype(jnp.int16)


def finish_kernel(parts_ref, section_ref):
    count, rows, _ = parts_ref.shape
    for first in range(0, rows, 16):
        chunk = slice(first, first + 16)
        total = 0.0
        for part in range(count):
            level = parts_ref[part, chunk].astype(jnp.int32).astype(jnp.float32)
            flow = jnp.exp((level - CODE_ZERO) * (1.0 / CODE_SCALE))
            total += jnp.where(level == -CODE_TOP, 0.0, flow)
        section_ref[chunk] = jnp.log(1.0 + total)


def per_device(
    rain,
    soil,
    tile_area,
    tile_dest,
    tile_reach,
    reach_basin,
    reach_kind,
    reach_lag,
    irf,
    outlet_level,
    outlet_parent,
):
    owners = lax.axis_size("tile")
    tile_rows, hours = rain.shape
    basin_rows = outlet_parent.shape[0]
    kinds = irf.shape[0]
    params = pltpu.CompilerParams(vmem_limit_bytes=VMEM_BYTES)
    held = pl.BlockSpec(memory_space=pltpu.HBM)
    whole = pl.BlockSpec(memory_space=pltpu.VMEM)
    block = (tile_rows + SIDE_ROWS, hours)

    def in_hbm(values, shape):
        return pltpu.with_memory_space_constraint(values.reshape(shape), pltpu.HBM)

    numbers = [
        in_hbm(values, (1, -1))
        for values in (
            reach_basin, reach_kind, reach_lag, outlet_parent, soil, tile_area, tile_dest, tile_reach,
        )
    ]
    meta, own = pl.pallas_call(
        lambda *refs: pack_kernel(*refs, basin_rows=basin_rows),
        out_shape=(
            jax.ShapeDtypeStruct((owners * FIELDS, LANES), jnp.bfloat16),
            jax.ShapeDtypeStruct(block, jnp.bfloat16),
        ),
        in_specs=[held] * (len(numbers) + 1),
        out_specs=(held, whole),
        scratch_shapes=[pltpu.VMEM(values.shape, values.dtype) for values in numbers]
        + [
            pltpu.VMEM((owners * FIELDS, LANES), jnp.bfloat16),
            pltpu.SemaphoreType.DMA((len(numbers) + 2,)),
        ],
        compiler_params=params,
        cost_estimate=SMALL,
        name="pack",
    )(*numbers, in_hbm(rain, rain.shape))
    other = lax.ppermute(own, "tile", [(i, i ^ 1) for i in range(owners)])
    meta = lax.all_to_all(
        meta.reshape(owners, FIELDS, LANES), "tile", split_axis=0, concat_axis=0, tiled=True
    ).reshape(-1, LANES)

    chip_tiles = CORES * tile_rows
    early = kinds // 2
    prepared = pl.pallas_call(
        prepare_kernel,
        out_shape=(
            jax.ShapeDtypeStruct((hours, chip_tiles), jnp.bfloat16),
            jax.ShapeDtypeStruct((8, chip_tiles), jnp.int32),
            jax.ShapeDtypeStruct((reach_basin.size, chip_tiles), jnp.bfloat16),
            jax.ShapeDtypeStruct((hours, (kinds - early) * hours), jnp.bfloat16),
            jax.ShapeDtypeStruct((early, hours, chip_tiles), jnp.float32),
        ),
        in_specs=[held, whole, whole],
        scratch_shapes=[pltpu.VMEM(irf.shape, irf.dtype), pltpu.SemaphoreType.DMA((1,))],
        compiler_params=params,
        cost_estimate=SMALL,
        name="prepare",
    )(in_hbm(irf, irf.shape), own, other)

    flow = pl.pallas_call(
        lambda *refs: route_kernel(*refs, basin_rows=basin_rows),
        out_shape=jax.ShapeDtypeStruct((owners // CORES * basin_rows, hours), jnp.int16),
        scratch_shapes=[pltpu.VMEM(meta.shape, jnp.float32)],
        compiler_params=params,
        name="route",
    )(meta, *prepared)

    parts = lax.all_to_all(
        flow.reshape(owners // CORES, basin_rows, hours),
        "tile",
        split_axis=0,
        concat_axis=0,
        axis_index_groups=[list(range(core, owners, CORES)) for core in range(CORES)],
        tiled=True,
    )
    return pl.pallas_call(
        finish_kernel,
        out_shape=jax.ShapeDtypeStruct((basin_rows, hours), jnp.float32),
        compiler_params=params,
        name="finish",
    )(parts)


def solution(mesh):
    rows = P(("ens", "tile"))
    table = P(("ens", "tile"), None)
    in_specs = (table, rows, rows, table, rows, rows, rows, rows, P(), rows, rows)
    return jax.shard_map(
        per_device, mesh=mesh, in_specs=in_specs, out_specs=table, check_vma=False
    )
```

```python
import math

import jax
import jax.numpy as jnp
from jax import lax
from jax.experimental import pallas as pl
from jax.experimental.pallas import tpu as pltpu
from jax.sharding import PartitionSpec as P

LINK = 6
LANES = 128
CORES = 2
FIELDS = 8
SIDE_ROWS = 16
VMEM_BYTES = 40 * 1024 * 1024
CODE_TOP = 32767
CODE_OCTAVES = 44
CODE_LOWEST = -26
CODE_SCALE = 2 * CODE_TOP / (CODE_OCTAVES * math.log(2.0))
CODE_FLOOR = 2.0 ** (2 * CODE_LOWEST)
CODE_ZERO = -CODE_TOP + 1 - CODE_LOWEST * math.log(2.0) * CODE_SCALE

SMALL = pl.CostEstimate(flops=1, bytes_accessed=1, transcendentals=0)
NT = (((1,), (1,)), ((), ()))
NN = (((1,), (0,)), ((), ()))


def iota(shape, axis):
    return lax.broadcasted_iota(jnp.int32, shape, axis)


def split(values):
    high = values.astype(jnp.bfloat16)
    return high, (values - high.astype(jnp.float32)).astype(jnp.bfloat16)


def one_hot(row, count):
    return (iota((count, row.shape[1]), 0) == row).astype(jnp.float32).astype(jnp.bfloat16)


def later_rows(values, hours):
    rows = values.shape[0]
    if hours % 8 == 0:
        padding = jnp.zeros((hours, values.shape[1]), values.dtype)
        return jnp.concatenate([padding, values[: rows - hours]], axis=0)
    return jnp.where(iota(values.shape, 0) < hours, 0.0, pltpu.roll(values, hours, 0))


def later_lanes(values, hours):
    return jnp.where(iota(values.shape, 1) < hours, 0.0, pltpu.roll(values, hours, 1))


def lane_rows(values):
    return [values[:, first : first + LANES] for first in range(0, values.shape[1], LANES)]


def parts_of(values):
    high = values.astype(jnp.bfloat16).astype(jnp.float32)
    middle = (values - high).astype(jnp.bfloat16).astype(jnp.float32)
    return [high, middle, values - high - middle]


def pack_kernel(*refs, basin_rows):
    sources, (meta_ref, block_ref, *scratch, arrived) = refs[:9], refs[9:]
    tile_rows = block_ref.shape[0] - SIDE_ROWS
    targets = (*scratch, block_ref.at[pl.ds(0, tile_rows)])
    copies = [
        pltpu.make_async_copy(source, target, arrived.at[j])
        for j, (source, target) in enumerate(zip(sources, targets))
    ]
    for copy in copies:
        copy.start()
    for copy in copies[:4]:
        copy.wait()
    basin, kind, lag, parent = [ref[...] for ref in scratch[:4]]
    shift = basin_rows.bit_length() - 1
    empty = jnp.zeros((1, LANES - basin_rows), jnp.int32)
    rows = lane_rows(basin) + lane_rows(kind) + lane_rows(lag)
    rows.append(jnp.concatenate([lax.shift_right_arithmetic(parent, shift) + 1, empty], axis=1))
    rows.append(jnp.concatenate([parent & (basin_rows - 1), empty], axis=1))
    numbers = jnp.concatenate(rows, axis=0).astype(jnp.float32)
    repeated = jnp.concatenate([numbers] * (meta_ref.shape[0] // FIELDS), axis=0)
    mine = iota(meta_ref.shape, 0) // FIELDS == lax.axis_index("tile")
    meta_ref[...] = jnp.where(mine, repeated, 0.0).astype(jnp.bfloat16)
    for copy in copies[4:8]:
        copy.wait()
    soil, area, dest, reach = [ref[...] for ref in scratch[4:]]
    sides = parts_of(soil) + parts_of(area) + [dest.astype(jnp.float32), reach.astype(jnp.float32)]
    sides = jnp.concatenate(sides + [jnp.zeros((SIDE_ROWS - len(sides), tile_rows), jnp.float32)], axis=0)
    block_ref[tile_rows:] = sides.astype(jnp.bfloat16)
    copies[8].wait()


def prepare_kernel(
    irf_hbm, own_ref, other_ref, runoff_ref, dest_ref, reach_marks_ref, late_ref, responses_ref, irf_ref, arrived
):
    copy = pltpu.make_async_copy(irf_hbm, irf_ref, arrived.at[0])
    copy.start()
    hours = own_ref.shape[1]
    half = hours // 2
    tile_rows = own_ref.shape[0] - SIDE_ROWS
    kinds, taps = irf_ref.shape
    early = responses_ref.shape[0]
    sides = jnp.concatenate([own_ref[tile_rows:], other_ref[tile_rows:]], axis=1).astype(jnp.float32)
    rainfall = jnp.concatenate(
        [ref[:tile_rows].astype(jnp.float32).T for ref in (own_ref, other_ref)], axis=1
    )
    storage = sides[0:1] + sides[1:2] + sides[2:3]
    area = sides[3:4] + sides[4:5] + sides[5:6]
    excess = jnp.maximum(rainfall - 0.2 * storage, 0.0)
    runoff = (area * excess * excess / (rainfall + 0.8 * storage)).astype(jnp.bfloat16)
    runoff_ref[...] = runoff
    dest_ref[...] = jnp.broadcast_to(sides[6:7], dest_ref.shape).astype(jnp.int32)
    reach_marks_ref[...] = one_hot(sides[7:8].astype(jnp.int32), reach_marks_ref.shape[0])
    backward = (
        iota((taps, hours), 1) == lax.rem(hours - iota((taps, hours), 0), hours)
    ).astype(jnp.float32)
    copy.wait()
    reversed_taps = lax.dot_general(
        irf_ref[...], backward, NN, precision=lax.Precision.HIGHEST, preferred_element_type=jnp.float32
    )
    causal = iota((half, hours), 1) <= iota((half, hours), 0) + half
    for kind in range(kinds):
        row = jnp.broadcast_to(reversed_taps[kind : kind + 1], (half, hours))
        matrix = jnp.where(causal, pltpu.roll(row, half, 1, stride=1, stride_axis=0), 0.0)
        matrix = jnp.concatenate(split(matrix), axis=0)
        if kind < early:
            responses_ref[kind] = respond(matrix, runoff)
        else:
            late_ref[:, (kind - early) * hours : (kind - early + 1) * hours] = matrix


def respond(matrices, runoffs):
    hours = matrices.shape[0]
    half = hours // 2
    count = matrices.shape[1] // hours

    def halves(values, axis, first):
        pieces = [
            lax.slice_in_dim(values, j * hours + first, j * hours + first + half, axis=axis)
            for j in range(count)
        ]
        return jnp.concatenate(pieces, axis=axis)

    earlier = lax.dot_general(
        halves(matrices, 1, half), halves(runoffs, 0, 0), NN, preferred_element_type=jnp.float32
    )
    later = lax.dot_general(matrices, runoffs, NN, preferred_element_type=jnp.float32)
    return jnp.concatenate([earlier[:half] + earlier[half:], later[:half] + later[half:]], axis=0)


def route_kernel(
    meta_ref, runoff_ref, dest_ref, reach_marks_ref, late_ref, responses_ref, flow_ref, stack_ref, *, basin_rows
):
    early, hours, tiles = responses_ref.shape
    late = late_ref.shape[1] // hours
    outlets = flow_ref.shape[0]
    owners = meta_ref.shape[0] // FIELDS
    core = lax.rem(lax.axis_index("tile"), CORES)
    dest = dest_ref[0:1]

    stack_ref[...] = meta_ref[...].astype(jnp.float32)

    def table(field):
        return stack_ref[pl.ds(field, owners, stride=FIELDS), :].astype(jnp.bfloat16)

    def picked(values, owner):
        chosen = iota((owners, tiles), 0) == owner
        return jnp.sum(jnp.where(chosen, values, 0.0), axis=0, keepdims=True).astype(jnp.int32)

    spans = (FIELDS - 2) // 3
    reach_table = jnp.concatenate(
        [
            jnp.concatenate([table(item * spans + j) for j in range(spans)], axis=1)
            for item in range(3)
        ],
        axis=0,
    )
    by_reach = lax.dot_general(
        reach_table, reach_marks_ref[...], NN, preferred_element_type=jnp.float32
    )
    basin, kind, lag = [picked(by_reach[j * owners : (j + 1) * owners], dest) for j in range(3)]
    tree_table = jnp.concatenate([table(3 * spans), table(3 * spans + 1)], axis=0)

    def parent_of(owner, local):
        by_basin = lax.dot_general(
            tree_table, one_hot(local, LANES), NN, preferred_element_type=jnp.float32
        )
        return picked(by_basin[:owners], owner) - 1, picked(by_basin[owners:], owner)

    parent_owner, parent_local = parent_of(dest, basin)
    second_owner, second_local = parent_of(parent_owner, parent_local)

    def row_of(owner, local):
        mine = jnp.logical_and(owner >= 0, (owner & (CORES - 1)) == core)
        return jnp.where(mine, (owner // CORES) * basin_rows + local, -1)

    placements = jnp.concatenate(
        [
            one_hot(row_of(owner, local), outlets)
            for owner, local in (
                (dest, basin),
                (parent_owner, parent_local),
                (second_owner, second_local),
            )
        ],
        axis=0,
    )

    runoff = runoff_ref[...]
    by_kind = jnp.concatenate(
        [
            runoff * (kind == early + k).astype(jnp.float32).astype(jnp.bfloat16)
            for k in range(late)
        ],
        axis=0,
    )
    routed = respond(late_ref[...], by_kind)
    for k in range(early):
        routed = jnp.where(kind == k, responses_ref[k], routed)
    step = 64
    while step:
        routed = jnp.where((lag & step) != 0, later_rows(routed, step), routed)
        step //= 2
    flows = lax.dot_general(
        jnp.concatenate([placements, placements], axis=1),
        jnp.concatenate(split(routed), axis=1),
        NT,
        preferred_element_type=jnp.float32,
    )
    flow = later_lanes(flows[2 * outlets :], LINK)
    flow = later_lanes(flows[outlets : 2 * outlets] + flow, LINK)
    flow = flows[:outlets] + flow
    level = jnp.log(jnp.maximum(flow, CODE_FLOOR)) * CODE_SCALE + (CODE_ZERO + CODE_TOP + 0.5)
    level = jnp.clip(level, 0.0, 2.0 * CODE_TOP).astype(jnp.int32) - CODE_TOP
    flow_ref[...] = level.astype(jnp.int16)


def finish_kernel(parts_ref, section_ref):
    level = parts_ref[...].astype(jnp.int32)
    flow = jnp.exp((level.astype(jnp.float32) - CODE_ZERO) * (1.0 / CODE_SCALE))
    flow = jnp.sum(jnp.where(level == -CODE_TOP, 0.0, flow), axis=0)
    section_ref[...] = jnp.log(1.0 + flow)


def per_device(
    rain,
    soil,
    tile_area,
    tile_dest,
    tile_reach,
    reach_basin,
    reach_kind,
    reach_lag,
    irf,
    outlet_level,
    outlet_parent,
):
    owners = lax.axis_size("tile")
    tile_rows, hours = rain.shape
    basin_rows = outlet_parent.shape[0]
    kinds = irf.shape[0]
    params = pltpu.CompilerParams(vmem_limit_bytes=VMEM_BYTES)
    held = pl.BlockSpec(memory_space=pltpu.HBM)
    whole = pl.BlockSpec(memory_space=pltpu.VMEM)
    block = (tile_rows + SIDE_ROWS, hours)

    def in_hbm(values, shape):
        return pltpu.with_memory_space_constraint(values.reshape(shape), pltpu.HBM)

    numbers = [
        in_hbm(values, (1, -1))
        for values in (
            reach_basin, reach_kind, reach_lag, outlet_parent, soil, tile_area, tile_dest, tile_reach,
        )
    ]
    meta, own = pl.pallas_call(
        lambda *refs: pack_kernel(*refs, basin_rows=basin_rows),
        out_shape=(
            jax.ShapeDtypeStruct((owners * FIELDS, LANES), jnp.bfloat16),
            jax.ShapeDtypeStruct(block, jnp.bfloat16),
        ),
        in_specs=[held] * (len(numbers) + 1),
        scratch_shapes=[pltpu.VMEM(values.shape, values.dtype) for values in numbers]
        + [pltpu.SemaphoreType.DMA((len(numbers) + 1,))],
        compiler_params=params,
        cost_estimate=SMALL,
        name="pack",
    )(*numbers, in_hbm(rain, rain.shape))
    other = lax.ppermute(own, "tile", [(i, i ^ 1) for i in range(owners)])
    meta = lax.psum(meta, "tile")

    chip_tiles = CORES * tile_rows
    early = kinds // 2
    prepared = pl.pallas_call(
        prepare_kernel,
        out_shape=(
            jax.ShapeDtypeStruct((hours, chip_tiles), jnp.bfloat16),
            jax.ShapeDtypeStruct((8, chip_tiles), jnp.int32),
            jax.ShapeDtypeStruct((reach_basin.size, chip_tiles), jnp.bfloat16),
            jax.ShapeDtypeStruct((hours, (kinds - early) * hours), jnp.bfloat16),
            jax.ShapeDtypeStruct((early, hours, chip_tiles), jnp.float32),
        ),
        in_specs=[held, whole, whole],
        scratch_shapes=[pltpu.VMEM(irf.shape, irf.dtype), pltpu.SemaphoreType.DMA((1,))],
        compiler_params=params,
        cost_estimate=SMALL,
        name="prepare",
    )(in_hbm(irf, irf.shape), own, other)

    flow = pl.pallas_call(
        lambda *refs: route_kernel(*refs, basin_rows=basin_rows),
        out_shape=jax.ShapeDtypeStruct((owners // CORES * basin_rows, hours), jnp.int16),
        scratch_shapes=[pltpu.VMEM(meta.shape, jnp.float32)],
        compiler_params=params,
        name="route",
    )(meta, *prepared)

    parts = lax.all_to_all(
        flow.reshape(owners // CORES, basin_rows, hours),
        "tile",
        split_axis=0,
        concat_axis=0,
        axis_index_groups=[list(range(core, owners, CORES)) for core in range(CORES)],
        tiled=True,
    )
    return pl.pallas_call(
        finish_kernel,
        out_shape=jax.ShapeDtypeStruct((basin_rows, hours), jnp.float32),
        compiler_params=params,
        name="finish",
    )(parts)


def solution(mesh):
    rows = P(("ens", "tile"))
    table = P(("ens", "tile"), None)
    in_specs = (table, rows, rows, table, rows, rows, rows, rows, P(), rows, rows)
    return jax.shard_map(
        per_device, mesh=mesh, in_specs=in_specs, out_specs=table, check_vma=False
    )
```

```python
import math

import jax
import jax.numpy as jnp
from jax import lax
from jax.experimental import pallas as pl
from jax.experimental.pallas import tpu as pltpu
from jax.sharding import PartitionSpec as P

LINK = 6
LANES = 128
CORES = 2
FIELDS = 8
SIDE_ROWS = 16
VMEM_BYTES = 40 * 1024 * 1024
CODE_TOP = 32767
CODE_OCTAVES = 44
CODE_LOWEST = -26
CODE_SCALE = 2 * CODE_TOP / (CODE_OCTAVES * math.log(2.0))
CODE_FLOOR = 2.0 ** (2 * CODE_LOWEST)
CODE_ZERO = -CODE_TOP + 1 - CODE_LOWEST * math.log(2.0) * CODE_SCALE

SMALL = pl.CostEstimate(flops=1, bytes_accessed=1, transcendentals=0)
NT = (((1,), (1,)), ((), ()))
NN = (((1,), (0,)), ((), ()))


def iota(shape, axis):
    return lax.broadcasted_iota(jnp.int32, shape, axis)


def split(values):
    high = values.astype(jnp.bfloat16)
    return high, (values - high.astype(jnp.float32)).astype(jnp.bfloat16)


def one_hot(row, count):
    return (iota((count, row.shape[1]), 0) == row).astype(jnp.float32).astype(jnp.bfloat16)


def later_rows(values, hours):
    rows = values.shape[0]
    if hours % 8 == 0:
        padding = jnp.zeros((hours, values.shape[1]), values.dtype)
        return jnp.concatenate([padding, values[: rows - hours]], axis=0)
    return jnp.where(iota(values.shape, 0) < hours, 0.0, pltpu.roll(values, hours, 0))


def later_lanes(values, hours):
    return jnp.where(iota(values.shape, 1) < hours, 0.0, pltpu.roll(values, hours, 1))


def lane_rows(values):
    return [values[:, first : first + LANES] for first in range(0, values.shape[1], LANES)]


def parts_of(values):
    high = values.astype(jnp.bfloat16).astype(jnp.float32)
    middle = (values - high).astype(jnp.bfloat16).astype(jnp.float32)
    return [high, middle, values - high - middle]


def pack_kernel(*refs, basin_rows):
    sources, (meta_ref, block_ref, *scratch, arrived) = refs[:9], refs[9:]
    tile_rows = block_ref.shape[0] - SIDE_ROWS
    targets = (*scratch, block_ref.at[pl.ds(0, tile_rows)])
    copies = [
        pltpu.make_async_copy(source, target, arrived.at[j])
        for j, (source, target) in enumerate(zip(sources, targets))
    ]
    for copy in copies:
        copy.start()
    for copy in copies[:4]:
        copy.wait()
    basin, kind, lag, parent = [ref[...] for ref in scratch[:4]]
    shift = basin_rows.bit_length() - 1
    empty = jnp.zeros((1, LANES - basin_rows), jnp.int32)
    rows = lane_rows(basin) + lane_rows(kind) + lane_rows(lag)
    rows.append(jnp.concatenate([lax.shift_right_arithmetic(parent, shift) + 1, empty], axis=1))
    rows.append(jnp.concatenate([parent & (basin_rows - 1), empty], axis=1))
    numbers = jnp.concatenate(rows, axis=0).astype(jnp.float32)
    meta_ref[...] = numbers.astype(jnp.bfloat16)
    for copy in copies[4:8]:
        copy.wait()
    soil, area, dest, reach = [ref[...] for ref in scratch[4:]]
    sides = parts_of(soil) + parts_of(area) + [dest.astype(jnp.float32), reach.astype(jnp.float32)]
    sides = jnp.concatenate(sides + [jnp.zeros((SIDE_ROWS - len(sides), tile_rows), jnp.float32)], axis=0)
    block_ref[tile_rows:] = sides.astype(jnp.bfloat16)
    copies[8].wait()


def prepare_kernel(
    irf_hbm, own_ref, other_ref, dest_ref, reach_marks_ref, responses_ref, irf_ref, arrived
):
    copy = pltpu.make_async_copy(irf_hbm, irf_ref, arrived.at[0])
    copy.start()
    hours = own_ref.shape[1]
    half = hours // 2
    tile_rows = own_ref.shape[0] - SIDE_ROWS
    kinds, taps = irf_ref.shape
    sides = jnp.concatenate([own_ref[tile_rows:], other_ref[tile_rows:]], axis=1).astype(jnp.float32)
    rainfall = jnp.concatenate(
        [ref[:tile_rows].astype(jnp.float32).T for ref in (own_ref, other_ref)], axis=1
    )
    storage = sides[0:1] + sides[1:2] + sides[2:3]
    area = sides[3:4] + sides[4:5] + sides[5:6]
    excess = jnp.maximum(rainfall - 0.2 * storage, 0.0)
    runoff = (area * excess * excess / (rainfall + 0.8 * storage)).astype(jnp.bfloat16)
    dest_ref[...] = jnp.broadcast_to(sides[6:7], dest_ref.shape).astype(jnp.int32)
    reach_marks_ref[...] = one_hot(sides[7:8].astype(jnp.int32), reach_marks_ref.shape[0])
    backward = (
        iota((taps, hours), 1) == lax.rem(hours - iota((taps, hours), 0), hours)
    ).astype(jnp.float32)
    copy.wait()
    reversed_taps = lax.dot_general(
        irf_ref[...], backward, NN, precision=lax.Precision.HIGHEST, preferred_element_type=jnp.float32
    )
    causal = iota((half, hours), 1) <= iota((half, hours), 0) + half
    for kind in range(kinds):
        row = jnp.broadcast_to(reversed_taps[kind : kind + 1], (half, hours))
        matrix = jnp.where(causal, pltpu.roll(row, half, 1, stride=1, stride_axis=0), 0.0)
        matrix = jnp.concatenate(split(matrix), axis=0)
        responses_ref[kind] = respond(matrix, runoff)


def respond(matrix, runoff):
    half = matrix.shape[0] // 2
    earlier = lax.dot_general(matrix[:, half:], runoff[:half], NN, preferred_element_type=jnp.float32)
    later = lax.dot_general(matrix, runoff, NN, preferred_element_type=jnp.float32)
    return jnp.concatenate([earlier[:half] + earlier[half:], later[:half] + later[half:]], axis=0)


def route_kernel(*refs, basin_rows):
    *meta_refs, dest_ref, reach_marks_ref, responses_ref, flow_ref, stack_ref = refs
    kinds, _, tiles = responses_ref.shape
    outlets = flow_ref.shape[0]
    owners = (stack_ref.shape[0] - FIELDS) // FIELDS
    me = lax.axis_index("tile")
    core = lax.rem(me, CORES)
    dest = dest_ref[0:1]

    first = 0
    for meta_ref in meta_refs:
        stack_ref[first : first + meta_ref.shape[0]] = meta_ref[...].astype(jnp.float32)
        first += meta_ref.shape[0]

    def table(field):
        return stack_ref[pl.ds(field, owners, stride=FIELDS), :].astype(jnp.bfloat16)

    def picked(values, owner):
        chosen = iota((owners, tiles), 0) == owners - 1 - (owner ^ me)
        return jnp.sum(jnp.where(chosen, values, 0.0), axis=0, keepdims=True).astype(jnp.int32)

    spans = (FIELDS - 2) // 3
    reach_table = jnp.concatenate(
        [
            jnp.concatenate([table(item * spans + j) for j in range(spans)], axis=1)
            for item in range(3)
        ],
        axis=0,
    )
    by_reach = lax.dot_general(
        reach_table, reach_marks_ref[...], NN, preferred_element_type=jnp.float32
    )
    basin, kind, lag = [picked(by_reach[j * owners : (j + 1) * owners], dest) for j in range(3)]
    tree_table = jnp.concatenate([table(3 * spans), table(3 * spans + 1)], axis=0)

    def parent_of(owner, local):
        by_basin = lax.dot_general(
            tree_table, one_hot(local, LANES), NN, preferred_element_type=jnp.float32
        )
        return picked(by_basin[:owners], owner) - 1, picked(by_basin[owners:], owner)

    parent_owner, parent_local = parent_of(dest, basin)
    second_owner, second_local = parent_of(parent_owner, parent_local)

    def row_of(owner, local):
        mine = jnp.logical_and(owner >= 0, (owner & (CORES - 1)) == core)
        return jnp.where(mine, (owner // CORES) * basin_rows + local, -1)

    placements = jnp.concatenate(
        [
            one_hot(row_of(owner, local), outlets)
            for owner, local in (
                (dest, basin),
                (parent_owner, parent_local),
                (second_owner, second_local),
            )
        ],
        axis=0,
    )

    routed = responses_ref[0]
    for k in range(1, kinds):
        routed = jnp.where(kind == k, responses_ref[k], routed)
    step = 64
    while step:
        routed = jnp.where((lag & step) != 0, later_rows(routed, step), routed)
        step //= 2
    flows = lax.dot_general(
        jnp.concatenate([placements, placements], axis=1),
        jnp.concatenate(split(routed), axis=1),
        NT,
        preferred_element_type=jnp.float32,
    )
    flow = later_lanes(flows[2 * outlets :], LINK)
    flow = later_lanes(flows[outlets : 2 * outlets] + flow, LINK)
    flow = flows[:outlets] + flow
    level = jnp.log(jnp.maximum(flow, CODE_FLOOR)) * CODE_SCALE + (CODE_ZERO + CODE_TOP + 0.5)
    level = jnp.clip(level, 0.0, 2.0 * CODE_TOP).astype(jnp.int32) - CODE_TOP
    flow_ref[...] = level.astype(jnp.int16)


def finish_kernel(parts_ref, section_ref):
    level = parts_ref[...].astype(jnp.int32)
    flow = jnp.exp((level.astype(jnp.float32) - CODE_ZERO) * (1.0 / CODE_SCALE))
    flow = jnp.sum(jnp.where(level == -CODE_TOP, 0.0, flow), axis=0)
    section_ref[...] = jnp.log(1.0 + flow)


def per_device(
    rain,
    soil,
    tile_area,
    tile_dest,
    tile_reach,
    reach_basin,
    reach_kind,
    reach_lag,
    irf,
    outlet_level,
    outlet_parent,
):
    owners = lax.axis_size("tile")
    tile_rows, hours = rain.shape
    basin_rows = outlet_parent.shape[0]
    kinds = irf.shape[0]
    params = pltpu.CompilerParams(vmem_limit_bytes=VMEM_BYTES)
    held = pl.BlockSpec(memory_space=pltpu.HBM)
    whole = pl.BlockSpec(memory_space=pltpu.VMEM)
    block = (tile_rows + SIDE_ROWS, hours)

    def in_hbm(values, shape):
        return pltpu.with_memory_space_constraint(values.reshape(shape), pltpu.HBM)

    numbers = [
        in_hbm(values, (1, -1))
        for values in (
            reach_basin, reach_kind, reach_lag, outlet_parent, soil, tile_area, tile_dest, tile_reach,
        )
    ]
    meta, own = pl.pallas_call(
        lambda *refs: pack_kernel(*refs, basin_rows=basin_rows),
        out_shape=(
            jax.ShapeDtypeStruct((FIELDS, LANES), jnp.bfloat16),
            jax.ShapeDtypeStruct(block, jnp.bfloat16),
        ),
        in_specs=[held] * (len(numbers) + 1),
        scratch_shapes=[pltpu.VMEM(values.shape, values.dtype) for values in numbers]
        + [pltpu.SemaphoreType.DMA((len(numbers) + 1,))],
        compiler_params=params,
        cost_estimate=SMALL,
        name="pack",
    )(*numbers, in_hbm(rain, rain.shape))
    other = lax.ppermute(own, "tile", [(i, i ^ 1) for i in range(owners)])
    metas = [meta]
    held_owners = 1
    while held_owners < owners:
        radix = min(4, owners // held_owners)
        stack = jnp.concatenate(metas, axis=0) if len(metas) > 1 else metas[0]
        met = {
            step: lax.ppermute(stack, "tile", [(i, i ^ (held_owners * step)) for i in range(owners)])
            for step in range(1, radix)
        }
        metas = [met[step] for step in range(radix - 1, 0, -1)] + [stack]
        held_owners *= radix

    chip_tiles = CORES * tile_rows
    prepared = pl.pallas_call(
        prepare_kernel,
        out_shape=(
            jax.ShapeDtypeStruct((8, chip_tiles), jnp.int32),
            jax.ShapeDtypeStruct((reach_basin.size, chip_tiles), jnp.bfloat16),
            jax.ShapeDtypeStruct((kinds, hours, chip_tiles), jnp.float32),
        ),
        in_specs=[held, whole, whole],
        scratch_shapes=[pltpu.VMEM(irf.shape, irf.dtype), pltpu.SemaphoreType.DMA((1,))],
        compiler_params=params,
        cost_estimate=SMALL,
        name="prepare",
    )(in_hbm(irf, irf.shape), own, other)

    flow = pl.pallas_call(
        lambda *refs: route_kernel(*refs, basin_rows=basin_rows),
        out_shape=jax.ShapeDtypeStruct((owners // CORES * basin_rows, hours), jnp.int16),
        scratch_shapes=[pltpu.VMEM(((owners + 1) * FIELDS, LANES), jnp.float32)],
        compiler_params=params,
        name="route",
    )(*metas, *prepared)

    parts = lax.all_to_all(
        flow.reshape(owners // CORES, basin_rows, hours),
        "tile",
        split_axis=0,
        concat_axis=0,
        axis_index_groups=[list(range(core, owners, CORES)) for core in range(CORES)],
        tiled=True,
    )
    return pl.pallas_call(
        finish_kernel,
        out_shape=jax.ShapeDtypeStruct((basin_rows, hours), jnp.float32),
        compiler_params=params,
        name="finish",
    )(parts)


def solution(mesh):
    rows = P(("ens", "tile"))
    table = P(("ens", "tile"), None)
    in_specs = (table, rows, rows, table, rows, rows, rows, rows, P(), rows, rows)
    return jax.shard_map(
        per_device, mesh=mesh, in_specs=in_specs, out_specs=table, check_vma=False
    )
```

```python
import math

import jax
import jax.numpy as jnp
from jax import lax
from jax.experimental import pallas as pl
from jax.experimental.pallas import tpu as pltpu
from jax.sharding import PartitionSpec as P

LINK = 6
LANES = 128
CORES = 2
FIELDS = 8
SIDE_ROWS = 16
VMEM_BYTES = 40 * 1024 * 1024
CODE_TOP = 32767
CODE_OCTAVES = 44
CODE_LOWEST = -26
CODE_SCALE = 2 * CODE_TOP / (CODE_OCTAVES * math.log(2.0))
CODE_FLOOR = 2.0 ** (2 * CODE_LOWEST)
CODE_ZERO = -CODE_TOP + 1 - CODE_LOWEST * math.log(2.0) * CODE_SCALE

SMALL = pl.CostEstimate(flops=1, bytes_accessed=1, transcendentals=0)
NT = (((1,), (1,)), ((), ()))
NN = (((1,), (0,)), ((), ()))


def iota(shape, axis):
    return lax.broadcasted_iota(jnp.int32, shape, axis)


def split(values):
    high = values.astype(jnp.bfloat16)
    return high, (values - high.astype(jnp.float32)).astype(jnp.bfloat16)


def one_hot(row, count):
    return (iota((count, row.shape[1]), 0) == row).astype(jnp.float32).astype(jnp.bfloat16)


def group_of(owner, owners):
    upper = (owner + owners // 2) // owners
    return (owner + upper) % CORES


def later_rows(values, hours):
    rows = values.shape[0]
    if hours % 8 == 0:
        padding = jnp.zeros((hours, values.shape[1]), values.dtype)
        return jnp.concatenate([padding, values[: rows - hours]], axis=0)
    return jnp.where(iota(values.shape, 0) < hours, 0.0, pltpu.roll(values, hours, 0))


def later_lanes(values, hours):
    return jnp.where(iota(values.shape, 1) < hours, 0.0, pltpu.roll(values, hours, 1))


def lane_rows(values):
    return [values[:, first : first + LANES] for first in range(0, values.shape[1], LANES)]


def parts_of(values):
    high = values.astype(jnp.bfloat16).astype(jnp.float32)
    middle = (values - high).astype(jnp.bfloat16).astype(jnp.float32)
    return [high, middle, values - high - middle]


def pack_kernel(*refs, basin_rows):
    sources, (meta_hbm, block_ref, *scratch, meta_ref, arrived) = refs[:9], refs[9:]
    tile_rows = block_ref.shape[0] - SIDE_ROWS
    targets = (*scratch, block_ref.at[pl.ds(0, tile_rows)])
    copies = [
        pltpu.make_async_copy(source, target, arrived.at[j])
        for j, (source, target) in enumerate(zip(sources, targets))
    ]
    for copy in copies:
        copy.start()
    for copy in copies[:4]:
        copy.wait()
    basin, kind, lag, parent = [ref[...] for ref in scratch[:4]]
    shift = basin_rows.bit_length() - 1
    empty = jnp.zeros((1, LANES - basin_rows), jnp.int32)
    rows = lane_rows(basin) + lane_rows(kind) + lane_rows(lag)
    rows.append(jnp.concatenate([lax.shift_right_arithmetic(parent, shift) + 1, empty], axis=1))
    rows.append(jnp.concatenate([parent & (basin_rows - 1), empty], axis=1))
    numbers = jnp.concatenate(rows, axis=0).astype(jnp.float32)
    meta_ref[...] = jnp.concatenate([numbers] * (meta_ref.shape[0] // FIELDS), axis=0).astype(jnp.bfloat16)
    leaving = pltpu.make_async_copy(meta_ref, meta_hbm, arrived.at[len(copies)])
    leaving.start()
    for copy in copies[4:8]:
        copy.wait()
    soil, area, dest, reach = [ref[...] for ref in scratch[4:]]
    sides = parts_of(soil) + parts_of(area) + [dest.astype(jnp.float32), reach.astype(jnp.float32)]
    sides = jnp.concatenate(sides + [jnp.zeros((SIDE_ROWS - len(sides), tile_rows), jnp.float32)], axis=0)
    block_ref[tile_rows:] = sides.astype(jnp.bfloat16)
    copies[8].wait()
    leaving.wait()


def prepare_kernel(
    irf_hbm, own_ref, other_ref, runoff_ref, dest_ref, reach_marks_ref, late_ref, responses_ref, irf_ref, arrived
):
    copy = pltpu.make_async_copy(irf_hbm, irf_ref, arrived.at[0])
    copy.start()
    hours = own_ref.shape[1]
    half = hours // 2
    tile_rows = own_ref.shape[0] - SIDE_ROWS
    kinds, taps = irf_ref.shape
    early = responses_ref.shape[0]
    sides = jnp.concatenate([own_ref[tile_rows:], other_ref[tile_rows:]], axis=1).astype(jnp.float32)
    rainfall = jnp.concatenate(
        [ref[:tile_rows].astype(jnp.float32).T for ref in (own_ref, other_ref)], axis=1
    )
    storage = sides[0:1] + sides[1:2] + sides[2:3]
    area = sides[3:4] + sides[4:5] + sides[5:6]
    excess = jnp.maximum(rainfall - 0.2 * storage, 0.0)
    runoff = (area * excess * excess / (rainfall + 0.8 * storage)).astype(jnp.bfloat16)
    runoff_ref[...] = runoff
    dest_ref[...] = jnp.broadcast_to(sides[6:7], dest_ref.shape).astype(jnp.int32)
    reach_marks_ref[...] = one_hot(sides[7:8].astype(jnp.int32), reach_marks_ref.shape[0])
    backward = (
        iota((taps, hours), 1) == lax.rem(hours - iota((taps, hours), 0), hours)
    ).astype(jnp.float32)
    copy.wait()
    reversed_taps = lax.dot_general(
        irf_ref[...], backward, NN, precision=lax.Precision.HIGHEST, preferred_element_type=jnp.float32
    )
    causal = iota((half, hours), 1) <= iota((half, hours), 0) + half
    for kind in range(kinds):
        row = jnp.broadcast_to(reversed_taps[kind : kind + 1], (half, hours))
        matrix = jnp.where(causal, pltpu.roll(row, half, 1, stride=1, stride_axis=0), 0.0)
        matrix = jnp.concatenate(split(matrix), axis=0)
        if kind < early:
            responses_ref[kind] = respond(matrix, runoff)
        else:
            late_ref[:, (kind - early) * hours : (kind - early + 1) * hours] = matrix


def respond(matrices, runoffs):
    hours = matrices.shape[0]
    half = hours // 2
    count = matrices.shape[1] // hours

    def halves(values, axis, first):
        pieces = [
            lax.slice_in_dim(values, j * hours + first, j * hours + first + half, axis=axis)
            for j in range(count)
        ]
        return jnp.concatenate(pieces, axis=axis)

    earlier = lax.dot_general(
        halves(matrices, 1, half), halves(runoffs, 0, 0), NN, preferred_element_type=jnp.float32
    )
    later = lax.dot_general(matrices, runoffs, NN, preferred_element_type=jnp.float32)
    return jnp.concatenate([earlier[:half] + earlier[half:], later[:half] + later[half:]], axis=0)


def route_kernel(
    meta_ref, runoff_ref, dest_ref, reach_marks_ref, late_ref, responses_ref, flow_ref, stack_ref, *, basin_rows
):
    early, hours, tiles = responses_ref.shape
    late = late_ref.shape[1] // hours
    outlets = flow_ref.shape[0]
    owners = meta_ref.shape[0] // FIELDS
    side = group_of(lax.axis_index("tile"), owners)
    dest = dest_ref[0:1]

    stack_ref[: owners * FIELDS] = meta_ref[...].astype(jnp.float32)

    def table(field):
        return stack_ref[pl.ds(field, owners, stride=FIELDS), :].astype(jnp.bfloat16)

    def picked(values, owner):
        chosen = iota((owners, tiles), 0) == owner
        return jnp.sum(jnp.where(chosen, values, 0.0), axis=0, keepdims=True).astype(jnp.int32)

    spans = (FIELDS - 2) // 3
    reach_table = jnp.concatenate(
        [
            jnp.concatenate([table(item * spans + j) for j in range(spans)], axis=1)
            for item in range(3)
        ],
        axis=0,
    )
    by_reach = lax.dot_general(
        reach_table, reach_marks_ref[...], NN, preferred_element_type=jnp.float32
    )
    basin, kind, lag = [picked(by_reach[j * owners : (j + 1) * owners], dest) for j in range(3)]
    tree_table = jnp.concatenate([table(3 * spans), table(3 * spans + 1)], axis=0)

    def parent_of(owner, local):
        by_basin = lax.dot_general(
            tree_table, one_hot(local, LANES), NN, preferred_element_type=jnp.float32
        )
        return picked(by_basin[:owners], owner) - 1, picked(by_basin[owners:], owner)

    parent_owner, parent_local = parent_of(dest, basin)
    second_owner, second_local = parent_of(parent_owner, parent_local)

    def row_of(owner, local):
        mine = jnp.logical_and(owner >= 0, group_of(owner, owners) == side)
        return jnp.where(mine, (owner // CORES) * basin_rows + local, -1)

    placements = jnp.concatenate(
        [
            one_hot(row_of(owner, local), outlets)
            for owner, local in (
                (dest, basin),
                (parent_owner, parent_local),
                (second_owner, second_local),
            )
        ],
        axis=0,
    )

    runoff = runoff_ref[...]
    by_kind = jnp.concatenate(
        [
            runoff * (kind == early + k).astype(jnp.float32).astype(jnp.bfloat16)
            for k in range(late)
        ],
        axis=0,
    )
    routed = respond(late_ref[...], by_kind)
    for k in range(early):
        routed = jnp.where(kind == k, responses_ref[k], routed)
    step = 64
    while step:
        routed = jnp.where((lag & step) != 0, later_rows(routed, step), routed)
        step //= 2
    flows = lax.dot_general(
        jnp.concatenate([placements, placements], axis=1),
        jnp.concatenate(split(routed), axis=1),
        NT,
        preferred_element_type=jnp.float32,
    )
    flow = later_lanes(flows[2 * outlets :], LINK)
    flow = later_lanes(flows[outlets : 2 * outlets] + flow, LINK)
    flow = flows[:outlets] + flow
    level = jnp.log(jnp.maximum(flow, CODE_FLOOR)) * CODE_SCALE + (CODE_ZERO + CODE_TOP + 0.5)
    level = jnp.clip(level, 0.0, 2.0 * CODE_TOP).astype(jnp.int32) - CODE_TOP
    flow_ref[...] = level.astype(jnp.int16)


def finish_kernel(parts_ref, section_ref):
    level = parts_ref[...].astype(jnp.int32)
    flow = jnp.exp((level.astype(jnp.float32) - CODE_ZERO) * (1.0 / CODE_SCALE))
    flow = jnp.sum(jnp.where(level == -CODE_TOP, 0.0, flow), axis=0)
    section_ref[...] = jnp.log(1.0 + flow)


def per_device(
    rain,
    soil,
    tile_area,
    tile_dest,
    tile_reach,
    reach_basin,
    reach_kind,
    reach_lag,
    irf,
    outlet_level,
    outlet_parent,
):
    owners = lax.axis_size("tile")
    tile_rows, hours = rain.shape
    basin_rows = outlet_parent.shape[0]
    kinds = irf.shape[0]
    params = pltpu.CompilerParams(vmem_limit_bytes=VMEM_BYTES)
    held = pl.BlockSpec(memory_space=pltpu.HBM)
    whole = pl.BlockSpec(memory_space=pltpu.VMEM)
    block = (tile_rows + SIDE_ROWS, hours)

    def in_hbm(values, shape):
        return pltpu.with_memory_space_constraint(values.reshape(shape), pltpu.HBM)

    numbers = [
        in_hbm(values, (1, -1))
        for values in (
            reach_basin, reach_kind, reach_lag, outlet_parent, soil, tile_area, tile_dest, tile_reach,
        )
    ]
    meta, own = pl.pallas_call(
        lambda *refs: pack_kernel(*refs, basin_rows=basin_rows),
        out_shape=(
            jax.ShapeDtypeStruct((owners * FIELDS, LANES), jnp.bfloat16),
            jax.ShapeDtypeStruct(block, jnp.bfloat16),
        ),
        in_specs=[held] * (len(numbers) + 1),
        out_specs=(held, whole),
        scratch_shapes=[pltpu.VMEM(values.shape, values.dtype) for values in numbers]
        + [
            pltpu.VMEM((owners * FIELDS, LANES), jnp.bfloat16),
            pltpu.SemaphoreType.DMA((len(numbers) + 2,)),
        ],
        compiler_params=params,
        cost_estimate=SMALL,
        name="pack",
    )(*numbers, in_hbm(rain, rain.shape))
    other = lax.ppermute(own, "tile", [(i, i ^ 1) for i in range(owners)])
    meta = lax.all_to_all(
        meta.reshape(owners, FIELDS, LANES), "tile", split_axis=0, concat_axis=0, tiled=True
    ).reshape(-1, LANES)

    chip_tiles = CORES * tile_rows
    early = kinds // 2
    prepared = pl.pallas_call(
        prepare_kernel,
        out_shape=(
            jax.ShapeDtypeStruct((hours, chip_tiles), jnp.bfloat16),
            jax.ShapeDtypeStruct((8, chip_tiles), jnp.int32),
            jax.ShapeDtypeStruct((reach_basin.size, chip_tiles), jnp.bfloat16),
            jax.ShapeDtypeStruct((hours, (kinds - early) * hours), jnp.bfloat16),
            jax.ShapeDtypeStruct((early, hours, chip_tiles), jnp.float32),
        ),
        in_specs=[held, whole, whole],
        scratch_shapes=[pltpu.VMEM(irf.shape, irf.dtype), pltpu.SemaphoreType.DMA((1,))],
        compiler_params=params,
        cost_estimate=SMALL,
        name="prepare",
    )(in_hbm(irf, irf.shape), own, other)

    flow = pl.pallas_call(
        lambda *refs: route_kernel(*refs, basin_rows=basin_rows),
        out_shape=jax.ShapeDtypeStruct((owners // CORES * basin_rows, hours), jnp.int16),
        scratch_shapes=[pltpu.VMEM(((owners + 1) * FIELDS, LANES), jnp.float32)],
        compiler_params=params,
        name="route",
    )(meta, *prepared)

    parts = lax.all_to_all(
        flow.reshape(owners // CORES, basin_rows, hours),
        "tile",
        split_axis=0,
        concat_axis=0,
        axis_index_groups=[
            [owner for owner in range(owners) if group_of(owner, owners) == side] for side in range(CORES)
        ],
        tiled=True,
    )
    return pl.pallas_call(
        finish_kernel,
        out_shape=jax.ShapeDtypeStruct((basin_rows, hours), jnp.float32),
        compiler_params=params,
        name="finish",
    )(parts)


def solution(mesh):
    rows = P(("ens", "tile"))
    table = P(("ens", "tile"), None)
    in_specs = (table, rows, rows, table, rows, rows, rows, rows, P(), rows, rows)
    return jax.shard_map(
        per_device, mesh=mesh, in_specs=in_specs, out_specs=table, check_vma=False
    )
```

```python
import math

import jax
import jax.numpy as jnp
from jax import lax
from jax.experimental import pallas as pl
from jax.experimental.pallas import tpu as pltpu
from jax.sharding import PartitionSpec as P

LINK = 6
LANES = 128
CORES = 2
FIELDS = 8
SIDE_ROWS = 16
VMEM_BYTES = 40 * 1024 * 1024
CODE_TOP = 32767
CODE_OCTAVES = 44
CODE_LOWEST = -26
CODE_SCALE = 2 * CODE_TOP / (CODE_OCTAVES * math.log(2.0))
CODE_FLOOR = 2.0 ** (2 * CODE_LOWEST)
CODE_ZERO = -CODE_TOP + 1 - CODE_LOWEST * math.log(2.0) * CODE_SCALE

SMALL = pl.CostEstimate(flops=1, bytes_accessed=1, transcendentals=0)
NT = (((1,), (1,)), ((), ()))
NN = (((1,), (0,)), ((), ()))


def iota(shape, axis):
    return lax.broadcasted_iota(jnp.int32, shape, axis)


def split(values):
    high = values.astype(jnp.bfloat16)
    return high, (values - high.astype(jnp.float32)).astype(jnp.bfloat16)


def one_hot(row, count):
    return (iota((count, row.shape[1]), 0) == row).astype(jnp.float32).astype(jnp.bfloat16)


def later_rows(values, hours):
    rows = values.shape[0]
    if hours % 8 == 0:
        padding = jnp.zeros((hours, values.shape[1]), values.dtype)
        return jnp.concatenate([padding, values[: rows - hours]], axis=0)
    return jnp.where(iota(values.shape, 0) < hours, 0.0, pltpu.roll(values, hours, 0))


def later_lanes(values, hours):
    return jnp.where(iota(values.shape, 1) < hours, 0.0, pltpu.roll(values, hours, 1))


def lane_rows(values):
    return [values[:, first : first + LANES] for first in range(0, values.shape[1], LANES)]


def parts_of(values):
    high = values.astype(jnp.bfloat16).astype(jnp.float32)
    middle = (values - high).astype(jnp.bfloat16).astype(jnp.float32)
    return [high, middle, values - high - middle]


def pack_kernel(*refs, basin_rows):
    sources, (meta_hbm, block_ref, *scratch, meta_ref, arrived) = refs[:9], refs[9:]
    tile_rows = block_ref.shape[0] - SIDE_ROWS
    targets = (*scratch, block_ref.at[pl.ds(0, tile_rows)])
    copies = [
        pltpu.make_async_copy(source, target, arrived.at[j])
        for j, (source, target) in enumerate(zip(sources, targets))
    ]
    for copy in copies:
        copy.start()
    for copy in copies[:4]:
        copy.wait()
    basin, kind, lag, parent = [ref[...] for ref in scratch[:4]]
    shift = basin_rows.bit_length() - 1
    empty = jnp.zeros((1, LANES - basin_rows), jnp.int32)
    rows = lane_rows(basin) + lane_rows(kind) + lane_rows(lag)
    rows.append(jnp.concatenate([lax.shift_right_arithmetic(parent, shift) + 1, empty], axis=1))
    rows.append(jnp.concatenate([parent & (basin_rows - 1), empty], axis=1))
    numbers = jnp.concatenate(rows, axis=0).astype(jnp.float32)
    meta_ref[...] = jnp.concatenate([numbers] * (meta_ref.shape[0] // FIELDS), axis=0).astype(jnp.bfloat16)
    leaving = pltpu.make_async_copy(meta_ref, meta_hbm, arrived.at[len(copies)])
    leaving.start()
    for copy in copies[4:8]:
        copy.wait()
    soil, area, dest, reach = [ref[...] for ref in scratch[4:]]
    sides = parts_of(soil) + parts_of(area) + [dest.astype(jnp.float32), reach.astype(jnp.float32)]
    sides = jnp.concatenate(sides + [jnp.zeros((SIDE_ROWS - len(sides), tile_rows), jnp.float32)], axis=0)
    block_ref[tile_rows:] = sides.astype(jnp.bfloat16)
    copies[8].wait()
    leaving.wait()


def prepare_kernel(
    irf_hbm, own_ref, other_ref, runoff_ref, dest_ref, reach_marks_ref, late_ref, responses_ref, irf_ref, arrived
):
    copy = pltpu.make_async_copy(irf_hbm, irf_ref, arrived.at[0])
    copy.start()
    hours = own_ref.shape[1]
    half = hours // 2
    tile_rows = own_ref.shape[0] - SIDE_ROWS
    kinds, taps = irf_ref.shape
    early = responses_ref.shape[0]
    sides = jnp.concatenate([own_ref[tile_rows:], other_ref[tile_rows:]], axis=1).astype(jnp.float32)
    rainfall = jnp.concatenate(
        [ref[:tile_rows].astype(jnp.float32).T for ref in (own_ref, other_ref)], axis=1
    )
    storage = sides[0:1] + sides[1:2] + sides[2:3]
    area = sides[3:4] + sides[4:5] + sides[5:6]
    excess = jnp.maximum(rainfall - 0.2 * storage, 0.0)
    runoff = (area * excess * excess / (rainfall + 0.8 * storage)).astype(jnp.bfloat16)
    runoff_ref[...] = runoff
    dest_ref[...] = jnp.broadcast_to(sides[6:7], dest_ref.shape).astype(jnp.int32)
    reach_marks_ref[...] = one_hot(sides[7:8].astype(jnp.int32), reach_marks_ref.shape[0])
    backward = (
        iota((taps, hours), 1) == lax.rem(hours - iota((taps, hours), 0), hours)
    ).astype(jnp.float32)
    copy.wait()
    reversed_taps = lax.dot_general(
        irf_ref[...], backward, NN, precision=lax.Precision.HIGHEST, preferred_element_type=jnp.float32
    )
    causal = iota((half, hours), 1) <= iota((half, hours), 0) + half
    for kind in range(kinds):
        row = jnp.broadcast_to(reversed_taps[kind : kind + 1], (half, hours))
        matrix = jnp.where(causal, pltpu.roll(row, half, 1, stride=1, stride_axis=0), 0.0)
        matrix = jnp.concatenate(split(matrix), axis=0)
        if kind < early:
            responses_ref[kind] = respond(matrix, runoff)
        else:
            late_ref[:, (kind - early) * hours : (kind - early + 1) * hours] = matrix


def respond(matrices, runoffs):
    hours = matrices.shape[0]
    half = hours // 2
    count = matrices.shape[1] // hours

    def halves(values, axis, first):
        pieces = [
            lax.slice_in_dim(values, j * hours + first, j * hours + first + half, axis=axis)
            for j in range(count)
        ]
        return jnp.concatenate(pieces, axis=axis)

    earlier = lax.dot_general(
        halves(matrices, 1, half), halves(runoffs, 0, 0), NN, preferred_element_type=jnp.float32
    )
    later = lax.dot_general(matrices, runoffs, NN, preferred_element_type=jnp.float32)
    return jnp.concatenate([earlier[:half] + earlier[half:], later[:half] + later[half:]], axis=0)


def route_kernel(
    meta_ref, runoff_ref, dest_ref, reach_marks_ref, late_ref, responses_ref, flow_ref, stack_ref, *, basin_rows
):
    early, hours, tiles = responses_ref.shape
    late = late_ref.shape[1] // hours
    outlets = flow_ref.shape[0]
    owners = meta_ref.shape[0] // FIELDS
    core = lax.rem(lax.axis_index("tile"), CORES)
    dest = dest_ref[0:1]

    stack_ref[: owners * FIELDS] = meta_ref[...].astype(jnp.float32)

    def table(field):
        return stack_ref[pl.ds(field, owners, stride=FIELDS), :].astype(jnp.bfloat16)

    def picked(values, owner):
        chosen = iota((owners, tiles), 0) == owner
        return jnp.sum(jnp.where(chosen, values, 0.0), axis=0, keepdims=True).astype(jnp.int32)

    spans = (FIELDS - 2) // 3
    reach_table = jnp.concatenate(
        [
            jnp.concatenate([table(item * spans + j) for j in range(spans)], axis=1)
            for item in range(3)
        ],
        axis=0,
    )
    by_reach = lax.dot_general(
        reach_table, reach_marks_ref[...], NN, preferred_element_type=jnp.float32
    )
    basin, kind, lag = [picked(by_reach[j * owners : (j + 1) * owners], dest) for j in range(3)]
    tree_table = jnp.concatenate([table(3 * spans), table(3 * spans + 1)], axis=0)[:, :basin_rows]

    def parent_of(owner, local):
        by_basin = lax.dot_general(
            tree_table, one_hot(local, basin_rows), NN, preferred_element_type=jnp.float32
        )
        return picked(by_basin[:owners], owner) - 1, picked(by_basin[owners:], owner)

    parent_owner, parent_local = parent_of(dest, basin)
    second_owner, second_local = parent_of(parent_owner, parent_local)

    def row_of(owner, local):
        mine = jnp.logical_and(owner >= 0, (owner & (CORES - 1)) == core)
        return jnp.where(mine, (owner // CORES) * basin_rows + local, -1)

    placements = jnp.concatenate(
        [
            one_hot(row_of(owner, local), outlets)
            for owner, local in (
                (dest, basin),
                (parent_owner, parent_local),
                (second_owner, second_local),
            )
        ],
        axis=0,
    )

    runoff = runoff_ref[...]
    by_kind = jnp.concatenate(
        [
            runoff * (kind == early + k).astype(jnp.float32).astype(jnp.bfloat16)
            for k in range(late)
        ],
        axis=0,
    )
    routed = respond(late_ref[...], by_kind)
    for k in range(early):
        routed = jnp.where(kind == k, responses_ref[k], routed)
    step = 64
    while step:
        routed = jnp.where((lag & step) != 0, later_rows(routed, step), routed)
        step //= 2
    flows = lax.dot_general(
        jnp.concatenate([placements, placements], axis=1),
        jnp.concatenate(split(routed), axis=1),
        NT,
        preferred_element_type=jnp.float32,
    )
    flow = later_lanes(flows[2 * outlets :], LINK)
    flow = later_lanes(flows[outlets : 2 * outlets] + flow, LINK)
    flow = flows[:outlets] + flow
    level = jnp.log(jnp.maximum(flow, CODE_FLOOR)) * CODE_SCALE + (CODE_ZERO + CODE_TOP + 0.5)
    level = jnp.clip(level, 0.0, 2.0 * CODE_TOP).astype(jnp.int32) - CODE_TOP
    flow_ref[...] = level.astype(jnp.int16)


def finish_kernel(parts_ref, section_ref):
    level = parts_ref[...].astype(jnp.int32)
    flow = jnp.exp((level.astype(jnp.float32) - CODE_ZERO) * (1.0 / CODE_SCALE))
    flow = jnp.sum(jnp.where(level == -CODE_TOP, 0.0, flow), axis=0)
    section_ref[...] = jnp.log(1.0 + flow)


def per_device(
    rain,
    soil,
    tile_area,
    tile_dest,
    tile_reach,
    reach_basin,
    reach_kind,
    reach_lag,
    irf,
    outlet_level,
    outlet_parent,
):
    owners = lax.axis_size("tile")
    tile_rows, hours = rain.shape
    basin_rows = outlet_parent.shape[0]
    kinds = irf.shape[0]
    params = pltpu.CompilerParams(vmem_limit_bytes=VMEM_BYTES)
    held = pl.BlockSpec(memory_space=pltpu.HBM)
    whole = pl.BlockSpec(memory_space=pltpu.VMEM)
    block = (tile_rows + SIDE_ROWS, hours)

    def in_hbm(values, shape):
        return pltpu.with_memory_space_constraint(values.reshape(shape), pltpu.HBM)

    numbers = [
        in_hbm(values, (1, -1))
        for values in (
            reach_basin, reach_kind, reach_lag, outlet_parent, soil, tile_area, tile_dest, tile_reach,
        )
    ]
    meta, own = pl.pallas_call(
        lambda *refs: pack_kernel(*refs, basin_rows=basin_rows),
        out_shape=(
            jax.ShapeDtypeStruct((owners * FIELDS, LANES), jnp.bfloat16),
            jax.ShapeDtypeStruct(block, jnp.bfloat16),
        ),
        in_specs=[held] * (len(numbers) + 1),
        out_specs=(held, whole),
        scratch_shapes=[pltpu.VMEM(values.shape, values.dtype) for values in numbers]
        + [
            pltpu.VMEM((owners * FIELDS, LANES), jnp.bfloat16),
            pltpu.SemaphoreType.DMA((len(numbers) + 2,)),
        ],
        compiler_params=params,
        cost_estimate=SMALL,
        name="pack",
    )(*numbers, in_hbm(rain, rain.shape))
    other = lax.ppermute(own, "tile", [(i, i ^ 1) for i in range(owners)])
    meta = lax.all_to_all(
        meta.reshape(owners, FIELDS, LANES), "tile", split_axis=0, concat_axis=0, tiled=True
    ).reshape(-1, LANES)

    chip_tiles = CORES * tile_rows
    early = kinds // 2
    prepared = pl.pallas_call(
        prepare_kernel,
        out_shape=(
            jax.ShapeDtypeStruct((hours, chip_tiles), jnp.bfloat16),
            jax.ShapeDtypeStruct((8, chip_tiles), jnp.int32),
            jax.ShapeDtypeStruct((reach_basin.size, chip_tiles), jnp.bfloat16),
            jax.ShapeDtypeStruct((hours, (kinds - early) * hours), jnp.bfloat16),
            jax.ShapeDtypeStruct((early, hours, chip_tiles), jnp.float32),
        ),
        in_specs=[held, whole, whole],
        scratch_shapes=[pltpu.VMEM(irf.shape, irf.dtype), pltpu.SemaphoreType.DMA((1,))],
        compiler_params=params,
        cost_estimate=SMALL,
        name="prepare",
    )(in_hbm(irf, irf.shape), own, other)

    flow = pl.pallas_call(
        lambda *refs: route_kernel(*refs, basin_rows=basin_rows),
        out_shape=jax.ShapeDtypeStruct((owners // CORES * basin_rows, hours), jnp.int16),
        scratch_shapes=[pltpu.VMEM(((owners + 1) * FIELDS, LANES), jnp.float32)],
        compiler_params=params,
        name="route",
    )(meta, *prepared)

    parts = lax.all_to_all(
        flow.reshape(owners // CORES, basin_rows, hours),
        "tile",
        split_axis=0,
        concat_axis=0,
        axis_index_groups=[list(range(core, owners, CORES)) for core in range(CORES)],
        tiled=True,
    )
    return pl.pallas_call(
        finish_kernel,
        out_shape=jax.ShapeDtypeStruct((basin_rows, hours), jnp.float32),
        compiler_params=params,
        name="finish",
    )(parts)


def solution(mesh):
    rows = P(("ens", "tile"))
    table = P(("ens", "tile"), None)
    in_specs = (table, rows, rows, table, rows, rows, rows, rows, P(), rows, rows)
    return jax.shard_map(
        per_device, mesh=mesh, in_specs=in_specs, out_specs=table, check_vma=False
    )
```

```python
import math

import jax
import jax.numpy as jnp
from jax import lax
from jax.experimental import pallas as pl
from jax.experimental.pallas import tpu as pltpu
from jax.sharding import PartitionSpec as P

LINK = 6
LANES = 128
CORES = 2
FIELDS = 8
SIDE_ROWS = 16
VMEM_BYTES = 40 * 1024 * 1024
CODE_TOP = 32767
CODE_OCTAVES = 44
CODE_LOWEST = -26
CODE_SCALE = 2 * CODE_TOP / (CODE_OCTAVES * math.log(2.0))
CODE_FLOOR = 2.0 ** (2 * CODE_LOWEST)
CODE_ZERO = -CODE_TOP + 1 - CODE_LOWEST * math.log(2.0) * CODE_SCALE

SMALL = pl.CostEstimate(flops=1, bytes_accessed=1, transcendentals=0)
NT = (((1,), (1,)), ((), ()))
NN = (((1,), (0,)), ((), ()))


def iota(shape, axis):
    return lax.broadcasted_iota(jnp.int32, shape, axis)


def split(values):
    high = values.astype(jnp.bfloat16)
    return high, (values - high.astype(jnp.float32)).astype(jnp.bfloat16)


def one_hot(row, count):
    return (iota((count, row.shape[1]), 0) == row).astype(jnp.float32).astype(jnp.bfloat16)


def later_rows(values, hours):
    padding = jnp.zeros((hours, values.shape[1]), values.dtype)
    return jnp.concatenate([padding, values[: values.shape[0] - hours]], axis=0)


def turned(values, hours):
    place = iota((8, values.shape[1]), 0)
    source = (place - hours) & 7
    stays = place >= hours
    before = jnp.zeros((8, values.shape[1]), values.dtype)
    rows = []
    for first in range(0, values.shape[0], 8):
        now = jnp.take_along_axis(values[first : first + 8], source, axis=0, mode="promise_in_bounds")
        rows.append(jnp.where(stays, now, before))
        before = now
    return jnp.concatenate(rows, axis=0)


def later_lanes(values, hours):
    return jnp.where(iota(values.shape, 1) < hours, 0.0, pltpu.roll(values, hours, 1))


def lane_rows(values):
    return [values[:, first : first + LANES] for first in range(0, values.shape[1], LANES)]


def parts_of(values):
    high = values.astype(jnp.bfloat16).astype(jnp.float32)
    middle = (values - high).astype(jnp.bfloat16).astype(jnp.float32)
    return [high, middle, values - high - middle]


def pack_kernel(*refs, basin_rows):
    sources, (meta_hbm, block_ref, *scratch, meta_ref, arrived) = refs[:9], refs[9:]
    tile_rows = block_ref.shape[0] - SIDE_ROWS
    targets = (*scratch, block_ref.at[pl.ds(0, tile_rows)])
    copies = [
        pltpu.make_async_copy(source, target, arrived.at[j])
        for j, (source, target) in enumerate(zip(sources, targets))
    ]
    for copy in copies:
        copy.start()
    for copy in copies[:4]:
        copy.wait()
    basin, kind, lag, parent = [ref[...] for ref in scratch[:4]]
    shift = basin_rows.bit_length() - 1
    empty = jnp.zeros((1, LANES - basin_rows), jnp.int32)
    rows = lane_rows(basin) + lane_rows(kind) + lane_rows(lag)
    rows.append(jnp.concatenate([lax.shift_right_arithmetic(parent, shift) + 1, empty], axis=1))
    rows.append(jnp.concatenate([parent & (basin_rows - 1), empty], axis=1))
    numbers = jnp.concatenate(rows, axis=0).astype(jnp.float32)
    meta_ref[...] = jnp.concatenate([numbers] * (meta_ref.shape[0] // FIELDS), axis=0).astype(jnp.bfloat16)
    leaving = pltpu.make_async_copy(meta_ref, meta_hbm, arrived.at[len(copies)])
    leaving.start()
    for copy in copies[4:8]:
        copy.wait()
    soil, area, dest, reach = [ref[...] for ref in scratch[4:]]
    sides = parts_of(soil) + parts_of(area) + [dest.astype(jnp.float32), reach.astype(jnp.float32)]
    sides = jnp.concatenate(sides + [jnp.zeros((SIDE_ROWS - len(sides), tile_rows), jnp.float32)], axis=0)
    block_ref[tile_rows:] = sides.astype(jnp.bfloat16)
    copies[8].wait()
    leaving.wait()


def prepare_kernel(
    irf_hbm, own_ref, other_ref, runoff_ref, dest_ref, reach_marks_ref, late_ref, responses_ref, irf_ref, arrived
):
    copy = pltpu.make_async_copy(irf_hbm, irf_ref, arrived.at[0])
    copy.start()
    hours = own_ref.shape[1]
    half = hours // 2
    tile_rows = own_ref.shape[0] - SIDE_ROWS
    kinds, taps = irf_ref.shape
    early = responses_ref.shape[0]
    sides = jnp.concatenate([own_ref[tile_rows:], other_ref[tile_rows:]], axis=1).astype(jnp.float32)
    rainfall = jnp.concatenate(
        [ref[:tile_rows].astype(jnp.float32).T for ref in (own_ref, other_ref)], axis=1
    )
    storage = sides[0:1] + sides[1:2] + sides[2:3]
    area = sides[3:4] + sides[4:5] + sides[5:6]
    excess = jnp.maximum(rainfall - 0.2 * storage, 0.0)
    runoff = (area * excess * excess / (rainfall + 0.8 * storage)).astype(jnp.bfloat16)
    runoff_ref[...] = runoff
    dest_ref[...] = jnp.broadcast_to(sides[6:7], dest_ref.shape).astype(jnp.int32)
    reach_marks_ref[...] = one_hot(sides[7:8].astype(jnp.int32), reach_marks_ref.shape[0])
    backward = (
        iota((taps, hours), 1) == lax.rem(hours - iota((taps, hours), 0), hours)
    ).astype(jnp.float32)
    copy.wait()
    reversed_taps = lax.dot_general(
        irf_ref[...], backward, NN, precision=lax.Precision.HIGHEST, preferred_element_type=jnp.float32
    )
    causal = iota((half, hours), 1) <= iota((half, hours), 0) + half
    for kind in range(kinds):
        row = jnp.broadcast_to(reversed_taps[kind : kind + 1], (half, hours))
        matrix = jnp.where(causal, pltpu.roll(row, half, 1, stride=1, stride_axis=0), 0.0)
        matrix = jnp.concatenate(split(matrix), axis=0)
        if kind < early:
            responses_ref[kind] = respond(matrix, runoff)
        else:
            late_ref[:, (kind - early) * hours : (kind - early + 1) * hours] = matrix


def respond(matrices, runoffs):
    hours = matrices.shape[0]
    half = hours // 2
    count = matrices.shape[1] // hours

    def halves(values, axis, first):
        pieces = [
            lax.slice_in_dim(values, j * hours + first, j * hours + first + half, axis=axis)
            for j in range(count)
        ]
        return jnp.concatenate(pieces, axis=axis)

    earlier = lax.dot_general(
        halves(matrices, 1, half), halves(runoffs, 0, 0), NN, preferred_element_type=jnp.float32
    )
    later = lax.dot_general(matrices, runoffs, NN, preferred_element_type=jnp.float32)
    return jnp.concatenate([earlier[:half] + earlier[half:], later[:half] + later[half:]], axis=0)


def route_kernel(
    meta_ref, runoff_ref, dest_ref, reach_marks_ref, late_ref, responses_ref, flow_ref, stack_ref, *, basin_rows
):
    early, hours, tiles = responses_ref.shape
    late = late_ref.shape[1] // hours
    outlets = flow_ref.shape[0]
    owners = meta_ref.shape[0] // FIELDS
    core = lax.rem(lax.axis_index("tile"), CORES)
    dest = dest_ref[0:1]

    stack_ref[: owners * FIELDS] = meta_ref[...].astype(jnp.float32)

    def table(field):
        return stack_ref[pl.ds(field, owners, stride=FIELDS), :].astype(jnp.bfloat16)

    def picked(values, owner):
        chosen = iota((owners, tiles), 0) == owner
        return jnp.sum(jnp.where(chosen, values, 0.0), axis=0, keepdims=True).astype(jnp.int32)

    spans = (FIELDS - 2) // 3
    reach_table = jnp.concatenate(
        [
            jnp.concatenate([table(item * spans + j) for j in range(spans)], axis=1)
            for item in range(3)
        ],
        axis=0,
    )
    by_reach = lax.dot_general(
        reach_table, reach_marks_ref[...], NN, preferred_element_type=jnp.float32
    )
    basin, kind, lag = [picked(by_reach[j * owners : (j + 1) * owners], dest) for j in range(3)]
    tree_table = jnp.concatenate([table(3 * spans), table(3 * spans + 1)], axis=0)[:, :basin_rows]

    def parent_of(owner, local):
        by_basin = lax.dot_general(
            tree_table, one_hot(local, basin_rows), NN, preferred_element_type=jnp.float32
        )
        return picked(by_basin[:owners], owner) - 1, picked(by_basin[owners:], owner)

    parent_owner, parent_local = parent_of(dest, basin)
    second_owner, second_local = parent_of(parent_owner, parent_local)

    def row_of(owner, local):
        mine = jnp.logical_and(owner >= 0, (owner & (CORES - 1)) == core)
        return jnp.where(mine, (owner // CORES) * basin_rows + local, -1)

    placements = jnp.concatenate(
        [
            one_hot(row_of(owner, local), outlets)
            for owner, local in (
                (dest, basin),
                (parent_owner, parent_local),
                (second_owner, second_local),
            )
        ],
        axis=0,
    )

    runoff = runoff_ref[...]
    by_kind = jnp.concatenate(
        [
            runoff * (kind == early + k).astype(jnp.float32).astype(jnp.bfloat16)
            for k in range(late)
        ],
        axis=0,
    )
    routed = respond(late_ref[...], by_kind)
    for k in range(early):
        routed = jnp.where(kind == k, responses_ref[k], routed)
    for step in (64, 32, 16, 8):
        routed = jnp.where((lag & step) != 0, later_rows(routed, step), routed)
    routed = turned(routed, lag & 7)
    flows = lax.dot_general(
        jnp.concatenate([placements, placements], axis=1),
        jnp.concatenate(split(routed), axis=1),
        NT,
        preferred_element_type=jnp.float32,
    )
    flow = later_lanes(flows[2 * outlets :], LINK)
    flow = later_lanes(flows[outlets : 2 * outlets] + flow, LINK)
    flow = flows[:outlets] + flow
    level = jnp.log(jnp.maximum(flow, CODE_FLOOR)) * CODE_SCALE + (CODE_ZERO + CODE_TOP + 0.5)
    level = jnp.clip(level, 0.0, 2.0 * CODE_TOP).astype(jnp.int32) - CODE_TOP
    flow_ref[...] = level.astype(jnp.int16)


def finish_kernel(parts_ref, section_ref):
    level = parts_ref[...].astype(jnp.int32)
    flow = jnp.exp((level.astype(jnp.float32) - CODE_ZERO) * (1.0 / CODE_SCALE))
    flow = jnp.sum(jnp.where(level == -CODE_TOP, 0.0, flow), axis=0)
    section_ref[...] = jnp.log(1.0 + flow)


def per_device(
    rain,
    soil,
    tile_area,
    tile_dest,
    tile_reach,
    reach_basin,
    reach_kind,
    reach_lag,
    irf,
    outlet_level,
    outlet_parent,
):
    owners = lax.axis_size("tile")
    tile_rows, hours = rain.shape
    basin_rows = outlet_parent.shape[0]
    kinds = irf.shape[0]
    params = pltpu.CompilerParams(vmem_limit_bytes=VMEM_BYTES)
    held = pl.BlockSpec(memory_space=pltpu.HBM)
    whole = pl.BlockSpec(memory_space=pltpu.VMEM)
    block = (tile_rows + SIDE_ROWS, hours)

    def in_hbm(values, shape):
        return pltpu.with_memory_space_constraint(values.reshape(shape), pltpu.HBM)

    numbers = [
        in_hbm(values, (1, -1))
        for values in (
            reach_basin, reach_kind, reach_lag, outlet_parent, soil, tile_area, tile_dest, tile_reach,
        )
    ]
    meta, own = pl.pallas_call(
        lambda *refs: pack_kernel(*refs, basin_rows=basin_rows),
        out_shape=(
            jax.ShapeDtypeStruct((owners * FIELDS, LANES), jnp.bfloat16),
            jax.ShapeDtypeStruct(block, jnp.bfloat16),
        ),
        in_specs=[held] * (len(numbers) + 1),
        out_specs=(held, whole),
        scratch_shapes=[pltpu.VMEM(values.shape, values.dtype) for values in numbers]
        + [
            pltpu.VMEM((owners * FIELDS, LANES), jnp.bfloat16),
            pltpu.SemaphoreType.DMA((len(numbers) + 2,)),
        ],
        compiler_params=params,
        cost_estimate=SMALL,
        name="pack",
    )(*numbers, in_hbm(rain, rain.shape))
    other = lax.ppermute(own, "tile", [(i, i ^ 1) for i in range(owners)])
    meta = lax.all_to_all(
        meta.reshape(owners, FIELDS, LANES), "tile", split_axis=0, concat_axis=0, tiled=True
    ).reshape(-1, LANES)

    chip_tiles = CORES * tile_rows
    early = kinds // 2
    prepared = pl.pallas_call(
        prepare_kernel,
        out_shape=(
            jax.ShapeDtypeStruct((hours, chip_tiles), jnp.bfloat16),
            jax.ShapeDtypeStruct((8, chip_tiles), jnp.int32),
            jax.ShapeDtypeStruct((reach_basin.size, chip_tiles), jnp.bfloat16),
            jax.ShapeDtypeStruct((hours, (kinds - early) * hours), jnp.bfloat16),
            jax.ShapeDtypeStruct((early, hours, chip_tiles), jnp.float32),
        ),
        in_specs=[held, whole, whole],
        scratch_shapes=[pltpu.VMEM(irf.shape, irf.dtype), pltpu.SemaphoreType.DMA((1,))],
        compiler_params=params,
        cost_estimate=SMALL,
        name="prepare",
    )(in_hbm(irf, irf.shape), own, other)

    flow = pl.pallas_call(
        lambda *refs: route_kernel(*refs, basin_rows=basin_rows),
        out_shape=jax.ShapeDtypeStruct((owners // CORES * basin_rows, hours), jnp.int16),
        scratch_shapes=[pltpu.VMEM(((owners + 1) * FIELDS, LANES), jnp.float32)],
        compiler_params=params,
        name="route",
    )(meta, *prepared)

    parts = lax.all_to_all(
        flow.reshape(owners // CORES, basin_rows, hours),
        "tile",
        split_axis=0,
        concat_axis=0,
        axis_index_groups=[list(range(core, owners, CORES)) for core in range(CORES)],
        tiled=True,
    )
    return pl.pallas_call(
        finish_kernel,
        out_shape=jax.ShapeDtypeStruct((basin_rows, hours), jnp.float32),
        compiler_params=params,
        name="finish",
    )(parts)


def solution(mesh):
    rows = P(("ens", "tile"))
    table = P(("ens", "tile"), None)
    in_specs = (table, rows, rows, table, rows, rows, rows, rows, P(), rows, rows)
    return jax.shard_map(
        per_device, mesh=mesh, in_specs=in_specs, out_specs=table, check_vma=False
    )
```

```python
import math

import jax
import jax.numpy as jnp
from jax import lax
from jax.experimental import pallas as pl
from jax.experimental.pallas import tpu as pltpu
from jax.sharding import PartitionSpec as P

LINK = 6
LANES = 128
CORES = 2
FIELDS = 8
SIDE_ROWS = 16
VMEM_BYTES = 40 * 1024 * 1024
CODE_TOP = 32767
CODE_OCTAVES = 44
CODE_LOWEST = -26
CODE_SCALE = 2 * CODE_TOP / (CODE_OCTAVES * math.log(2.0))
CODE_FLOOR = 2.0 ** (2 * CODE_LOWEST)
CODE_ZERO = -CODE_TOP + 1 - CODE_LOWEST * math.log(2.0) * CODE_SCALE

SMALL = pl.CostEstimate(flops=1, bytes_accessed=1, transcendentals=0)
NT = (((1,), (1,)), ((), ()))
NN = (((1,), (0,)), ((), ()))


def iota(shape, axis):
    return lax.broadcasted_iota(jnp.int32, shape, axis)


def split(values):
    high = values.astype(jnp.bfloat16)
    return high, (values - high.astype(jnp.float32)).astype(jnp.bfloat16)


def one_hot(row, count):
    return (iota((count, row.shape[1]), 0) == row).astype(jnp.float32).astype(jnp.bfloat16)


def later_rows(values, hours):
    padding = jnp.zeros((hours, values.shape[1]), values.dtype)
    return jnp.concatenate([padding, values[: values.shape[0] - hours]], axis=0)


def turned(values, hours):
    place = iota((8, values.shape[1]), 0)
    source = (place - hours) & 7
    stays = place >= hours
    before = jnp.zeros((8, values.shape[1]), values.dtype)
    rows = []
    for first in range(0, values.shape[0], 8):
        now = jnp.take_along_axis(values[first : first + 8], source, axis=0, mode="promise_in_bounds")
        rows.append(jnp.where(stays, now, before))
        before = now
    return jnp.concatenate(rows, axis=0)


def later_lanes(values, hours):
    return jnp.where(iota(values.shape, 1) < hours, 0.0, pltpu.roll(values, hours, 1))


def lane_rows(values):
    return [values[:, first : first + LANES] for first in range(0, values.shape[1], LANES)]


def parts_of(values):
    high = values.astype(jnp.bfloat16).astype(jnp.float32)
    middle = (values - high).astype(jnp.bfloat16).astype(jnp.float32)
    return [high, middle, values - high - middle]


def pack_kernel(*refs, basin_rows):
    sources, (meta_hbm, block_ref, *scratch, meta_ref, arrived) = refs[:9], refs[9:]
    tile_rows = block_ref.shape[0] - SIDE_ROWS
    targets = (*scratch, block_ref.at[pl.ds(0, tile_rows)])
    copies = [
        pltpu.make_async_copy(source, target, arrived.at[j])
        for j, (source, target) in enumerate(zip(sources, targets))
    ]
    for copy in copies:
        copy.start()
    for copy in copies[:4]:
        copy.wait()
    basin, kind, lag, parent = [ref[...] for ref in scratch[:4]]
    shift = basin_rows.bit_length() - 1
    empty = jnp.zeros((1, LANES - basin_rows), jnp.int32)
    rows = lane_rows(basin) + lane_rows(kind) + lane_rows(lag)
    rows.append(jnp.concatenate([lax.shift_right_arithmetic(parent, shift) + 1, empty], axis=1))
    rows.append(jnp.concatenate([parent & (basin_rows - 1), empty], axis=1))
    numbers = jnp.concatenate(rows, axis=0).astype(jnp.float32)
    meta_ref[...] = jnp.concatenate([numbers] * (meta_ref.shape[0] // FIELDS), axis=0).astype(jnp.bfloat16)
    leaving = pltpu.make_async_copy(meta_ref, meta_hbm, arrived.at[len(copies)])
    leaving.start()
    for copy in copies[4:8]:
        copy.wait()
    soil, area, dest, reach = [ref[...] for ref in scratch[4:]]
    sides = parts_of(soil) + parts_of(area) + [dest.astype(jnp.float32), reach.astype(jnp.float32)]
    sides = jnp.concatenate(sides + [jnp.zeros((SIDE_ROWS - len(sides), tile_rows), jnp.float32)], axis=0)
    block_ref[tile_rows:] = sides.astype(jnp.bfloat16)
    copies[8].wait()
    leaving.wait()


def prepare_kernel(
    irf_hbm, own_ref, other_ref, runoff_ref, dest_ref, reach_marks_ref, late_ref, responses_ref, irf_ref, arrived
):
    copy = pltpu.make_async_copy(irf_hbm, irf_ref, arrived.at[0])
    copy.start()
    hours = own_ref.shape[1]
    half = hours // 2
    tile_rows = own_ref.shape[0] - SIDE_ROWS
    kinds, taps = irf_ref.shape
    early = responses_ref.shape[0]
    sides = jnp.concatenate([own_ref[tile_rows:], other_ref[tile_rows:]], axis=1).astype(jnp.float32)
    rainfall = jnp.concatenate(
        [ref[:tile_rows].astype(jnp.float32).T for ref in (own_ref, other_ref)], axis=1
    )
    storage = sides[0:1] + sides[1:2] + sides[2:3]
    area = sides[3:4] + sides[4:5] + sides[5:6]
    excess = jnp.maximum(rainfall - 0.2 * storage, 0.0)
    runoff = (area * excess * excess / (rainfall + 0.8 * storage)).astype(jnp.bfloat16)
    runoff_ref[...] = runoff
    dest_ref[...] = jnp.broadcast_to(sides[6:7], dest_ref.shape).astype(jnp.int32)
    reach_marks_ref[...] = one_hot(sides[7:8].astype(jnp.int32), reach_marks_ref.shape[0])
    backward = (
        iota((taps, hours), 1) == lax.rem(hours - iota((taps, hours), 0), hours)
    ).astype(jnp.float32)
    copy.wait()
    reversed_taps = lax.dot_general(
        irf_ref[...], backward, NN, precision=lax.Precision.HIGHEST, preferred_element_type=jnp.float32
    )
    causal = iota((half, hours), 1) <= iota((half, hours), 0) + half
    for kind in range(kinds):
        row = jnp.broadcast_to(reversed_taps[kind : kind + 1], (half, hours))
        matrix = jnp.where(causal, pltpu.roll(row, half, 1, stride=1, stride_axis=0), 0.0)
        matrix = jnp.concatenate(split(matrix), axis=0)
        if kind < early:
            responses_ref[kind] = respond(matrix, runoff)
        else:
            late_ref[:, (kind - early) * hours : (kind - early + 1) * hours] = matrix


def respond(matrix, runoff):
    half = matrix.shape[0] // 2
    earlier = lax.dot_general(matrix[:, half:], runoff[:half], NN, preferred_element_type=jnp.float32)
    later = lax.dot_general(matrix, runoff, NN, preferred_element_type=jnp.float32)
    return jnp.concatenate([earlier[:half] + earlier[half:], later[:half] + later[half:]], axis=0)


def route_kernel(
    meta_ref, runoff_ref, dest_ref, reach_marks_ref, late_ref, responses_ref, flow_ref, stack_ref, *, basin_rows
):
    early, hours, tiles = responses_ref.shape
    outlets = flow_ref.shape[0]
    owners = meta_ref.shape[0] // FIELDS
    core = lax.rem(lax.axis_index("tile"), CORES)
    dest = dest_ref[0:1]

    runoff = runoff_ref[...]
    late_responses = [
        respond(late_ref[:, first : first + hours], runoff) for first in range(0, late_ref.shape[1], hours)
    ]
    stack_ref[: owners * FIELDS] = meta_ref[...].astype(jnp.float32)

    def table(field):
        return stack_ref[pl.ds(field, owners, stride=FIELDS), :].astype(jnp.bfloat16)

    def picked(values, owner):
        chosen = iota((owners, tiles), 0) == owner
        return jnp.sum(jnp.where(chosen, values, 0.0), axis=0, keepdims=True).astype(jnp.int32)

    spans = (FIELDS - 2) // 3
    reach_table = jnp.concatenate(
        [
            jnp.concatenate([table(item * spans + j) for j in range(spans)], axis=1)
            for item in range(3)
        ],
        axis=0,
    )
    by_reach = lax.dot_general(
        reach_table, reach_marks_ref[...], NN, preferred_element_type=jnp.float32
    )
    basin, kind, lag = [picked(by_reach[j * owners : (j + 1) * owners], dest) for j in range(3)]
    tree_table = jnp.concatenate([table(3 * spans), table(3 * spans + 1)], axis=0)[:, :basin_rows]

    def parent_of(owner, local):
        by_basin = lax.dot_general(
            tree_table, one_hot(local, basin_rows), NN, preferred_element_type=jnp.float32
        )
        return picked(by_basin[:owners], owner) - 1, picked(by_basin[owners:], owner)

    parent_owner, parent_local = parent_of(dest, basin)
    second_owner, second_local = parent_of(parent_owner, parent_local)

    def row_of(owner, local):
        mine = jnp.logical_and(owner >= 0, (owner & (CORES - 1)) == core)
        return jnp.where(mine, (owner // CORES) * basin_rows + local, -1)

    placements = jnp.concatenate(
        [
            one_hot(row_of(owner, local), outlets)
            for owner, local in (
                (dest, basin),
                (parent_owner, parent_local),
                (second_owner, second_local),
            )
        ],
        axis=0,
    )

    routed = responses_ref[0]
    for k in range(1, early):
        routed = jnp.where(kind == k, responses_ref[k], routed)
    for k, response in enumerate(late_responses, early):
        routed = jnp.where(kind == k, response, routed)
    for step in (64, 32, 16, 8):
        routed = jnp.where((lag & step) != 0, later_rows(routed, step), routed)
    routed = turned(routed, lag & 7)
    flows = lax.dot_general(
        jnp.concatenate([placements, placements], axis=1),
        jnp.concatenate(split(routed), axis=1),
        NT,
        preferred_element_type=jnp.float32,
    )
    flow = later_lanes(flows[2 * outlets :], LINK)
    flow = later_lanes(flows[outlets : 2 * outlets] + flow, LINK)
    flow = flows[:outlets] + flow
    level = jnp.log(jnp.maximum(flow, CODE_FLOOR)) * CODE_SCALE + (CODE_ZERO + CODE_TOP + 0.5)
    level = jnp.clip(level, 0.0, 2.0 * CODE_TOP).astype(jnp.int32) - CODE_TOP
    flow_ref[...] = level.astype(jnp.int16)


def finish_kernel(parts_ref, section_ref):
    level = parts_ref[...].astype(jnp.int32)
    flow = jnp.exp((level.astype(jnp.float32) - CODE_ZERO) * (1.0 / CODE_SCALE))
    flow = jnp.sum(jnp.where(level == -CODE_TOP, 0.0, flow), axis=0)
    section_ref[...] = jnp.log(1.0 + flow)


def per_device(
    rain,
    soil,
    tile_area,
    tile_dest,
    tile_reach,
    reach_basin,
    reach_kind,
    reach_lag,
    irf,
    outlet_level,
    outlet_parent,
):
    owners = lax.axis_size("tile")
    tile_rows, hours = rain.shape
    basin_rows = outlet_parent.shape[0]
    kinds = irf.shape[0]
    params = pltpu.CompilerParams(vmem_limit_bytes=VMEM_BYTES)
    held = pl.BlockSpec(memory_space=pltpu.HBM)
    whole = pl.BlockSpec(memory_space=pltpu.VMEM)
    block = (tile_rows + SIDE_ROWS, hours)

    def in_hbm(values, shape):
        return pltpu.with_memory_space_constraint(values.reshape(shape), pltpu.HBM)

    numbers = [
        in_hbm(values, (1, -1))
        for values in (
            reach_basin, reach_kind, reach_lag, outlet_parent, soil, tile_area, tile_dest, tile_reach,
        )
    ]
    meta, own = pl.pallas_call(
        lambda *refs: pack_kernel(*refs, basin_rows=basin_rows),
        out_shape=(
            jax.ShapeDtypeStruct((owners * FIELDS, LANES), jnp.bfloat16),
            jax.ShapeDtypeStruct(block, jnp.bfloat16),
        ),
        in_specs=[held] * (len(numbers) + 1),
        out_specs=(held, whole),
        scratch_shapes=[pltpu.VMEM(values.shape, values.dtype) for values in numbers]
        + [
            pltpu.VMEM((owners * FIELDS, LANES), jnp.bfloat16),
            pltpu.SemaphoreType.DMA((len(numbers) + 2,)),
        ],
        compiler_params=params,
        cost_estimate=SMALL,
        name="pack",
    )(*numbers, in_hbm(rain, rain.shape))
    other = lax.ppermute(own, "tile", [(i, i ^ 1) for i in range(owners)])
    meta = lax.all_to_all(
        meta.reshape(owners, FIELDS, LANES), "tile", split_axis=0, concat_axis=0, tiled=True
    ).reshape(-1, LANES)

    chip_tiles = CORES * tile_rows
    early = kinds // 2
    prepared = pl.pallas_call(
        prepare_kernel,
        out_shape=(
            jax.ShapeDtypeStruct((hours, chip_tiles), jnp.bfloat16),
            jax.ShapeDtypeStruct((8, chip_tiles), jnp.int32),
            jax.ShapeDtypeStruct((reach_basin.size, chip_tiles), jnp.bfloat16),
            jax.ShapeDtypeStruct((hours, (kinds - early) * hours), jnp.bfloat16),
            jax.ShapeDtypeStruct((early, hours, chip_tiles), jnp.float32),
        ),
        in_specs=[held, whole, whole],
        scratch_shapes=[pltpu.VMEM(irf.shape, irf.dtype), pltpu.SemaphoreType.DMA((1,))],
        compiler_params=params,
        cost_estimate=SMALL,
        name="prepare",
    )(in_hbm(irf, irf.shape), own, other)

    flow = pl.pallas_call(
        lambda *refs: route_kernel(*refs, basin_rows=basin_rows),
        out_shape=jax.ShapeDtypeStruct((owners // CORES * basin_rows, hours), jnp.int16),
        scratch_shapes=[pltpu.VMEM(((owners + 1) * FIELDS, LANES), jnp.float32)],
        compiler_params=params,
        name="route",
    )(meta, *prepared)

    parts = lax.all_to_all(
        flow.reshape(owners // CORES, basin_rows, hours),
        "tile",
        split_axis=0,
        concat_axis=0,
        axis_index_groups=[list(range(core, owners, CORES)) for core in range(CORES)],
        tiled=True,
    )
    return pl.pallas_call(
        finish_kernel,
        out_shape=jax.ShapeDtypeStruct((basin_rows, hours), jnp.float32),
        compiler_params=params,
        name="finish",
    )(parts)


def solution(mesh):
    rows = P(("ens", "tile"))
    table = P(("ens", "tile"), None)
    in_specs = (table, rows, rows, table, rows, rows, rows, rows, P(), rows, rows)
    return jax.shard_map(
        per_device, mesh=mesh, in_specs=in_specs, out_specs=table, check_vma=False
    )
```

```python
import math

import jax
import jax.numpy as jnp
from jax import lax
from jax.experimental import pallas as pl
from jax.experimental.pallas import tpu as pltpu
from jax.sharding import PartitionSpec as P

LINK = 6
LANES = 128
CORES = 2
FIELDS = 8
SIDE_ROWS = 16
VMEM_BYTES = 40 * 1024 * 1024
CODE_TOP = 32767
CODE_OCTAVES = 44
CODE_LOWEST = -26
CODE_SCALE = 2 * CODE_TOP / (CODE_OCTAVES * math.log(2.0))
CODE_FLOOR = 2.0 ** (2 * CODE_LOWEST)
CODE_ZERO = -CODE_TOP + 1 - CODE_LOWEST * math.log(2.0) * CODE_SCALE

SMALL = pl.CostEstimate(flops=1, bytes_accessed=1, transcendentals=0)
NT = (((1,), (1,)), ((), ()))
NN = (((1,), (0,)), ((), ()))


def iota(shape, axis):
    return lax.broadcasted_iota(jnp.int32, shape, axis)


def split(values):
    high = values.astype(jnp.bfloat16)
    return high, (values - high.astype(jnp.float32)).astype(jnp.bfloat16)


def one_hot(row, count):
    return (iota((count, row.shape[1]), 0) == row).astype(jnp.float32).astype(jnp.bfloat16)


def later_rows(values, hours):
    padding = jnp.zeros((hours, values.shape[1]), values.dtype)
    return jnp.concatenate([padding, values[: values.shape[0] - hours]], axis=0)


def turned(values, hours):
    place = iota((8, values.shape[1]), 0)
    source = (place - hours) & 7
    stays = place >= hours
    before = jnp.zeros((8, values.shape[1]), values.dtype)
    rows = []
    for first in range(0, values.shape[0], 8):
        now = jnp.take_along_axis(values[first : first + 8], source, axis=0, mode="promise_in_bounds")
        rows.append(jnp.where(stays, now, before))
        before = now
    return jnp.concatenate(rows, axis=0)


def later_lanes(values, hours):
    return jnp.where(iota(values.shape, 1) < hours, 0.0, pltpu.roll(values, hours, 1))


def lane_rows(values):
    return [values[:, first : first + LANES] for first in range(0, values.shape[1], LANES)]


def parts_of(values):
    high = values.astype(jnp.bfloat16).astype(jnp.float32)
    middle = (values - high).astype(jnp.bfloat16).astype(jnp.float32)
    return [high, middle, values - high - middle]


def pack_kernel(*refs, basin_rows):
    sources, (meta_hbm, block_ref, *scratch, meta_ref, arrived) = refs[:9], refs[9:]
    tile_rows = block_ref.shape[0] - SIDE_ROWS
    targets = (*scratch, block_ref.at[pl.ds(0, tile_rows)])
    copies = [
        pltpu.make_async_copy(source, target, arrived.at[j])
        for j, (source, target) in enumerate(zip(sources, targets))
    ]
    for copy in copies:
        copy.start()
    for copy in copies[:4]:
        copy.wait()
    basin, kind, lag, parent = [ref[...] for ref in scratch[:4]]
    shift = basin_rows.bit_length() - 1
    empty = jnp.zeros((1, LANES - basin_rows), jnp.int32)
    rows = lane_rows(basin) + lane_rows(kind) + lane_rows(lag)
    rows.append(jnp.concatenate([lax.shift_right_arithmetic(parent, shift) + 1, empty], axis=1))
    rows.append(jnp.concatenate([parent & (basin_rows - 1), empty], axis=1))
    numbers = jnp.concatenate(rows, axis=0).astype(jnp.float32)
    meta_ref[...] = jnp.concatenate([numbers] * (meta_ref.shape[0] // FIELDS), axis=0).astype(jnp.bfloat16)
    leaving = pltpu.make_async_copy(meta_ref, meta_hbm, arrived.at[len(copies)])
    leaving.start()
    for copy in copies[4:8]:
        copy.wait()
    soil, area, dest, reach = [ref[...] for ref in scratch[4:]]
    sides = parts_of(soil) + parts_of(area) + [dest.astype(jnp.float32), reach.astype(jnp.float32)]
    sides = jnp.concatenate(sides + [jnp.zeros((SIDE_ROWS - len(sides), tile_rows), jnp.float32)], axis=0)
    block_ref[tile_rows:] = sides.astype(jnp.bfloat16)
    copies[8].wait()
    leaving.wait()


def prepare_kernel(
    irf_hbm, own_ref, other_ref, runoff_ref, dest_ref, reach_marks_ref, late_ref, responses_ref, irf_ref, arrived
):
    copy = pltpu.make_async_copy(irf_hbm, irf_ref, arrived.at[0])
    copy.start()
    hours = own_ref.shape[1]
    half = hours // 2
    tile_rows = own_ref.shape[0] - SIDE_ROWS
    kinds, taps = irf_ref.shape
    early = responses_ref.shape[0]
    sides = jnp.concatenate([own_ref[tile_rows:], other_ref[tile_rows:]], axis=1).astype(jnp.float32)
    rainfall = jnp.concatenate(
        [ref[:tile_rows].astype(jnp.float32).T for ref in (own_ref, other_ref)], axis=1
    )
    storage = sides[0:1] + sides[1:2] + sides[2:3]
    area = sides[3:4] + sides[4:5] + sides[5:6]
    excess = jnp.maximum(rainfall - 0.2 * storage, 0.0)
    runoff = (area * excess * excess / (rainfall + 0.8 * storage)).astype(jnp.bfloat16)
    runoff_ref[...] = runoff
    dest_ref[...] = jnp.broadcast_to(sides[6:7], dest_ref.shape).astype(jnp.int32)
    reach_marks_ref[...] = one_hot(sides[7:8].astype(jnp.int32), reach_marks_ref.shape[0])
    backward = (
        iota((taps, hours), 1) == lax.rem(hours - iota((taps, hours), 0), hours)
    ).astype(jnp.float32)
    copy.wait()
    reversed_taps = lax.dot_general(
        irf_ref[...], backward, NN, precision=lax.Precision.HIGHEST, preferred_element_type=jnp.float32
    )
    causal = iota((half, hours), 1) <= iota((half, hours), 0) + half
    for kind in range(kinds):
        row = jnp.broadcast_to(reversed_taps[kind : kind + 1], (half, hours))
        matrix = jnp.where(causal, pltpu.roll(row, half, 1, stride=1, stride_axis=0), 0.0)
        matrix = jnp.concatenate(split(matrix), axis=0)
        if kind < early:
            responses_ref[kind] = respond(matrix, runoff)
        else:
            late_ref[:, (kind - early) * hours : (kind - early + 1) * hours] = matrix


def respond(matrices, runoffs):
    hours = matrices.shape[0]
    half = hours // 2
    count = matrices.shape[1] // hours

    def halves(values, axis, first):
        pieces = [
            lax.slice_in_dim(values, j * hours + first, j * hours + first + half, axis=axis)
            for j in range(count)
        ]
        return jnp.concatenate(pieces, axis=axis)

    earlier = lax.dot_general(
        halves(matrices, 1, half), halves(runoffs, 0, 0), NN, preferred_element_type=jnp.float32
    )
    later = lax.dot_general(matrices, runoffs, NN, preferred_element_type=jnp.float32)
    return jnp.concatenate([earlier[:half] + earlier[half:], later[:half] + later[half:]], axis=0)


def route_kernel(
    meta_ref, runoff_ref, dest_ref, reach_marks_ref, late_ref, responses_ref, flow_ref, stack_ref, *, basin_rows
):
    early, hours, tiles = responses_ref.shape
    late = late_ref.shape[1] // hours
    outlets = flow_ref.shape[0]
    owners = meta_ref.shape[0] // FIELDS
    core = lax.rem(lax.axis_index("tile"), CORES)
    dest = dest_ref[0:1]

    stack_ref[: owners * FIELDS] = meta_ref[...].astype(jnp.float32)

    def table(field):
        return stack_ref[pl.ds(field, owners, stride=FIELDS), :].astype(jnp.bfloat16)

    def picked(values, owner):
        chosen = iota((owners, tiles), 0) == owner
        return jnp.sum(jnp.where(chosen, values, 0.0), axis=0, keepdims=True).astype(jnp.int32)

    spans = (FIELDS - 2) // 3
    reach_table = jnp.concatenate(
        [
            jnp.concatenate([table(item * spans + j) for j in range(spans)], axis=1)
            for item in range(3)
        ],
        axis=0,
    )
    by_reach = lax.dot_general(
        reach_table, reach_marks_ref[...], NN, preferred_element_type=jnp.float32
    )
    basin, kind, lag = [picked(by_reach[j * owners : (j + 1) * owners], dest) for j in range(3)]
    tree_table = jnp.concatenate([table(3 * spans), table(3 * spans + 1)], axis=0)[:, :basin_rows]

    def parent_of(owner, local):
        by_basin = lax.dot_general(
            tree_table, one_hot(local, basin_rows), NN, preferred_element_type=jnp.float32
        )
        return picked(by_basin[:owners], owner) - 1, picked(by_basin[owners:], owner)

    parent_owner, parent_local = parent_of(dest, basin)
    second_owner, second_local = parent_of(parent_owner, parent_local)

    def row_of(owner, local):
        mine = jnp.logical_and(owner >= 0, (owner & (CORES - 1)) == core)
        return jnp.where(mine, (owner // CORES) * basin_rows + local, -1)

    placements = jnp.concatenate(
        [
            one_hot(row_of(owner, local), outlets)
            for owner, local in (
                (dest, basin),
                (parent_owner, parent_local),
                (second_owner, second_local),
            )
        ],
        axis=0,
    )

    runoff = runoff_ref[...]
    by_kind = jnp.concatenate(
        [
            runoff * (kind == early + k).astype(jnp.float32).astype(jnp.bfloat16)
            for k in range(late)
        ],
        axis=0,
    )
    routed = respond(late_ref[...], by_kind)
    highs, lows = [], []
    for first in range(0, tiles, LANES):
        lanes = slice(first, first + LANES)
        column = routed[:, lanes]
        for k in range(early):
            column = jnp.where(kind[:, lanes] == k, responses_ref[k, :, lanes], column)
        for step in (64, 32, 16, 8):
            column = jnp.where((lag[:, lanes] & step) != 0, later_rows(column, step), column)
        high, low = split(turned(column, lag[:, lanes] & 7))
        highs.append(high)
        lows.append(low)
    flows = lax.dot_general(
        jnp.concatenate([placements, placements], axis=1),
        jnp.concatenate(highs + lows, axis=1),
        NT,
        preferred_element_type=jnp.float32,
    )
    flow = later_lanes(flows[2 * outlets :], LINK)
    flow = later_lanes(flows[outlets : 2 * outlets] + flow, LINK)
    flow = flows[:outlets] + flow
    level = jnp.log(jnp.maximum(flow, CODE_FLOOR)) * CODE_SCALE + (CODE_ZERO + CODE_TOP + 0.5)
    level = jnp.clip(level, 0.0, 2.0 * CODE_TOP).astype(jnp.int32) - CODE_TOP
    flow_ref[...] = level.astype(jnp.int16)


def finish_kernel(parts_ref, section_ref):
    level = parts_ref[...].astype(jnp.int32)
    flow = jnp.exp((level.astype(jnp.float32) - CODE_ZERO) * (1.0 / CODE_SCALE))
    flow = jnp.sum(jnp.where(level == -CODE_TOP, 0.0, flow), axis=0)
    section_ref[...] = jnp.log(1.0 + flow)


def per_device(
    rain,
    soil,
    tile_area,
    tile_dest,
    tile_reach,
    reach_basin,
    reach_kind,
    reach_lag,
    irf,
    outlet_level,
    outlet_parent,
):
    owners = lax.axis_size("tile")
    tile_rows, hours = rain.shape
    basin_rows = outlet_parent.shape[0]
    kinds = irf.shape[0]
    params = pltpu.CompilerParams(vmem_limit_bytes=VMEM_BYTES)
    held = pl.BlockSpec(memory_space=pltpu.HBM)
    whole = pl.BlockSpec(memory_space=pltpu.VMEM)
    block = (tile_rows + SIDE_ROWS, hours)

    def in_hbm(values, shape):
        return pltpu.with_memory_space_constraint(values.reshape(shape), pltpu.HBM)

    numbers = [
        in_hbm(values, (1, -1))
        for values in (
            reach_basin, reach_kind, reach_lag, outlet_parent, soil, tile_area, tile_dest, tile_reach,
        )
    ]
    meta, own = pl.pallas_call(
        lambda *refs: pack_kernel(*refs, basin_rows=basin_rows),
        out_shape=(
            jax.ShapeDtypeStruct((owners * FIELDS, LANES), jnp.bfloat16),
            jax.ShapeDtypeStruct(block, jnp.bfloat16),
        ),
        in_specs=[held] * (len(numbers) + 1),
        out_specs=(held, whole),
        scratch_shapes=[pltpu.VMEM(values.shape, values.dtype) for values in numbers]
        + [
            pltpu.VMEM((owners * FIELDS, LANES), jnp.bfloat16),
            pltpu.SemaphoreType.DMA((len(numbers) + 2,)),
        ],
        compiler_params=params,
        cost_estimate=SMALL,
        name="pack",
    )(*numbers, in_hbm(rain, rain.shape))
    other = lax.ppermute(own, "tile", [(i, i ^ 1) for i in range(owners)])
    meta = lax.all_to_all(
        meta.reshape(owners, FIELDS, LANES), "tile", split_axis=0, concat_axis=0, tiled=True
    ).reshape(-1, LANES)

    chip_tiles = CORES * tile_rows
    early = kinds // 2
    prepared = pl.pallas_call(
        prepare_kernel,
        out_shape=(
            jax.ShapeDtypeStruct((hours, chip_tiles), jnp.bfloat16),
            jax.ShapeDtypeStruct((8, chip_tiles), jnp.int32),
            jax.ShapeDtypeStruct((reach_basin.size, chip_tiles), jnp.bfloat16),
            jax.ShapeDtypeStruct((hours, (kinds - early) * hours), jnp.bfloat16),
            jax.ShapeDtypeStruct((early, hours, chip_tiles), jnp.float32),
        ),
        in_specs=[held, whole, whole],
        scratch_shapes=[pltpu.VMEM(irf.shape, irf.dtype), pltpu.SemaphoreType.DMA((1,))],
        compiler_params=params,
        cost_estimate=SMALL,
        name="prepare",
    )(in_hbm(irf, irf.shape), own, other)

    flow = pl.pallas_call(
        lambda *refs: route_kernel(*refs, basin_rows=basin_rows),
        out_shape=jax.ShapeDtypeStruct((owners // CORES * basin_rows, hours), jnp.int16),
        scratch_shapes=[pltpu.VMEM(((owners + 1) * FIELDS, LANES), jnp.float32)],
        compiler_params=params,
        name="route",
    )(meta, *prepared)

    parts = lax.all_to_all(
        flow.reshape(owners // CORES, basin_rows, hours),
        "tile",
        split_axis=0,
        concat_axis=0,
        axis_index_groups=[list(range(core, owners, CORES)) for core in range(CORES)],
        tiled=True,
    )
    return pl.pallas_call(
        finish_kernel,
        out_shape=jax.ShapeDtypeStruct((basin_rows, hours), jnp.float32),
        compiler_params=params,
        name="finish",
    )(parts)


def solution(mesh):
    rows = P(("ens", "tile"))
    table = P(("ens", "tile"), None)
    in_specs = (table, rows, rows, table, rows, rows, rows, rows, P(), rows, rows)
    return jax.shard_map(
        per_device, mesh=mesh, in_specs=in_specs, out_specs=table, check_vma=False
    )
```

```python
import math

import jax
import jax.numpy as jnp
from jax import lax
from jax.experimental import pallas as pl
from jax.experimental.pallas import tpu as pltpu
from jax.sharding import PartitionSpec as P

LINK = 6
LANES = 128
CORES = 2
FIELDS = 8
SIDE_ROWS = 16
VMEM_BYTES = 40 * 1024 * 1024
CODE_TOP = 32767
CODE_OCTAVES = 44
CODE_LOWEST = -26
CODE_SCALE = 2 * CODE_TOP / (CODE_OCTAVES * math.log(2.0))
CODE_FLOOR = 2.0 ** (2 * CODE_LOWEST)
CODE_ZERO = -CODE_TOP + 1 - CODE_LOWEST * math.log(2.0) * CODE_SCALE

SMALL = pl.CostEstimate(flops=1, bytes_accessed=1, transcendentals=0)
NT = (((1,), (1,)), ((), ()))
NN = (((1,), (0,)), ((), ()))


def iota(shape, axis):
    return lax.broadcasted_iota(jnp.int32, shape, axis)


def split(values):
    high = values.astype(jnp.bfloat16)
    return high, (values - high.astype(jnp.float32)).astype(jnp.bfloat16)


def one_hot(row, count):
    return (iota((count, row.shape[1]), 0) == row).astype(jnp.float32).astype(jnp.bfloat16)


def later_rows(values, hours):
    padding = jnp.zeros((hours, values.shape[1]), values.dtype)
    return jnp.concatenate([padding, values[: values.shape[0] - hours]], axis=0)


def turned(values, hours):
    place = iota((8, values.shape[1]), 0)
    source = (place - hours) & 7
    stays = place >= hours
    before = jnp.zeros((8, values.shape[1]), values.dtype)
    rows = []
    for first in range(0, values.shape[0], 8):
        now = jnp.take_along_axis(values[first : first + 8], source, axis=0, mode="promise_in_bounds")
        rows.append(jnp.where(stays, now, before))
        before = now
    return jnp.concatenate(rows, axis=0)


def later_lanes(values, hours):
    return jnp.where(iota(values.shape, 1) < hours, 0.0, pltpu.roll(values, hours, 1))


def lane_rows(values):
    return [values[:, first : first + LANES] for first in range(0, values.shape[1], LANES)]


def parts_of(values):
    high = values.astype(jnp.bfloat16).astype(jnp.float32)
    middle = (values - high).astype(jnp.bfloat16).astype(jnp.float32)
    return [high, middle, values - high - middle]


def pack_kernel(*refs, basin_rows):
    sources, (meta_hbm, block_ref, *scratch, meta_ref, arrived) = refs[:9], refs[9:]
    tile_rows = block_ref.shape[0] - SIDE_ROWS
    targets = (*scratch, block_ref.at[pl.ds(0, tile_rows)])
    copies = [
        pltpu.make_async_copy(source, target, arrived.at[j])
        for j, (source, target) in enumerate(zip(sources, targets))
    ]
    for copy in copies:
        copy.start()
    for copy in copies[:4]:
        copy.wait()
    basin, kind, lag, parent = [ref[...] for ref in scratch[:4]]
    shift = basin_rows.bit_length() - 1
    empty = jnp.zeros((1, LANES - basin_rows), jnp.int32)
    rows = lane_rows(basin) + lane_rows(kind) + lane_rows(lag)
    rows.append(jnp.concatenate([lax.shift_right_arithmetic(parent, shift) + 1, empty], axis=1))
    rows.append(jnp.concatenate([parent & (basin_rows - 1), empty], axis=1))
    numbers = jnp.concatenate(rows, axis=0).astype(jnp.float32)
    meta_ref[...] = jnp.concatenate([numbers] * (meta_ref.shape[0] // FIELDS), axis=0).astype(jnp.bfloat16)
    leaving = pltpu.make_async_copy(meta_ref, meta_hbm, arrived.at[len(copies)])
    leaving.start()
    for copy in copies[4:8]:
        copy.wait()
    soil, area, dest, reach = [ref[...] for ref in scratch[4:]]
    sides = parts_of(soil) + parts_of(area) + [dest.astype(jnp.float32), reach.astype(jnp.float32)]
    sides = jnp.concatenate(sides + [jnp.zeros((SIDE_ROWS - len(sides), tile_rows), jnp.float32)], axis=0)
    block_ref[tile_rows:] = sides.astype(jnp.bfloat16)
    copies[8].wait()
    leaving.wait()


def prepare_kernel(
    irf_hbm, own_ref, other_ref, runoff_ref, dest_ref, reach_marks_ref, late_ref, responses_ref, irf_ref, arrived
):
    copy = pltpu.make_async_copy(irf_hbm, irf_ref, arrived.at[0])
    copy.start()
    hours = own_ref.shape[1]
    half = hours // 2
    tile_rows = own_ref.shape[0] - SIDE_ROWS
    kinds, taps = irf_ref.shape
    early = responses_ref.shape[0]
    sides = jnp.concatenate([own_ref[tile_rows:], other_ref[tile_rows:]], axis=1).astype(jnp.float32)
    rainfall = jnp.concatenate(
        [ref[:tile_rows].astype(jnp.float32).T for ref in (own_ref, other_ref)], axis=1
    )
    storage = sides[0:1] + sides[1:2] + sides[2:3]
    area = sides[3:4] + sides[4:5] + sides[5:6]
    excess = jnp.maximum(rainfall - 0.2 * storage, 0.0)
    runoff = (area * excess * excess / (rainfall + 0.8 * storage)).astype(jnp.bfloat16)
    runoff_ref[...] = runoff
    dest_ref[...] = jnp.broadcast_to(sides[6:7], dest_ref.shape).astype(jnp.int32)
    reach_marks_ref[...] = one_hot(sides[7:8].astype(jnp.int32), reach_marks_ref.shape[0])
    backward = (
        iota((taps, hours), 1) == lax.rem(hours - iota((taps, hours), 0), hours)
    ).astype(jnp.float32)
    copy.wait()
    reversed_taps = lax.dot_general(
        irf_ref[...], backward, NN, precision=lax.Precision.HIGHEST, preferred_element_type=jnp.float32
    )
    causal = iota((half, hours), 1) <= iota((half, hours), 0) + half
    for kind in range(kinds):
        row = jnp.broadcast_to(reversed_taps[kind : kind + 1], (half, hours))
        matrix = jnp.where(causal, pltpu.roll(row, half, 1, stride=1, stride_axis=0), 0.0)
        matrix = jnp.concatenate(split(matrix), axis=0)
        if kind < early:
            responses_ref[kind] = respond(matrix, runoff)
        else:
            late_ref[:, (kind - early) * hours : (kind - early + 1) * hours] = matrix


def respond(matrices, runoffs):
    hours = matrices.shape[0]
    half = hours // 2
    count = matrices.shape[1] // hours

    def halves(values, axis, first):
        pieces = [
            lax.slice_in_dim(values, j * hours + first, j * hours + first + half, axis=axis)
            for j in range(count)
        ]
        return jnp.concatenate(pieces, axis=axis)

    earlier = lax.dot_general(
        halves(matrices, 1, half), halves(runoffs, 0, 0), NN, preferred_element_type=jnp.float32
    )
    later = lax.dot_general(matrices, runoffs, NN, preferred_element_type=jnp.float32)
    return jnp.concatenate([earlier[:half] + earlier[half:], later[:half] + later[half:]], axis=0)


def route_kernel(
    meta_ref, runoff_ref, dest_ref, reach_marks_ref, late_ref, responses_ref, flow_ref, stack_ref, *, basin_rows
):
    early, hours, tiles = responses_ref.shape
    late = late_ref.shape[1] // hours
    outlets = flow_ref.shape[0]
    owners = meta_ref.shape[0] // FIELDS
    core = lax.rem(lax.axis_index("tile"), CORES)
    dest = dest_ref[0:1]

    stack_ref[: owners * FIELDS] = meta_ref[...].astype(jnp.float32)

    def table(field):
        return stack_ref[pl.ds(field, owners, stride=FIELDS), :].astype(jnp.bfloat16)

    def picked(values, owner):
        chosen = iota((owners, tiles), 0) == owner
        return jnp.sum(jnp.where(chosen, values, 0.0), axis=0, keepdims=True).astype(jnp.int32)

    spans = (FIELDS - 2) // 3
    reach_table = jnp.concatenate(
        [
            jnp.concatenate([table(item * spans + j) for j in range(spans)], axis=1)
            for item in range(3)
        ],
        axis=0,
    )
    by_reach = lax.dot_general(
        reach_table, reach_marks_ref[...], NN, preferred_element_type=jnp.float32
    )
    basin, kind, lag = [picked(by_reach[j * owners : (j + 1) * owners], dest) for j in range(3)]
    tree_table = jnp.concatenate([table(3 * spans), table(3 * spans + 1)], axis=0)[:, :basin_rows]

    def parent_of(owner, local):
        by_basin = lax.dot_general(
            tree_table, one_hot(local, basin_rows), NN, preferred_element_type=jnp.float32
        )
        return picked(by_basin[:owners], owner) - 1, picked(by_basin[owners:], owner)

    parent_owner, parent_local = parent_of(dest, basin)
    second_owner, second_local = parent_of(parent_owner, parent_local)

    def row_of(owner, local):
        mine = jnp.logical_and(owner >= 0, (owner & (CORES - 1)) == core)
        return jnp.where(mine, (owners // CORES - 1 - owner // CORES) * basin_rows + local, -1)

    placements = jnp.concatenate(
        [
            one_hot(row_of(owner, local), outlets)
            for owner, local in (
                (dest, basin),
                (parent_owner, parent_local),
                (second_owner, second_local),
            )
        ],
        axis=0,
    )

    runoff = runoff_ref[...]
    by_kind = jnp.concatenate(
        [
            runoff * (kind == early + k).astype(jnp.float32).astype(jnp.bfloat16)
            for k in range(late)
        ],
        axis=0,
    )
    routed = respond(late_ref[...], by_kind)
    for k in range(early):
        routed = jnp.where(kind == k, responses_ref[k], routed)
    for step in (64, 32, 16, 8):
        routed = jnp.where((lag & step) != 0, later_rows(routed, step), routed)
    routed = turned(routed, lag & 7)
    flows = lax.dot_general(
        jnp.concatenate([placements, placements], axis=1),
        jnp.concatenate(split(routed), axis=1),
        NT,
        preferred_element_type=jnp.float32,
    )
    flow = later_lanes(flows[2 * outlets :], LINK)
    flow = later_lanes(flows[outlets : 2 * outlets] + flow, LINK)
    flow = flows[:outlets] + flow
    level = jnp.log(jnp.maximum(flow, CODE_FLOOR)) * CODE_SCALE + (CODE_ZERO + CODE_TOP + 0.5)
    level = jnp.clip(level, 0.0, 2.0 * CODE_TOP).astype(jnp.int32) - CODE_TOP
    flow_ref[...] = level.astype(jnp.int16)


def finish_kernel(parts_ref, section_ref):
    level = parts_ref[...].astype(jnp.int32)
    flow = jnp.exp((level.astype(jnp.float32) - CODE_ZERO) * (1.0 / CODE_SCALE))
    flow = jnp.sum(jnp.where(level == -CODE_TOP, 0.0, flow), axis=0)
    section_ref[...] = jnp.log(1.0 + flow)


def per_device(
    rain,
    soil,
    tile_area,
    tile_dest,
    tile_reach,
    reach_basin,
    reach_kind,
    reach_lag,
    irf,
    outlet_level,
    outlet_parent,
):
    owners = lax.axis_size("tile")
    tile_rows, hours = rain.shape
    basin_rows = outlet_parent.shape[0]
    kinds = irf.shape[0]
    params = pltpu.CompilerParams(vmem_limit_bytes=VMEM_BYTES)
    held = pl.BlockSpec(memory_space=pltpu.HBM)
    whole = pl.BlockSpec(memory_space=pltpu.VMEM)
    block = (tile_rows + SIDE_ROWS, hours)

    def in_hbm(values, shape):
        return pltpu.with_memory_space_constraint(values.reshape(shape), pltpu.HBM)

    numbers = [
        in_hbm(values, (1, -1))
        for values in (
            reach_basin, reach_kind, reach_lag, outlet_parent, soil, tile_area, tile_dest, tile_reach,
        )
    ]
    meta, own = pl.pallas_call(
        lambda *refs: pack_kernel(*refs, basin_rows=basin_rows),
        out_shape=(
            jax.ShapeDtypeStruct((owners * FIELDS, LANES), jnp.bfloat16),
            jax.ShapeDtypeStruct(block, jnp.bfloat16),
        ),
        in_specs=[held] * (len(numbers) + 1),
        out_specs=(held, whole),
        scratch_shapes=[pltpu.VMEM(values.shape, values.dtype) for values in numbers]
        + [
            pltpu.VMEM((owners * FIELDS, LANES), jnp.bfloat16),
            pltpu.SemaphoreType.DMA((len(numbers) + 2,)),
        ],
        compiler_params=params,
        cost_estimate=SMALL,
        name="pack",
    )(*numbers, in_hbm(rain, rain.shape))
    other = lax.ppermute(own, "tile", [(i, i ^ 1) for i in range(owners)])
    meta = lax.all_to_all(
        meta.reshape(owners, FIELDS, LANES), "tile", split_axis=0, concat_axis=0, tiled=True
    ).reshape(-1, LANES)

    chip_tiles = CORES * tile_rows
    early = kinds // 2
    prepared = pl.pallas_call(
        prepare_kernel,
        out_shape=(
            jax.ShapeDtypeStruct((hours, chip_tiles), jnp.bfloat16),
            jax.ShapeDtypeStruct((8, chip_tiles), jnp.int32),
            jax.ShapeDtypeStruct((reach_basin.size, chip_tiles), jnp.bfloat16),
            jax.ShapeDtypeStruct((hours, (kinds - early) * hours), jnp.bfloat16),
            jax.ShapeDtypeStruct((early, hours, chip_tiles), jnp.float32),
        ),
        in_specs=[held, whole, whole],
        scratch_shapes=[pltpu.VMEM(irf.shape, irf.dtype), pltpu.SemaphoreType.DMA((1,))],
        compiler_params=params,
        cost_estimate=SMALL,
        name="prepare",
    )(in_hbm(irf, irf.shape), own, other)

    flow = pl.pallas_call(
        lambda *refs: route_kernel(*refs, basin_rows=basin_rows),
        out_shape=jax.ShapeDtypeStruct((owners // CORES * basin_rows, hours), jnp.int16),
        scratch_shapes=[pltpu.VMEM(((owners + 1) * FIELDS, LANES), jnp.float32)],
        compiler_params=params,
        name="route",
    )(meta, *prepared)

    parts = lax.all_to_all(
        flow.reshape(owners // CORES, basin_rows, hours),
        "tile",
        split_axis=0,
        concat_axis=0,
        axis_index_groups=[list(range(core, owners, CORES))[::-1] for core in range(CORES)],
        tiled=True,
    )
    return pl.pallas_call(
        finish_kernel,
        out_shape=jax.ShapeDtypeStruct((basin_rows, hours), jnp.float32),
        compiler_params=params,
        name="finish",
    )(parts)


def solution(mesh):
    rows = P(("ens", "tile"))
    table = P(("ens", "tile"), None)
    in_specs = (table, rows, rows, table, rows, rows, rows, rows, P(), rows, rows)
    return jax.shard_map(
        per_device, mesh=mesh, in_specs=in_specs, out_specs=table, check_vma=False
    )
```

```python
import math

import jax
import jax.numpy as jnp
from jax import lax
from jax.experimental import pallas as pl
from jax.experimental.pallas import tpu as pltpu
from jax.sharding import PartitionSpec as P

LINK = 6
LANES = 128
CORES = 2
FIELDS = 8
SIDE_ROWS = 16
VMEM_BYTES = 40 * 1024 * 1024
CODE_TOP = 32767
CODE_OCTAVES = 44
CODE_LOWEST = -26
CODE_SCALE = 2 * CODE_TOP / (CODE_OCTAVES * math.log(2.0))
CODE_FLOOR = 2.0 ** (2 * CODE_LOWEST)
CODE_ZERO = -CODE_TOP + 1 - CODE_LOWEST * math.log(2.0) * CODE_SCALE

SMALL = pl.CostEstimate(flops=1, bytes_accessed=1, transcendentals=0)
NT = (((1,), (1,)), ((), ()))
NN = (((1,), (0,)), ((), ()))


def iota(shape, axis):
    return lax.broadcasted_iota(jnp.int32, shape, axis)


def split(values):
    high = values.astype(jnp.bfloat16)
    return high, (values - high.astype(jnp.float32)).astype(jnp.bfloat16)


def one_hot(row, count):
    return (iota((count, row.shape[1]), 0) == row).astype(jnp.float32).astype(jnp.bfloat16)


def later_rows(values, hours):
    padding = jnp.zeros((hours, values.shape[1]), values.dtype)
    return jnp.concatenate([padding, values[: values.shape[0] - hours]], axis=0)


def turned(values, hours):
    place = iota((8, values.shape[1]), 0)
    source = (place - hours) & 7
    stays = place >= hours
    before = jnp.zeros((8, values.shape[1]), values.dtype)
    rows = []
    for first in range(0, values.shape[0], 8):
        now = jnp.take_along_axis(values[first : first + 8], source, axis=0, mode="promise_in_bounds")
        rows.append(jnp.where(stays, now, before))
        before = now
    return jnp.concatenate(rows, axis=0)


def later_lanes(values, hours):
    return jnp.where(iota(values.shape, 1) < hours, 0.0, pltpu.roll(values, hours, 1))


def lane_rows(values):
    return [values[:, first : first + LANES] for first in range(0, values.shape[1], LANES)]


def parts_of(values):
    high = values.astype(jnp.bfloat16).astype(jnp.float32)
    middle = (values - high).astype(jnp.bfloat16).astype(jnp.float32)
    return [high, middle, values - high - middle]


def pack_kernel(*refs, basin_rows):
    sources, (meta_hbm, block_ref, *scratch, meta_ref, arrived) = refs[:9], refs[9:]
    tile_rows = block_ref.shape[0] - SIDE_ROWS
    targets = (*scratch, block_ref.at[pl.ds(0, tile_rows)])
    copies = [
        pltpu.make_async_copy(source, target, arrived.at[j])
        for j, (source, target) in enumerate(zip(sources, targets))
    ]
    for copy in copies:
        copy.start()
    for copy in copies[:4]:
        copy.wait()
    basin, kind, lag, parent = [ref[...] for ref in scratch[:4]]
    shift = basin_rows.bit_length() - 1
    empty = jnp.zeros((1, LANES - basin_rows), jnp.int32)
    rows = lane_rows(basin) + lane_rows(kind) + lane_rows(lag)
    rows.append(jnp.concatenate([lax.shift_right_arithmetic(parent, shift) + 1, empty], axis=1))
    rows.append(jnp.concatenate([parent & (basin_rows - 1), empty], axis=1))
    numbers = jnp.concatenate(rows, axis=0).astype(jnp.float32)
    meta_ref[...] = jnp.concatenate([numbers] * (meta_ref.shape[0] // FIELDS), axis=0).astype(jnp.bfloat16)
    leaving = pltpu.make_async_copy(meta_ref, meta_hbm, arrived.at[len(copies)])
    leaving.start()
    for copy in copies[4:8]:
        copy.wait()
    soil, area, dest, reach = [ref[...] for ref in scratch[4:]]
    sides = parts_of(soil) + parts_of(area) + [dest.astype(jnp.float32), reach.astype(jnp.float32)]
    sides = jnp.concatenate(sides + [jnp.zeros((SIDE_ROWS - len(sides), tile_rows), jnp.float32)], axis=0)
    block_ref[tile_rows:] = sides.astype(jnp.bfloat16)
    copies[8].wait()
    leaving.wait()


def prepare_kernel(
    irf_hbm, own_ref, other_ref, runoff_ref, dest_ref, reach_marks_ref, late_ref, responses_ref, irf_ref, arrived
):
    copy = pltpu.make_async_copy(irf_hbm, irf_ref, arrived.at[0])
    copy.start()
    hours = own_ref.shape[1]
    half = hours // 2
    tile_rows = own_ref.shape[0] - SIDE_ROWS
    kinds, taps = irf_ref.shape
    early = responses_ref.shape[0]
    sides = jnp.concatenate([own_ref[tile_rows:], other_ref[tile_rows:]], axis=1).astype(jnp.float32)
    rainfall = jnp.concatenate(
        [ref[:tile_rows].astype(jnp.float32).T for ref in (own_ref, other_ref)], axis=1
    )
    storage = sides[0:1] + sides[1:2] + sides[2:3]
    area = sides[3:4] + sides[4:5] + sides[5:6]
    excess = jnp.maximum(rainfall - 0.2 * storage, 0.0)
    runoff = (area * excess * excess / (rainfall + 0.8 * storage)).astype(jnp.bfloat16)
    runoff_ref[...] = runoff
    dest_ref[...] = jnp.broadcast_to(sides[6:7], dest_ref.shape).astype(jnp.int32)
    reach_marks_ref[...] = one_hot(sides[7:8].astype(jnp.int32), reach_marks_ref.shape[0])
    backward = (
        iota((taps, hours), 1) == lax.rem(hours - iota((taps, hours), 0), hours)
    ).astype(jnp.float32)
    copy.wait()
    reversed_taps = lax.dot_general(
        irf_ref[...], backward, NN, precision=lax.Precision.HIGHEST, preferred_element_type=jnp.float32
    )
    causal = iota((half, hours), 1) <= iota((half, hours), 0) + half
    for kind in range(kinds):
        row = jnp.broadcast_to(reversed_taps[kind : kind + 1], (half, hours))
        matrix = jnp.where(causal, pltpu.roll(row, half, 1, stride=1, stride_axis=0), 0.0)
        matrix = jnp.concatenate(split(matrix), axis=0)
        if kind < early:
            responses_ref[kind] = respond(matrix, runoff)
        else:
            late_ref[:, (kind - early) * hours : (kind - early + 1) * hours] = matrix


def respond(matrices, runoffs):
    hours = matrices.shape[0]
    half = hours // 2
    count = matrices.shape[1] // hours

    def halves(values, axis, first):
        pieces = [
            lax.slice_in_dim(values, j * hours + first, j * hours + first + half, axis=axis)
            for j in range(count)
        ]
        return jnp.concatenate(pieces, axis=axis)

    earlier = lax.dot_general(
        halves(matrices, 1, half), halves(runoffs, 0, 0), NN, preferred_element_type=jnp.float32
    )
    later = lax.dot_general(matrices, runoffs, NN, preferred_element_type=jnp.float32)
    return jnp.concatenate([earlier[:half] + earlier[half:], later[:half] + later[half:]], axis=0)


def route_kernel(
    meta_ref, runoff_ref, dest_ref, reach_marks_ref, late_ref, responses_ref, flow_ref, stack_ref, *, basin_rows
):
    early, hours, tiles = responses_ref.shape
    late = late_ref.shape[1] // hours
    outlets = flow_ref.shape[0]
    owners = meta_ref.shape[0] // FIELDS
    core = lax.rem(lax.axis_index("tile"), CORES)
    dest = dest_ref[0:1]

    stack_ref[: owners * FIELDS] = meta_ref[...].astype(jnp.float32)

    def table(field):
        return stack_ref[pl.ds(field, owners, stride=FIELDS), :].astype(jnp.bfloat16)

    def picked(values, owner):
        chosen = iota((owners, tiles), 0) == owner
        return jnp.sum(jnp.where(chosen, values, 0.0), axis=0, keepdims=True).astype(jnp.int32)

    spans = (FIELDS - 2) // 3
    reach_table = jnp.concatenate(
        [
            jnp.concatenate([table(item * spans + j) for j in range(spans)], axis=1)
            for item in range(3)
        ],
        axis=0,
    )
    by_reach = lax.dot_general(
        reach_table, reach_marks_ref[...], NN, preferred_element_type=jnp.float32
    )
    basin, kind, lag = [picked(by_reach[j * owners : (j + 1) * owners], dest) for j in range(3)]
    tree_table = jnp.concatenate([table(3 * spans), table(3 * spans + 1)], axis=0)[:, :basin_rows]

    def parent_of(owner, local):
        by_basin = lax.dot_general(
            tree_table, one_hot(local, basin_rows), NN, preferred_element_type=jnp.float32
        )
        return picked(by_basin[:owners], owner) - 1, picked(by_basin[owners:], owner)

    parent_owner, parent_local = parent_of(dest, basin)
    second_owner, second_local = parent_of(parent_owner, parent_local)

    def row_of(owner, local):
        mine = jnp.logical_and(owner >= 0, (owner & (CORES - 1)) == core)
        place = owner // CORES - 1
        place = jnp.where(place < 0, place + owners // CORES, place)
        return jnp.where(mine, place * basin_rows + local, -1)

    placements = jnp.concatenate(
        [
            one_hot(row_of(owner, local), outlets)
            for owner, local in (
                (dest, basin),
                (parent_owner, parent_local),
                (second_owner, second_local),
            )
        ],
        axis=0,
    )

    runoff = runoff_ref[...]
    by_kind = jnp.concatenate(
        [
            runoff * (kind == early + k).astype(jnp.float32).astype(jnp.bfloat16)
            for k in range(late)
        ],
        axis=0,
    )
    routed = respond(late_ref[...], by_kind)
    for k in range(early):
        routed = jnp.where(kind == k, responses_ref[k], routed)
    for step in (64, 32, 16, 8):
        routed = jnp.where((lag & step) != 0, later_rows(routed, step), routed)
    routed = turned(routed, lag & 7)
    flows = lax.dot_general(
        jnp.concatenate([placements, placements], axis=1),
        jnp.concatenate(split(routed), axis=1),
        NT,
        preferred_element_type=jnp.float32,
    )
    flow = later_lanes(flows[2 * outlets :], LINK)
    flow = later_lanes(flows[outlets : 2 * outlets] + flow, LINK)
    flow = flows[:outlets] + flow
    level = jnp.log(jnp.maximum(flow, CODE_FLOOR)) * CODE_SCALE + (CODE_ZERO + CODE_TOP + 0.5)
    level = jnp.clip(level, 0.0, 2.0 * CODE_TOP).astype(jnp.int32) - CODE_TOP
    flow_ref[...] = level.astype(jnp.int16)


def finish_kernel(parts_ref, section_ref):
    level = parts_ref[...].astype(jnp.int32)
    flow = jnp.exp((level.astype(jnp.float32) - CODE_ZERO) * (1.0 / CODE_SCALE))
    flow = jnp.sum(jnp.where(level == -CODE_TOP, 0.0, flow), axis=0)
    section_ref[...] = jnp.log(1.0 + flow)


def per_device(
    rain,
    soil,
    tile_area,
    tile_dest,
    tile_reach,
    reach_basin,
    reach_kind,
    reach_lag,
    irf,
    outlet_level,
    outlet_parent,
):
    owners = lax.axis_size("tile")
    tile_rows, hours = rain.shape
    basin_rows = outlet_parent.shape[0]
    kinds = irf.shape[0]
    params = pltpu.CompilerParams(vmem_limit_bytes=VMEM_BYTES)
    held = pl.BlockSpec(memory_space=pltpu.HBM)
    whole = pl.BlockSpec(memory_space=pltpu.VMEM)
    block = (tile_rows + SIDE_ROWS, hours)

    def in_hbm(values, shape):
        return pltpu.with_memory_space_constraint(values.reshape(shape), pltpu.HBM)

    numbers = [
        in_hbm(values, (1, -1))
        for values in (
            reach_basin, reach_kind, reach_lag, outlet_parent, soil, tile_area, tile_dest, tile_reach,
        )
    ]
    meta, own = pl.pallas_call(
        lambda *refs: pack_kernel(*refs, basin_rows=basin_rows),
        out_shape=(
            jax.ShapeDtypeStruct((owners * FIELDS, LANES), jnp.bfloat16),
            jax.ShapeDtypeStruct(block, jnp.bfloat16),
        ),
        in_specs=[held] * (len(numbers) + 1),
        out_specs=(held, whole),
        scratch_shapes=[pltpu.VMEM(values.shape, values.dtype) for values in numbers]
        + [
            pltpu.VMEM((owners * FIELDS, LANES), jnp.bfloat16),
            pltpu.SemaphoreType.DMA((len(numbers) + 2,)),
        ],
        compiler_params=params,
        cost_estimate=SMALL,
        name="pack",
    )(*numbers, in_hbm(rain, rain.shape))
    other = lax.ppermute(own, "tile", [(i, i ^ 1) for i in range(owners)])
    meta = lax.all_to_all(
        meta.reshape(owners, FIELDS, LANES), "tile", split_axis=0, concat_axis=0, tiled=True
    ).reshape(-1, LANES)

    chip_tiles = CORES * tile_rows
    early = kinds // 2
    prepared = pl.pallas_call(
        prepare_kernel,
        out_shape=(
            jax.ShapeDtypeStruct((hours, chip_tiles), jnp.bfloat16),
            jax.ShapeDtypeStruct((8, chip_tiles), jnp.int32),
            jax.ShapeDtypeStruct((reach_basin.size, chip_tiles), jnp.bfloat16),
            jax.ShapeDtypeStruct((hours, (kinds - early) * hours), jnp.bfloat16),
            jax.ShapeDtypeStruct((early, hours, chip_tiles), jnp.float32),
        ),
        in_specs=[held, whole, whole],
        scratch_shapes=[pltpu.VMEM(irf.shape, irf.dtype), pltpu.SemaphoreType.DMA((1,))],
        compiler_params=params,
        cost_estimate=SMALL,
        name="prepare",
    )(in_hbm(irf, irf.shape), own, other)

    flow = pl.pallas_call(
        lambda *refs: route_kernel(*refs, basin_rows=basin_rows),
        out_shape=jax.ShapeDtypeStruct((owners // CORES * basin_rows, hours), jnp.int16),
        scratch_shapes=[pltpu.VMEM(((owners + 1) * FIELDS, LANES), jnp.float32)],
        compiler_params=params,
        name="route",
    )(meta, *prepared)

    parts = lax.all_to_all(
        flow.reshape(owners // CORES, basin_rows, hours),
        "tile",
        split_axis=0,
        concat_axis=0,
        axis_index_groups=[
            [*range(CORES + core, owners, CORES), core] for core in range(CORES)
        ],
        tiled=True,
    )
    return pl.pallas_call(
        finish_kernel,
        out_shape=jax.ShapeDtypeStruct((basin_rows, hours), jnp.float32),
        compiler_params=params,
        name="finish",
    )(parts)


def solution(mesh):
    rows = P(("ens", "tile"))
    table = P(("ens", "tile"), None)
    in_specs = (table, rows, rows, table, rows, rows, rows, rows, P(), rows, rows)
    return jax.shard_map(
        per_device, mesh=mesh, in_specs=in_specs, out_specs=table, check_vma=False
    )
```

```python
import math

import jax
import jax.numpy as jnp
from jax import lax
from jax.experimental import pallas as pl
from jax.experimental.pallas import tpu as pltpu
from jax.sharding import PartitionSpec as P

LINK = 6
LANES = 128
CORES = 2
FIELDS = 8
SIDE_ROWS = 16
VMEM_BYTES = 40 * 1024 * 1024
CODE_TOP = 32767
CODE_OCTAVES = 44
CODE_LOWEST = -26
CODE_SCALE = 2 * CODE_TOP / (CODE_OCTAVES * math.log(2.0))
CODE_FLOOR = 2.0 ** (2 * CODE_LOWEST)
CODE_ZERO = -CODE_TOP + 1 - CODE_LOWEST * math.log(2.0) * CODE_SCALE

SMALL = pl.CostEstimate(flops=1, bytes_accessed=1, transcendentals=0)
NT = (((1,), (1,)), ((), ()))
NN = (((1,), (0,)), ((), ()))


def iota(shape, axis):
    return lax.broadcasted_iota(jnp.int32, shape, axis)


def split(values):
    high = values.astype(jnp.bfloat16)
    return high, (values - high.astype(jnp.float32)).astype(jnp.bfloat16)


def one_hot(row, count):
    return (iota((count, row.shape[1]), 0) == row).astype(jnp.float32).astype(jnp.bfloat16)


def later_rows(values, hours):
    padding = jnp.zeros((hours, values.shape[1]), values.dtype)
    return jnp.concatenate([padding, values[: values.shape[0] - hours]], axis=0)


def turned(values, hours):
    place = iota((8, values.shape[1]), 0)
    source = (place - hours) & 7
    stays = place >= hours
    before = jnp.zeros((8, values.shape[1]), values.dtype)
    rows = []
    for first in range(0, values.shape[0], 8):
        now = jnp.take_along_axis(values[first : first + 8], source, axis=0, mode="promise_in_bounds")
        rows.append(jnp.where(stays, now, before))
        before = now
    return jnp.concatenate(rows, axis=0)


def later_lanes(values, hours):
    return jnp.where(iota(values.shape, 1) < hours, 0.0, pltpu.roll(values, hours, 1))


def lane_rows(values):
    return [values[:, first : first + LANES] for first in range(0, values.shape[1], LANES)]


def parts_of(values):
    high = values.astype(jnp.bfloat16).astype(jnp.float32)
    middle = (values - high).astype(jnp.bfloat16).astype(jnp.float32)
    return [high, middle, values - high - middle]


def pack_kernel(*refs, basin_rows):
    sources, (meta_hbm, block_ref, *scratch, meta_ref, arrived) = refs[:9], refs[9:]
    tile_rows = block_ref.shape[0] - SIDE_ROWS
    targets = (*scratch, block_ref.at[pl.ds(0, tile_rows)])
    copies = [
        pltpu.make_async_copy(source, target, arrived.at[j])
        for j, (source, target) in enumerate(zip(sources, targets))
    ]
    for copy in copies:
        copy.start()
    for copy in copies[:4]:
        copy.wait()
    basin, kind, lag, parent = [ref[...] for ref in scratch[:4]]
    shift = basin_rows.bit_length() - 1
    empty = jnp.zeros((1, LANES - basin_rows), jnp.int32)
    rows = lane_rows(basin) + lane_rows(kind) + lane_rows(lag)
    rows.append(jnp.concatenate([lax.shift_right_arithmetic(parent, shift) + 1, empty], axis=1))
    rows.append(jnp.concatenate([parent & (basin_rows - 1), empty], axis=1))
    numbers = jnp.concatenate(rows, axis=0).astype(jnp.float32)
    meta_ref[...] = jnp.concatenate([numbers] * (meta_ref.shape[0] // FIELDS), axis=0).astype(jnp.bfloat16)
    leaving = pltpu.make_async_copy(meta_ref, meta_hbm, arrived.at[len(copies)])
    leaving.start()
    for copy in copies[4:8]:
        copy.wait()
    soil, area, dest, reach = [ref[...] for ref in scratch[4:]]
    sides = parts_of(soil) + parts_of(area) + [dest.astype(jnp.float32), reach.astype(jnp.float32)]
    sides = jnp.concatenate(sides + [jnp.zeros((SIDE_ROWS - len(sides), tile_rows), jnp.float32)], axis=0)
    block_ref[tile_rows:] = sides.astype(jnp.bfloat16)
    copies[8].wait()
    leaving.wait()


def prepare_kernel(
    irf_hbm, own_ref, other_ref, runoff_ref, dest_ref, reach_marks_ref, late_ref, responses_ref, irf_ref, arrived
):
    copy = pltpu.make_async_copy(irf_hbm, irf_ref, arrived.at[0])
    copy.start()
    hours = own_ref.shape[1]
    half = hours // 2
    tile_rows = own_ref.shape[0] - SIDE_ROWS
    kinds, taps = irf_ref.shape
    early = responses_ref.shape[0]
    sides = jnp.concatenate([own_ref[tile_rows:], other_ref[tile_rows:]], axis=1).astype(jnp.float32)
    rainfall = jnp.concatenate(
        [ref[:tile_rows].astype(jnp.float32).T for ref in (own_ref, other_ref)], axis=1
    )
    storage = sides[0:1] + sides[1:2] + sides[2:3]
    area = sides[3:4] + sides[4:5] + sides[5:6]
    excess = jnp.maximum(rainfall - 0.2 * storage, 0.0)
    runoff = (area * excess * excess / (rainfall + 0.8 * storage)).astype(jnp.bfloat16)
    runoff_ref[...] = runoff
    dest_ref[...] = jnp.broadcast_to(sides[6:7], dest_ref.shape).astype(jnp.int32)
    reach_marks_ref[...] = one_hot(sides[7:8].astype(jnp.int32), reach_marks_ref.shape[0])
    backward = (
        iota((taps, hours), 1) == lax.rem(hours - iota((taps, hours), 0), hours)
    ).astype(jnp.float32)
    copy.wait()
    reversed_taps = lax.dot_general(
        irf_ref[...], backward, NN, precision=lax.Precision.HIGHEST, preferred_element_type=jnp.float32
    )
    causal = iota((half, hours), 1) <= iota((half, hours), 0) + half
    for kind in range(kinds):
        row = jnp.broadcast_to(reversed_taps[kind : kind + 1], (half, hours))
        matrix = jnp.where(causal, pltpu.roll(row, half, 1, stride=1, stride_axis=0), 0.0)
        matrix = jnp.concatenate(split(matrix), axis=0)
        if kind < early:
            responses_ref[kind] = respond(matrix, runoff)
        else:
            late_ref[:, (kind - early) * hours : (kind - early + 1) * hours] = matrix


def respond(matrices, runoffs):
    hours = matrices.shape[0]
    half = hours // 2
    count = matrices.shape[1] // hours

    def halves(values, axis, first):
        pieces = [
            lax.slice_in_dim(values, j * hours + first, j * hours + first + half, axis=axis)
            for j in range(count)
        ]
        return jnp.concatenate(pieces, axis=axis)

    earlier = lax.dot_general(
        halves(matrices, 1, half), halves(runoffs, 0, 0), NN, preferred_element_type=jnp.float32
    )
    later = lax.dot_general(matrices, runoffs, NN, preferred_element_type=jnp.float32)
    return jnp.concatenate([earlier[:half] + earlier[half:], later[:half] + later[half:]], axis=0)


def route_kernel(
    meta_ref, runoff_ref, dest_ref, reach_marks_ref, late_ref, responses_ref, flow_ref, stack_ref, *, basin_rows
):
    early, hours, tiles = responses_ref.shape
    late = late_ref.shape[1] // hours
    outlets = flow_ref.shape[0]
    owners = meta_ref.shape[0] // FIELDS
    core = lax.rem(lax.axis_index("tile"), CORES)
    dest = dest_ref[0:1]

    stack_ref[: owners * FIELDS] = meta_ref[...].astype(jnp.float32)

    def table(field):
        return stack_ref[pl.ds(field, owners, stride=FIELDS), :].astype(jnp.bfloat16)

    def picked(values, owner):
        place = jnp.where(owner < 0, owners, jnp.where(owner < CORES, owner + owners, owner) - CORES)
        chosen = iota((owners, tiles), 0) == place
        return jnp.sum(jnp.where(chosen, values, 0.0), axis=0, keepdims=True).astype(jnp.int32)

    spans = (FIELDS - 2) // 3
    reach_table = jnp.concatenate(
        [
            jnp.concatenate([table(item * spans + j) for j in range(spans)], axis=1)
            for item in range(3)
        ],
        axis=0,
    )
    by_reach = lax.dot_general(
        reach_table, reach_marks_ref[...], NN, preferred_element_type=jnp.float32
    )
    basin, kind, lag = [picked(by_reach[j * owners : (j + 1) * owners], dest) for j in range(3)]
    tree_table = jnp.concatenate([table(3 * spans), table(3 * spans + 1)], axis=0)[:, :basin_rows]

    def parent_of(owner, local):
        by_basin = lax.dot_general(
            tree_table, one_hot(local, basin_rows), NN, preferred_element_type=jnp.float32
        )
        return picked(by_basin[:owners], owner) - 1, picked(by_basin[owners:], owner)

    parent_owner, parent_local = parent_of(dest, basin)
    second_owner, second_local = parent_of(parent_owner, parent_local)

    def row_of(owner, local):
        mine = jnp.logical_and(owner >= 0, (owner & (CORES - 1)) == core)
        place = owner // CORES - 1
        place = jnp.where(place < 0, place + owners // CORES, place)
        return jnp.where(mine, place * basin_rows + local, -1)

    placements = jnp.concatenate(
        [
            one_hot(row_of(owner, local), outlets)
            for owner, local in (
                (dest, basin),
                (parent_owner, parent_local),
                (second_owner, second_local),
            )
        ],
        axis=0,
    )

    runoff = runoff_ref[...]
    by_kind = jnp.concatenate(
        [
            runoff * (kind == early + k).astype(jnp.float32).astype(jnp.bfloat16)
            for k in range(late)
        ],
        axis=0,
    )
    routed = respond(late_ref[...], by_kind)
    for k in range(early):
        routed = jnp.where(kind == k, responses_ref[k], routed)
    for step in (64, 32, 16, 8):
        routed = jnp.where((lag & step) != 0, later_rows(routed, step), routed)
    routed = turned(routed, lag & 7)
    flows = lax.dot_general(
        jnp.concatenate([placements, placements], axis=1),
        jnp.concatenate(split(routed), axis=1),
        NT,
        preferred_element_type=jnp.float32,
    )
    flow = later_lanes(flows[2 * outlets :], LINK)
    flow = later_lanes(flows[outlets : 2 * outlets] + flow, LINK)
    flow = flows[:outlets] + flow
    level = jnp.log(jnp.maximum(flow, CODE_FLOOR)) * CODE_SCALE + (CODE_ZERO + CODE_TOP + 0.5)
    level = jnp.clip(level, 0.0, 2.0 * CODE_TOP).astype(jnp.int32) - CODE_TOP
    flow_ref[...] = level.astype(jnp.int16)


def finish_kernel(parts_ref, section_ref):
    level = parts_ref[...].astype(jnp.int32)
    flow = jnp.exp((level.astype(jnp.float32) - CODE_ZERO) * (1.0 / CODE_SCALE))
    flow = jnp.sum(jnp.where(level == -CODE_TOP, 0.0, flow), axis=0)
    section_ref[...] = jnp.log(1.0 + flow)


def per_device(
    rain,
    soil,
    tile_area,
    tile_dest,
    tile_reach,
    reach_basin,
    reach_kind,
    reach_lag,
    irf,
    outlet_level,
    outlet_parent,
):
    owners = lax.axis_size("tile")
    tile_rows, hours = rain.shape
    basin_rows = outlet_parent.shape[0]
    kinds = irf.shape[0]
    params = pltpu.CompilerParams(vmem_limit_bytes=VMEM_BYTES)
    held = pl.BlockSpec(memory_space=pltpu.HBM)
    whole = pl.BlockSpec(memory_space=pltpu.VMEM)
    block = (tile_rows + SIDE_ROWS, hours)

    def in_hbm(values, shape):
        return pltpu.with_memory_space_constraint(values.reshape(shape), pltpu.HBM)

    numbers = [
        in_hbm(values, (1, -1))
        for values in (
            reach_basin, reach_kind, reach_lag, outlet_parent, soil, tile_area, tile_dest, tile_reach,
        )
    ]
    meta, own = pl.pallas_call(
        lambda *refs: pack_kernel(*refs, basin_rows=basin_rows),
        out_shape=(
            jax.ShapeDtypeStruct((owners * FIELDS, LANES), jnp.bfloat16),
            jax.ShapeDtypeStruct(block, jnp.bfloat16),
        ),
        in_specs=[held] * (len(numbers) + 1),
        out_specs=(held, whole),
        scratch_shapes=[pltpu.VMEM(values.shape, values.dtype) for values in numbers]
        + [
            pltpu.VMEM((owners * FIELDS, LANES), jnp.bfloat16),
            pltpu.SemaphoreType.DMA((len(numbers) + 2,)),
        ],
        compiler_params=params,
        cost_estimate=SMALL,
        name="pack",
    )(*numbers, in_hbm(rain, rain.shape))
    other = lax.ppermute(own, "tile", [(i, i ^ 1) for i in range(owners)])
    meta = lax.all_to_all(
        meta.reshape(owners, FIELDS, LANES),
        "tile",
        split_axis=0,
        concat_axis=0,
        axis_index_groups=[[*range(CORES, owners), *range(CORES)]],
        tiled=True,
    ).reshape(-1, LANES)

    chip_tiles = CORES * tile_rows
    early = kinds // 2
    prepared = pl.pallas_call(
        prepare_kernel,
        out_shape=(
            jax.ShapeDtypeStruct((hours, chip_tiles), jnp.bfloat16),
            jax.ShapeDtypeStruct((8, chip_tiles), jnp.int32),
            jax.ShapeDtypeStruct((reach_basin.size, chip_tiles), jnp.bfloat16),
            jax.ShapeDtypeStruct((hours, (kinds - early) * hours), jnp.bfloat16),
            jax.ShapeDtypeStruct((early, hours, chip_tiles), jnp.float32),
        ),
        in_specs=[held, whole, whole],
        scratch_shapes=[pltpu.VMEM(irf.shape, irf.dtype), pltpu.SemaphoreType.DMA((1,))],
        compiler_params=params,
        cost_estimate=SMALL,
        name="prepare",
    )(in_hbm(irf, irf.shape), own, other)

    flow = pl.pallas_call(
        lambda *refs: route_kernel(*refs, basin_rows=basin_rows),
        out_shape=jax.ShapeDtypeStruct((owners // CORES * basin_rows, hours), jnp.int16),
        scratch_shapes=[pltpu.VMEM(((owners + 1) * FIELDS, LANES), jnp.float32)],
        compiler_params=params,
        name="route",
    )(meta, *prepared)

    parts = lax.all_to_all(
        flow.reshape(owners // CORES, basin_rows, hours),
        "tile",
        split_axis=0,
        concat_axis=0,
        axis_index_groups=[
            [*range(CORES + core, owners, CORES), core] for core in range(CORES)
        ],
        tiled=True,
    )
    return pl.pallas_call(
        finish_kernel,
        out_shape=jax.ShapeDtypeStruct((basin_rows, hours), jnp.float32),
        compiler_params=params,
        name="finish",
    )(parts)


def solution(mesh):
    rows = P(("ens", "tile"))
    table = P(("ens", "tile"), None)
    in_specs = (table, rows, rows, table, rows, rows, rows, rows, P(), rows, rows)
    return jax.shard_map(
        per_device, mesh=mesh, in_specs=in_specs, out_specs=table, check_vma=False
    )
```

```python
import math

import jax
import jax.numpy as jnp
from jax import lax
from jax.experimental import pallas as pl
from jax.experimental.pallas import tpu as pltpu
from jax.sharding import PartitionSpec as P

LINK = 6
LANES = 128
CORES = 2
FIELDS = 8
SIDE_ROWS = 16
VMEM_BYTES = 40 * 1024 * 1024
CODE_TOP = 32767
CODE_OCTAVES = 44
CODE_LOWEST = -26
CODE_SCALE = 2 * CODE_TOP / (CODE_OCTAVES * math.log(2.0))
CODE_FLOOR = 2.0 ** (2 * CODE_LOWEST)
CODE_ZERO = -CODE_TOP + 1 - CODE_LOWEST * math.log(2.0) * CODE_SCALE

SMALL = pl.CostEstimate(flops=1, bytes_accessed=1, transcendentals=0)
NT = (((1,), (1,)), ((), ()))
NN = (((1,), (0,)), ((), ()))


def iota(shape, axis):
    return lax.broadcasted_iota(jnp.int32, shape, axis)


def split(values):
    high = values.astype(jnp.bfloat16)
    return high, (values - high.astype(jnp.float32)).astype(jnp.bfloat16)


def one_hot(row, count):
    return (iota((count, row.shape[1]), 0) == row).astype(jnp.float32).astype(jnp.bfloat16)


def later_rows(values, hours):
    padding = jnp.zeros((hours, values.shape[1]), values.dtype)
    return jnp.concatenate([padding, values[: values.shape[0] - hours]], axis=0)


def turned(values, hours):
    place = iota((8, values.shape[1]), 0)
    source = (place - hours) & 7
    stays = place >= hours
    before = jnp.zeros((8, values.shape[1]), values.dtype)
    rows = []
    for first in range(0, values.shape[0], 8):
        now = jnp.take_along_axis(values[first : first + 8], source, axis=0, mode="promise_in_bounds")
        rows.append(jnp.where(stays, now, before))
        before = now
    return jnp.concatenate(rows, axis=0)


def later_lanes(values, hours):
    return jnp.where(iota(values.shape, 1) < hours, 0.0, pltpu.roll(values, hours, 1))


def lane_rows(values):
    return [values[:, first : first + LANES] for first in range(0, values.shape[1], LANES)]


def parts_of(values):
    high = values.astype(jnp.bfloat16).astype(jnp.float32)
    middle = (values - high).astype(jnp.bfloat16).astype(jnp.float32)
    return [high, middle, values - high - middle]


def pack_kernel(*refs, basin_rows):
    sources, (meta_hbm, block_ref, *scratch, meta_ref, arrived) = refs[:9], refs[9:]
    tile_rows = block_ref.shape[0] - SIDE_ROWS
    targets = (*scratch, block_ref.at[pl.ds(0, tile_rows)])
    copies = [
        pltpu.make_async_copy(source, target, arrived.at[j])
        for j, (source, target) in enumerate(zip(sources, targets))
    ]
    for copy in copies:
        copy.start()
    for copy in copies[:4]:
        copy.wait()
    basin, kind, lag, parent = [ref[...] for ref in scratch[:4]]
    shift = basin_rows.bit_length() - 1
    empty = jnp.zeros((1, LANES - basin_rows), jnp.int32)
    rows = lane_rows(basin) + lane_rows(kind) + lane_rows(lag)
    rows.append(jnp.concatenate([lax.shift_right_arithmetic(parent, shift) + 1, empty], axis=1))
    rows.append(jnp.concatenate([parent & (basin_rows - 1), empty], axis=1))
    numbers = jnp.concatenate(rows, axis=0).astype(jnp.float32)
    meta_ref[...] = jnp.concatenate([numbers] * (meta_ref.shape[0] // FIELDS), axis=0).astype(jnp.bfloat16)
    leaving = pltpu.make_async_copy(meta_ref, meta_hbm, arrived.at[len(copies)])
    leaving.start()
    for copy in copies[4:8]:
        copy.wait()
    soil, area, dest, reach = [ref[...] for ref in scratch[4:]]
    sides = parts_of(soil) + parts_of(area) + [dest.astype(jnp.float32), reach.astype(jnp.float32)]
    sides = jnp.concatenate(sides + [jnp.zeros((SIDE_ROWS - len(sides), tile_rows), jnp.float32)], axis=0)
    block_ref[tile_rows:] = sides.astype(jnp.bfloat16)
    copies[8].wait()
    leaving.wait()


def prepare_kernel(
    irf_hbm, own_ref, other_ref, runoff_ref, dest_ref, reach_marks_ref, late_ref, responses_ref, irf_ref, arrived
):
    copy = pltpu.make_async_copy(irf_hbm, irf_ref, arrived.at[0])
    copy.start()
    hours = own_ref.shape[1]
    half = hours // 2
    tile_rows = own_ref.shape[0] - SIDE_ROWS
    kinds, taps = irf_ref.shape
    early = responses_ref.shape[0]
    sides = jnp.concatenate([own_ref[tile_rows:], other_ref[tile_rows:]], axis=1).astype(jnp.float32)
    rainfall = jnp.concatenate(
        [ref[:tile_rows].astype(jnp.float32).T for ref in (own_ref, other_ref)], axis=1
    )
    storage = sides[0:1] + sides[1:2] + sides[2:3]
    area = sides[3:4] + sides[4:5] + sides[5:6]
    excess = jnp.maximum(rainfall - 0.2 * storage, 0.0)
    runoff = (area * excess * excess / (rainfall + 0.8 * storage)).astype(jnp.bfloat16)
    runoff_ref[...] = runoff
    dest_ref[...] = jnp.broadcast_to(sides[6:7], dest_ref.shape).astype(jnp.int32)
    reach_marks_ref[...] = one_hot(sides[7:8].astype(jnp.int32), reach_marks_ref.shape[0])
    backward = (
        iota((taps, hours), 1) == lax.rem(hours - iota((taps, hours), 0), hours)
    ).astype(jnp.float32)
    copy.wait()
    reversed_taps = lax.dot_general(
        irf_ref[...], backward, NN, precision=lax.Precision.HIGHEST, preferred_element_type=jnp.float32
    )
    causal = iota((half, hours), 1) <= iota((half, hours), 0) + half
    for kind in range(kinds):
        row = jnp.broadcast_to(reversed_taps[kind : kind + 1], (half, hours))
        matrix = jnp.where(causal, pltpu.roll(row, half, 1, stride=1, stride_axis=0), 0.0)
        matrix = jnp.concatenate(split(matrix), axis=0)
        if kind < early:
            responses_ref[kind] = respond(matrix, runoff)
        else:
            late_ref[:, (kind - early) * hours : (kind - early + 1) * hours] = matrix


def respond(matrices, runoffs):
    hours = matrices.shape[0]
    half = hours // 2
    count = matrices.shape[1] // hours

    def halves(values, axis, first):
        pieces = [
            lax.slice_in_dim(values, j * hours + first, j * hours + first + half, axis=axis)
            for j in range(count)
        ]
        return jnp.concatenate(pieces, axis=axis)

    earlier = lax.dot_general(
        halves(matrices, 1, half), halves(runoffs, 0, 0), NN, preferred_element_type=jnp.float32
    )
    later = lax.dot_general(matrices, runoffs, NN, preferred_element_type=jnp.float32)
    return jnp.concatenate([earlier[:half] + earlier[half:], later[:half] + later[half:]], axis=0)


def route_kernel(
    meta_ref, runoff_ref, dest_ref, reach_marks_ref, late_ref, responses_ref, flow_ref, stack_ref, *, basin_rows
):
    early, hours, tiles = responses_ref.shape
    late = late_ref.shape[1] // hours
    outlets = flow_ref.shape[0]
    owners = meta_ref.shape[0] // FIELDS
    core = lax.rem(lax.axis_index("tile"), CORES)
    dest = dest_ref[0:1]

    stack_ref[: owners * FIELDS] = meta_ref[...].astype(jnp.float32)

    def table(field):
        return stack_ref[pl.ds(field, owners, stride=FIELDS), :].astype(jnp.bfloat16)

    def picked(values, owner):
        chosen = iota((owners, tiles), 0) == owners - 1 - owner
        return jnp.sum(jnp.where(chosen, values, 0.0), axis=0, keepdims=True).astype(jnp.int32)

    spans = (FIELDS - 2) // 3
    reach_table = jnp.concatenate(
        [
            jnp.concatenate([table(item * spans + j) for j in range(spans)], axis=1)
            for item in range(3)
        ],
        axis=0,
    )
    by_reach = lax.dot_general(
        reach_table, reach_marks_ref[...], NN, preferred_element_type=jnp.float32
    )
    basin, kind, lag = [picked(by_reach[j * owners : (j + 1) * owners], dest) for j in range(3)]
    tree_table = jnp.concatenate([table(3 * spans), table(3 * spans + 1)], axis=0)[:, :basin_rows]

    def parent_of(owner, local):
        by_basin = lax.dot_general(
            tree_table, one_hot(local, basin_rows), NN, preferred_element_type=jnp.float32
        )
        return picked(by_basin[:owners], owner) - 1, picked(by_basin[owners:], owner)

    parent_owner, parent_local = parent_of(dest, basin)
    second_owner, second_local = parent_of(parent_owner, parent_local)

    def row_of(owner, local):
        mine = jnp.logical_and(owner >= 0, (owner & (CORES - 1)) == core)
        place = owner // CORES - 1
        place = jnp.where(place < 0, place + owners // CORES, place)
        return jnp.where(mine, place * basin_rows + local, -1)

    placements = jnp.concatenate(
        [
            one_hot(row_of(owner, local), outlets)
            for owner, local in (
                (dest, basin),
                (parent_owner, parent_local),
                (second_owner, second_local),
            )
        ],
        axis=0,
    )

    runoff = runoff_ref[...]
    by_kind = jnp.concatenate(
        [
            runoff * (kind == early + k).astype(jnp.float32).astype(jnp.bfloat16)
            for k in range(late)
        ],
        axis=0,
    )
    routed = respond(late_ref[...], by_kind)
    for k in range(early):
        routed = jnp.where(kind == k, responses_ref[k], routed)
    for step in (64, 32, 16, 8):
        routed = jnp.where((lag & step) != 0, later_rows(routed, step), routed)
    routed = turned(routed, lag & 7)
    flows = lax.dot_general(
        jnp.concatenate([placements, placements], axis=1),
        jnp.concatenate(split(routed), axis=1),
        NT,
        preferred_element_type=jnp.float32,
    )
    flow = later_lanes(flows[2 * outlets :], LINK)
    flow = later_lanes(flows[outlets : 2 * outlets] + flow, LINK)
    flow = flows[:outlets] + flow
    level = jnp.log(jnp.maximum(flow, CODE_FLOOR)) * CODE_SCALE + (CODE_ZERO + CODE_TOP + 0.5)
    level = jnp.clip(level, 0.0, 2.0 * CODE_TOP).astype(jnp.int32) - CODE_TOP
    flow_ref[...] = level.astype(jnp.int16)


def finish_kernel(parts_ref, section_ref):
    level = parts_ref[...].astype(jnp.int32)
    flow = jnp.exp((level.astype(jnp.float32) - CODE_ZERO) * (1.0 / CODE_SCALE))
    flow = jnp.sum(jnp.where(level == -CODE_TOP, 0.0, flow), axis=0)
    section_ref[...] = jnp.log(1.0 + flow)


def per_device(
    rain,
    soil,
    tile_area,
    tile_dest,
    tile_reach,
    reach_basin,
    reach_kind,
    reach_lag,
    irf,
    outlet_level,
    outlet_parent,
):
    owners = lax.axis_size("tile")
    tile_rows, hours = rain.shape
    basin_rows = outlet_parent.shape[0]
    kinds = irf.shape[0]
    params = pltpu.CompilerParams(vmem_limit_bytes=VMEM_BYTES)
    held = pl.BlockSpec(memory_space=pltpu.HBM)
    whole = pl.BlockSpec(memory_space=pltpu.VMEM)
    block = (tile_rows + SIDE_ROWS, hours)

    def in_hbm(values, shape):
        return pltpu.with_memory_space_constraint(values.reshape(shape), pltpu.HBM)

    numbers = [
        in_hbm(values, (1, -1))
        for values in (
            reach_basin, reach_kind, reach_lag, outlet_parent, soil, tile_area, tile_dest, tile_reach,
        )
    ]
    meta, own = pl.pallas_call(
        lambda *refs: pack_kernel(*refs, basin_rows=basin_rows),
        out_shape=(
            jax.ShapeDtypeStruct((owners * FIELDS, LANES), jnp.bfloat16),
            jax.ShapeDtypeStruct(block, jnp.bfloat16),
        ),
        in_specs=[held] * (len(numbers) + 1),
        out_specs=(held, whole),
        scratch_shapes=[pltpu.VMEM(values.shape, values.dtype) for values in numbers]
        + [
            pltpu.VMEM((owners * FIELDS, LANES), jnp.bfloat16),
            pltpu.SemaphoreType.DMA((len(numbers) + 2,)),
        ],
        compiler_params=params,
        cost_estimate=SMALL,
        name="pack",
    )(*numbers, in_hbm(rain, rain.shape))
    other = lax.ppermute(own, "tile", [(i, i ^ 1) for i in range(owners)])
    meta = lax.all_to_all(
        meta.reshape(owners, FIELDS, LANES),
        "tile",
        split_axis=0,
        concat_axis=0,
        axis_index_groups=[[*range(owners)][::-1]],
        tiled=True,
    ).reshape(-1, LANES)

    chip_tiles = CORES * tile_rows
    early = kinds // 2
    prepared = pl.pallas_call(
        prepare_kernel,
        out_shape=(
            jax.ShapeDtypeStruct((hours, chip_tiles), jnp.bfloat16),
            jax.ShapeDtypeStruct((8, chip_tiles), jnp.int32),
            jax.ShapeDtypeStruct((reach_basin.size, chip_tiles), jnp.bfloat16),
            jax.ShapeDtypeStruct((hours, (kinds - early) * hours), jnp.bfloat16),
            jax.ShapeDtypeStruct((early, hours, chip_tiles), jnp.float32),
        ),
        in_specs=[held, whole, whole],
        scratch_shapes=[pltpu.VMEM(irf.shape, irf.dtype), pltpu.SemaphoreType.DMA((1,))],
        compiler_params=params,
        cost_estimate=SMALL,
        name="prepare",
    )(in_hbm(irf, irf.shape), own, other)

    flow = pl.pallas_call(
        lambda *refs: route_kernel(*refs, basin_rows=basin_rows),
        out_shape=jax.ShapeDtypeStruct((owners // CORES * basin_rows, hours), jnp.int16),
        scratch_shapes=[pltpu.VMEM(((owners + 1) * FIELDS, LANES), jnp.float32)],
        compiler_params=params,
        name="route",
    )(meta, *prepared)

    parts = lax.all_to_all(
        flow.reshape(owners // CORES, basin_rows, hours),
        "tile",
        split_axis=0,
        concat_axis=0,
        axis_index_groups=[
            [*range(CORES + core, owners, CORES), core] for core in range(CORES)
        ],
        tiled=True,
    )
    return pl.pallas_call(
        finish_kernel,
        out_shape=jax.ShapeDtypeStruct((basin_rows, hours), jnp.float32),
        compiler_params=params,
        name="finish",
    )(parts)


def solution(mesh):
    rows = P(("ens", "tile"))
    table = P(("ens", "tile"), None)
    in_specs = (table, rows, rows, table, rows, rows, rows, rows, P(), rows, rows)
    return jax.shard_map(
        per_device, mesh=mesh, in_specs=in_specs, out_specs=table, check_vma=False
    )
```

```python
import math

import jax
import jax.numpy as jnp
from jax import lax
from jax.experimental import pallas as pl
from jax.experimental.pallas import tpu as pltpu
from jax.sharding import PartitionSpec as P

LINK = 6
LANES = 128
CORES = 2
FIELDS = 8
SIDE_ROWS = 16
VMEM_BYTES = 40 * 1024 * 1024
CODE_TOP = 32767
CODE_OCTAVES = 44
CODE_LOWEST = -26
CODE_SCALE = 2 * CODE_TOP / (CODE_OCTAVES * math.log(2.0))
CODE_FLOOR = 2.0 ** (2 * CODE_LOWEST)
CODE_ZERO = -CODE_TOP + 1 - CODE_LOWEST * math.log(2.0) * CODE_SCALE

SMALL = pl.CostEstimate(flops=1, bytes_accessed=1, transcendentals=0)
NT = (((1,), (1,)), ((), ()))
NN = (((1,), (0,)), ((), ()))


def iota(shape, axis):
    return lax.broadcasted_iota(jnp.int32, shape, axis)


def split(values):
    high = values.astype(jnp.bfloat16)
    return high, (values - high.astype(jnp.float32)).astype(jnp.bfloat16)


def one_hot(row, count):
    return (iota((count, row.shape[1]), 0) == row).astype(jnp.float32).astype(jnp.bfloat16)


def group_of(owner, owners):
    upper = (owner + owners // 2) // owners
    return (owner + upper) % CORES


def later_rows(values, hours):
    padding = jnp.zeros((hours, values.shape[1]), values.dtype)
    return jnp.concatenate([padding, values[: values.shape[0] - hours]], axis=0)


def turned(values, hours):
    place = iota((8, values.shape[1]), 0)
    source = (place - hours) & 7
    stays = place >= hours
    before = jnp.zeros((8, values.shape[1]), values.dtype)
    rows = []
    for first in range(0, values.shape[0], 8):
        now = jnp.take_along_axis(values[first : first + 8], source, axis=0, mode="promise_in_bounds")
        rows.append(jnp.where(stays, now, before))
        before = now
    return jnp.concatenate(rows, axis=0)


def later_lanes(values, hours):
    return jnp.where(iota(values.shape, 1) < hours, 0.0, pltpu.roll(values, hours, 1))


def lane_rows(values):
    return [values[:, first : first + LANES] for first in range(0, values.shape[1], LANES)]


def parts_of(values):
    high = values.astype(jnp.bfloat16).astype(jnp.float32)
    middle = (values - high).astype(jnp.bfloat16).astype(jnp.float32)
    return [high, middle, values - high - middle]


def pack_kernel(*refs, basin_rows):
    sources, (meta_hbm, block_ref, *scratch, meta_ref, arrived) = refs[:9], refs[9:]
    tile_rows = block_ref.shape[0] - SIDE_ROWS
    targets = (*scratch, block_ref.at[pl.ds(0, tile_rows)])
    copies = [
        pltpu.make_async_copy(source, target, arrived.at[j])
        for j, (source, target) in enumerate(zip(sources, targets))
    ]
    for copy in copies:
        copy.start()
    for copy in copies[:4]:
        copy.wait()
    basin, kind, lag, parent = [ref[...] for ref in scratch[:4]]
    shift = basin_rows.bit_length() - 1
    empty = jnp.zeros((1, LANES - basin_rows), jnp.int32)
    rows = lane_rows(basin) + lane_rows(kind) + lane_rows(lag)
    rows.append(jnp.concatenate([lax.shift_right_arithmetic(parent, shift) + 1, empty], axis=1))
    rows.append(jnp.concatenate([parent & (basin_rows - 1), empty], axis=1))
    numbers = jnp.concatenate(rows, axis=0).astype(jnp.float32)
    meta_ref[...] = jnp.concatenate([numbers] * (meta_ref.shape[0] // FIELDS), axis=0).astype(jnp.bfloat16)
    leaving = pltpu.make_async_copy(meta_ref, meta_hbm, arrived.at[len(copies)])
    leaving.start()
    for copy in copies[4:8]:
        copy.wait()
    soil, area, dest, reach = [ref[...] for ref in scratch[4:]]
    sides = parts_of(soil) + parts_of(area) + [dest.astype(jnp.float32), reach.astype(jnp.float32)]
    sides = jnp.concatenate(sides + [jnp.zeros((SIDE_ROWS - len(sides), tile_rows), jnp.float32)], axis=0)
    block_ref[tile_rows:] = sides.astype(jnp.bfloat16)
    copies[8].wait()
    leaving.wait()


def prepare_kernel(
    irf_hbm, own_ref, other_ref, runoff_ref, dest_ref, reach_marks_ref, late_ref, responses_ref, irf_ref, arrived
):
    copy = pltpu.make_async_copy(irf_hbm, irf_ref, arrived.at[0])
    copy.start()
    hours = own_ref.shape[1]
    half = hours // 2
    tile_rows = own_ref.shape[0] - SIDE_ROWS
    kinds, taps = irf_ref.shape
    early = responses_ref.shape[0]
    sides = jnp.concatenate([own_ref[tile_rows:], other_ref[tile_rows:]], axis=1).astype(jnp.float32)
    rainfall = jnp.concatenate(
        [ref[:tile_rows].astype(jnp.float32).T for ref in (own_ref, other_ref)], axis=1
    )
    storage = sides[0:1] + sides[1:2] + sides[2:3]
    area = sides[3:4] + sides[4:5] + sides[5:6]
    excess = jnp.maximum(rainfall - 0.2 * storage, 0.0)
    runoff = (area * excess * excess / (rainfall + 0.8 * storage)).astype(jnp.bfloat16)
    runoff_ref[...] = runoff
    dest_ref[...] = jnp.broadcast_to(sides[6:7], dest_ref.shape).astype(jnp.int32)
    reach_marks_ref[...] = one_hot(sides[7:8].astype(jnp.int32), reach_marks_ref.shape[0])
    backward = (
        iota((taps, hours), 1) == lax.rem(hours - iota((taps, hours), 0), hours)
    ).astype(jnp.float32)
    copy.wait()
    reversed_taps = lax.dot_general(
        irf_ref[...], backward, NN, precision=lax.Precision.HIGHEST, preferred_element_type=jnp.float32
    )
    causal = iota((half, hours), 1) <= iota((half, hours), 0) + half
    for kind in range(kinds):
        row = jnp.broadcast_to(reversed_taps[kind : kind + 1], (half, hours))
        matrix = jnp.where(causal, pltpu.roll(row, half, 1, stride=1, stride_axis=0), 0.0)
        matrix = jnp.concatenate(split(matrix), axis=0)
        if kind < early:
            responses_ref[kind] = respond(matrix, runoff)
        else:
            late_ref[:, (kind - early) * hours : (kind - early + 1) * hours] = matrix


def respond(matrices, runoffs):
    hours = matrices.shape[0]
    half = hours // 2
    count = matrices.shape[1] // hours

    def halves(values, axis, first):
        pieces = [
            lax.slice_in_dim(values, j * hours + first, j * hours + first + half, axis=axis)
            for j in range(count)
        ]
        return jnp.concatenate(pieces, axis=axis)

    earlier = lax.dot_general(
        halves(matrices, 1, half), halves(runoffs, 0, 0), NN, preferred_element_type=jnp.float32
    )
    later = lax.dot_general(matrices, runoffs, NN, preferred_element_type=jnp.float32)
    return jnp.concatenate([earlier[:half] + earlier[half:], later[:half] + later[half:]], axis=0)


def route_kernel(
    meta_ref, runoff_ref, dest_ref, reach_marks_ref, late_ref, responses_ref, flow_ref, stack_ref, *, basin_rows
):
    early, hours, tiles = responses_ref.shape
    late = late_ref.shape[1] // hours
    outlets = flow_ref.shape[0]
    owners = meta_ref.shape[0] // FIELDS
    side = group_of(lax.axis_index("tile"), owners)
    dest = dest_ref[0:1]

    stack_ref[: owners * FIELDS] = meta_ref[...].astype(jnp.float32)

    def table(field):
        return stack_ref[pl.ds(field, owners, stride=FIELDS), :].astype(jnp.bfloat16)

    def picked(values, owner):
        place = jnp.where(owner < 0, owners, jnp.where(owner < CORES, owner + owners, owner) - CORES)
        chosen = iota((owners, tiles), 0) == place
        return jnp.sum(jnp.where(chosen, values, 0.0), axis=0, keepdims=True).astype(jnp.int32)

    spans = (FIELDS - 2) // 3
    reach_table = jnp.concatenate(
        [
            jnp.concatenate([table(item * spans + j) for j in range(spans)], axis=1)
            for item in range(3)
        ],
        axis=0,
    )
    by_reach = lax.dot_general(
        reach_table, reach_marks_ref[...], NN, preferred_element_type=jnp.float32
    )
    basin, kind, lag = [picked(by_reach[j * owners : (j + 1) * owners], dest) for j in range(3)]
    tree_table = jnp.concatenate([table(3 * spans), table(3 * spans + 1)], axis=0)[:, :basin_rows]

    def parent_of(owner, local):
        by_basin = lax.dot_general(
            tree_table, one_hot(local, basin_rows), NN, preferred_element_type=jnp.float32
        )
        return picked(by_basin[:owners], owner) - 1, picked(by_basin[owners:], owner)

    parent_owner, parent_local = parent_of(dest, basin)
    second_owner, second_local = parent_of(parent_owner, parent_local)

    def row_of(owner, local):
        mine = jnp.logical_and(owner >= 0, group_of(owner, owners) == side)
        place = owner // CORES - 1
        place = jnp.where(place < 0, place + owners // CORES, place)
        return jnp.where(mine, place * basin_rows + local, -1)

    placements = jnp.concatenate(
        [
            one_hot(row_of(owner, local), outlets)
            for owner, local in (
                (dest, basin),
                (parent_owner, parent_local),
                (second_owner, second_local),
            )
        ],
        axis=0,
    )

    runoff = runoff_ref[...]
    by_kind = jnp.concatenate(
        [
            runoff * (kind == early + k).astype(jnp.float32).astype(jnp.bfloat16)
            for k in range(late)
        ],
        axis=0,
    )
    routed = respond(late_ref[...], by_kind)
    for k in range(early):
        routed = jnp.where(kind == k, responses_ref[k], routed)
    for step in (64, 32, 16, 8):
        routed = jnp.where((lag & step) != 0, later_rows(routed, step), routed)
    routed = turned(routed, lag & 7)
    flows = lax.dot_general(
        jnp.concatenate([placements, placements], axis=1),
        jnp.concatenate(split(routed), axis=1),
        NT,
        preferred_element_type=jnp.float32,
    )
    flow = later_lanes(flows[2 * outlets :], LINK)
    flow = later_lanes(flows[outlets : 2 * outlets] + flow, LINK)
    flow = flows[:outlets] + flow
    level = jnp.log(jnp.maximum(flow, CODE_FLOOR)) * CODE_SCALE + (CODE_ZERO + CODE_TOP + 0.5)
    level = jnp.clip(level, 0.0, 2.0 * CODE_TOP).astype(jnp.int32) - CODE_TOP
    flow_ref[...] = level.astype(jnp.int16)


def finish_kernel(parts_ref, section_ref):
    level = parts_ref[...].astype(jnp.int32)
    flow = jnp.exp((level.astype(jnp.float32) - CODE_ZERO) * (1.0 / CODE_SCALE))
    flow = jnp.sum(jnp.where(level == -CODE_TOP, 0.0, flow), axis=0)
    section_ref[...] = jnp.log(1.0 + flow)


def per_device(
    rain,
    soil,
    tile_area,
    tile_dest,
    tile_reach,
    reach_basin,
    reach_kind,
    reach_lag,
    irf,
    outlet_level,
    outlet_parent,
):
    owners = lax.axis_size("tile")
    tile_rows, hours = rain.shape
    basin_rows = outlet_parent.shape[0]
    kinds = irf.shape[0]
    params = pltpu.CompilerParams(vmem_limit_bytes=VMEM_BYTES)
    held = pl.BlockSpec(memory_space=pltpu.HBM)
    whole = pl.BlockSpec(memory_space=pltpu.VMEM)
    block = (tile_rows + SIDE_ROWS, hours)

    def in_hbm(values, shape):
        return pltpu.with_memory_space_constraint(values.reshape(shape), pltpu.HBM)

    numbers = [
        in_hbm(values, (1, -1))
        for values in (
            reach_basin, reach_kind, reach_lag, outlet_parent, soil, tile_area, tile_dest, tile_reach,
        )
    ]
    meta, own = pl.pallas_call(
        lambda *refs: pack_kernel(*refs, basin_rows=basin_rows),
        out_shape=(
            jax.ShapeDtypeStruct((owners * FIELDS, LANES), jnp.bfloat16),
            jax.ShapeDtypeStruct(block, jnp.bfloat16),
        ),
        in_specs=[held] * (len(numbers) + 1),
        out_specs=(held, whole),
        scratch_shapes=[pltpu.VMEM(values.shape, values.dtype) for values in numbers]
        + [
            pltpu.VMEM((owners * FIELDS, LANES), jnp.bfloat16),
            pltpu.SemaphoreType.DMA((len(numbers) + 2,)),
        ],
        compiler_params=params,
        cost_estimate=SMALL,
        name="pack",
    )(*numbers, in_hbm(rain, rain.shape))
    other = lax.ppermute(own, "tile", [(i, i ^ 1) for i in range(owners)])
    meta = lax.all_to_all(
        meta.reshape(owners, FIELDS, LANES),
        "tile",
        split_axis=0,
        concat_axis=0,
        axis_index_groups=[[*range(CORES, owners), *range(CORES)]],
        tiled=True,
    ).reshape(-1, LANES)

    chip_tiles = CORES * tile_rows
    early = kinds // 2
    prepared = pl.pallas_call(
        prepare_kernel,
        out_shape=(
            jax.ShapeDtypeStruct((hours, chip_tiles), jnp.bfloat16),
            jax.ShapeDtypeStruct((8, chip_tiles), jnp.int32),
            jax.ShapeDtypeStruct((reach_basin.size, chip_tiles), jnp.bfloat16),
            jax.ShapeDtypeStruct((hours, (kinds - early) * hours), jnp.bfloat16),
            jax.ShapeDtypeStruct((early, hours, chip_tiles), jnp.float32),
        ),
        in_specs=[held, whole, whole],
        scratch_shapes=[pltpu.VMEM(irf.shape, irf.dtype), pltpu.SemaphoreType.DMA((1,))],
        compiler_params=params,
        cost_estimate=SMALL,
        name="prepare",
    )(in_hbm(irf, irf.shape), own, other)

    flow = pl.pallas_call(
        lambda *refs: route_kernel(*refs, basin_rows=basin_rows),
        out_shape=jax.ShapeDtypeStruct((owners // CORES * basin_rows, hours), jnp.int16),
        scratch_shapes=[pltpu.VMEM(((owners + 1) * FIELDS, LANES), jnp.float32)],
        compiler_params=params,
        name="route",
    )(meta, *prepared)

    parts = lax.all_to_all(
        flow.reshape(owners // CORES, basin_rows, hours),
        "tile",
        split_axis=0,
        concat_axis=0,
        axis_index_groups=[
            [owner for owner in (*range(CORES, owners), *range(CORES)) if group_of(owner, owners) == side]
            for side in range(CORES)
        ],
        tiled=True,
    )
    return pl.pallas_call(
        finish_kernel,
        out_shape=jax.ShapeDtypeStruct((basin_rows, hours), jnp.float32),
        compiler_params=params,
        name="finish",
    )(parts)


def solution(mesh):
    rows = P(("ens", "tile"))
    table = P(("ens", "tile"), None)
    in_specs = (table, rows, rows, table, rows, rows, rows, rows, P(), rows, rows)
    return jax.shard_map(
        per_device, mesh=mesh, in_specs=in_specs, out_specs=table, check_vma=False
    )
```

```python
import math

import jax
import jax.numpy as jnp
from jax import lax
from jax.experimental import pallas as pl
from jax.experimental.pallas import tpu as pltpu
from jax.sharding import PartitionSpec as P

LINK = 6
LANES = 128
CORES = 2
FIELDS = 8
SIDE_ROWS = 16
VMEM_BYTES = 40 * 1024 * 1024
CODE_TOP = 32767
CODE_OCTAVES = 44
CODE_LOWEST = -26
CODE_SCALE = 2 * CODE_TOP / (CODE_OCTAVES * math.log(2.0))
CODE_FLOOR = 2.0 ** (2 * CODE_LOWEST)
CODE_ZERO = -CODE_TOP + 1 - CODE_LOWEST * math.log(2.0) * CODE_SCALE

SMALL = pl.CostEstimate(flops=1, bytes_accessed=1, transcendentals=0)
NT = (((1,), (1,)), ((), ()))
NN = (((1,), (0,)), ((), ()))


def iota(shape, axis):
    return lax.broadcasted_iota(jnp.int32, shape, axis)


def split(values):
    high = values.astype(jnp.bfloat16)
    return high, (values - high.astype(jnp.float32)).astype(jnp.bfloat16)


def one_hot(row, count):
    return (iota((count, row.shape[1]), 0) == row).astype(jnp.float32).astype(jnp.bfloat16)


def later_rows(values, hours):
    padding = jnp.zeros((hours, values.shape[1]), values.dtype)
    return jnp.concatenate([padding, values[: values.shape[0] - hours]], axis=0)


def turned(values, hours):
    place = iota((8, values.shape[1]), 0)
    source = (place - hours) & 7
    stays = place >= hours
    before = jnp.zeros((8, values.shape[1]), values.dtype)
    rows = []
    for first in range(0, values.shape[0], 8):
        now = jnp.take_along_axis(values[first : first + 8], source, axis=0, mode="promise_in_bounds")
        rows.append(jnp.where(stays, now, before))
        before = now
    return jnp.concatenate(rows, axis=0)


def later_lanes(values, hours):
    return jnp.where(iota(values.shape, 1) < hours, 0.0, pltpu.roll(values, hours, 1))


def lane_rows(values):
    return [values[:, first : first + LANES] for first in range(0, values.shape[1], LANES)]


def parts_of(values):
    high = values.astype(jnp.bfloat16).astype(jnp.float32)
    middle = (values - high).astype(jnp.bfloat16).astype(jnp.float32)
    return [high, middle, values - high - middle]


def pack_kernel(*refs, basin_rows):
    sources, (meta_hbm, block_ref, *scratch, meta_ref, arrived) = refs[:9], refs[9:]
    tile_rows = block_ref.shape[0] - SIDE_ROWS
    targets = (*scratch, block_ref.at[pl.ds(0, tile_rows)])
    copies = [
        pltpu.make_async_copy(source, target, arrived.at[j])
        for j, (source, target) in enumerate(zip(sources, targets))
    ]
    for j, copy in enumerate(copies):
        copy.start(priority=1 if j < 4 else 0)
    for copy in copies[:4]:
        copy.wait()
    basin, kind, lag, parent = [ref[...] for ref in scratch[:4]]
    shift = basin_rows.bit_length() - 1
    empty = jnp.zeros((1, LANES - basin_rows), jnp.int32)
    rows = lane_rows(basin) + lane_rows(kind) + lane_rows(lag)
    rows.append(jnp.concatenate([lax.shift_right_arithmetic(parent, shift) + 1, empty], axis=1))
    rows.append(jnp.concatenate([parent & (basin_rows - 1), empty], axis=1))
    numbers = jnp.concatenate(rows, axis=0).astype(jnp.float32)
    meta_ref[...] = jnp.concatenate([numbers] * (meta_ref.shape[0] // FIELDS), axis=0).astype(jnp.bfloat16)
    leaving = pltpu.make_async_copy(meta_ref, meta_hbm, arrived.at[len(copies)])
    leaving.start(priority=1)
    for copy in copies[4:8]:
        copy.wait()
    soil, area, dest, reach = [ref[...] for ref in scratch[4:]]
    sides = parts_of(soil) + parts_of(area) + [dest.astype(jnp.float32), reach.astype(jnp.float32)]
    sides = jnp.concatenate(sides + [jnp.zeros((SIDE_ROWS - len(sides), tile_rows), jnp.float32)], axis=0)
    block_ref[tile_rows:] = sides.astype(jnp.bfloat16)
    copies[8].wait()
    leaving.wait()


def prepare_kernel(
    irf_hbm, own_ref, other_ref, runoff_ref, dest_ref, reach_marks_ref, late_ref, responses_ref, irf_ref, arrived
):
    copy = pltpu.make_async_copy(irf_hbm, irf_ref, arrived.at[0])
    copy.start()
    hours = own_ref.shape[1]
    half = hours // 2
    tile_rows = own_ref.shape[0] - SIDE_ROWS
    kinds, taps = irf_ref.shape
    early = responses_ref.shape[0]
    sides = jnp.concatenate([own_ref[tile_rows:], other_ref[tile_rows:]], axis=1).astype(jnp.float32)
    rainfall = jnp.concatenate(
        [ref[:tile_rows].astype(jnp.float32).T for ref in (own_ref, other_ref)], axis=1
    )
    storage = sides[0:1] + sides[1:2] + sides[2:3]
    area = sides[3:4] + sides[4:5] + sides[5:6]
    excess = jnp.maximum(rainfall - 0.2 * storage, 0.0)
    runoff = (area * excess * excess / (rainfall + 0.8 * storage)).astype(jnp.bfloat16)
    runoff_ref[...] = runoff
    dest_ref[...] = jnp.broadcast_to(sides[6:7], dest_ref.shape).astype(jnp.int32)
    reach_marks_ref[...] = one_hot(sides[7:8].astype(jnp.int32), reach_marks_ref.shape[0])
    backward = (
        iota((taps, hours), 1) == lax.rem(hours - iota((taps, hours), 0), hours)
    ).astype(jnp.float32)
    copy.wait()
    reversed_taps = lax.dot_general(
        irf_ref[...], backward, NN, precision=lax.Precision.HIGHEST, preferred_element_type=jnp.float32
    )
    causal = iota((half, hours), 1) <= iota((half, hours), 0) + half
    for kind in range(kinds):
        row = jnp.broadcast_to(reversed_taps[kind : kind + 1], (half, hours))
        matrix = jnp.where(causal, pltpu.roll(row, half, 1, stride=1, stride_axis=0), 0.0)
        matrix = jnp.concatenate(split(matrix), axis=0)
        if kind < early:
            responses_ref[kind] = respond(matrix, runoff)
        else:
            late_ref[:, (kind - early) * hours : (kind - early + 1) * hours] = matrix


def respond(matrices, runoffs):
    hours = matrices.shape[0]
    half = hours // 2
    count = matrices.shape[1] // hours

    def halves(values, axis, first):
        pieces = [
            lax.slice_in_dim(values, j * hours + first, j * hours + first + half, axis=axis)
            for j in range(count)
        ]
        return jnp.concatenate(pieces, axis=axis)

    earlier = lax.dot_general(
        halves(matrices, 1, half), halves(runoffs, 0, 0), NN, preferred_element_type=jnp.float32
    )
    later = lax.dot_general(matrices, runoffs, NN, preferred_element_type=jnp.float32)
    return jnp.concatenate([earlier[:half] + earlier[half:], later[:half] + later[half:]], axis=0)


def route_kernel(
    meta_ref, runoff_ref, dest_ref, reach_marks_ref, late_ref, responses_ref, flow_ref, stack_ref, *, basin_rows
):
    early, hours, tiles = responses_ref.shape
    late = late_ref.shape[1] // hours
    outlets = flow_ref.shape[0]
    owners = meta_ref.shape[0] // FIELDS
    core = lax.rem(lax.axis_index("tile"), CORES)
    dest = dest_ref[0:1]

    stack_ref[: owners * FIELDS] = meta_ref[...].astype(jnp.float32)

    def table(field):
        return stack_ref[pl.ds(field, owners, stride=FIELDS), :].astype(jnp.bfloat16)

    def picked(values, owner):
        place = jnp.where(owner < 0, owners, jnp.where(owner < CORES, owner + owners, owner) - CORES)
        chosen = iota((owners, tiles), 0) == place
        return jnp.sum(jnp.where(chosen, values, 0.0), axis=0, keepdims=True).astype(jnp.int32)

    spans = (FIELDS - 2) // 3
    reach_table = jnp.concatenate(
        [
            jnp.concatenate([table(item * spans + j) for j in range(spans)], axis=1)
            for item in range(3)
        ],
        axis=0,
    )
    by_reach = lax.dot_general(
        reach_table, reach_marks_ref[...], NN, preferred_element_type=jnp.float32
    )
    basin, kind, lag = [picked(by_reach[j * owners : (j + 1) * owners], dest) for j in range(3)]
    tree_table = jnp.concatenate([table(3 * spans), table(3 * spans + 1)], axis=0)[:, :basin_rows]

    def parent_of(owner, local):
        by_basin = lax.dot_general(
            tree_table, one_hot(local, basin_rows), NN, preferred_element_type=jnp.float32
        )
        return picked(by_basin[:owners], owner) - 1, picked(by_basin[owners:], owner)

    parent_owner, parent_local = parent_of(dest, basin)
    second_owner, second_local = parent_of(parent_owner, parent_local)

    def row_of(owner, local):
        mine = jnp.logical_and(owner >= 0, (owner & (CORES - 1)) == core)
        place = owner // CORES - 1
        place = jnp.where(place < 0, place + owners // CORES, place)
        return jnp.where(mine, place * basin_rows + local, -1)

    placements = jnp.concatenate(
        [
            one_hot(row_of(owner, local), outlets)
            for owner, local in (
                (dest, basin),
                (parent_owner, parent_local),
                (second_owner, second_local),
            )
        ],
        axis=0,
    )

    runoff = runoff_ref[...]
    by_kind = jnp.concatenate(
        [
            runoff * (kind == early + k).astype(jnp.float32).astype(jnp.bfloat16)
            for k in range(late)
        ],
        axis=0,
    )
    routed = respond(late_ref[...], by_kind)
    for k in range(early):
        routed = jnp.where(kind == k, responses_ref[k], routed)
    for step in (64, 32, 16, 8):
        routed = jnp.where((lag & step) != 0, later_rows(routed, step), routed)
    routed = turned(routed, lag & 7)
    flows = lax.dot_general(
        jnp.concatenate([placements, placements], axis=1),
        jnp.concatenate(split(routed), axis=1),
        NT,
        preferred_element_type=jnp.float32,
    )
    flow = later_lanes(flows[2 * outlets :], LINK)
    flow = later_lanes(flows[outlets : 2 * outlets] + flow, LINK)
    flow = flows[:outlets] + flow
    level = jnp.log(jnp.maximum(flow, CODE_FLOOR)) * CODE_SCALE + (CODE_ZERO + CODE_TOP + 0.5)
    level = jnp.clip(level, 0.0, 2.0 * CODE_TOP).astype(jnp.int32) - CODE_TOP
    flow_ref[...] = level.astype(jnp.int16)


def finish_kernel(parts_ref, section_hbm, section_ref, left):
    copies = []
    for j, first in enumerate(range(0, section_ref.shape[0], 16)):
        rows = pl.ds(first, 16)
        level = parts_ref[:, first : first + 16].astype(jnp.int32)
        flow = jnp.exp((level.astype(jnp.float32) - CODE_ZERO) * (1.0 / CODE_SCALE))
        flow = jnp.sum(jnp.where(level == -CODE_TOP, 0.0, flow), axis=0)
        section_ref[first : first + 16] = jnp.log(1.0 + flow)
        copies.append(pltpu.make_async_copy(section_ref.at[rows], section_hbm.at[rows], left.at[j]))
        copies[-1].start()
    for copy in copies:
        copy.wait()


def per_device(
    rain,
    soil,
    tile_area,
    tile_dest,
    tile_reach,
    reach_basin,
    reach_kind,
    reach_lag,
    irf,
    outlet_level,
    outlet_parent,
):
    owners = lax.axis_size("tile")
    tile_rows, hours = rain.shape
    basin_rows = outlet_parent.shape[0]
    kinds = irf.shape[0]
    params = pltpu.CompilerParams(vmem_limit_bytes=VMEM_BYTES)
    held = pl.BlockSpec(memory_space=pltpu.HBM)
    whole = pl.BlockSpec(memory_space=pltpu.VMEM)
    block = (tile_rows + SIDE_ROWS, hours)

    def in_hbm(values, shape):
        return pltpu.with_memory_space_constraint(values.reshape(shape), pltpu.HBM)

    numbers = [
        in_hbm(values, (1, -1))
        for values in (
            reach_basin, reach_kind, reach_lag, outlet_parent, soil, tile_area, tile_dest, tile_reach,
        )
    ]
    meta, own = pl.pallas_call(
        lambda *refs: pack_kernel(*refs, basin_rows=basin_rows),
        out_shape=(
            jax.ShapeDtypeStruct((owners * FIELDS, LANES), jnp.bfloat16),
            jax.ShapeDtypeStruct(block, jnp.bfloat16),
        ),
        in_specs=[held] * (len(numbers) + 1),
        out_specs=(held, whole),
        scratch_shapes=[pltpu.VMEM(values.shape, values.dtype) for values in numbers]
        + [
            pltpu.VMEM((owners * FIELDS, LANES), jnp.bfloat16),
            pltpu.SemaphoreType.DMA((len(numbers) + 2,)),
        ],
        compiler_params=params,
        cost_estimate=SMALL,
        name="pack",
    )(*numbers, in_hbm(rain, rain.shape))
    other = lax.ppermute(own, "tile", [(i, i ^ 1) for i in range(owners)])
    meta = lax.all_to_all(
        meta.reshape(owners, FIELDS, LANES),
        "tile",
        split_axis=0,
        concat_axis=0,
        axis_index_groups=[[*range(CORES, owners), *range(CORES)]],
        tiled=True,
    ).reshape(-1, LANES)

    chip_tiles = CORES * tile_rows
    early = kinds // 2
    prepared = pl.pallas_call(
        prepare_kernel,
        out_shape=(
            jax.ShapeDtypeStruct((hours, chip_tiles), jnp.bfloat16),
            jax.ShapeDtypeStruct((8, chip_tiles), jnp.int32),
            jax.ShapeDtypeStruct((reach_basin.size, chip_tiles), jnp.bfloat16),
            jax.ShapeDtypeStruct((hours, (kinds - early) * hours), jnp.bfloat16),
            jax.ShapeDtypeStruct((early, hours, chip_tiles), jnp.float32),
        ),
        in_specs=[held, whole, whole],
        scratch_shapes=[pltpu.VMEM(irf.shape, irf.dtype), pltpu.SemaphoreType.DMA((1,))],
        compiler_params=params,
        cost_estimate=SMALL,
        name="prepare",
    )(in_hbm(irf, irf.shape), own, other)

    flow = pl.pallas_call(
        lambda *refs: route_kernel(*refs, basin_rows=basin_rows),
        out_shape=jax.ShapeDtypeStruct((owners // CORES * basin_rows, hours), jnp.int16),
        scratch_shapes=[pltpu.VMEM(((owners + 1) * FIELDS, LANES), jnp.float32)],
        compiler_params=params,
        name="route",
    )(meta, *prepared)

    parts = lax.all_to_all(
        flow.reshape(owners // CORES, basin_rows, hours),
        "tile",
        split_axis=0,
        concat_axis=0,
        axis_index_groups=[
            [*range(CORES + core, owners, CORES), core] for core in range(CORES)
        ],
        tiled=True,
    )
    return pl.pallas_call(
        finish_kernel,
        out_shape=jax.ShapeDtypeStruct((basin_rows, hours), jnp.float32),
        out_specs=held,
        scratch_shapes=[
            pltpu.VMEM((basin_rows, hours), jnp.float32),
            pltpu.SemaphoreType.DMA((basin_rows // 16,)),
        ],
        compiler_params=params,
        name="finish",
    )(parts)


def solution(mesh):
    rows = P(("ens", "tile"))
    table = P(("ens", "tile"), None)
    in_specs = (table, rows, rows, table, rows, rows, rows, rows, P(), rows, rows)
    return jax.shard_map(
        per_device, mesh=mesh, in_specs=in_specs, out_specs=table, check_vma=False
    )
```

```python
import math

import jax
import jax.numpy as jnp
from jax import lax
from jax.experimental import pallas as pl
from jax.experimental.pallas import tpu as pltpu
from jax.sharding import PartitionSpec as P

LINK = 6
LANES = 128
CORES = 2
FIELDS = 8
SIDE_ROWS = 16
VMEM_BYTES = 40 * 1024 * 1024
CODE_TOP = 32767
CODE_OCTAVES = 44
CODE_LOWEST = -26
CODE_SCALE = 2 * CODE_TOP / (CODE_OCTAVES * math.log(2.0))
CODE_FLOOR = 2.0 ** (2 * CODE_LOWEST)
CODE_ZERO = -CODE_TOP + 1 - CODE_LOWEST * math.log(2.0) * CODE_SCALE

SMALL = pl.CostEstimate(flops=1, bytes_accessed=1, transcendentals=0)
NT = (((1,), (1,)), ((), ()))
NN = (((1,), (0,)), ((), ()))


def iota(shape, axis):
    return lax.broadcasted_iota(jnp.int32, shape, axis)


def split(values):
    high = values.astype(jnp.bfloat16)
    return high, (values - high.astype(jnp.float32)).astype(jnp.bfloat16)


def one_hot(row, count):
    return (iota((count, row.shape[1]), 0) == row).astype(jnp.float32).astype(jnp.bfloat16)


def later_rows(values, hours):
    padding = jnp.zeros((hours, values.shape[1]), values.dtype)
    return jnp.concatenate([padding, values[: values.shape[0] - hours]], axis=0)


def turned(values, hours):
    place = iota((8, values.shape[1]), 0)
    source = (place - hours) & 7
    stays = place >= hours
    before = jnp.zeros((8, values.shape[1]), values.dtype)
    rows = []
    for first in range(0, values.shape[0], 8):
        now = jnp.take_along_axis(values[first : first + 8], source, axis=0, mode="promise_in_bounds")
        rows.append(jnp.where(stays, now, before))
        before = now
    return jnp.concatenate(rows, axis=0)


def later_lanes(values, hours):
    return jnp.where(iota(values.shape, 1) < hours, 0.0, pltpu.roll(values, hours, 1))


def lane_rows(values):
    return [values[:, first : first + LANES] for first in range(0, values.shape[1], LANES)]


def parts_of(values):
    high = values.astype(jnp.bfloat16).astype(jnp.float32)
    middle = (values - high).astype(jnp.bfloat16).astype(jnp.float32)
    return [high, middle, values - high - middle]


def pack_kernel(*refs, basin_rows):
    sources, (meta_hbm, block_ref, *scratch, meta_ref, arrived) = refs[:9], refs[9:]
    tile_rows = block_ref.shape[0] - SIDE_ROWS
    targets = (*scratch, block_ref.at[pl.ds(0, tile_rows)])
    copies = [
        pltpu.make_async_copy(source, target, arrived.at[j])
        for j, (source, target) in enumerate(zip(sources, targets))
    ]
    for copy in copies:
        copy.start()
    for copy in copies[:4]:
        copy.wait()
    basin, kind, lag, parent = [ref[...] for ref in scratch[:4]]
    shift = basin_rows.bit_length() - 1
    empty = jnp.zeros((1, LANES - basin_rows), jnp.int32)
    rows = lane_rows(basin) + lane_rows(kind) + lane_rows(lag)
    rows.append(jnp.concatenate([lax.shift_right_arithmetic(parent, shift) + 1, empty], axis=1))
    rows.append(jnp.concatenate([parent & (basin_rows - 1), empty], axis=1))
    numbers = jnp.concatenate(rows, axis=0).astype(jnp.float32)
    meta_ref[...] = jnp.concatenate([numbers] * (meta_ref.shape[0] // FIELDS), axis=0).astype(jnp.bfloat16)
    leaving = pltpu.make_async_copy(meta_ref, meta_hbm, arrived.at[len(copies)])
    leaving.start()
    for copy in copies[4:8]:
        copy.wait()
    soil, area, dest, reach = [ref[...] for ref in scratch[4:]]
    sides = parts_of(soil) + parts_of(area) + [dest.astype(jnp.float32), reach.astype(jnp.float32)]
    sides = jnp.concatenate(sides + [jnp.zeros((SIDE_ROWS - len(sides), tile_rows), jnp.float32)], axis=0)
    block_ref[tile_rows:] = sides.astype(jnp.bfloat16)
    copies[8].wait()
    leaving.wait()


def prepare_kernel(
    irf_hbm, own_ref, other_ref, runoff_ref, dest_ref, reach_marks_ref, late_ref, responses_ref, irf_ref, arrived
):
    copy = pltpu.make_async_copy(irf_hbm, irf_ref, arrived.at[0])
    copy.start()
    hours = own_ref.shape[1]
    half = hours // 2
    tile_rows = own_ref.shape[0] - SIDE_ROWS
    kinds, taps = irf_ref.shape
    early = responses_ref.shape[0]
    sides = jnp.concatenate([own_ref[tile_rows:], other_ref[tile_rows:]], axis=1).astype(jnp.float32)
    rainfall = jnp.concatenate(
        [ref[:tile_rows].astype(jnp.float32).T for ref in (own_ref, other_ref)], axis=1
    )
    storage = sides[0:1] + sides[1:2] + sides[2:3]
    area = sides[3:4] + sides[4:5] + sides[5:6]
    excess = jnp.maximum(rainfall - 0.2 * storage, 0.0)
    runoff = (area * excess * excess / (rainfall + 0.8 * storage)).astype(jnp.bfloat16)
    runoff_ref[...] = runoff
    dest_ref[...] = jnp.broadcast_to(sides[6:7], dest_ref.shape).astype(jnp.int32)
    reach_marks_ref[...] = one_hot(sides[7:8].astype(jnp.int32), reach_marks_ref.shape[0])
    backward = (
        iota((taps, hours), 1) == lax.rem(hours - iota((taps, hours), 0), hours)
    ).astype(jnp.float32)
    copy.wait()
    reversed_taps = lax.dot_general(
        irf_ref[...], backward, NN, precision=lax.Precision.HIGHEST, preferred_element_type=jnp.float32
    )
    causal = iota((half, hours), 1) <= iota((half, hours), 0) + half
    for kind in range(kinds):
        row = jnp.broadcast_to(reversed_taps[kind : kind + 1], (half, hours))
        matrix = jnp.where(causal, pltpu.roll(row, half, 1, stride=1, stride_axis=0), 0.0)
        matrix = jnp.concatenate(split(matrix), axis=0)
        if kind < early:
            responses_ref[kind] = respond(matrix, runoff)
        else:
            late_ref[:, (kind - early) * hours : (kind - early + 1) * hours] = matrix


def respond(matrices, runoffs):
    hours = matrices.shape[0]
    half = hours // 2
    count = matrices.shape[1] // hours

    def halves(values, axis, first):
        pieces = [
            lax.slice_in_dim(values, j * hours + first, j * hours + first + half, axis=axis)
            for j in range(count)
        ]
        return jnp.concatenate(pieces, axis=axis)

    earlier = lax.dot_general(
        halves(matrices, 1, half), halves(runoffs, 0, 0), NN, preferred_element_type=jnp.float32
    )
    later = lax.dot_general(matrices, runoffs, NN, preferred_element_type=jnp.float32)
    return jnp.concatenate([earlier[:half] + earlier[half:], later[:half] + later[half:]], axis=0)


def route_kernel(
    meta_ref, runoff_ref, dest_ref, reach_marks_ref, late_ref, responses_ref, flow_ref, stack_ref, *, basin_rows
):
    early, hours, tiles = responses_ref.shape
    late = late_ref.shape[1] // hours
    outlets = flow_ref.shape[0]
    owners = meta_ref.shape[0] // FIELDS
    core = lax.rem(lax.axis_index("tile"), CORES)
    dest = dest_ref[0:1]

    stack_ref[: owners * FIELDS] = meta_ref[...].astype(jnp.float32)

    def table(field):
        return stack_ref[pl.ds(field, owners, stride=FIELDS), :].astype(jnp.bfloat16)

    def picked(values, owner):
        place = jnp.where(owner < 0, owners, jnp.where(owner < CORES, owner + owners, owner) - CORES)
        chosen = iota((owners, tiles), 0) == place
        return jnp.sum(jnp.where(chosen, values, 0.0), axis=0, keepdims=True).astype(jnp.int32)

    spans = (FIELDS - 2) // 3
    reach_table = jnp.concatenate(
        [
            jnp.concatenate([table(item * spans + j) for j in range(spans)], axis=1)
            for item in range(3)
        ],
        axis=0,
    )
    by_reach = lax.dot_general(
        reach_table, reach_marks_ref[...], NN, preferred_element_type=jnp.float32
    )
    basin, kind, lag = [picked(by_reach[j * owners : (j + 1) * owners], dest) for j in range(3)]
    tree_table = jnp.concatenate([table(3 * spans), table(3 * spans + 1)], axis=0)[:, :basin_rows]

    def parent_of(owner, local):
        by_basin = lax.dot_general(
            tree_table, one_hot(local, basin_rows), NN, preferred_element_type=jnp.float32
        )
        return picked(by_basin[:owners], owner) - 1, picked(by_basin[owners:], owner)

    parent_owner, parent_local = parent_of(dest, basin)
    second_owner, second_local = parent_of(parent_owner, parent_local)

    def row_of(owner, local):
        mine = jnp.logical_and(owner >= 0, (owner & (CORES - 1)) == core)
        place = owner // CORES - 1
        place = jnp.where(place < 0, place + owners // CORES, place)
        return jnp.where(mine, place * basin_rows + local, -1)

    placements = jnp.concatenate(
        [
            one_hot(row_of(owner, local), outlets)
            for owner, local in (
                (dest, basin),
                (parent_owner, parent_local),
                (second_owner, second_local),
            )
        ],
        axis=0,
    )

    runoff = runoff_ref[...]
    by_kind = jnp.concatenate(
        [
            runoff * (kind == early + k).astype(jnp.float32).astype(jnp.bfloat16)
            for k in range(late)
        ],
        axis=0,
    )
    routed = respond(late_ref[...], by_kind)
    for k in range(early):
        routed = jnp.where(kind == k, responses_ref[k], routed)
    for step in (64, 32, 16, 8):
        routed = jnp.where((lag & step) != 0, later_rows(routed, step), routed)
    routed = turned(routed, lag & 7)
    flows = lax.dot_general(
        jnp.concatenate([placements, placements], axis=1),
        jnp.concatenate(split(routed), axis=1),
        NT,
        preferred_element_type=jnp.float32,
    )
    flow = later_lanes(flows[2 * outlets :], LINK)
    flow = later_lanes(flows[outlets : 2 * outlets] + flow, LINK)
    flow = flows[:outlets] + flow
    level = jnp.log(jnp.maximum(flow, CODE_FLOOR)) * CODE_SCALE + (CODE_ZERO + CODE_TOP + 0.5)
    level = jnp.clip(level, 0.0, 2.0 * CODE_TOP).astype(jnp.int32) - CODE_TOP
    flow_ref[...] = level.astype(jnp.int16)


def finish(parts):
    level = parts.astype(jnp.float32)
    flow = jnp.exp((level - CODE_ZERO) * (1.0 / CODE_SCALE))
    return jnp.log(1.0 + jnp.sum(jnp.where(level == -CODE_TOP, 0.0, flow), axis=0))


def per_device(
    rain,
    soil,
    tile_area,
    tile_dest,
    tile_reach,
    reach_basin,
    reach_kind,
    reach_lag,
    irf,
    outlet_level,
    outlet_parent,
):
    owners = lax.axis_size("tile")
    tile_rows, hours = rain.shape
    basin_rows = outlet_parent.shape[0]
    kinds = irf.shape[0]
    params = pltpu.CompilerParams(vmem_limit_bytes=VMEM_BYTES)
    held = pl.BlockSpec(memory_space=pltpu.HBM)
    whole = pl.BlockSpec(memory_space=pltpu.VMEM)
    block = (tile_rows + SIDE_ROWS, hours)

    def in_hbm(values, shape):
        return pltpu.with_memory_space_constraint(values.reshape(shape), pltpu.HBM)

    numbers = [
        in_hbm(values, (1, -1))
        for values in (
            reach_basin, reach_kind, reach_lag, outlet_parent, soil, tile_area, tile_dest, tile_reach,
        )
    ]
    meta, own = pl.pallas_call(
        lambda *refs: pack_kernel(*refs, basin_rows=basin_rows),
        out_shape=(
            jax.ShapeDtypeStruct((owners * FIELDS, LANES), jnp.bfloat16),
            jax.ShapeDtypeStruct(block, jnp.bfloat16),
        ),
        in_specs=[held] * (len(numbers) + 1),
        out_specs=(held, whole),
        scratch_shapes=[pltpu.VMEM(values.shape, values.dtype) for values in numbers]
        + [
            pltpu.VMEM((owners * FIELDS, LANES), jnp.bfloat16),
            pltpu.SemaphoreType.DMA((len(numbers) + 2,)),
        ],
        compiler_params=params,
        cost_estimate=SMALL,
        name="pack",
    )(*numbers, in_hbm(rain, rain.shape))
    other = lax.ppermute(own, "tile", [(i, i ^ 1) for i in range(owners)])
    meta = lax.all_to_all(
        meta.reshape(owners, FIELDS, LANES),
        "tile",
        split_axis=0,
        concat_axis=0,
        axis_index_groups=[[*range(CORES, owners), *range(CORES)]],
        tiled=True,
    ).reshape(-1, LANES)

    chip_tiles = CORES * tile_rows
    early = kinds // 2
    prepared = pl.pallas_call(
        prepare_kernel,
        out_shape=(
            jax.ShapeDtypeStruct((hours, chip_tiles), jnp.bfloat16),
            jax.ShapeDtypeStruct((8, chip_tiles), jnp.int32),
            jax.ShapeDtypeStruct((reach_basin.size, chip_tiles), jnp.bfloat16),
            jax.ShapeDtypeStruct((hours, (kinds - early) * hours), jnp.bfloat16),
            jax.ShapeDtypeStruct((early, hours, chip_tiles), jnp.float32),
        ),
        in_specs=[held, whole, whole],
        scratch_shapes=[pltpu.VMEM(irf.shape, irf.dtype), pltpu.SemaphoreType.DMA((1,))],
        compiler_params=params,
        cost_estimate=SMALL,
        name="prepare",
    )(in_hbm(irf, irf.shape), own, other)

    flow = pl.pallas_call(
        lambda *refs: route_kernel(*refs, basin_rows=basin_rows),
        out_shape=jax.ShapeDtypeStruct((owners // CORES * basin_rows, hours), jnp.int16),
        scratch_shapes=[pltpu.VMEM(((owners + 1) * FIELDS, LANES), jnp.float32)],
        compiler_params=params,
        name="route",
    )(meta, *prepared)

    parts = lax.all_to_all(
        flow.reshape(owners // CORES, basin_rows, hours),
        "tile",
        split_axis=0,
        concat_axis=0,
        axis_index_groups=[
            [*range(CORES + core, owners, CORES), core] for core in range(CORES)
        ],
        tiled=True,
    )
    return finish(parts)


def solution(mesh):
    rows = P(("ens", "tile"))
    table = P(("ens", "tile"), None)
    in_specs = (table, rows, rows, table, rows, rows, rows, rows, P(), rows, rows)
    return jax.shard_map(
        per_device, mesh=mesh, in_specs=in_specs, out_specs=table, check_vma=False
    )
```

```python
import math

import jax
import jax.numpy as jnp
from jax import lax
from jax.experimental import pallas as pl
from jax.experimental.pallas import tpu as pltpu
from jax.sharding import PartitionSpec as P

LINK = 6
LANES = 128
CORES = 2
FIELDS = 8
SIDE_ROWS = 16
VMEM_BYTES = 40 * 1024 * 1024
CODE_TOP = 32767
CODE_OCTAVES = 44
CODE_LOWEST = -26
CODE_SCALE = 2 * CODE_TOP / (CODE_OCTAVES * math.log(2.0))
CODE_FLOOR = 2.0 ** (2 * CODE_LOWEST)
CODE_ZERO = -CODE_TOP + 1 - CODE_LOWEST * math.log(2.0) * CODE_SCALE

SMALL = pl.CostEstimate(flops=1, bytes_accessed=1, transcendentals=0)
NT = (((1,), (1,)), ((), ()))
NN = (((1,), (0,)), ((), ()))


def iota(shape, axis):
    return lax.broadcasted_iota(jnp.int32, shape, axis)


def split(values):
    high = values.astype(jnp.bfloat16)
    return high, (values - high.astype(jnp.float32)).astype(jnp.bfloat16)


def one_hot(row, count):
    return (iota((count, row.shape[1]), 0) == row).astype(jnp.float32).astype(jnp.bfloat16)


def moves(owners):
    quarter = owners // 4
    return ((2 * quarter, quarter - CORES), (3 * quarter, -quarter - CORES))


def place_of(owner, owners):
    if owner < CORES:
        return owner + owners - CORES
    place = owner - CORES
    for start, moved in moves(owners):
        place = owner + moved if owner >= start else place
    return place


def later_rows(values, hours):
    padding = jnp.zeros((hours, values.shape[1]), values.dtype)
    return jnp.concatenate([padding, values[: values.shape[0] - hours]], axis=0)


def turned(values, hours):
    place = iota((8, values.shape[1]), 0)
    source = (place - hours) & 7
    stays = place >= hours
    before = jnp.zeros((8, values.shape[1]), values.dtype)
    rows = []
    for first in range(0, values.shape[0], 8):
        now = jnp.take_along_axis(values[first : first + 8], source, axis=0, mode="promise_in_bounds")
        rows.append(jnp.where(stays, now, before))
        before = now
    return jnp.concatenate(rows, axis=0)


def later_lanes(values, hours):
    return jnp.where(iota(values.shape, 1) < hours, 0.0, pltpu.roll(values, hours, 1))


def lane_rows(values):
    return [values[:, first : first + LANES] for first in range(0, values.shape[1], LANES)]


def parts_of(values):
    high = values.astype(jnp.bfloat16).astype(jnp.float32)
    middle = (values - high).astype(jnp.bfloat16).astype(jnp.float32)
    return [high, middle, values - high - middle]


def pack_kernel(*refs, basin_rows):
    sources, (meta_hbm, block_ref, *scratch, meta_ref, arrived) = refs[:9], refs[9:]
    tile_rows = block_ref.shape[0] - SIDE_ROWS
    targets = (*scratch, block_ref.at[pl.ds(0, tile_rows)])
    copies = [
        pltpu.make_async_copy(source, target, arrived.at[j])
        for j, (source, target) in enumerate(zip(sources, targets))
    ]
    for copy in copies:
        copy.start()
    for copy in copies[:4]:
        copy.wait()
    basin, kind, lag, parent = [ref[...] for ref in scratch[:4]]
    shift = basin_rows.bit_length() - 1
    empty = jnp.zeros((1, LANES - basin_rows), jnp.int32)
    rows = lane_rows(basin) + lane_rows(kind) + lane_rows(lag)
    rows.append(jnp.concatenate([lax.shift_right_arithmetic(parent, shift) + 1, empty], axis=1))
    rows.append(jnp.concatenate([parent & (basin_rows - 1), empty], axis=1))
    numbers = jnp.concatenate(rows, axis=0).astype(jnp.float32)
    meta_ref[...] = jnp.concatenate([numbers] * (meta_ref.shape[0] // FIELDS), axis=0).astype(jnp.bfloat16)
    leaving = pltpu.make_async_copy(meta_ref, meta_hbm, arrived.at[len(copies)])
    leaving.start()
    for copy in copies[4:8]:
        copy.wait()
    soil, area, dest, reach = [ref[...] for ref in scratch[4:]]
    sides = parts_of(soil) + parts_of(area) + [dest.astype(jnp.float32), reach.astype(jnp.float32)]
    sides = jnp.concatenate(sides + [jnp.zeros((SIDE_ROWS - len(sides), tile_rows), jnp.float32)], axis=0)
    block_ref[tile_rows:] = sides.astype(jnp.bfloat16)
    copies[8].wait()
    leaving.wait()


def prepare_kernel(
    irf_hbm, own_ref, other_ref, runoff_ref, dest_ref, reach_marks_ref, late_ref, responses_ref, irf_ref, arrived
):
    copy = pltpu.make_async_copy(irf_hbm, irf_ref, arrived.at[0])
    copy.start()
    hours = own_ref.shape[1]
    half = hours // 2
    tile_rows = own_ref.shape[0] - SIDE_ROWS
    kinds, taps = irf_ref.shape
    early = responses_ref.shape[0]
    sides = jnp.concatenate([own_ref[tile_rows:], other_ref[tile_rows:]], axis=1).astype(jnp.float32)
    rainfall = jnp.concatenate(
        [ref[:tile_rows].astype(jnp.float32).T for ref in (own_ref, other_ref)], axis=1
    )
    storage = sides[0:1] + sides[1:2] + sides[2:3]
    area = sides[3:4] + sides[4:5] + sides[5:6]
    excess = jnp.maximum(rainfall - 0.2 * storage, 0.0)
    runoff = (area * excess * excess / (rainfall + 0.8 * storage)).astype(jnp.bfloat16)
    runoff_ref[...] = runoff
    dest_ref[...] = jnp.broadcast_to(sides[6:7], dest_ref.shape).astype(jnp.int32)
    reach_marks_ref[...] = one_hot(sides[7:8].astype(jnp.int32), reach_marks_ref.shape[0])
    backward = (
        iota((taps, hours), 1) == lax.rem(hours - iota((taps, hours), 0), hours)
    ).astype(jnp.float32)
    copy.wait()
    reversed_taps = lax.dot_general(
        irf_ref[...], backward, NN, precision=lax.Precision.HIGHEST, preferred_element_type=jnp.float32
    )
    causal = iota((half, hours), 1) <= iota((half, hours), 0) + half
    for kind in range(kinds):
        row = jnp.broadcast_to(reversed_taps[kind : kind + 1], (half, hours))
        matrix = jnp.where(causal, pltpu.roll(row, half, 1, stride=1, stride_axis=0), 0.0)
        matrix = jnp.concatenate(split(matrix), axis=0)
        if kind < early:
            responses_ref[kind] = respond(matrix, runoff)
        else:
            late_ref[:, (kind - early) * hours : (kind - early + 1) * hours] = matrix


def respond(matrices, runoffs):
    hours = matrices.shape[0]
    half = hours // 2
    count = matrices.shape[1] // hours

    def halves(values, axis, first):
        pieces = [
            lax.slice_in_dim(values, j * hours + first, j * hours + first + half, axis=axis)
            for j in range(count)
        ]
        return jnp.concatenate(pieces, axis=axis)

    earlier = lax.dot_general(
        halves(matrices, 1, half), halves(runoffs, 0, 0), NN, preferred_element_type=jnp.float32
    )
    later = lax.dot_general(matrices, runoffs, NN, preferred_element_type=jnp.float32)
    return jnp.concatenate([earlier[:half] + earlier[half:], later[:half] + later[half:]], axis=0)


def route_kernel(
    meta_ref, runoff_ref, dest_ref, reach_marks_ref, late_ref, responses_ref, flow_ref, stack_ref, *, basin_rows
):
    early, hours, tiles = responses_ref.shape
    late = late_ref.shape[1] // hours
    outlets = flow_ref.shape[0]
    owners = meta_ref.shape[0] // FIELDS
    core = lax.rem(lax.axis_index("tile"), CORES)
    dest = dest_ref[0:1]

    stack_ref[: owners * FIELDS] = meta_ref[...].astype(jnp.float32)

    def table(field):
        return stack_ref[pl.ds(field, owners, stride=FIELDS), :].astype(jnp.bfloat16)

    def picked(values, owner):
        place = owner - CORES
        for start, moved in moves(owners):
            place = jnp.where(owner >= start, owner + moved, place)
        place = jnp.where(owner < CORES, owner + owners - CORES, place)
        chosen = iota((owners, tiles), 0) == jnp.where(owner < 0, owners, place)
        return jnp.sum(jnp.where(chosen, values, 0.0), axis=0, keepdims=True).astype(jnp.int32)

    spans = (FIELDS - 2) // 3
    reach_table = jnp.concatenate(
        [
            jnp.concatenate([table(item * spans + j) for j in range(spans)], axis=1)
            for item in range(3)
        ],
        axis=0,
    )
    by_reach = lax.dot_general(
        reach_table, reach_marks_ref[...], NN, preferred_element_type=jnp.float32
    )
    basin, kind, lag = [picked(by_reach[j * owners : (j + 1) * owners], dest) for j in range(3)]
    tree_table = jnp.concatenate([table(3 * spans), table(3 * spans + 1)], axis=0)[:, :basin_rows]

    def parent_of(owner, local):
        by_basin = lax.dot_general(
            tree_table, one_hot(local, basin_rows), NN, preferred_element_type=jnp.float32
        )
        return picked(by_basin[:owners], owner) - 1, picked(by_basin[owners:], owner)

    parent_owner, parent_local = parent_of(dest, basin)
    second_owner, second_local = parent_of(parent_owner, parent_local)

    def row_of(owner, local):
        mine = jnp.logical_and(owner >= 0, (owner & (CORES - 1)) == core)
        place = owner // CORES - 1
        place = jnp.where(place < 0, place + owners // CORES, place)
        return jnp.where(mine, place * basin_rows + local, -1)

    placements = jnp.concatenate(
        [
            one_hot(row_of(owner, local), outlets)
            for owner, local in (
                (dest, basin),
                (parent_owner, parent_local),
                (second_owner, second_local),
            )
        ],
        axis=0,
    )

    runoff = runoff_ref[...]
    by_kind = jnp.concatenate(
        [
            runoff * (kind == early + k).astype(jnp.float32).astype(jnp.bfloat16)
            for k in range(late)
        ],
        axis=0,
    )
    routed = respond(late_ref[...], by_kind)
    for k in range(early):
        routed = jnp.where(kind == k, responses_ref[k], routed)
    for step in (64, 32, 16, 8):
        routed = jnp.where((lag & step) != 0, later_rows(routed, step), routed)
    routed = turned(routed, lag & 7)
    flows = lax.dot_general(
        jnp.concatenate([placements, placements], axis=1),
        jnp.concatenate(split(routed), axis=1),
        NT,
        preferred_element_type=jnp.float32,
    )
    flow = later_lanes(flows[2 * outlets :], LINK)
    flow = later_lanes(flows[outlets : 2 * outlets] + flow, LINK)
    flow = flows[:outlets] + flow
    level = jnp.log(jnp.maximum(flow, CODE_FLOOR)) * CODE_SCALE + (CODE_ZERO + CODE_TOP + 0.5)
    level = jnp.clip(level, 0.0, 2.0 * CODE_TOP).astype(jnp.int32) - CODE_TOP
    flow_ref[...] = level.astype(jnp.int16)


def finish_kernel(parts_ref, section_ref):
    level = parts_ref[...].astype(jnp.int32)
    flow = jnp.exp((level.astype(jnp.float32) - CODE_ZERO) * (1.0 / CODE_SCALE))
    flow = jnp.sum(jnp.where(level == -CODE_TOP, 0.0, flow), axis=0)
    section_ref[...] = jnp.log(1.0 + flow)


def per_device(
    rain,
    soil,
    tile_area,
    tile_dest,
    tile_reach,
    reach_basin,
    reach_kind,
    reach_lag,
    irf,
    outlet_level,
    outlet_parent,
):
    owners = lax.axis_size("tile")
    tile_rows, hours = rain.shape
    basin_rows = outlet_parent.shape[0]
    kinds = irf.shape[0]
    params = pltpu.CompilerParams(vmem_limit_bytes=VMEM_BYTES)
    held = pl.BlockSpec(memory_space=pltpu.HBM)
    whole = pl.BlockSpec(memory_space=pltpu.VMEM)
    block = (tile_rows + SIDE_ROWS, hours)

    def in_hbm(values, shape):
        return pltpu.with_memory_space_constraint(values.reshape(shape), pltpu.HBM)

    numbers = [
        in_hbm(values, (1, -1))
        for values in (
            reach_basin, reach_kind, reach_lag, outlet_parent, soil, tile_area, tile_dest, tile_reach,
        )
    ]
    meta, own = pl.pallas_call(
        lambda *refs: pack_kernel(*refs, basin_rows=basin_rows),
        out_shape=(
            jax.ShapeDtypeStruct((owners * FIELDS, LANES), jnp.bfloat16),
            jax.ShapeDtypeStruct(block, jnp.bfloat16),
        ),
        in_specs=[held] * (len(numbers) + 1),
        out_specs=(held, whole),
        scratch_shapes=[pltpu.VMEM(values.shape, values.dtype) for values in numbers]
        + [
            pltpu.VMEM((owners * FIELDS, LANES), jnp.bfloat16),
            pltpu.SemaphoreType.DMA((len(numbers) + 2,)),
        ],
        compiler_params=params,
        cost_estimate=SMALL,
        name="pack",
    )(*numbers, in_hbm(rain, rain.shape))
    other = lax.ppermute(own, "tile", [(i, i ^ 1) for i in range(owners)])
    meta = lax.all_to_all(
        meta.reshape(owners, FIELDS, LANES),
        "tile",
        split_axis=0,
        concat_axis=0,
        axis_index_groups=[sorted(range(owners), key=lambda owner: place_of(owner, owners))],
        tiled=True,
    ).reshape(-1, LANES)

    chip_tiles = CORES * tile_rows
    early = kinds // 2
    prepared = pl.pallas_call(
        prepare_kernel,
        out_shape=(
            jax.ShapeDtypeStruct((hours, chip_tiles), jnp.bfloat16),
            jax.ShapeDtypeStruct((8, chip_tiles), jnp.int32),
            jax.ShapeDtypeStruct((reach_basin.size, chip_tiles), jnp.bfloat16),
            jax.ShapeDtypeStruct((hours, (kinds - early) * hours), jnp.bfloat16),
            jax.ShapeDtypeStruct((early, hours, chip_tiles), jnp.float32),
        ),
        in_specs=[held, whole, whole],
        scratch_shapes=[pltpu.VMEM(irf.shape, irf.dtype), pltpu.SemaphoreType.DMA((1,))],
        compiler_params=params,
        cost_estimate=SMALL,
        name="prepare",
    )(in_hbm(irf, irf.shape), own, other)

    flow = pl.pallas_call(
        lambda *refs: route_kernel(*refs, basin_rows=basin_rows),
        out_shape=jax.ShapeDtypeStruct((owners // CORES * basin_rows, hours), jnp.int16),
        scratch_shapes=[pltpu.VMEM(((owners + 1) * FIELDS, LANES), jnp.float32)],
        compiler_params=params,
        name="route",
    )(meta, *prepared)

    parts = lax.all_to_all(
        flow.reshape(owners // CORES, basin_rows, hours),
        "tile",
        split_axis=0,
        concat_axis=0,
        axis_index_groups=[
            [*range(CORES + core, owners, CORES), core] for core in range(CORES)
        ],
        tiled=True,
    )
    return pl.pallas_call(
        finish_kernel,
        out_shape=jax.ShapeDtypeStruct((basin_rows, hours), jnp.float32),
        compiler_params=params,
        name="finish",
    )(parts)


def solution(mesh):
    rows = P(("ens", "tile"))
    table = P(("ens", "tile"), None)
    in_specs = (table, rows, rows, table, rows, rows, rows, rows, P(), rows, rows)
    return jax.shard_map(
        per_device, mesh=mesh, in_specs=in_specs, out_specs=table, check_vma=False
    )
```

```python
import math

import jax
import jax.numpy as jnp
from jax import lax
from jax.experimental import pallas as pl
from jax.experimental.pallas import tpu as pltpu
from jax.sharding import PartitionSpec as P

LINK = 6
LANES = 128
CORES = 2
FIELDS = 8
SIDE_ROWS = 16
VMEM_BYTES = 40 * 1024 * 1024
CODE_TOP = 32767
CODE_OCTAVES = 44
CODE_LOWEST = -26
CODE_SCALE = 2 * CODE_TOP / (CODE_OCTAVES * math.log(2.0))
CODE_FLOOR = 2.0 ** (2 * CODE_LOWEST)
CODE_ZERO = -CODE_TOP + 1 - CODE_LOWEST * math.log(2.0) * CODE_SCALE

SMALL = pl.CostEstimate(flops=1, bytes_accessed=1, transcendentals=0)
NT = (((1,), (1,)), ((), ()))
NN = (((1,), (0,)), ((), ()))


def iota(shape, axis):
    return lax.broadcasted_iota(jnp.int32, shape, axis)


def split(values):
    high = values.astype(jnp.bfloat16)
    return high, (values - high.astype(jnp.float32)).astype(jnp.bfloat16)


def one_hot(row, count):
    return (iota((count, row.shape[1]), 0) == row).astype(jnp.float32).astype(jnp.bfloat16)


def later_rows(values, hours):
    padding = jnp.zeros((hours, values.shape[1]), values.dtype)
    return jnp.concatenate([padding, values[: values.shape[0] - hours]], axis=0)


def turned(values, hours):
    place = iota((8, values.shape[1]), 0)
    source = (place - hours) & 7
    stays = place >= hours
    before = jnp.zeros((8, values.shape[1]), values.dtype)
    rows = []
    for first in range(0, values.shape[0], 8):
        now = jnp.take_along_axis(values[first : first + 8], source, axis=0, mode="promise_in_bounds")
        rows.append(jnp.where(stays, now, before))
        before = now
    return jnp.concatenate(rows, axis=0)


def later_lanes(values, hours):
    return jnp.where(iota(values.shape, 1) < hours, 0.0, pltpu.roll(values, hours, 1))


def lane_rows(values):
    return [values[:, first : first + LANES] for first in range(0, values.shape[1], LANES)]


def parts_of(values):
    high = values.astype(jnp.bfloat16).astype(jnp.float32)
    middle = (values - high).astype(jnp.bfloat16).astype(jnp.float32)
    return [high, middle, values - high - middle]


def pack_kernel(*refs, basin_rows):
    sources, (meta_hbm, block_ref, *scratch, meta_ref, arrived) = refs[:9], refs[9:]
    tile_rows = block_ref.shape[0] - SIDE_ROWS
    targets = (*scratch, block_ref.at[pl.ds(0, tile_rows)])
    copies = [
        pltpu.make_async_copy(source, target, arrived.at[j])
        for j, (source, target) in enumerate(zip(sources, targets))
    ]
    for copy in copies:
        copy.start()
    for copy in copies[:4]:
        copy.wait()
    basin, kind, lag, parent = [ref[...] for ref in scratch[:4]]
    shift = basin_rows.bit_length() - 1
    empty = jnp.zeros((1, LANES - basin_rows), jnp.int32)
    rows = lane_rows(basin) + lane_rows(kind) + lane_rows(lag)
    rows.append(jnp.concatenate([lax.shift_right_arithmetic(parent, shift) + 1, empty], axis=1))
    rows.append(jnp.concatenate([parent & (basin_rows - 1), empty], axis=1))
    numbers = jnp.concatenate(rows, axis=0).astype(jnp.float32)
    meta_ref[...] = jnp.concatenate([numbers] * (meta_ref.shape[0] // FIELDS), axis=0).astype(jnp.bfloat16)
    leaving = pltpu.make_async_copy(meta_ref, meta_hbm, arrived.at[len(copies)])
    leaving.start()
    for copy in copies[4:8]:
        copy.wait()
    soil, area, dest, reach = [ref[...] for ref in scratch[4:]]
    sides = parts_of(soil) + parts_of(area) + [dest.astype(jnp.float32), reach.astype(jnp.float32)]
    sides = jnp.concatenate(sides + [jnp.zeros((SIDE_ROWS - len(sides), tile_rows), jnp.float32)], axis=0)
    block_ref[tile_rows:] = sides.astype(jnp.bfloat16)
    copies[8].wait()
    leaving.wait()


def prepare_kernel(
    irf_hbm, own_ref, other_ref, runoff_ref, dest_ref, reach_marks_ref, late_ref, responses_ref, irf_ref, arrived
):
    copy = pltpu.make_async_copy(irf_hbm, irf_ref, arrived.at[0])
    copy.start()
    hours = own_ref.shape[1]
    half = hours // 2
    tile_rows = own_ref.shape[0] - SIDE_ROWS
    kinds, taps = irf_ref.shape
    early = responses_ref.shape[0]
    sides = jnp.concatenate([own_ref[tile_rows:], other_ref[tile_rows:]], axis=1).astype(jnp.float32)
    rainfall = jnp.concatenate(
        [ref[:tile_rows].astype(jnp.float32).T for ref in (own_ref, other_ref)], axis=1
    )
    storage = sides[0:1] + sides[1:2] + sides[2:3]
    area = sides[3:4] + sides[4:5] + sides[5:6]
    excess = jnp.maximum(rainfall - 0.2 * storage, 0.0)
    runoff = (area * excess * excess / (rainfall + 0.8 * storage)).astype(jnp.bfloat16)
    runoff_ref[...] = runoff
    dest_ref[...] = jnp.broadcast_to(sides[6:7], dest_ref.shape).astype(jnp.int32)
    reach_marks_ref[...] = one_hot(sides[7:8].astype(jnp.int32), reach_marks_ref.shape[0])
    backward = (
        iota((taps, hours), 1) == lax.rem(hours - iota((taps, hours), 0), hours)
    ).astype(jnp.float32)
    copy.wait()
    reversed_taps = lax.dot_general(
        irf_ref[...], backward, NN, precision=lax.Precision.HIGHEST, preferred_element_type=jnp.float32
    )
    causal = iota((half, hours), 1) <= iota((half, hours), 0) + half
    for kind in range(kinds):
        row = jnp.broadcast_to(reversed_taps[kind : kind + 1], (half, hours))
        matrix = jnp.where(causal, pltpu.roll(row, half, 1, stride=1, stride_axis=0), 0.0)
        matrix = jnp.concatenate(split(matrix), axis=0)
        if kind < early:
            responses_ref[kind] = respond(matrix, runoff)
        else:
            late_ref[:, (kind - early) * hours : (kind - early + 1) * hours] = matrix


def respond(matrices, runoffs):
    hours = matrices.shape[0]
    half = hours // 2
    count = matrices.shape[1] // hours

    def halves(values, axis, first):
        pieces = [
            lax.slice_in_dim(values, j * hours + first, j * hours + first + half, axis=axis)
            for j in range(count)
        ]
        return jnp.concatenate(pieces, axis=axis)

    earlier = lax.dot_general(
        halves(matrices, 1, half), halves(runoffs, 0, 0), NN, preferred_element_type=jnp.float32
    )
    later = lax.dot_general(matrices, runoffs, NN, preferred_element_type=jnp.float32)
    return jnp.concatenate([earlier[:half] + earlier[half:], later[:half] + later[half:]], axis=0)


def route_kernel(
    meta_ref, runoff_ref, dest_ref, reach_marks_ref, late_ref, responses_ref, flow_ref, stack_ref, *, basin_rows
):
    early, hours, tiles = responses_ref.shape
    late = late_ref.shape[1] // hours
    outlets = flow_ref.shape[0]
    owners = meta_ref.shape[0] // FIELDS
    core = lax.rem(lax.axis_index("tile"), CORES)
    dest = dest_ref[0:1]

    stack_ref[: owners * FIELDS] = meta_ref[...].astype(jnp.float32)

    def table(field):
        return stack_ref[pl.ds(field, owners, stride=FIELDS), :].astype(jnp.bfloat16)

    def picked(values, owner):
        place = jnp.where(owner < 2 * CORES, owner + owners - 3 * CORES, owner - 2 * CORES)
        place = jnp.where(owner < CORES, owner + owners - CORES, place)
        place = jnp.where(owner < 0, owners, place)
        chosen = iota((owners, tiles), 0) == place
        return jnp.sum(jnp.where(chosen, values, 0.0), axis=0, keepdims=True).astype(jnp.int32)

    spans = (FIELDS - 2) // 3
    reach_table = jnp.concatenate(
        [
            jnp.concatenate([table(item * spans + j) for j in range(spans)], axis=1)
            for item in range(3)
        ],
        axis=0,
    )
    by_reach = lax.dot_general(
        reach_table, reach_marks_ref[...], NN, preferred_element_type=jnp.float32
    )
    basin, kind, lag = [picked(by_reach[j * owners : (j + 1) * owners], dest) for j in range(3)]
    tree_table = jnp.concatenate([table(3 * spans), table(3 * spans + 1)], axis=0)[:, :basin_rows]

    def parent_of(owner, local):
        by_basin = lax.dot_general(
            tree_table, one_hot(local, basin_rows), NN, preferred_element_type=jnp.float32
        )
        return picked(by_basin[:owners], owner) - 1, picked(by_basin[owners:], owner)

    parent_owner, parent_local = parent_of(dest, basin)
    second_owner, second_local = parent_of(parent_owner, parent_local)

    def row_of(owner, local):
        mine = jnp.logical_and(owner >= 0, (owner & (CORES - 1)) == core)
        place = owner // CORES - 1
        place = jnp.where(place < 0, place + owners // CORES, place)
        return jnp.where(mine, place * basin_rows + local, -1)

    placements = jnp.concatenate(
        [
            one_hot(row_of(owner, local), outlets)
            for owner, local in (
                (dest, basin),
                (parent_owner, parent_local),
                (second_owner, second_local),
            )
        ],
        axis=0,
    )

    runoff = runoff_ref[...]
    by_kind = jnp.concatenate(
        [
            runoff * (kind == early + k).astype(jnp.float32).astype(jnp.bfloat16)
            for k in range(late)
        ],
        axis=0,
    )
    routed = respond(late_ref[...], by_kind)
    for k in range(early):
        routed = jnp.where(kind == k, responses_ref[k], routed)
    for step in (64, 32, 16, 8):
        routed = jnp.where((lag & step) != 0, later_rows(routed, step), routed)
    routed = turned(routed, lag & 7)
    flows = lax.dot_general(
        jnp.concatenate([placements, placements], axis=1),
        jnp.concatenate(split(routed), axis=1),
        NT,
        preferred_element_type=jnp.float32,
    )
    flow = later_lanes(flows[2 * outlets :], LINK)
    flow = later_lanes(flows[outlets : 2 * outlets] + flow, LINK)
    flow = flows[:outlets] + flow
    level = jnp.log(jnp.maximum(flow, CODE_FLOOR)) * CODE_SCALE + (CODE_ZERO + CODE_TOP + 0.5)
    level = jnp.clip(level, 0.0, 2.0 * CODE_TOP).astype(jnp.int32) - CODE_TOP
    flow_ref[...] = level.astype(jnp.int16)


def finish_kernel(parts_ref, section_ref):
    level = parts_ref[...].astype(jnp.int32)
    flow = jnp.exp((level.astype(jnp.float32) - CODE_ZERO) * (1.0 / CODE_SCALE))
    flow = jnp.sum(jnp.where(level == -CODE_TOP, 0.0, flow), axis=0)
    section_ref[...] = jnp.log(1.0 + flow)


def per_device(
    rain,
    soil,
    tile_area,
    tile_dest,
    tile_reach,
    reach_basin,
    reach_kind,
    reach_lag,
    irf,
    outlet_level,
    outlet_parent,
):
    owners = lax.axis_size("tile")
    tile_rows, hours = rain.shape
    basin_rows = outlet_parent.shape[0]
    kinds = irf.shape[0]
    params = pltpu.CompilerParams(vmem_limit_bytes=VMEM_BYTES)
    held = pl.BlockSpec(memory_space=pltpu.HBM)
    whole = pl.BlockSpec(memory_space=pltpu.VMEM)
    block = (tile_rows + SIDE_ROWS, hours)

    def in_hbm(values, shape):
        return pltpu.with_memory_space_constraint(values.reshape(shape), pltpu.HBM)

    numbers = [
        in_hbm(values, (1, -1))
        for values in (
            reach_basin, reach_kind, reach_lag, outlet_parent, soil, tile_area, tile_dest, tile_reach,
        )
    ]
    meta, own = pl.pallas_call(
        lambda *refs: pack_kernel(*refs, basin_rows=basin_rows),
        out_shape=(
            jax.ShapeDtypeStruct((owners * FIELDS, LANES), jnp.bfloat16),
            jax.ShapeDtypeStruct(block, jnp.bfloat16),
        ),
        in_specs=[held] * (len(numbers) + 1),
        out_specs=(held, whole),
        scratch_shapes=[pltpu.VMEM(values.shape, values.dtype) for values in numbers]
        + [
            pltpu.VMEM((owners * FIELDS, LANES), jnp.bfloat16),
            pltpu.SemaphoreType.DMA((len(numbers) + 2,)),
        ],
        compiler_params=params,
        cost_estimate=SMALL,
        name="pack",
    )(*numbers, in_hbm(rain, rain.shape))
    other = lax.ppermute(own, "tile", [(i, i ^ 1) for i in range(owners)])
    meta = lax.all_to_all(
        meta.reshape(owners, FIELDS, LANES),
        "tile",
        split_axis=0,
        concat_axis=0,
        axis_index_groups=[
            [*range(2 * CORES, owners), *range(CORES, 2 * CORES), *range(CORES)]
        ],
        tiled=True,
    ).reshape(-1, LANES)

    chip_tiles = CORES * tile_rows
    early = kinds // 2
    prepared = pl.pallas_call(
        prepare_kernel,
        out_shape=(
            jax.ShapeDtypeStruct((hours, chip_tiles), jnp.bfloat16),
            jax.ShapeDtypeStruct((8, chip_tiles), jnp.int32),
            jax.ShapeDtypeStruct((reach_basin.size, chip_tiles), jnp.bfloat16),
            jax.ShapeDtypeStruct((hours, (kinds - early) * hours), jnp.bfloat16),
            jax.ShapeDtypeStruct((early, hours, chip_tiles), jnp.float32),
        ),
        in_specs=[held, whole, whole],
        scratch_shapes=[pltpu.VMEM(irf.shape, irf.dtype), pltpu.SemaphoreType.DMA((1,))],
        compiler_params=params,
        cost_estimate=SMALL,
        name="prepare",
    )(in_hbm(irf, irf.shape), own, other)

    flow = pl.pallas_call(
        lambda *refs: route_kernel(*refs, basin_rows=basin_rows),
        out_shape=jax.ShapeDtypeStruct((owners // CORES * basin_rows, hours), jnp.int16),
        scratch_shapes=[pltpu.VMEM(((owners + 1) * FIELDS, LANES), jnp.float32)],
        compiler_params=params,
        name="route",
    )(meta, *prepared)

    parts = lax.all_to_all(
        flow.reshape(owners // CORES, basin_rows, hours),
        "tile",
        split_axis=0,
        concat_axis=0,
        axis_index_groups=[
            [*range(CORES + core, owners, CORES), core] for core in range(CORES)
        ],
        tiled=True,
    )
    return pl.pallas_call(
        finish_kernel,
        out_shape=jax.ShapeDtypeStruct((basin_rows, hours), jnp.float32),
        compiler_params=params,
        name="finish",
    )(parts)


def solution(mesh):
    rows = P(("ens", "tile"))
    table = P(("ens", "tile"), None)
    in_specs = (table, rows, rows, table, rows, rows, rows, rows, P(), rows, rows)
    return jax.shard_map(
        per_device, mesh=mesh, in_specs=in_specs, out_specs=table, check_vma=False
    )
```
